32 devices in a mesh: dp: 4 (over x, core), row: 2 (over y), col: 4 (over z).
Axes of the slice: x: 2, y: 2, z: 4, core: 2. Of those that a mesh axis runs over, the one named last changes fastest.
Arguments:
- tokens_in: bfloat16 [8192, 1536], P(('dp', 'row')), may hold values from -6 to 6
- segment_ids: int32 [4, 2048], P('dp'), may hold values from 0 to 3, never falling along the last dimension, each value on 1 to 1024 neighbouring positions
- norm_gain: float32 [1536], replicated, may hold values from 0.5 to 1.5
- proj_gate: bfloat16 [1536, 3072], P('col', 'row'), may hold values from -0.15625 to 0.15625
- proj_inner: bfloat16 [1536, 3072], P('col', 'row'), may hold values from -0.15625 to 0.15625
- proj_step: bfloat16 [1536, 48], P('col', 'row'), may hold values from -0.15625 to 0.15625
- proj_states: bfloat16 [1536, 256], replicated, may hold values from -0.15625 to 0.15625
- conv_inner: float32 [4, 3072], P(None, ('row', 'col')), may hold values from -3 to 3
- conv_inner_bias: float32 [3072], P(('row', 'col')), may hold values from -1.5 to 1.5
- conv_states: float32 [4, 256], replicated, may hold values from -3 to 3
- conv_states_bias: float32 [256], replicated, may hold values from -1.5 to 1.5
- step_bias: float32 [48], P(('row', 'col')), may hold values from -6 to -1
- decay_log: float32 [48], P(('row', 'col')), may hold values from 0 to 2.77
- skip_gain: float32 [48], P(('row', 'col')), may hold values from 0.5 to 1.5
- gate_gain: float32 [3072], P(('row', 'col')), may hold values from 0.5 to 1.5
- proj_out: bfloat16 [3072, 1536], P('row', 'col'), may hold values from -0.109375 to 0.109375
- cotangent: bfloat16 [8192, 1536], P(('dp', 'row'), 'col'), may hold values from -6 to 6
Outputs:
- mixed_out: bfloat16 [8192, 1536], P(('dp', 'row'), 'col')
- grad_tokens: bfloat16 [8192, 1536], P(('dp', 'row'), 'col')
- grad_norm_gain: float32 [1536], P('col')
- grad_proj_gate: float32 [1536, 3072], P('col', 'row')
- grad_proj_inner: float32 [1536, 3072], P('col', 'row')
- grad_proj_step: float32 [1536, 48], P('col', 'row')
- grad_proj_states: float32 [1536, 256], replicated
- grad_conv_inner: float32 [4, 3072], P(None, ('row', 'col'))
- grad_conv_inner_bias: float32 [3072], P(('row', 'col'))
- grad_conv_states: float32 [4, 256], replicated
- grad_conv_states_bias: float32 [256], replicated
- grad_step_bias: float32 [48], P(('row', 'col'))
- grad_decay_log: float32 [48], P(('row', 'col'))
- grad_skip_gain: float32 [48], P(('row', 'col'))
- grad_gate_gain: float32 [3072], P(('row', 'col'))
- grad_proj_out: float32 [3072, 1536], P('row', 'col')
The draws below stay inside these ranges and needn't reach their ends.
Inputs may be any that keep to these rules, and one draw needn't show every extreme that they name: `segment_ids`: in each sequence the numbers never fall; each number covers 1 to 1024 consecutive positions, and some number covers exactly 1024.
All inputs are finite; a program needn't handle non-finite values.
Results may differ from the reference program's by a relative error of at most 0.01.
Values may be sent and summed in bfloat16 or wider, within the bound.
A program may use at most 256 MiB of HBM per device.

```python
import math
import jax
import jax.numpy as jnp
import numpy as np
from jax import lax

D = 1536
HEADS = 48
STATE = 128
CONV = 4
SPAN = 256
LENGTH = 2048
SEQ_GRP = 1
INNER = 3072
SEQS = 4
TOKENS = 8192


def steps_of(own_key, extent, shards, least, largest):
    def one(axis_at, parts):
        heights = jax.random.uniform(jax.random.fold_in(jax.random.fold_in(own_key, 6), axis_at), (parts,), jnp.float32, least / len(shards), largest / len(shards))
        return jnp.repeat(jnp.exp(heights), extent[axis_at] // parts).reshape((-1,) + (1,) * (len(extent) - axis_at - 1))

    factor_of = one(*shards[0])
    for cut in shards[1:]:
        factor_of = factor_of * one(*cut)
    return factor_of


def split_up(amount, total, reach, lean):
    portions = [(1 << 20) // math.isqrt(grade ** lean) + 1 for grade in range(2, amount + 1)]
    rest, counts = total - reach - (amount - 1), [1] * (amount - 1)
    while rest > 0:
        movable = [i for i in range(amount - 1) if counts[i] < reach]
        whole, left = sum([portions[i] for i in movable]), rest
        for i in movable:
            extra = min(reach - counts[i], max(1, left * portions[i] // whole), rest)
            counts[i] = counts[i] + extra
            rest = rest - extra
    return np.array([reach] + counts)


def ragged(stream_key, count, total, reach, lean):
    if count == 2:
        one = jax.random.randint(stream_key, (), max(1, total - reach), min(reach, total - 1) + 1)
        return jnp.stack([one, total - one])
    lengths = jnp.asarray(split_up(count, total, reach, lean), jnp.int32)
    twos = (count - 1) // 2
    donor, sink = lengths[1:1 + 2 * twos:2], lengths[2:2 + 2 * twos:2]
    room = jnp.minimum(donor - 1, reach - sink)
    passed = jax.random.randint(jax.random.fold_in(stream_key, 1), (twos,), 0, 1 << 20) % (room + 1)
    lengths = lengths.at[1:1 + 2 * twos:2].set(donor - passed).at[2:2 + 2 * twos:2].set(sink + passed)
    return lengths[jax.random.permutation(jax.random.fold_in(stream_key, 2), count)]


def gaussian(own_key, extent, spread, limit, cuts=(), held_as=jnp.bfloat16):
    gain = steps_of(own_key, extent, cuts, -0.22, 0.18) if cuts else 1.0
    values = jax.random.normal(own_key, extent, jnp.float32) * spread * gain
    return jnp.minimum(jnp.maximum(values, -limit), limit).astype(held_as)


def setup_inputs(seed: int = 0) -> dict:
    seeds = jax.random.split(jax.random.key(seed), 18)
    tokens_in = gaussian(seeds[0], (TOKENS, D), 1.0, 6.0, ((0, 8),))
    segment_ids = jax.vmap(lambda own: jnp.searchsorted(jnp.cumsum(ragged(own, 4, LENGTH, LENGTH // 2, 0)), jnp.arange(LENGTH), side="right"))(jax.random.split(seeds[1], SEQS)).reshape((SEQS, LENGTH)).astype(jnp.int32)
    norm_gain = jnp.clip(1.0 + 0.1 * jax.random.normal(seeds[2], (D,), jnp.float32), 0.5, 1.5)
    proj_gate = gaussian(seeds[3], (D, INNER), D ** -0.5, 0.15625, ((0, 4), (1, 2)))
    proj_inner = gaussian(seeds[4], (D, INNER), D ** -0.5, 0.15625, ((0, 4), (1, 2)))
    proj_step = gaussian(seeds[5], (D, HEADS), D ** -0.5, 0.15625, ((0, 4), (1, 2)))
    proj_states = gaussian(seeds[6], (D, 2 * STATE), D ** -0.5, 0.15625)
    conv_inner = gaussian(seeds[7], (CONV, INNER), CONV ** -0.5, 3.0, ((1, 8),), jnp.float32)
    conv_inner_bias = gaussian(seeds[8], (INNER,), 0.3, 1.5, ((0, 8),), jnp.float32)
    conv_states = gaussian(seeds[9], (CONV, 2 * STATE), CONV ** -0.5, 3.0, (), jnp.float32)
    conv_states_bias = gaussian(seeds[10], (2 * STATE,), 0.3, 1.5, (), jnp.float32)
    step_bias = jnp.clip(-6.0 + 5.0 * jax.random.uniform(seeds[11], (HEADS,), jnp.float32) ** steps_of(seeds[11], (HEADS,), ((0, 8),), -0.2, 0.2), -6.0, -1.0)
    decay_log = jnp.clip(2.77 * jax.random.uniform(seeds[12], (HEADS,), jnp.float32) ** steps_of(seeds[12], (HEADS,), ((0, 8),), -0.2, 0.2), 0.0, 2.77)
    skip_gain = jnp.clip(0.5 + 1.0 * jax.random.uniform(seeds[13], (HEADS,), jnp.float32) ** steps_of(seeds[13], (HEADS,), ((0, 8),), -0.2, 0.2), 0.5, 1.5)
    gate_gain = jnp.clip(1.0 + 0.1 * jax.random.normal(seeds[14], (INNER,), jnp.float32), 0.5, 1.5)
    proj_out = gaussian(seeds[15], (INNER, D), INNER ** -0.5, 0.109375, ((0, 2), (1, 4)))
    cotangent = gaussian(seeds[16], (TOKENS, D), 1.0, 6.0, ((0, 8), (1, 4)))
    return dict(tokens_in=tokens_in, segment_ids=segment_ids, norm_gain=norm_gain, proj_gate=proj_gate, proj_inner=proj_inner, proj_step=proj_step, proj_states=proj_states, conv_inner=conv_inner, conv_inner_bias=conv_inner_bias, conv_states=conv_states, conv_states_bias=conv_states_bias, step_bias=step_bias, decay_log=decay_log, skip_gain=skip_gain, gate_gain=gate_gain, proj_out=proj_out, cotangent=cotangent)


@jax.custom_vjp
def low(v):
    return lax.optimization_barrier(v.astype(jnp.bfloat16)).astype(jnp.float32)

@jax.custom_vjp
def low_back(v):
    return v

def low_keep(v):
    return (low(v), None)

def low_pass(kept, grad):
    return (grad,)

def back_keep(v):
    return (v, None)

def back_low(kept, grad):
    return (low(grad),)
low.defvjp(low_keep, low_pass)
low_back.defvjp(back_keep, back_low)
epsilon = 1e-05

def mult(left, right):
    return jnp.dot(left, right, precision=lax.Precision.HIGHEST, preferred_element_type=jnp.float32)

def causal_conv(signal, kernel, offset, segments):
    length = signal.shape[1]
    running = offset + kernel[0] * signal
    for back_step in range(1, kernel.shape[0]):
        shifted = jnp.pad(signal, ((0, 0), (back_step, 0), (0, 0)))[:, :length]
        earlier = jnp.pad(segments, ((0, 0), (back_step, 0)), constant_values=-1)[:, :length]
        same_doc = (earlier == segments)[:, :, None]
        running = running + jnp.where(same_doc, kernel[back_step] * shifted, 0.0)
    return running

def span_scan(inner_seq, write_seq, read_seq, step_seq, decay_rate, skip_gain, doc_seq):
    length, heads, width = inner_seq.shape
    blocks = length // SPAN
    pieces = (inner_seq.reshape(blocks, SPAN, heads, width), write_seq.reshape(blocks, SPAN, -1), read_seq.reshape(blocks, SPAN, -1), step_seq.reshape(blocks, SPAN, heads), doc_seq.reshape(blocks, SPAN))
    positions = jnp.arange(SPAN)
    causal = positions[:, None] >= positions[None, :]

    def advance(carry, block):
        memory, previous = carry
        inner_part, write_part, read_part, step_part, doc_part = block
        log_decay = step_part * decay_rate[None, :]
        running = jnp.cumsum(log_decay, axis=0)
        allowed = (causal & (doc_part[:, None] == doc_part[None, :]))[:, :, None]
        differ = running[:, None, :] - running[None, :, :]
        weights_in = jnp.where(allowed, jnp.exp(jnp.where(allowed, differ, 0.0)), 0.0)
        scores = jnp.dot(read_part, write_part.T, precision=lax.Precision.HIGHEST)
        mixing = scores[:, :, None] * weights_in * step_part[None, :, :]
        within = jnp.einsum('tsh,shp->thp', mixing, inner_part, precision=lax.Precision.HIGHEST)
        linked = jnp.where((doc_part == previous)[:, None], jnp.exp(running), 0.0)
        carried = jnp.einsum('tn,hnp->thp', read_part, memory, precision=lax.Precision.HIGHEST) * linked[:, :, None]
        output = within + carried + skip_gain[None, :, None] * inner_part
        last_doc = doc_part[-1]
        to_end = jnp.where((doc_part == last_doc)[:, None], jnp.exp(running[-1][None, :] - running), 0.0) * step_part
        fresh = jnp.einsum('sh,sn,shp->hnp', to_end, write_part, inner_part, precision=lax.Precision.HIGHEST)
        retained = jnp.where(last_doc == previous, jnp.exp(running[-1])[:, None, None] * memory, 0.0)
        return ((fresh + retained, last_doc), output)
    start = (jnp.zeros((heads, write_seq.shape[1], width), jnp.float32), jnp.array(-1, jnp.int32))
    _, outputs = lax.scan(jax.checkpoint(advance), start, pieces)
    return outputs.reshape(length, heads, width)

def mixer(inner_low, write_low, read_low, step_raw, gate_pre, step_bias, decay_log, skip_gain, segments):
    seqs, length = segments.shape
    heads = step_raw.shape[1]
    width = inner_low.shape[1] // heads
    step = jax.nn.softplus(step_raw + step_bias)
    decay_rate = -jnp.exp(decay_log)

    def one_sequence(inner_seq, write_seq, read_seq, step_seq, doc_seq):
        return span_scan(inner_seq, write_seq, read_seq, step_seq, decay_rate, skip_gain, doc_seq)
    outputs = jax.vmap(one_sequence)(inner_low.reshape(seqs, length, heads, width), write_low.reshape(seqs, length, -1), read_low.reshape(seqs, length, -1), step.reshape(seqs, length, heads), segments)
    return outputs.reshape(seqs * length, heads * width) * jax.nn.silu(gate_pre)

def block(tokens, segments, norm_gain, proj_gate, proj_inner, proj_step, proj_states, conv_inner, conv_inner_bias, conv_states, conv_states_bias, step_bias, decay_log, skip_gain, gate_gain, proj_out):
    seqs, length = segments.shape
    inverse = lax.rsqrt(lax.optimization_barrier(jnp.mean(tokens * tokens, -1, keepdims=True)) + epsilon)
    normed = low(tokens * inverse * norm_gain)
    gate_pre = low_back(mult(normed, proj_gate))
    inner_pre = low_back(mult(normed, proj_inner))
    step_raw = low_back(mult(normed, proj_step))
    states_pre = low_back(mult(normed, proj_states))
    inner_act = jax.nn.silu(causal_conv(inner_pre.reshape(seqs, length, -1), conv_inner, conv_inner_bias, segments))
    states_act = jax.nn.silu(causal_conv(states_pre.reshape(seqs, length, -1), conv_states, conv_states_bias, segments))
    inner_act = inner_act.reshape(seqs * length, -1)
    states_act = states_act.reshape(seqs * length, -1)
    half = states_act.shape[1] // 2
    mixed = mixer(low(inner_act), low(states_act[:, :half]), low(states_act[:, half:]), step_raw, gate_pre, step_bias, decay_log, skip_gain, segments)
    scale = lax.rsqrt(lax.optimization_barrier(jnp.mean(mixed * mixed, -1, keepdims=True)) + epsilon)
    gated = low(mixed * scale * gate_gain)
    return tokens + mult(gated, proj_out)

def reference(tokens_in, segment_ids, norm_gain, proj_gate, proj_inner, proj_step, proj_states, conv_inner, conv_inner_bias, conv_states, conv_states_bias, step_bias, decay_log, skip_gain, gate_gain, proj_out, cotangent):
    groups = segment_ids.shape[0] // SEQ_GRP
    params = tuple((weight.astype(jnp.float32) for weight in (norm_gain, proj_gate, proj_inner, proj_step, proj_states, conv_inner, conv_inner_bias, conv_states, conv_states_bias, step_bias, decay_log, skip_gain, gate_gain, proj_out)))
    tokens = tokens_in.astype(jnp.float32).reshape(groups, SEQ_GRP * LENGTH, D)
    segments = segment_ids.reshape(groups, SEQ_GRP, LENGTH)
    stepper = jax.checkpoint(block)

    def forward(tokens, *weights):

        def advance(carry, pieces):
            return (carry, stepper(pieces[0], pieces[1], *weights))
        _, outputs = lax.scan(advance, jnp.zeros((), jnp.float32), (tokens, segments))
        return outputs
    outputs, backward = jax.vjp(forward, tokens, *params)
    grads = backward(cotangent.astype(jnp.float32).reshape(outputs.shape))
    mixed_out = outputs.reshape(TOKENS, D).astype(jnp.bfloat16)
    grad_tokens = grads[0].reshape(TOKENS, D).astype(jnp.bfloat16)
    return (mixed_out, grad_tokens, grads[1], grads[2], grads[3], grads[4], grads[5], grads[6], grads[7], grads[8], grads[9], grads[10], grads[11], grads[12], grads[13], grads[14])
```

```python
import functools

import jax
import jax.numpy as jnp
from jax import lax
from jax.experimental import pallas as pl
from jax.experimental.pallas import tpu as pltpu
from jax.sharding import PartitionSpec as P

SPAN = 256
HEAD = 64
epsilon = 1e-05
LOG2E = 1.4426950408889634
f32 = jnp.float32
bf16 = jnp.bfloat16
ANY = pl.ANY


def mm(a, b):
    return lax.dot_general(a, b, (((1,), (0,)), ((), ())), preferred_element_type=f32)


def mm_nt(a, b):
    return lax.dot_general(a, b, (((1,), (1,)), ((), ())), preferred_element_type=f32)


def split(v, terms):
    parts = []
    for _ in range(terms):
        part = v.astype(bf16)
        parts.append(part)
        v = v - part.astype(f32)
    return parts


def mm_split(a, exact, terms=2):
    return sum(mm(part, exact) for part in split(a, terms))


def split_mm(exact, b, terms=3):
    return sum(mm(exact, part) for part in split(b, terms))


def spread_matrix(channels):
    heads = lax.broadcasted_iota(jnp.int32, (128, channels), 0)
    cols = lax.broadcasted_iota(jnp.int32, (128, channels), 1)
    low = heads * HEAD
    return jnp.where((cols >= low) & (cols < low + HEAD), 1.0, 0.0).astype(bf16)


def gather_matrix(channels):
    heads = lax.broadcasted_iota(jnp.int32, (channels, 128), 1)
    rows = lax.broadcasted_iota(jnp.int32, (channels, 128), 0)
    low = heads * HEAD
    return jnp.where((rows >= low) & (rows < low + HEAD), 1.0, 0.0).astype(bf16)


def lower_ones():
    rows = lax.broadcasted_iota(jnp.int32, (SPAN, SPAN), 0)
    cols = lax.broadcasted_iota(jnp.int32, (SPAN, SPAN), 1)
    return jnp.where(rows >= cols, 1.0, 0.0).astype(bf16)


def upper_ones():
    rows = lax.broadcasted_iota(jnp.int32, (SPAN, SPAN), 0)
    cols = lax.broadcasted_iota(jnp.int32, (SPAN, SPAN), 1)
    return jnp.where(rows <= cols, 1.0, 0.0).astype(bf16)


def sigmoid(v):
    return 1.0 / (1.0 + jnp.exp(-v))


def half_masks():
    lane = lax.broadcasted_iota(jnp.int32, (SPAN, 128), 1)
    return lane < HEAD


def rms_rows(tok, gain):
    wide = tok.astype(f32)
    inverse = lax.rsqrt(jnp.mean(wide * wide, -1, keepdims=True) + epsilon)
    return (wide * inverse * gain).astype(bf16)


def entry_kernel(
    tok, halo, ngain, w_inner, w_states, w_step, par, spar, head, meta,
    normed_o, pre_o, spre_o, sd_o, ssd_o, x_o, wr_o, step_o, r_o, sig_o, fresh_o, end_o,
    hpre_o, hspre_o,
    xbuf, sbuf, mem,
):
    at = pl.program_id(0)
    channels = w_inner.shape[1]
    gain = ngain[...]

    @pl.when(at == 0)
    def _():
        hn = rms_rows(halo[...], gain)
        hp = mm(hn, w_inner[...])[8:16]
        hs = mm(hn, w_states[...])[8:16]
        xbuf[0:8, :] = hp
        sbuf[0:8, :] = hs
        hpre_o[...] = hp
        hspre_o[...] = hs
        mem[...] = jnp.zeros_like(mem)

    @pl.when(at > 0)
    def _():
        xbuf[0:8, :] = xbuf[SPAN:SPAN + 8, :]
        sbuf[0:8, :] = sbuf[SPAN:SPAN + 8, :]

    normed = rms_rows(tok[...], gain)
    normed_o[...] = normed
    x_pre = mm(normed, w_inner[...])
    s_pre = mm(normed, w_states[...])
    xbuf[8:SPAN + 8, :] = x_pre
    sbuf[8:SPAN + 8, :] = s_pre
    pre_o[...] = x_pre.astype(bf16)
    spre_o[...] = s_pre.astype(bf16)

    def conv_silu(buf, here, taps):
        v = taps[4:5, :] + taps[0:1, :] * here
        for k in range(1, 4):
            v = v + meta[:, k:k + 1] * (taps[k:k + 1, :] * buf[8 - k:8 - k + SPAN, :])
        sg = sigmoid(v)
        return v * sg, sg * (1.0 + v * (1.0 - sg))

    act, slope = conv_silu(xbuf, x_pre, par)
    x_low = act.astype(bf16)
    x_o[...] = x_low
    sd_o[...] = slope.astype(bf16)
    sact, sslope = conv_silu(sbuf, s_pre, spar)
    wr = sact.astype(bf16)
    wr_o[...] = wr
    ssd_o[...] = sslope.astype(bf16)

    raw = mm(normed, w_step[...]) + head[0:1, :]
    step = jnp.maximum(raw, 0.0) + jnp.log1p(jnp.exp(-jnp.abs(raw)))
    sig_o[...] = sigmoid(raw)
    step_o[...] = step
    r = split_mm(lower_ones(), step * head[1:2, :])
    r_o[...] = r
    last = r[SPAN - 1:SPAN, :]
    to_end = jnp.exp2(jnp.minimum(last - r, 0.0)) * meta[:, 5:6]
    spread = spread_matrix(channels)
    coef = mm_split(to_end * step, spread)
    w_t = jnp.transpose(wr[:, 0:128].astype(f32)).astype(bf16)
    fresh = mm(w_t, (coef * x_low.astype(f32)).astype(bf16))
    fresh_o[...] = fresh[None]
    keep = mm_split(jnp.broadcast_to(jnp.exp2(last) * meta[0:1, 6:7], (8, 128)), spread)[0:1]
    mem[...] = keep * mem[...] + fresh
    end_o[...] = mem[...]


def scan_kernel(
    x, wr, r_ref, step_ref, meta, docrow, fresh, state_in, head, par, gate, ggated,
    y_o, sums_o, sprev_o,
    mem, ybuf,
):
    at = pl.program_id(0)
    channels = x.shape[1]

    @pl.when(at == 0)
    def _():
        mem[...] = state_in[...]

    spread = spread_matrix(channels)
    w_low = wr[:, 0:128]
    r_low = wr[:, 128:256]
    r = r_ref[...]
    r_t = jnp.transpose(r)
    rows = lax.broadcasted_iota(jnp.int32, (SPAN, SPAN), 0)
    cols = lax.broadcasted_iota(jnp.int32, (SPAN, SPAN), 1)
    allowed = (rows >= cols) & (meta[:, 0:1] == docrow[...])
    scores = jnp.where(allowed, mm_nt(r_low, w_low), 0.0)
    wide = x[...].astype(f32)
    xd = (mm_split(step_ref[...], spread) * wide).astype(bf16)
    sprev = mem[...].astype(bf16)
    sprev_o[...] = sprev[None]
    linked = jnp.exp2(r) * meta[:, 4:5]
    carried = mm(r_low, sprev) * mm_split(linked, spread)
    skip = mm_split(jnp.broadcast_to(head[2:3, :], (8, 128)), spread)[0:1]
    ybuf[...] = carried + skip * wide
    first = half_masks()
    for pair in range(channels // 128):
        lanes = slice(pair * 128, pair * 128 + 128)
        xp = xd[:, lanes]
        total = ybuf[:, lanes]
        for half in range(2):
            h = 2 * pair + half
            decay = jnp.exp2(jnp.minimum(r[:, h:h + 1] - r_t[h:h + 1, :], 0.0))
            mixing = (scores * decay).astype(bf16)
            own = jnp.where(first if half == 0 else ~first, xp, jnp.zeros_like(xp))
            total = total + mm(mixing, own)
        ybuf[:, lanes] = total
    last = r[SPAN - 1:SPAN, :]
    keep = mm_split(jnp.broadcast_to(jnp.exp2(last) * meta[0:1, 6:7], (8, 128)), spread)[0:1]
    mem[...] = keep * mem[...] + fresh[0]
    y = ybuf[...]
    y_o[...] = y
    g = gate[...]
    mixed = y * (g * sigmoid(g))
    ones = jnp.ones((8, channels), bf16)
    sq = sum(mm_nt(ones, part) for part in split(mixed * mixed, 2))
    pr = sum(mm_nt(ones, part) for part in split(mixed * (par[5:6, :] * ggated[...]), 2))
    row = lax.broadcasted_iota(jnp.int32, (8, SPAN), 0)
    sums_o[...] = jnp.where(row == 0, sq, jnp.where(row == 1, pr, 0.0))


def turn_kernel(
    inner, y_ref, gate, ggated, sums, x, wr, r_ref, meta, head, par,
    gated_o, ggate_o, gy_o, dr_o, dsf_o, dsout_o, acc_o,
    dmem,
):
    at = pl.program_id(0)
    channels = x.shape[1]

    @pl.when(at == 0)
    def _():
        dmem[...] = jnp.zeros_like(dmem)
        acc_o[...] = jnp.zeros_like(acc_o)

    spread = spread_matrix(channels)
    totals = jnp.transpose(sums[...])
    scale = lax.rsqrt(totals[:, 0:1] / inner + epsilon)
    cross = totals[:, 1:2] / inner
    y = y_ref[...]
    g = gate[...]
    sg = sigmoid(g)
    sl = g * sg
    mixed = y * sl
    gg = ggated[...]
    gain = par[5:6, :]
    normal = mixed * scale
    gated_o[...] = (normal * gain).astype(bf16)
    g_mixed = scale * (gain * gg - normal * (scale * cross))
    ggate_o[...] = (g_mixed * y * (sg * (1.0 + g * (1.0 - sg)))).astype(bf16)
    gy = (g_mixed * sl).astype(bf16)
    gy_o[...] = gy
    gyw = gy.astype(f32)
    wide = x[...].astype(f32)
    skip = mm_split(jnp.broadcast_to(head[2:3, :], (8, 128)), spread)[0:1]
    dr_o[...] = mm_split(gyw * (y - skip * wide), gather_matrix(channels))
    row = lax.broadcasted_iota(jnp.int32, (8, channels), 0)
    ggain = jnp.sum(gg * normal, 0, keepdims=True)
    gskip = jnp.sum(gyw * wide, 0, keepdims=True)
    acc_o[...] += jnp.where(row == 0, ggain, jnp.where(row == 1, gskip, 0.0))
    r = r_ref[...]
    linked = mm_split(jnp.exp2(r) * meta[:, 4:5], spread)
    r_t = jnp.transpose(wr[:, 128:256].astype(f32)).astype(bf16)
    dfresh = mm(r_t, (linked * gyw).astype(bf16))
    dsf_o[...] = dfresh[None]
    last = r[SPAN - 1:SPAN, :]
    keep = mm_split(jnp.broadcast_to(jnp.exp2(last) * meta[0:1, 6:7], (8, 128)), spread)[0:1]
    dmem[...] = keep * dmem[...] + dfresh
    dsout_o[...] = dmem[...]


def back_kernel(
    x, wr, gy_ref, r_ref, step_ref, sig_ref, meta, docrow, dr_ref, sprev, dsf, ds_in,
    pre, spre, sd, ssd, hpre, hspre, hmeta, head, par, spar,
    gx_o, gs_o, gz_o, hx_o, hs_o, accx_o, accs_o, acch_o,
    dmem, gbuf, hbuf, dxd,
):
    at = pl.program_id(0)
    channels = x.shape[1]

    @pl.when(at == 0)
    def _():
        dmem[...] = ds_in[...]
        accx_o[...] = jnp.zeros_like(accx_o)
        accs_o[...] = jnp.zeros_like(accs_o)
        acch_o[...] = jnp.zeros_like(acch_o)
        gbuf[...] = jnp.zeros_like(gbuf)
        hbuf[...] = jnp.zeros_like(hbuf)

    @pl.when(at > 0)
    def _():
        gbuf[SPAN + 8:SPAN + 16, :] = gbuf[8:16, :]
        hbuf[SPAN + 8:SPAN + 16, :] = hbuf[8:16, :]

    spread = spread_matrix(channels)
    gather = gather_matrix(channels)
    w_low = wr[:, 0:128]
    r_low = wr[:, 128:256]
    r = r_ref[...]
    r_t = jnp.transpose(r)
    step = step_ref[...]
    last = r[SPAN - 1:SPAN, :]
    rows = lax.broadcasted_iota(jnp.int32, (SPAN, SPAN), 0)
    cols = lax.broadcasted_iota(jnp.int32, (SPAN, SPAN), 1)
    allowed = (rows <= cols) & (meta[:, 0:1] == docrow[...])
    scores = jnp.where(allowed, mm_nt(w_low, r_low), 0.0)
    wide = x[...].astype(f32)
    step_wide = mm_split(step, spread)
    xd = (step_wide * wide).astype(bf16)
    gy = gy_ref[...]
    gyw = gy.astype(f32)
    ds = dmem[...]
    ds_low = ds.astype(bf16)
    te = mm_split(jnp.exp2(jnp.minimum(last - r, 0.0)) * meta[:, 5:6], spread)
    linked = mm_split(jnp.exp2(r) * meta[:, 4:5], spread)
    from_end = te * mm(w_low, ds_low)
    dxd[...] = from_end
    keep = mm_split(jnp.broadcast_to(jnp.exp2(last) * meta[0:1, 6:7], (8, 128)), spread)[0:1]
    ending = jnp.sum(xd.astype(f32) * from_end, 0, keepdims=True) + keep * jnp.sum(
        sprev[0].astype(f32) * ds, 0, keepdims=True
    )
    first = half_masks()
    dscores = jnp.zeros((SPAN, SPAN), f32)
    for pair in range(channels // 128):
        lanes = slice(pair * 128, pair * 128 + 128)
        xp = xd[:, lanes]
        gp = gy[:, lanes]
        total = dxd[:, lanes]
        for half in range(2):
            h = 2 * pair + half
            own = first if half == 0 else ~first
            decay = jnp.exp2(jnp.minimum(r_t[h:h + 1, :] - r[:, h:h + 1], 0.0))
            mixing = (scores * decay).astype(bf16)
            gown = jnp.where(own, gp, jnp.zeros_like(gp))
            total = total + mm(mixing, gown)
            dscores = dscores + mm_nt(xp, gown) * decay
        dxd[:, lanes] = total
    dscores = jnp.where(allowed, dscores, 0.0)
    dlow = dscores.astype(bf16)
    xdw = xd.astype(f32)
    g_write = mm(dlow, r_low) + mm_nt((te * xdw).astype(bf16), ds_low)
    g_read = mm(jnp.transpose(dscores).astype(bf16), w_low) + mm_nt(
        (linked * gyw).astype(bf16), sprev[0]
    )
    skip = mm_split(jnp.broadcast_to(head[2:3, :], (8, 128)), spread)[0:1]
    full = dxd[...]
    g_x = step_wide * full + skip * gyw
    dr = dr_ref[...] - mm_split(xdw * full, gather)
    at_end = mm_split(jnp.broadcast_to(ending, (8, channels)), gather, 3)[0:1]
    tail = lax.broadcasted_iota(jnp.int32, (SPAN, 128), 0) == SPAN - 1
    dr = dr + jnp.where(tail, at_end, 0.0)
    da = split_mm(upper_ones(), dr)
    dstep = mm_split(wide * full, gather) + head[3:4, :] * da
    gz = dstep * sig_ref[...]
    gz_o[...] = gz.astype(bf16)
    row = lax.broadcasted_iota(jnp.int32, (8, 128), 0)
    gbias = jnp.sum(gz, 0, keepdims=True)
    grate = jnp.sum(da * step, 0, keepdims=True)
    acch_o[...] += jnp.where(row == 0, gbias, jnp.where(row == 1, grate, 0.0))
    dmem[...] = keep * ds + dsf[0]

    def conv_back(buf, gv, base, taps, acc, halo_pre, out, halo_out):
        buf[8:SPAN + 8, :] = gv
        width = gv.shape[1]
        total = taps[0:1, :] * gv
        sums = [jnp.sum(gv * base, 0, keepdims=True)]
        halo = jnp.zeros((8, width), f32)
        hsum = []
        for k in range(1, 4):
            moved = meta[:, 7 + k:8 + k] * buf[8 + k:8 + k + SPAN, :]
            total = total + taps[k:k + 1, :] * moved
            sums.append(jnp.sum(moved * base, 0, keepdims=True))
            hmoved = hmeta[:, 7 + k:8 + k] * buf[k:8 + k, :]
            halo = halo + taps[k:k + 1, :] * hmoved
            hsum.append(jnp.sum(hmoved * halo_pre, 0, keepdims=True))
        sums.append(jnp.sum(gv, 0, keepdims=True))
        out[...] = total.astype(bf16)
        halo_out[...] = halo
        rows8 = lax.broadcasted_iota(jnp.int32, (8, width), 0)
        final = jnp.where(at == pl.num_programs(0) - 1, 1.0, 0.0)
        add = jnp.zeros((8, width), f32)
        for i, s in enumerate(sums):
            if 1 <= i <= 3:
                s = s + final * hsum[i - 1]
            add = add + jnp.where(rows8 == i, s, 0.0)
        acc[...] += add

    conv_back(gbuf, g_x * sd[...].astype(f32), pre[...].astype(f32), par, accx_o,
              hpre[...], gx_o, hx_o)
    g_wr = jnp.concatenate([g_write, g_read], 1)
    conv_back(hbuf, g_wr * ssd[...].astype(f32), spre[...].astype(f32), spar, accs_o,
              hspre[...], gs_o, hs_o)


PARAMS = dict(vmem_limit_bytes=56 * 1024 * 1024)


def whole(shape):
    return pl.BlockSpec(shape, lambda i: (0,) * len(shape))


def by_rows(cols, count=None):
    if count is None:
        return pl.BlockSpec((SPAN, cols), lambda i: (i, 0))
    return pl.BlockSpec((SPAN, cols), lambda i: (count - 1 - i, 0))


def swap(values, axis):
    return lax.ppermute(values, axis, [(0, 1), (1, 0)])


def per_device(
    tokens_in, segment_ids, norm_gain, proj_gate, proj_inner, proj_step, proj_states,
    conv_inner, conv_inner_bias, conv_states, conv_states_bias, step_bias, decay_log,
    skip_gain, gate_gain, proj_out, cotangent,
):
    tokens, width = tokens_in.shape
    blocks = tokens // SPAN
    row = lax.axis_index("row")
    col = lax.axis_index("col")
    cols = lax.axis_size("col")
    own_ch = conv_inner.shape[1]
    own_heads = step_bias.shape[0]
    channels = 2 * own_ch
    inner_all = channels * cols
    col_width = width // cols

    def fetch_columns(weight):
        moved = lax.all_to_all(weight, "col", 1, 0, tiled=True)
        return lax.all_gather(moved, "row", axis=1, tiled=True)

    halo = lax.ppermute(tokens_in[-16:], "row", [(0, 1)])
    w_inner = fetch_columns(proj_inner)
    step_all = lax.all_gather(
        lax.all_gather(proj_step, "col", axis=0, tiled=True), "row", axis=1, tiled=True
    )
    w_step = step_all.reshape(width, 2, cols, own_heads)
    w_step = lax.dynamic_index_in_dim(w_step, col, 2, keepdims=False).reshape(width, 2 * own_heads)
    w_step = jnp.pad(w_step, ((0, 0), (0, 128 - 2 * own_heads)))
    w_gate = fetch_columns(proj_gate)
    w_out = lax.all_gather(
        lax.all_to_all(proj_out, "col", 0, 1, tiled=True), "row", axis=0, tiled=True
    )
    cot_all = lax.all_gather(cotangent, "col", axis=1, tiled=True)

    heads_own = jnp.stack([step_bias, decay_log, skip_gain])
    own = jnp.concatenate(
        [
            conv_inner,
            conv_inner_bias[None],
            gate_gain[None],
            jnp.pad(heads_own.reshape(1, -1), ((0, 0), (0, own_ch - 3 * own_heads))),
            jnp.zeros((1, own_ch), f32),
        ],
        0,
    )
    both = lax.all_gather(own, "row", axis=0)
    par = jnp.concatenate([both[0], both[1]], 1)
    hp = jnp.concatenate(
        [both[i, 6, : 3 * own_heads].reshape(3, own_heads) for i in range(2)], 1
    )
    rate = -jnp.exp(hp[1])
    head = jnp.pad(
        jnp.stack([hp[0], rate * LOG2E, hp[2], rate]), ((0, 4), (0, 128 - 2 * own_heads))
    )
    spar = jnp.concatenate([conv_states, conv_states_bias[None], jnp.zeros((3, 256), f32)], 0)

    docs = jnp.pad(segment_ids[0].astype(f32), (8, 8), constant_values=-1.0)
    docs = lax.dynamic_slice_in_dim(docs, row * tokens, tokens + 16, 0)
    here = docs[8:8 + tokens]
    spans = here.reshape(blocks, SPAN)
    before = jnp.concatenate([docs[7:8], spans[:-1, -1]])
    after = spans[:, -1]

    def flat(cond):
        return jnp.broadcast_to(cond, (blocks, SPAN)).reshape(tokens)

    def forward_same(start, count):
        own_docs = docs[start:start + count]
        return [own_docs == docs[start + k:start + k + count] for k in range(1, 4)]

    meta = jnp.stack(
        [here]
        + [(here == docs[8 - k:8 - k + tokens]) for k in range(1, 4)]
        + [
            flat(spans == before[:, None]),
            flat(spans == after[:, None]),
            flat((before == after)[:, None]),
            jnp.zeros_like(here),
        ]
        + forward_same(8, tokens)
        + [jnp.zeros_like(here)] * 5,
        1,
    ).astype(f32)
    hmeta = jnp.stack(
        [jnp.zeros((8,), f32)] * 8
        + forward_same(0, 8)
        + [jnp.zeros((8,), f32)] * 5,
        1,
    ).astype(f32)
    docrow = here[None, :]

    sds = jax.ShapeDtypeStruct
    (
        normed, pre, spre, sd, ssd, x_low, wr, step, r, sig, fresh, end, hpre, hspre,
    ) = pl.pallas_call(
        entry_kernel,
        grid=(blocks,),
        in_specs=[
            by_rows(width), whole((16, width)), whole((1, width)), whole((width, channels)),
            whole((width, 256)), whole((width, 128)), whole((8, channels)), whole((8, 256)),
            whole((8, 128)), by_rows(16),
        ],
        out_specs=[
            by_rows(width), by_rows(channels), by_rows(256), by_rows(channels), by_rows(256),
            by_rows(channels), by_rows(256), by_rows(128), by_rows(128), by_rows(128),
            pl.BlockSpec((1, 128, channels), lambda i: (i, 0, 0)), whole((128, channels)),
            whole((8, channels)), whole((8, 256)),
        ],
        out_shape=[
            sds((tokens, width), bf16), sds((tokens, channels), bf16), sds((tokens, 256), bf16),
            sds((tokens, channels), bf16), sds((tokens, 256), bf16),
            sds((tokens, channels), bf16), sds((tokens, 256), bf16),
            sds((tokens, 128), f32), sds((tokens, 128), f32), sds((tokens, 128), f32),
            sds((blocks, 128, channels), f32), sds((128, channels), f32),
            sds((8, channels), f32), sds((8, 256), f32),
        ],
        scratch_shapes=[
            pltpu.VMEM((SPAN + 8, channels), f32),
            pltpu.VMEM((SPAN + 8, 256), f32),
            pltpu.VMEM((128, channels), f32),
        ],
        compiler_params=pltpu.CompilerParams(**PARAMS),
        name="entry",
    )(tokens_in, halo, norm_gain[None], w_inner, proj_states, w_step, par, spar, head, meta)

    state_in = lax.ppermute(end, "row", [(0, 1)])
    gate = mm(normed, w_gate)
    ggated = mm_nt(cot_all, w_out)

    y, sums, sprev = pl.pallas_call(
        scan_kernel,
        grid=(blocks,),
        in_specs=[
            by_rows(channels), by_rows(256), by_rows(128), by_rows(128), by_rows(16),
            pl.BlockSpec((1, SPAN), lambda i: (0, i)),
            pl.BlockSpec((1, 128, channels), lambda i: (i, 0, 0)), whole((128, channels)),
            whole((8, 128)), whole((8, channels)), by_rows(channels), by_rows(channels),
        ],
        out_specs=[
            by_rows(channels), pl.BlockSpec((8, SPAN), lambda i: (0, i)),
            pl.BlockSpec((1, 128, channels), lambda i: (i, 0, 0)),
        ],
        out_shape=[
            sds((tokens, channels), f32), sds((8, tokens), f32),
            sds((blocks, 128, channels), bf16),
        ],
        scratch_shapes=[pltpu.VMEM((128, channels), f32), pltpu.VMEM((SPAN, channels), f32)],
        compiler_params=pltpu.CompilerParams(**PARAMS),
        name="scan",
    )(x_low, wr, r, step, meta, docrow, fresh, state_in, head, par, gate, ggated)

    sums = lax.psum(sums, "col")

    back3 = pl.BlockSpec((1, 128, channels), lambda i: (blocks - 1 - i, 0, 0))
    gated, g_gate, gy, dr, dsf, dsout, acc1 = pl.pallas_call(
        functools.partial(turn_kernel, float(inner_all)),
        grid=(blocks,),
        in_specs=[
            by_rows(channels, blocks), by_rows(channels, blocks), by_rows(channels, blocks),
            pl.BlockSpec((8, SPAN), lambda i: (0, blocks - 1 - i)),
            by_rows(channels, blocks), by_rows(256, blocks), by_rows(128, blocks),
            by_rows(16, blocks), whole((8, 128)), whole((8, channels)),
        ],
        out_specs=[
            by_rows(channels, blocks), by_rows(channels, blocks), by_rows(channels, blocks),
            by_rows(128, blocks), back3, whole((128, channels)), whole((8, channels)),
        ],
        out_shape=[
            sds((tokens, channels), bf16), sds((tokens, channels), bf16),
            sds((tokens, channels), bf16), sds((tokens, 128), f32),
            sds((blocks, 128, channels), f32), sds((128, channels), f32),
            sds((8, channels), f32),
        ],
        scratch_shapes=[pltpu.VMEM((128, channels), f32)],
        compiler_params=pltpu.CompilerParams(**PARAMS),
        name="turn",
    )(y, gate, ggated, sums, x_low, wr, r, meta, head, par)

    ds_in = lax.ppermute(dsout, "row", [(1, 0)])
    out_part = mm(gated, w_out).astype(bf16)
    out_cols = lax.psum_scatter(out_part, "col", scatter_dimension=1, tiled=True)
    own_tokens = lax.dynamic_slice_in_dim(tokens_in, col * col_width, col_width, 1).astype(f32)
    mixed_out = (own_tokens + out_cols.astype(f32)).astype(bf16)
    grad_out_part = lax.dot_general(
        gated, cot_all, (((0,), (0,)), ((), ())), preferred_element_type=f32
    )

    gx, gs, gz, hx, hs, accx, accs, acch = pl.pallas_call(
        back_kernel,
        grid=(blocks,),
        in_specs=[
            by_rows(channels, blocks), by_rows(256, blocks), by_rows(channels, blocks),
            by_rows(128, blocks), by_rows(128, blocks), by_rows(128, blocks),
            by_rows(16, blocks), pl.BlockSpec((1, SPAN), lambda i: (0, blocks - 1 - i)),
            by_rows(128, blocks), back3, back3, whole((128, channels)),
            by_rows(channels, blocks), by_rows(256, blocks), by_rows(channels, blocks),
            by_rows(256, blocks), whole((8, channels)), whole((8, 256)), whole((8, 16)),
            whole((8, 128)), whole((8, channels)), whole((8, 256)),
        ],
        out_specs=[
            by_rows(channels, blocks), by_rows(256, blocks), by_rows(128, blocks),
            whole((8, channels)), whole((8, 256)), whole((8, channels)), whole((8, 256)),
            whole((8, 128)),
        ],
        out_shape=[
            sds((tokens, channels), bf16), sds((tokens, 256), bf16), sds((tokens, 128), bf16),
            sds((8, channels), f32), sds((8, 256), f32), sds((8, channels), f32),
            sds((8, 256), f32), sds((8, 128), f32),
        ],
        scratch_shapes=[
            pltpu.VMEM((128, channels), f32),
            pltpu.VMEM((SPAN + 16, channels), f32),
            pltpu.VMEM((SPAN + 16, 256), f32),
            pltpu.VMEM((SPAN, channels), f32),
        ],
        compiler_params=pltpu.CompilerParams(**PARAMS),
        name="back",
    )(
        x_low, wr, gy, r, step, sig, meta, docrow, dr, sprev, dsf, ds_in,
        pre, spre, sd, ssd, hpre, hspre, hmeta, head, par, spar,
    )

    hx_in, hs_in = lax.ppermute((hx, hs), "row", [(1, 0)])
    gx = gx.at[-8:].add(hx_in.astype(bf16))
    gs = gs.at[-8:].add(hs_in.astype(bf16))

    normed_grad = (
        mm_nt(g_gate, w_gate) + mm_nt(gx, w_inner) + mm_nt(gz, w_step) + mm_nt(gs, proj_states)
    )
    wide = tokens_in.astype(f32)
    inverse = lax.rsqrt(jnp.mean(wide * wide, -1, keepdims=True) + epsilon)
    input_share = jnp.sum(normed_grad * norm_gain * wide, -1)
    gain_share = jnp.sum(normed_grad * (wide * inverse), 0)
    own_grad = lax.psum_scatter(
        normed_grad.astype(bf16), "col", scatter_dimension=1, tiled=True
    ).astype(f32)
    input_total = lax.psum(input_share, "col")[:, None]
    gain_cols = lax.dynamic_slice_in_dim(norm_gain, col * col_width, col_width, 0)
    grad_input = inverse * (own_grad * gain_cols) - own_tokens * inverse**3 * (input_total / width)
    grad_tokens = (grad_input + cotangent.astype(f32)).astype(bf16)

    def weight_grad(left, right):
        return lax.dot_general(
            left, right, (((0,), (0,)), ((), ())), preferred_element_type=f32
        )

    def reduce_columns(part):
        part = part.reshape(width, 2, own_ch).astype(bf16)
        part = lax.psum_scatter(part, "row", scatter_dimension=1)
        part = lax.psum(part, "dp")
        return lax.all_to_all(part, "col", 0, 1, tiled=True).astype(f32)

    grad_gate = reduce_columns(weight_grad(normed, g_gate))
    grad_inner = reduce_columns(weight_grad(normed, gx))
    go = lax.psum_scatter(
        grad_out_part.astype(bf16), "row", scatter_dimension=0, tiled=True
    )
    go = lax.psum(go, "dp")
    grad_out = lax.all_to_all(go, "col", 1, 0, tiled=True).astype(f32)

    g_rest = weight_grad(normed, jnp.concatenate([gs, gz], 1))
    grad_states = lax.psum(g_rest[:, :256], ("dp", "row", "col"))
    gz_part = g_rest[:, 256:256 + 2 * own_heads].reshape(width, 2, own_heads)
    gz_own = lax.psum(gz_part, ("dp", "row"))
    gz_all = lax.all_gather(gz_own, "col", axis=0)
    gz_all = lax.dynamic_index_in_dim(gz_all, row, 2, keepdims=False)
    gz_all = lax.dynamic_slice_in_dim(gz_all, col * col_width, col_width, 1)
    grad_step = jnp.moveaxis(gz_all, 0, 1).reshape(col_width, cols * own_heads)

    def head_sum(values):
        return values.reshape(2 * own_heads, HEAD).sum(-1)

    small = jnp.concatenate(
        [
            accx[0:5].reshape(5, 2, own_ch).transpose(1, 0, 2).reshape(2, -1),
            acc1[0].reshape(2, own_ch),
            acch[0, : 2 * own_heads].reshape(2, own_heads),
            (acch[1] * head[3])[: 2 * own_heads].reshape(2, own_heads),
            head_sum(acc1[1]).reshape(2, own_heads),
        ],
        1,
    )
    small = lax.psum(small, ("dp", "row"))
    small = lax.dynamic_index_in_dim(small, row, 0, keepdims=False)
    grad_conv_inner = small[: 4 * own_ch].reshape(4, own_ch)
    grad_conv_inner_bias = small[4 * own_ch:5 * own_ch]
    grad_gate_gain = small[5 * own_ch:6 * own_ch]
    rest = small[6 * own_ch:].reshape(3, own_heads)
    accs = lax.psum(accs, ("dp", "row", "col"))
    gain_all = lax.psum(gain_share, ("dp", "row", "col"))
    grad_norm_gain = lax.dynamic_slice_in_dim(gain_all, col * col_width, col_width, 0)

    return (
        mixed_out,
        grad_tokens,
        grad_norm_gain,
        grad_gate,
        grad_inner,
        grad_step,
        grad_states,
        grad_conv_inner,
        grad_conv_inner_bias,
        accs[0:4],
        accs[4],
        rest[0],
        rest[1],
        rest[2],
        grad_gate_gain,
        grad_out,
    )


def solution(mesh):
    in_specs = (
        P(("dp", "row"), None),
        P("dp", None),
        P(),
        P("col", "row"),
        P("col", "row"),
        P("col", "row"),
        P(),
        P(None, ("row", "col")),
        P(("row", "col")),
        P(),
        P(),
        P(("row", "col")),
        P(("row", "col")),
        P(("row", "col")),
        P(("row", "col")),
        P("row", "col"),
        P(("dp", "row"), "col"),
    )
    out_specs = (
        P(("dp", "row"), "col"),
        P(("dp", "row"), "col"),
        P("col"),
        P("col", "row"),
        P("col", "row"),
        P("col", "row"),
        P(),
        P(None, ("row", "col")),
        P(("row", "col")),
        P(),
        P(),
        P(("row", "col")),
        P(("row", "col")),
        P(("row", "col")),
        P(("row", "col")),
        P("row", "col"),
    )
    return jax.shard_map(
        per_device, mesh=mesh, in_specs=in_specs, out_specs=out_specs, check_vma=False
    )
```

```python
import functools

import jax
import jax.numpy as jnp
from jax import lax
from jax.experimental import pallas as pl
from jax.experimental.pallas import tpu as pltpu
from jax.sharding import PartitionSpec as P

SPAN = 256
HEAD = 64
epsilon = 1e-05
LOG2E = 1.4426950408889634
f32 = jnp.float32
bf16 = jnp.bfloat16
ANY = pl.ANY


def mm(a, b):
    return lax.dot_general(a, b, (((1,), (0,)), ((), ())), preferred_element_type=f32)


def mm_nt(a, b):
    return lax.dot_general(a, b, (((1,), (1,)), ((), ())), preferred_element_type=f32)


def split(v, terms):
    parts = []
    for _ in range(terms):
        part = v.astype(bf16)
        parts.append(part)
        v = v - part.astype(f32)
    return parts


def mm_split(a, exact, terms=2):
    return sum(mm(part, exact) for part in split(a, terms))


def split_mm(exact, b, terms=3):
    return sum(mm(exact, part) for part in split(b, terms))


def spread_matrix(channels):
    heads = lax.broadcasted_iota(jnp.int32, (128, channels), 0)
    cols = lax.broadcasted_iota(jnp.int32, (128, channels), 1)
    low = heads * HEAD
    return jnp.where((cols >= low) & (cols < low + HEAD), 1.0, 0.0).astype(bf16)


def gather_matrix(channels):
    heads = lax.broadcasted_iota(jnp.int32, (channels, 128), 1)
    rows = lax.broadcasted_iota(jnp.int32, (channels, 128), 0)
    low = heads * HEAD
    return jnp.where((rows >= low) & (rows < low + HEAD), 1.0, 0.0).astype(bf16)


def lower_ones():
    rows = lax.broadcasted_iota(jnp.int32, (SPAN, SPAN), 0)
    cols = lax.broadcasted_iota(jnp.int32, (SPAN, SPAN), 1)
    return jnp.where(rows >= cols, 1.0, 0.0).astype(bf16)


def upper_ones():
    rows = lax.broadcasted_iota(jnp.int32, (SPAN, SPAN), 0)
    cols = lax.broadcasted_iota(jnp.int32, (SPAN, SPAN), 1)
    return jnp.where(rows <= cols, 1.0, 0.0).astype(bf16)


def sigmoid(v):
    return 1.0 / (1.0 + jnp.exp(-v))


def half_masks():
    lane = lax.broadcasted_iota(jnp.int32, (SPAN, 128), 1)
    return lane < HEAD


def rms_rows(tok, gain):
    wide = tok.astype(f32)
    inverse = lax.rsqrt(jnp.mean(wide * wide, -1, keepdims=True) + epsilon)
    return (wide * inverse * gain).astype(bf16)


def entry_kernel(
    tok, halo, ngain, w_inner, w_states, w_step, par, spar, head, meta,
    normed_o, pre_o, spre_o, sd_o, ssd_o, x_o, wr_o, step_o, r_o, sig_o, fresh_o, end_o,
    hpre_o, hspre_o,
    xbuf, sbuf, mem,
):
    at = pl.program_id(0)
    channels = w_inner.shape[1]
    gain = ngain[...]

    @pl.when(at == 0)
    def _():
        hn = rms_rows(halo[...], gain)
        hp = mm(hn, w_inner[...])[8:16]
        hs = mm(hn, w_states[...])[8:16]
        xbuf[0:8, :] = hp
        sbuf[0:8, :] = hs
        hpre_o[...] = hp
        hspre_o[...] = hs
        mem[...] = jnp.zeros_like(mem)

    @pl.when(at > 0)
    def _():
        xbuf[0:8, :] = xbuf[SPAN:SPAN + 8, :]
        sbuf[0:8, :] = sbuf[SPAN:SPAN + 8, :]

    normed = rms_rows(tok[...], gain)
    normed_o[...] = normed
    x_pre = mm(normed, w_inner[...])
    s_pre = mm(normed, w_states[...])
    xbuf[8:SPAN + 8, :] = x_pre
    sbuf[8:SPAN + 8, :] = s_pre
    pre_o[...] = x_pre.astype(bf16)
    spre_o[...] = s_pre.astype(bf16)

    def conv_silu(buf, here, taps):
        v = taps[4:5, :] + taps[0:1, :] * here
        for k in range(1, 4):
            v = v + meta[:, k:k + 1] * (taps[k:k + 1, :] * buf[8 - k:8 - k + SPAN, :])
        sg = sigmoid(v)
        return v * sg, sg * (1.0 + v * (1.0 - sg))

    act, slope = conv_silu(xbuf, x_pre, par)
    x_low = act.astype(bf16)
    x_o[...] = x_low
    sd_o[...] = slope.astype(bf16)
    sact, sslope = conv_silu(sbuf, s_pre, spar)
    wr = sact.astype(bf16)
    wr_o[...] = wr
    ssd_o[...] = sslope.astype(bf16)

    raw = mm(normed, w_step[...]) + head[0:1, :]
    step = jnp.maximum(raw, 0.0) + jnp.log1p(jnp.exp(-jnp.abs(raw)))
    sig_o[...] = sigmoid(raw)
    step_o[...] = step
    r = split_mm(lower_ones(), step * head[1:2, :])
    r_o[...] = r
    last = r[SPAN - 1:SPAN, :]
    to_end = jnp.exp2(jnp.minimum(last - r, 0.0)) * meta[:, 5:6]
    spread = spread_matrix(channels)
    coef = mm_split(to_end * step, spread)
    w_t = jnp.transpose(wr[:, 0:128].astype(f32)).astype(bf16)
    fresh = mm(w_t, (coef * x_low.astype(f32)).astype(bf16))
    fresh_o[...] = fresh[None]
    keep = mm_split(jnp.broadcast_to(jnp.exp2(last) * meta[0:1, 6:7], (8, 128)), spread)[0:1]
    mem[...] = keep * mem[...] + fresh
    end_o[...] = mem[...]


def scan_kernel(
    x, wr, r_ref, step_ref, meta, docrow, fresh, state_in, head, par, gate, ggated,
    y_o, sums_o, sprev_o,
    mem, ybuf,
):
    at = pl.program_id(0)
    channels = x.shape[1]

    @pl.when(at == 0)
    def _():
        mem[...] = state_in[...]

    spread = spread_matrix(channels)
    w_low = wr[:, 0:128]
    r_low = wr[:, 128:256]
    r = r_ref[...]
    r_t = jnp.transpose(r)
    rows = lax.broadcasted_iota(jnp.int32, (SPAN, SPAN), 0)
    cols = lax.broadcasted_iota(jnp.int32, (SPAN, SPAN), 1)
    allowed = (rows >= cols) & (meta[:, 0:1] == docrow[...])
    scores = jnp.where(allowed, mm_nt(r_low, w_low), 0.0)
    wide = x[...].astype(f32)
    xd = (mm_split(step_ref[...], spread) * wide).astype(bf16)
    sprev = mem[...].astype(bf16)
    sprev_o[...] = sprev[None]
    linked = jnp.exp2(r) * meta[:, 4:5]
    carried = mm(r_low, sprev) * mm_split(linked, spread)
    skip = mm_split(jnp.broadcast_to(head[2:3, :], (8, 128)), spread)[0:1]
    ybuf[...] = carried + skip * wide
    first = half_masks()
    for pair in range(channels // 128):
        lanes = slice(pair * 128, pair * 128 + 128)
        xp = xd[:, lanes]
        total = ybuf[:, lanes]
        for half in range(2):
            h = 2 * pair + half
            decay = jnp.exp2(jnp.minimum(r[:, h:h + 1] - r_t[h:h + 1, :], 0.0))
            mixing = (scores * decay).astype(bf16)
            own = jnp.where(first if half == 0 else ~first, xp, jnp.zeros_like(xp))
            total = total + mm(mixing, own)
        ybuf[:, lanes] = total
    last = r[SPAN - 1:SPAN, :]
    keep = mm_split(jnp.broadcast_to(jnp.exp2(last) * meta[0:1, 6:7], (8, 128)), spread)[0:1]
    mem[...] = keep * mem[...] + fresh[0]
    y = ybuf[...]
    y_o[...] = y
    g = gate[...]
    mixed = y * (g * sigmoid(g))
    ones = jnp.ones((8, channels), bf16)
    sq = sum(mm_nt(ones, part) for part in split(mixed * mixed, 2))
    pr = sum(mm_nt(ones, part) for part in split(mixed * (par[5:6, :] * ggated[...]), 2))
    row = lax.broadcasted_iota(jnp.int32, (8, SPAN), 0)
    sums_o[...] = jnp.where(row == 0, sq, jnp.where(row == 1, pr, 0.0))


def turn_kernel(
    inner, y_ref, gate, ggated, sums, x, wr, r_ref, meta, head, par,
    gated_o, ggate_o, gy_o, dr_o, dsf_o, dsout_o, acc_o,
    dmem,
):
    at = pl.program_id(0)
    channels = x.shape[1]

    @pl.when(at == 0)
    def _():
        dmem[...] = jnp.zeros_like(dmem)
        acc_o[...] = jnp.zeros_like(acc_o)

    spread = spread_matrix(channels)
    totals = jnp.transpose(sums[...])
    scale = lax.rsqrt(totals[:, 0:1] / inner + epsilon)
    cross = totals[:, 1:2] / inner
    y = y_ref[...]
    g = gate[...]
    sg = sigmoid(g)
    sl = g * sg
    mixed = y * sl
    gg = ggated[...]
    gain = par[5:6, :]
    normal = mixed * scale
    gated_o[...] = (normal * gain).astype(bf16)
    g_mixed = scale * (gain * gg - normal * (scale * cross))
    ggate_o[...] = (g_mixed * y * (sg * (1.0 + g * (1.0 - sg)))).astype(bf16)
    gy = (g_mixed * sl).astype(bf16)
    gy_o[...] = gy
    gyw = gy.astype(f32)
    wide = x[...].astype(f32)
    skip = mm_split(jnp.broadcast_to(head[2:3, :], (8, 128)), spread)[0:1]
    dr_o[...] = mm_split(gyw * (y - skip * wide), gather_matrix(channels))
    row = lax.broadcasted_iota(jnp.int32, (8, channels), 0)
    ggain = jnp.sum(gg * normal, 0, keepdims=True)
    gskip = jnp.sum(gyw * wide, 0, keepdims=True)
    acc_o[...] += jnp.where(row == 0, ggain, jnp.where(row == 1, gskip, 0.0))
    r = r_ref[...]
    linked = mm_split(jnp.exp2(r) * meta[:, 4:5], spread)
    r_t = jnp.transpose(wr[:, 128:256].astype(f32)).astype(bf16)
    dfresh = mm(r_t, (linked * gyw).astype(bf16))
    dsf_o[...] = dfresh[None]
    last = r[SPAN - 1:SPAN, :]
    keep = mm_split(jnp.broadcast_to(jnp.exp2(last) * meta[0:1, 6:7], (8, 128)), spread)[0:1]
    dmem[...] = keep * dmem[...] + dfresh
    dsout_o[...] = dmem[...]


def back_kernel(
    x, wr, gy_ref, r_ref, step_ref, sig_ref, meta, docrow, dr_ref, sprev, dsf, ds_in,
    pre, spre, sd, ssd, hpre, hspre, hmeta, head, par, spar,
    gx_o, gs_o, gz_o, hx_o, hs_o, accx_o, accs_o, acch_o,
    dmem, gbuf, hbuf, dxd,
):
    at = pl.program_id(0)
    channels = x.shape[1]

    @pl.when(at == 0)
    def _():
        dmem[...] = ds_in[...]
        accx_o[...] = jnp.zeros_like(accx_o)
        accs_o[...] = jnp.zeros_like(accs_o)
        acch_o[...] = jnp.zeros_like(acch_o)
        gbuf[...] = jnp.zeros_like(gbuf)
        hbuf[...] = jnp.zeros_like(hbuf)

    @pl.when(at > 0)
    def _():
        gbuf[SPAN + 8:SPAN + 16, :] = gbuf[8:16, :]
        hbuf[SPAN + 8:SPAN + 16, :] = hbuf[8:16, :]

    spread = spread_matrix(channels)
    gather = gather_matrix(channels)
    w_low = wr[:, 0:128]
    r_low = wr[:, 128:256]
    r = r_ref[...]
    r_t = jnp.transpose(r)
    step = step_ref[...]
    last = r[SPAN - 1:SPAN, :]
    rows = lax.broadcasted_iota(jnp.int32, (SPAN, SPAN), 0)
    cols = lax.broadcasted_iota(jnp.int32, (SPAN, SPAN), 1)
    allowed = (rows <= cols) & (meta[:, 0:1] == docrow[...])
    scores = jnp.where(allowed, mm_nt(w_low, r_low), 0.0)
    wide = x[...].astype(f32)
    step_wide = mm_split(step, spread)
    xd = (step_wide * wide).astype(bf16)
    gy = gy_ref[...]
    gyw = gy.astype(f32)
    ds = dmem[...]
    ds_low = ds.astype(bf16)
    te = mm_split(jnp.exp2(jnp.minimum(last - r, 0.0)) * meta[:, 5:6], spread)
    linked = mm_split(jnp.exp2(r) * meta[:, 4:5], spread)
    from_end = te * mm(w_low, ds_low)
    dxd[...] = from_end
    keep = mm_split(jnp.broadcast_to(jnp.exp2(last) * meta[0:1, 6:7], (8, 128)), spread)[0:1]
    ending = jnp.sum(xd.astype(f32) * from_end, 0, keepdims=True) + keep * jnp.sum(
        sprev[0].astype(f32) * ds, 0, keepdims=True
    )
    first = half_masks()
    dscores = jnp.zeros((SPAN, SPAN), f32)
    for pair in range(channels // 128):
        lanes = slice(pair * 128, pair * 128 + 128)
        xp = xd[:, lanes]
        gp = gy[:, lanes]
        total = dxd[:, lanes]
        for half in range(2):
            h = 2 * pair + half
            own = first if half == 0 else ~first
            decay = jnp.exp2(jnp.minimum(r_t[h:h + 1, :] - r[:, h:h + 1], 0.0))
            mixing = (scores * decay).astype(bf16)
            gown = jnp.where(own, gp, jnp.zeros_like(gp))
            total = total + mm(mixing, gown)
            dscores = dscores + mm_nt(xp, gown) * decay
        dxd[:, lanes] = total
    dscores = jnp.where(allowed, dscores, 0.0)
    dlow = dscores.astype(bf16)
    xdw = xd.astype(f32)
    g_write = mm(dlow, r_low) + mm_nt((te * xdw).astype(bf16), ds_low)
    g_read = mm(jnp.transpose(dscores).astype(bf16), w_low) + mm_nt(
        (linked * gyw).astype(bf16), sprev[0]
    )
    skip = mm_split(jnp.broadcast_to(head[2:3, :], (8, 128)), spread)[0:1]
    full = dxd[...]
    g_x = step_wide * full + skip * gyw
    dr = dr_ref[...] - mm_split(xdw * full, gather)
    at_end = mm_split(jnp.broadcast_to(ending, (8, channels)), gather, 3)[0:1]
    tail = lax.broadcasted_iota(jnp.int32, (SPAN, 128), 0) == SPAN - 1
    dr = dr + jnp.where(tail, at_end, 0.0)
    da = split_mm(upper_ones(), dr)
    dstep = mm_split(wide * full, gather) + head[3:4, :] * da
    gz = dstep * sig_ref[...]
    gz_o[...] = gz.astype(bf16)
    row = lax.broadcasted_iota(jnp.int32, (8, 128), 0)
    gbias = jnp.sum(gz, 0, keepdims=True)
    grate = jnp.sum(da * step, 0, keepdims=True)
    acch_o[...] += jnp.where(row == 0, gbias, jnp.where(row == 1, grate, 0.0))
    dmem[...] = keep * ds + dsf[0]

    def conv_back(buf, gv, base, taps, acc, halo_pre, out, halo_out):
        buf[8:SPAN + 8, :] = gv
        width = gv.shape[1]
        total = taps[0:1, :] * gv
        sums = [jnp.sum(gv * base, 0, keepdims=True)]
        halo = jnp.zeros((8, width), f32)
        hsum = []
        for k in range(1, 4):
            moved = meta[:, 7 + k:8 + k] * buf[8 + k:8 + k + SPAN, :]
            total = total + taps[k:k + 1, :] * moved
            sums.append(jnp.sum(moved * base, 0, keepdims=True))
            hmoved = hmeta[:, 7 + k:8 + k] * buf[k:8 + k, :]
            halo = halo + taps[k:k + 1, :] * hmoved
            hsum.append(jnp.sum(hmoved * halo_pre, 0, keepdims=True))
        sums.append(jnp.sum(gv, 0, keepdims=True))
        out[...] = total.astype(bf16)
        halo_out[...] = halo
        rows8 = lax.broadcasted_iota(jnp.int32, (8, width), 0)
        final = jnp.where(at == pl.num_programs(0) - 1, 1.0, 0.0)
        add = jnp.zeros((8, width), f32)
        for i, s in enumerate(sums):
            if 1 <= i <= 3:
                s = s + final * hsum[i - 1]
            add = add + jnp.where(rows8 == i, s, 0.0)
        acc[...] += add

    conv_back(gbuf, g_x * sd[...].astype(f32), pre[...].astype(f32), par, accx_o,
              hpre[...], gx_o, hx_o)
    g_wr = jnp.concatenate([g_write, g_read], 1)
    conv_back(hbuf, g_wr * ssd[...].astype(f32), spre[...].astype(f32), spar, accs_o,
              hspre[...], gs_o, hs_o)


PARAMS = dict(vmem_limit_bytes=56 * 1024 * 1024)


def whole(shape):
    return pl.BlockSpec(shape, lambda i: (0,) * len(shape))


def by_rows(cols, count=None):
    if count is None:
        return pl.BlockSpec((SPAN, cols), lambda i: (i, 0))
    return pl.BlockSpec((SPAN, cols), lambda i: (count - 1 - i, 0))


MESH = pl.DeviceIdType.MESH
SHARE = 4


def lane_block(index, width):
    return pl.ds(pl.multiple_of(index * width, 128), width)


class Links:
    def __init__(self, send, recv):
        self.send, self.recv, self.used, self.all = send, recv, 0, []
        dp = lax.axis_index("dp")
        self.groups = lax.axis_size("dp") // SHARE
        self.group = dp // SHARE
        self.x = lax.rem(dp, SHARE) // 2
        self.core = lax.rem(dp, 2)
        self.y = lax.axis_index("row")
        self.z = lax.axis_index("col")
        self.cols = lax.axis_size("col")

    def dp_of(self, group, x, core):
        return group * SHARE + x * 2 + core

    def mate(self):
        return {"dp": self.dp_of(self.group, self.x, 1 - self.core)}

    def across(self):
        return {"dp": self.dp_of(self.group, 1 - self.x, self.core)}

    def other_row(self):
        return {"row": 1 - self.y}

    def col_peer(self, off):
        return lax.rem(self.z + off, self.cols)

    def group_peer(self, off):
        return {"dp": self.dp_of(lax.rem(self.group + off, self.groups), self.x, self.core)}

    def meet(self, far_groups):
        barrier = pltpu.get_barrier_semaphore()
        peers = [self.mate(), self.across(), self.other_row()]
        peers += [{"col": self.col_peer(off)} for off in range(1, self.cols)]
        if far_groups:
            peers += [self.group_peer(off) for off in range(1, self.groups)]
        for peer in peers:
            pl.semaphore_signal(barrier, inc=1, device_id=peer, device_id_type=MESH)
        pl.semaphore_wait(barrier, len(peers))

    def go(self, src, dst, peer):
        at = self.used
        self.used += 1
        copy = pltpu.make_async_remote_copy(
            src_ref=src, dst_ref=dst, send_sem=self.send.at[at], recv_sem=self.recv.at[at],
            device_id=peer, device_id_type=MESH,
        )
        copy.start()
        self.all.append(copy)
        return copy

    def finish(self):
        for copy in self.all:
            copy.wait_send()


def wavefront(stages, items):
    for turn in range(stages + len(items) - 1):
        for s in reversed(range(stages)):
            m = turn - s
            if 0 <= m < len(items):
                items[m](s)


def fetch_kernel(
    inner, gate, out, step, cot, par, halo,
    wi, wg, wo, ws, cots, pars, halo_in,
    send, recv, local,
):
    t = Links(send, recv)
    t.meet(False)
    x, y, z, core = t.x, t.y, t.z, t.core
    part = inner.shape[0] // SHARE
    block = inner.shape[1] // t.cols
    own_rows = pl.ds(pl.multiple_of((x * 2 + core) * part, 16), part)
    locals_ = []

    def keep(src, dst):
        copy = pltpu.make_async_copy(src, dst, local.at[len(locals_)])
        copy.start()
        locals_.append(copy)
        return copy

    small = [t.go(par, pars.at[y], t.other_row()), t.go(halo, halo_in, t.other_row())]
    keep(par, pars.at[y])

    def column_blocks(src, dst, width):
        lanes = lane_block(y, width)
        copies = []

        def run(s):
            if s == 0:
                for off in range(1, t.cols):
                    to = t.col_peer(off)
                    copies.append(
                        t.go(src.at[own_rows, lane_block(to, width)],
                             dst.at[z, x, core, :, lanes], {"col": to})
                    )
                copies.append(keep(src.at[own_rows, lane_block(z, width)],
                                   dst.at[z, x, core, :, lanes]))
            elif s == 1:
                for c in copies[:-1]:
                    c.wait_recv()
                copies[-1].wait()
                here = dst.at[:, x, core, :, lanes]
                copies.append(t.go(here, here, t.other_row()))
            elif s == 2:
                copies[-1].wait_recv()
                here = dst.at[:, x, core]
                copies.append(t.go(here, here, t.across()))
            elif s == 3:
                copies[-1].wait_recv()
                here = dst.at[:, :, core]
                copies.append(t.go(here, here, t.mate()))
            else:
                copies[-1].wait_recv()

        return run

    def row_blocks(src, dst, width):
        copies = []

        def rows_of(to):
            return pl.ds(pl.multiple_of((to * SHARE + x * 2 + core) * part, 16), part)

        def run(s):
            if s == 0:
                for off in range(1, t.cols):
                    to = t.col_peer(off)
                    copies.append(
                        t.go(src.at[rows_of(to), :], dst.at[y, x, core, :, lane_block(z, width)],
                             {"col": to})
                    )
                copies.append(keep(src.at[rows_of(z), :],
                                   dst.at[y, x, core, :, lane_block(z, width)]))
            elif s == 1:
                for c in copies[:-1]:
                    c.wait_recv()
                copies[-1].wait()
                here = dst.at[y, x, core]
                copies.append(t.go(here, here, t.other_row()))
            elif s == 2:
                copies[-1].wait_recv()
                here = dst.at[:, x, core]
                copies.append(t.go(here, here, t.across()))
            elif s == 3:
                copies[-1].wait_recv()
                here = dst.at[:, :, core]
                copies.append(t.go(here, here, t.mate()))
            else:
                copies[-1].wait_recv()

        return run

    def cot_blocks(s):
        if s == 0:
            lanes = lane_block(z, cot.shape[1])
            for off in range(1, t.cols):
                small.append(t.go(cot, cots.at[:, lanes], {"col": t.col_peer(off)}))
            keep(cot, cots.at[:, lanes])

    wavefront(5, [
        column_blocks(inner, wi, block), column_blocks(step, ws, step.shape[1] // t.cols),
        column_blocks(gate, wg, block), row_blocks(out, wo, out.shape[1]), cot_blocks,
    ])
    for c in small:
        c.wait_recv()
    locals_[0].wait()
    locals_[-1].wait()
    t.finish()


def fetch(inner, gate, out, step, cot, par, halo):
    rows, all_cols = inner.shape
    cols = lax.axis_size("col")
    part, block = rows // SHARE, all_cols // cols
    sds = jax.ShapeDtypeStruct
    wide = sds((cols, 2, 2, part, 2 * block), bf16)
    shapes = [
        wide, wide, sds((2, 2, 2, out.shape[0] // cols // SHARE, cols * out.shape[1]), bf16),
        sds((cols, 2, 2, part, 2 * (step.shape[1] // cols)), bf16),
        sds((cot.shape[0], cols * cot.shape[1]), bf16), sds((2,) + par.shape, f32),
        sds(halo.shape, bf16),
    ]
    got = pl.pallas_call(
        fetch_kernel,
        out_shape=shapes,
        in_specs=[pl.BlockSpec(memory_space=pl.ANY)] * 7,
        out_specs=[pl.BlockSpec(memory_space=pl.ANY)] * 7,
        scratch_shapes=[
            pltpu.SemaphoreType.DMA((40,)), pltpu.SemaphoreType.DMA((40,)),
            pltpu.SemaphoreType.DMA((8,)),
        ],
        compiler_params=pltpu.CompilerParams(collective_id=1, has_side_effects=True),
        name="fetch",
    )(inner, gate, out, step, cot, par, halo)
    wi, wg, wo, ws, cots, pars, halo_in = got
    width = rows * cols
    return (
        wi.reshape(width, -1), wg.reshape(width, -1), wo.reshape(2 * block, -1),
        ws.reshape(width, -1), cots, pars, halo_in,
    )


def col_sum_kernel(v, total, got, send, recv):
    t = Links(send, recv)
    barrier = pltpu.get_barrier_semaphore()
    for off in range(1, t.cols):
        pl.semaphore_signal(
            barrier, inc=1, device_id={"col": t.col_peer(off)}, device_id_type=MESH
        )
    pl.semaphore_wait(barrier, t.cols - 1)
    copies = [t.go(v, got.at[off - 1], {"col": t.col_peer(off)}) for off in range(1, t.cols)]
    for c in copies:
        c.wait_recv()
    total[...] = v[...] + got[0] + got[1] + got[2]
    t.finish()


def col_sum(v):
    cols = lax.axis_size("col")
    return pl.pallas_call(
        col_sum_kernel,
        out_shape=jax.ShapeDtypeStruct(v.shape, v.dtype),
        in_specs=[pl.BlockSpec(memory_space=pltpu.VMEM)],
        out_specs=pl.BlockSpec(memory_space=pltpu.VMEM),
        scratch_shapes=[
            pltpu.VMEM((cols - 1,) + v.shape, v.dtype),
            pltpu.SemaphoreType.DMA((cols - 1,)), pltpu.SemaphoreType.DMA((cols - 1,)),
        ],
        compiler_params=pltpu.CompilerParams(collective_id=2, has_side_effects=True),
        name="colsum",
    )(v)


def add_into(target, source, count, index_target, index_source):
    def body(i, carry):
        a, b = index_target(i), index_source(i)
        target[a] = (target[a].astype(f32) + source[b].astype(f32)).astype(target.dtype)
        return carry

    lax.fori_loop(0, count, body, 0)


def tail_kernel(
    part, ish, gi, gg, gz, go, gs, sm,
    own_o, ish_o, oi, og, oz, oo, os, sm_o,
    rpart, rish, i1, i2, i3, i4, g1, g2, g3, g4, z1, z2, z3, z4, o1, o2, o3, o4, s1, s2, s3, s4, s5,
    msum, mgot, far_i, far_g, far_o, far_z, far_s, send, recv,
):
    t = Links(send, recv)
    t.meet(True)
    x, y, z, core = t.x, t.y, t.z, t.core
    third = own_o.shape[1]
    rows = own_o.shape[0]

    sums = []
    for off in range(1, t.cols):
        to = t.col_peer(off)
        sums.append(t.go(ish, rish.at[off - 1], {"col": to}))
    parts = []

    def part_item(s):
        if s == 0:
            for off in range(1, t.cols):
                to = t.col_peer(off)
                parts.append(t.go(part.at[:, lane_block(to, third)], rpart.at[off - 1], {"col": to}))

    def matrix(g, a1, a2, a3, a4, far, o, by_col):
        width = a4.shape[-1] if by_col else a4.shape[-1] // t.cols
        copies = []
        lead = g.shape[0]

        def run(s):
            if s == 0:
                copies.append(t.go(g.at[:, :, 1 - core], a1, t.mate()))
            elif s == 1:
                copies[-1].wait_recv()

                def body(i, c):
                    for j in range(2):
                        a1[i, j] = (a1[i, j].astype(f32) + g[i, j, core].astype(f32)).astype(bf16)
                    return c

                lax.fori_loop(0, lead, body, 0)
                if by_col:
                    copies.append(t.go(a1.at[:, :, :, lane_block(1 - y, width)], a2, t.other_row()))
                else:
                    copies.append(t.go(a1.at[1 - y], a2, t.other_row()))
            elif s == 2:
                copies[-1].wait_recv()
                if by_col:
                    def body(i, c):
                        for j in range(2):
                            mine = a1[i, j, :, lane_block(y, width)]
                            a2[i, j] = (a2[i, j].astype(f32) + mine.astype(f32)).astype(bf16)
                        return c

                    lax.fori_loop(0, lead, body, 0)
                    copies.append(t.go(a2.at[:, 1 - x], a3, t.across()))
                else:
                    for j in range(2):
                        a2[j] = (a2[j].astype(f32) + a1[y, j].astype(f32)).astype(bf16)
                    copies.append(t.go(a2.at[1 - x], a3, t.across()))
            elif s == 3:
                copies[-1].wait_recv()
                if by_col:
                    def body(i, c):
                        a4[i] = (a3[i].astype(f32) + a2[i, x].astype(f32)).astype(bf16)
                        return c

                    lax.fori_loop(0, lead, body, 0)
                else:
                    a4[...] = (a3[...].astype(f32) + a2[x].astype(f32)).astype(bf16)
                if t.groups > 1:
                    more = [t.go(a4, far.at[off - 1], t.group_peer(off))
                            for off in range(1, t.groups)]
                    for c in more:
                        c.wait()
                    total = a4[...].astype(f32)
                    for off in range(1, t.groups):
                        total = total + far[off - 1].astype(f32)
                    a4[...] = total.astype(bf16)
                copies.clear()
                for off in range(1, t.cols):
                    to = t.col_peer(off)
                    if by_col:
                        copies.append(
                            t.go(a4.at[to], o.at[x, core, :, lane_block(z, width)], {"col": to})
                        )
                    else:
                        copies.append(
                            t.go(a4.at[:, lane_block(to, width)], o.at[z, x, core], {"col": to})
                        )
                if by_col:
                    o[x, core, :, lane_block(z, width)] = a4[z]
                else:
                    o[z, x, core] = a4[:, lane_block(z, width)]
            elif s == 4:
                for c in copies:
                    c.wait_recv()
                here = o.at[x, core] if by_col else o.at[:, x, core]
                copies.append(t.go(here, here, t.across()))
            elif s == 5:
                copies[-1].wait_recv()
                here = o.at[:, core] if by_col else o.at[:, :, core]
                copies.append(t.go(here, here, t.mate()))
            else:
                copies[-1].wait_recv()

        return run

    state_copies = []

    def states(s):
        copies = state_copies
        if s == 0:
            copies.append(t.go(gs.at[:, :, :, 1 - core], s1, t.mate()))
        elif s == 1:
            copies[-1].wait_recv()

            def body(i, c):
                for j in range(2):
                    for k in range(2):
                        s1[i, j, k] = (
                            s1[i, j, k].astype(f32) + gs[i, j, k, core].astype(f32)
                        ).astype(bf16)
                return c

            lax.fori_loop(0, t.cols, body, 0)
            copies.append(t.go(s1.at[:, 1 - y], s2, t.other_row()))
        elif s == 2:
            copies[-1].wait_recv()

            def body(i, c):
                for k in range(2):
                    s2[i, k] = (s2[i, k].astype(f32) + s1[i, y, k].astype(f32)).astype(bf16)
                return c

            lax.fori_loop(0, t.cols, body, 0)
            copies.append(t.go(s2.at[:, 1 - x], s3, t.across()))
        elif s == 3:
            copies[-1].wait_recv()

            def body(i, c):
                s4[i] = (s3[i].astype(f32) + s2[i, x].astype(f32)).astype(bf16)
                return c

            lax.fori_loop(0, t.cols, body, 0)
            if t.groups > 1:
                more = [t.go(s4, far_s.at[off - 1], t.group_peer(off))
                        for off in range(1, t.groups)]
                for c in more:
                    c.wait()
                total = s4[...].astype(f32)
                for off in range(1, t.groups):
                    total = total + far_s[off - 1].astype(f32)
                s4[...] = total.astype(bf16)
            copies.clear()
            for off in range(1, t.cols):
                to = t.col_peer(off)
                copies.append(t.go(s4.at[to], s5.at[off - 1], {"col": to}))
        elif s == 4:
            for c in copies:
                c.wait_recv()
            total = s4[z].astype(f32)
            for off in range(1, t.cols):
                total = total + s5[off - 1].astype(f32)
            os[z, y, x, core] = total.astype(bf16)
            copies.clear()
            here = os.at[z, y, x, core]
            for off in range(1, t.cols):
                copies.append(t.go(here, here, {"col": t.col_peer(off)}))
        elif s == 5:
            for c in copies:
                c.wait_recv()
            here = os.at[:, y, x, core]
            copies.append(t.go(here, here, t.other_row()))
        elif s == 6:
            copies[-1].wait_recv()
            here = os.at[:, :, x, core]
            copies.append(t.go(here, here, t.across()))
        elif s == 7:
            copies[-1].wait_recv()
            here = os.at[:, :, :, core]
            copies.append(t.go(here, here, t.mate()))
        else:
            copies[-1].wait_recv()

    few = []
    tail_rows = sm.shape[0] * 3 // 8

    def smalls(s):
        if s == 0:
            few.append(t.go(sm, mgot.at[0], t.mate()))
        elif s == 1:
            few[-1].wait_recv()
            msum[0] = sm[...] + mgot[0]
            few.append(t.go(msum.at[0], mgot.at[1], t.other_row()))
        elif s == 2:
            few[-1].wait_recv()
            msum[1] = msum[0] + mgot[1]
            few.append(t.go(msum.at[1], mgot.at[2], t.across()))
        elif s == 3:
            few[-1].wait_recv()
            msum[2] = msum[1] + mgot[2]
            if t.groups > 1:
                more = [t.go(msum.at[2], mgot.at[5 + off], t.group_peer(off))
                        for off in range(1, t.groups)]
                for c in more:
                    c.wait()
                total = msum[2]
                for off in range(1, t.groups):
                    total = total + mgot[5 + off]
                msum[2] = total
            few.clear()
            last = pl.ds(sm.shape[0] - tail_rows, tail_rows)
            for off in range(1, t.cols):
                few.append(t.go(msum.at[2, last], mgot.at[2 + off, last], {"col": t.col_peer(off)}))
        elif s == 4:
            for c in few:
                c.wait_recv()
            top = sm.shape[0] - tail_rows
            sm_o[0:top] = msum[2, 0:top]
            sm_o[top:] = msum[2, top:] + mgot[3, top:] + mgot[4, top:] + mgot[5, top:]

    def late(item, limit):
        return lambda s: item(s) if s <= limit else None

    wavefront(9, [
        late(matrix(go, o1, o2, o3, o4, far_o, oo, False), 6),
        late(part_item, 0),
        late(matrix(gi, i1, i2, i3, i4, far_i, oi, True), 6),
        late(matrix(gz, z1, z2, z3, z4, far_z, oz, True), 6),
        late(smalls, 4),
        states,
        late(matrix(gg, g1, g2, g3, g4, far_g, og, True), 6),
    ])
    for c in sums:
        c.wait_recv()
    ish_o[...] = ish[...] + rish[0] + rish[1] + rish[2]
    for c in parts:
        c.wait_recv()

    def add_rows(i, c):
        at = pl.ds(pl.multiple_of(i * 64, 64), 64)
        total = part[at, lane_block(z, third)].astype(f32)
        for j in range(t.cols - 1):
            total = total + rpart[j, at].astype(f32)
        own_o[at] = total
        return c

    lax.fori_loop(0, rows // 64, add_rows, 0)
    t.finish()


def tail(part, ish, gi, gg, gz, go, gs, sm):
    cols = lax.axis_size("col")
    groups = max(lax.axis_size("dp") // SHARE - 1, 1)
    rows, width = part.shape
    third = width // cols
    own = gi.shape[1] // 2
    q = third // SHARE
    qo = own // SHARE
    qs = width // (cols * 2 * SHARE)
    zl = gz.shape[1] // 2
    sds = jax.ShapeDtypeStruct
    V = pltpu.VMEM

    def col_scratch(w):
        return [
            V((cols, 2, q, 2 * w), bf16), V((cols, 2, q, w), bf16), V((cols, q, w), bf16),
            V((cols, q, w), bf16),
        ]

    got = pl.pallas_call(
        tail_kernel,
        out_shape=[
            sds((rows, third), f32), sds(ish.shape, f32),
            sds((2, 2, q, cols * own), bf16), sds((2, 2, q, cols * own), bf16),
            sds((2, 2, q, cols * zl), bf16), sds((cols, 2, 2, qo, third), bf16),
            sds((cols, 2, 2, 2, qs, gs.shape[1]), bf16), sds(sm.shape, f32),
        ],
        in_specs=[pl.BlockSpec(memory_space=V)] * 8,
        out_specs=[pl.BlockSpec(memory_space=V)] * 8,
        scratch_shapes=[
            V((cols - 1, rows, third), bf16), V((cols - 1,) + ish.shape, f32),
        ] + col_scratch(own) + col_scratch(own) + col_scratch(zl) + [
            V((2, 2, qo, width), bf16), V((2, qo, width), bf16), V((qo, width), bf16),
            V((qo, width), bf16),
            V((cols, 2, 2, qs, gs.shape[1]), bf16), V((cols, 2, qs, gs.shape[1]), bf16),
            V((cols, qs, gs.shape[1]), bf16), V((cols, qs, gs.shape[1]), bf16),
            V((cols - 1, qs, gs.shape[1]), bf16),
            V((3,) + sm.shape, f32), V((6 + groups,) + sm.shape, f32),
            V((groups, cols, q, own), bf16), V((groups, cols, q, own), bf16),
            V((groups, qo, width), bf16),
            V((groups, cols, q, zl), bf16), V((groups, cols, qs, gs.shape[1]), bf16),
            pltpu.SemaphoreType.DMA((80,)), pltpu.SemaphoreType.DMA((80,)),
        ],
        compiler_params=pltpu.CompilerParams(
            collective_id=3, has_side_effects=True, vmem_limit_bytes=56 * 1024 * 1024
        ),
        name="tail",
    )(
        part, ish, gi.reshape(cols, 2, 2, q, 2 * own), gg.reshape(cols, 2, 2, q, 2 * own),
        gz.reshape(cols, 2, 2, q, 2 * zl), go.reshape(2, 2, 2, qo, width),
        gs.reshape(cols, 2, 2, 2, qs, gs.shape[1]), sm,
    )
    own_o, ish_o, oi, og, oz, oo, os, sm_o = got
    return (
        own_o, ish_o, oi.reshape(third, -1), og.reshape(third, -1), oz.reshape(third, -1),
        oo.reshape(cols * own, third), os.reshape(width, -1), sm_o,
    )


def per_device(
    tokens_in, segment_ids, norm_gain, proj_gate, proj_inner, proj_step, proj_states,
    conv_inner, conv_inner_bias, conv_states, conv_states_bias, step_bias, decay_log,
    skip_gain, gate_gain, proj_out, cotangent,
):
    tokens, width = tokens_in.shape
    blocks = tokens // SPAN
    row = lax.axis_index("row")
    col = lax.axis_index("col")
    cols = lax.axis_size("col")
    own_ch = conv_inner.shape[1]
    own_heads = step_bias.shape[0]
    channels = 2 * own_ch
    inner_all = channels * cols
    col_width = width // cols

    heads_own = jnp.stack([step_bias, decay_log, skip_gain])
    own = jnp.concatenate(
        [
            conv_inner,
            conv_inner_bias[None],
            gate_gain[None],
            jnp.pad(heads_own.reshape(1, -1), ((0, 0), (0, own_ch - 3 * own_heads))),
            jnp.zeros((1, own_ch), f32),
        ],
        0,
    )
    pieces = jnp.pad(
        proj_step.reshape(col_width, cols, own_heads), ((0, 0), (0, 0), (0, 128 - own_heads))
    ).reshape(col_width, cols * 128)
    w_inner, w_gate, w_out, w_step, cot_all, both, halo = fetch(
        proj_inner, proj_gate, proj_out, pieces, cotangent, own, tokens_in[-16:]
    )
    w_step = jnp.concatenate([w_step[:, :own_heads], w_step[:, 128:128 + own_heads]], 1)
    w_step = jnp.pad(w_step, ((0, 0), (0, 128 - 2 * own_heads)))
    par = jnp.concatenate([both[0], both[1]], 1)
    hp = jnp.concatenate(
        [both[i, 6, : 3 * own_heads].reshape(3, own_heads) for i in range(2)], 1
    )
    rate = -jnp.exp(hp[1])
    head = jnp.pad(
        jnp.stack([hp[0], rate * LOG2E, hp[2], rate]), ((0, 4), (0, 128 - 2 * own_heads))
    )
    spar = jnp.concatenate([conv_states, conv_states_bias[None], jnp.zeros((3, 256), f32)], 0)

    docs = jnp.pad(segment_ids[0].astype(f32), (8, 8), constant_values=-1.0)
    docs = lax.dynamic_slice_in_dim(docs, row * tokens, tokens + 16, 0)
    here = docs[8:8 + tokens]
    spans = here.reshape(blocks, SPAN)
    before = jnp.concatenate([docs[7:8], spans[:-1, -1]])
    after = spans[:, -1]

    def flat(cond):
        return jnp.broadcast_to(cond, (blocks, SPAN)).reshape(tokens)

    def forward_same(start, count):
        own_docs = docs[start:start + count]
        return [own_docs == docs[start + k:start + k + count] for k in range(1, 4)]

    meta = jnp.stack(
        [here]
        + [(here == docs[8 - k:8 - k + tokens]) for k in range(1, 4)]
        + [
            flat(spans == before[:, None]),
            flat(spans == after[:, None]),
            flat((before == after)[:, None]),
            jnp.zeros_like(here),
        ]
        + forward_same(8, tokens)
        + [jnp.zeros_like(here)] * 5,
        1,
    ).astype(f32)
    hmeta = jnp.stack(
        [jnp.zeros((8,), f32)] * 8
        + forward_same(0, 8)
        + [jnp.zeros((8,), f32)] * 5,
        1,
    ).astype(f32)
    docrow = here[None, :]

    sds = jax.ShapeDtypeStruct
    (
        normed, pre, spre, sd, ssd, x_low, wr, step, r, sig, fresh, end, hpre, hspre,
    ) = pl.pallas_call(
        entry_kernel,
        grid=(blocks,),
        in_specs=[
            by_rows(width), whole((16, width)), whole((1, width)), whole((width, channels)),
            whole((width, 256)), whole((width, 128)), whole((8, channels)), whole((8, 256)),
            whole((8, 128)), by_rows(16),
        ],
        out_specs=[
            by_rows(width), by_rows(channels), by_rows(256), by_rows(channels), by_rows(256),
            by_rows(channels), by_rows(256), by_rows(128), by_rows(128), by_rows(128),
            pl.BlockSpec((1, 128, channels), lambda i: (i, 0, 0)), whole((128, channels)),
            whole((8, channels)), whole((8, 256)),
        ],
        out_shape=[
            sds((tokens, width), bf16), sds((tokens, channels), bf16), sds((tokens, 256), bf16),
            sds((tokens, channels), bf16), sds((tokens, 256), bf16),
            sds((tokens, channels), bf16), sds((tokens, 256), bf16),
            sds((tokens, 128), f32), sds((tokens, 128), f32), sds((tokens, 128), f32),
            sds((blocks, 128, channels), f32), sds((128, channels), f32),
            sds((8, channels), f32), sds((8, 256), f32),
        ],
        scratch_shapes=[
            pltpu.VMEM((SPAN + 8, channels), f32),
            pltpu.VMEM((SPAN + 8, 256), f32),
            pltpu.VMEM((128, channels), f32),
        ],
        compiler_params=pltpu.CompilerParams(**PARAMS),
        name="entry",
    )(tokens_in, halo, norm_gain[None], w_inner, proj_states, w_step, par, spar, head, meta)

    state_in = lax.ppermute(end, "row", [(0, 1)])
    gate = mm(normed, w_gate)
    ggated = mm_nt(cot_all, w_out)

    y, sums, sprev = pl.pallas_call(
        scan_kernel,
        grid=(blocks,),
        in_specs=[
            by_rows(channels), by_rows(256), by_rows(128), by_rows(128), by_rows(16),
            pl.BlockSpec((1, SPAN), lambda i: (0, i)),
            pl.BlockSpec((1, 128, channels), lambda i: (i, 0, 0)), whole((128, channels)),
            whole((8, 128)), whole((8, channels)), by_rows(channels), by_rows(channels),
        ],
        out_specs=[
            by_rows(channels), pl.BlockSpec((8, SPAN), lambda i: (0, i)),
            pl.BlockSpec((1, 128, channels), lambda i: (i, 0, 0)),
        ],
        out_shape=[
            sds((tokens, channels), f32), sds((8, tokens), f32),
            sds((blocks, 128, channels), bf16),
        ],
        scratch_shapes=[pltpu.VMEM((128, channels), f32), pltpu.VMEM((SPAN, channels), f32)],
        compiler_params=pltpu.CompilerParams(**PARAMS),
        name="scan",
    )(x_low, wr, r, step, meta, docrow, fresh, state_in, head, par, gate, ggated)

    sums = col_sum(sums)

    back3 = pl.BlockSpec((1, 128, channels), lambda i: (blocks - 1 - i, 0, 0))
    gated, g_gate, gy, dr, dsf, dsout, acc1 = pl.pallas_call(
        functools.partial(turn_kernel, float(inner_all)),
        grid=(blocks,),
        in_specs=[
            by_rows(channels, blocks), by_rows(channels, blocks), by_rows(channels, blocks),
            pl.BlockSpec((8, SPAN), lambda i: (0, blocks - 1 - i)),
            by_rows(channels, blocks), by_rows(256, blocks), by_rows(128, blocks),
            by_rows(16, blocks), whole((8, 128)), whole((8, channels)),
        ],
        out_specs=[
            by_rows(channels, blocks), by_rows(channels, blocks), by_rows(channels, blocks),
            by_rows(128, blocks), back3, whole((128, channels)), whole((8, channels)),
        ],
        out_shape=[
            sds((tokens, channels), bf16), sds((tokens, channels), bf16),
            sds((tokens, channels), bf16), sds((tokens, 128), f32),
            sds((blocks, 128, channels), f32), sds((128, channels), f32),
            sds((8, channels), f32),
        ],
        scratch_shapes=[pltpu.VMEM((128, channels), f32)],
        compiler_params=pltpu.CompilerParams(**PARAMS),
        name="turn",
    )(y, gate, ggated, sums, x_low, wr, r, meta, head, par)

    ds_in = lax.ppermute(dsout, "row", [(1, 0)])
    out_part = mm(gated, w_out).astype(bf16)
    out_cols = lax.psum_scatter(out_part, "col", scatter_dimension=1, tiled=True)
    own_tokens = lax.dynamic_slice_in_dim(tokens_in, col * col_width, col_width, 1).astype(f32)
    mixed_out = (own_tokens + out_cols.astype(f32)).astype(bf16)
    grad_out_part = lax.dot_general(
        gated, cot_all, (((0,), (0,)), ((), ())), preferred_element_type=f32
    )

    gx, gs, gz, hx, hs, accx, accs, acch = pl.pallas_call(
        back_kernel,
        grid=(blocks,),
        in_specs=[
            by_rows(channels, blocks), by_rows(256, blocks), by_rows(channels, blocks),
            by_rows(128, blocks), by_rows(128, blocks), by_rows(128, blocks),
            by_rows(16, blocks), pl.BlockSpec((1, SPAN), lambda i: (0, blocks - 1 - i)),
            by_rows(128, blocks), back3, back3, whole((128, channels)),
            by_rows(channels, blocks), by_rows(256, blocks), by_rows(channels, blocks),
            by_rows(256, blocks), whole((8, channels)), whole((8, 256)), whole((8, 16)),
            whole((8, 128)), whole((8, channels)), whole((8, 256)),
        ],
        out_specs=[
            by_rows(channels, blocks), by_rows(256, blocks), by_rows(128, blocks),
            whole((8, channels)), whole((8, 256)), whole((8, channels)), whole((8, 256)),
            whole((8, 128)),
        ],
        out_shape=[
            sds((tokens, channels), bf16), sds((tokens, 256), bf16), sds((tokens, 128), bf16),
            sds((8, channels), f32), sds((8, 256), f32), sds((8, channels), f32),
            sds((8, 256), f32), sds((8, 128), f32),
        ],
        scratch_shapes=[
            pltpu.VMEM((128, channels), f32),
            pltpu.VMEM((SPAN + 16, channels), f32),
            pltpu.VMEM((SPAN + 16, 256), f32),
            pltpu.VMEM((SPAN, channels), f32),
        ],
        compiler_params=pltpu.CompilerParams(**PARAMS),
        name="back",
    )(
        x_low, wr, gy, r, step, sig, meta, docrow, dr, sprev, dsf, ds_in,
        pre, spre, sd, ssd, hpre, hspre, hmeta, head, par, spar,
    )

    hx_in, hs_in = lax.ppermute((hx, hs), "row", [(1, 0)])
    gx = gx.at[-8:].add(hx_in.astype(bf16))
    gs = gs.at[-8:].add(hs_in.astype(bf16))

    normed_grad = (
        mm_nt(g_gate, w_gate) + mm_nt(gx, w_inner) + mm_nt(gz, w_step) + mm_nt(gs, proj_states)
    )
    wide = tokens_in.astype(f32)
    inverse = lax.rsqrt(jnp.mean(wide * wide, -1, keepdims=True) + epsilon)
    input_share = jnp.sum(normed_grad * norm_gain * wide, -1)
    gain_share = jnp.sum(normed_grad * (wide * inverse), 0)

    def weight_grad(left, right):
        return lax.dot_general(
            left, right, (((0,), (0,)), ((), ())), preferred_element_type=f32
        ).astype(bf16)

    def head_sum(values):
        return values.reshape(2 * own_heads, HEAD).sum(-1)

    def lanes(values, multiple):
        values = values.reshape(-1)
        return jnp.pad(values, (0, multiple * 128 - values.shape[0])).reshape(multiple, 128)

    small = jnp.concatenate(
        [
            accx[0:5].reshape(5, 2, own_ch).transpose(1, 0, 2).reshape(2, -1),
            acc1[0].reshape(2, own_ch),
            acch[0, : 2 * own_heads].reshape(2, own_heads),
            (acch[1] * head[3])[: 2 * own_heads].reshape(2, own_heads),
            head_sum(acc1[1]).reshape(2, own_heads),
        ],
        1,
    )
    few = jnp.concatenate(
        [lanes(small, 40), lanes(jnp.concatenate([accs[0:5].reshape(-1), gain_share]), 24)], 0
    )
    gz_rows = jnp.concatenate(
        [
            jnp.pad(gz[:, i * own_heads:(i + 1) * own_heads], ((0, 0), (0, 128 - own_heads)))
            for i in range(2)
        ],
        1,
    )
    own_grad, input_total, oi, og, oz, oo, os, few = tail(
        normed_grad.astype(bf16), input_share.reshape(8, -1), weight_grad(normed, gx),
        weight_grad(normed, g_gate), weight_grad(normed, gz_rows), grad_out_part.astype(bf16),
        weight_grad(normed, gs), few,
    )
    input_total = input_total.reshape(tokens, 1)
    gain_cols = lax.dynamic_slice_in_dim(norm_gain, col * col_width, col_width, 0)
    grad_input = inverse * (own_grad * gain_cols) - own_tokens * inverse**3 * (input_total / width)
    grad_tokens = (grad_input + cotangent.astype(f32)).astype(bf16)
    grad_inner = oi.astype(f32)
    grad_gate = og.astype(f32)
    grad_out = oo.astype(f32)
    grad_states = os.astype(f32)
    grad_step = oz.reshape(col_width, cols, 128)[:, :, :own_heads].astype(f32)
    grad_step = grad_step.reshape(col_width, cols * own_heads)
    small = few[:40].reshape(-1)[: small.size].reshape(2, -1)
    small = lax.dynamic_index_in_dim(small, row, 0, keepdims=False)
    grad_conv_inner = small[: 4 * own_ch].reshape(4, own_ch)
    grad_conv_inner_bias = small[4 * own_ch:5 * own_ch]
    grad_gate_gain = small[5 * own_ch:6 * own_ch]
    rest = small[6 * own_ch:].reshape(3, own_heads)
    summed = few[40:].reshape(-1)
    accs = summed[: 5 * 256].reshape(5, 256)
    grad_norm_gain = lax.dynamic_slice_in_dim(
        summed, 5 * 256 + col * col_width, col_width, 0
    )

    return (
        mixed_out,
        grad_tokens,
        grad_norm_gain,
        grad_gate,
        grad_inner,
        grad_step,
        grad_states,
        grad_conv_inner,
        grad_conv_inner_bias,
        accs[0:4],
        accs[4],
        rest[0],
        rest[1],
        rest[2],
        grad_gate_gain,
        grad_out,
    )


def solution(mesh):
    in_specs = (
        P(("dp", "row"), None),
        P("dp", None),
        P(),
        P("col", "row"),
        P("col", "row"),
        P("col", "row"),
        P(),
        P(None, ("row", "col")),
        P(("row", "col")),
        P(),
        P(),
        P(("row", "col")),
        P(("row", "col")),
        P(("row", "col")),
        P(("row", "col")),
        P("row", "col"),
        P(("dp", "row"), "col"),
    )
    out_specs = (
        P(("dp", "row"), "col"),
        P(("dp", "row"), "col"),
        P("col"),
        P("col", "row"),
        P("col", "row"),
        P("col", "row"),
        P(),
        P(None, ("row", "col")),
        P(("row", "col")),
        P(),
        P(),
        P(("row", "col")),
        P(("row", "col")),
        P(("row", "col")),
        P(("row", "col")),
        P("row", "col"),
    )
    return jax.shard_map(
        per_device, mesh=mesh, in_specs=in_specs, out_specs=out_specs, check_vma=False
    )
```

```python
import functools

import jax
import jax.numpy as jnp
from jax import lax
from jax.experimental import pallas as pl
from jax.experimental.pallas import tpu as pltpu
from jax.sharding import PartitionSpec as P

SPAN = 256
HEAD = 64
epsilon = 1e-05
LOG2E = 1.4426950408889634
f32 = jnp.float32
bf16 = jnp.bfloat16
ANY = pl.ANY


def mm(a, b):
    return lax.dot_general(a, b, (((1,), (0,)), ((), ())), preferred_element_type=f32)


def mm_nt(a, b):
    return lax.dot_general(a, b, (((1,), (1,)), ((), ())), preferred_element_type=f32)


def split(v, terms):
    parts = []
    for _ in range(terms):
        part = v.astype(bf16)
        parts.append(part)
        v = v - part.astype(f32)
    return parts


def mm_split(a, exact, terms=2):
    return sum(mm(part, exact) for part in split(a, terms))


def split_mm(exact, b, terms=3):
    return sum(mm(exact, part) for part in split(b, terms))


def spread_matrix(channels):
    heads = lax.broadcasted_iota(jnp.int32, (128, channels), 0)
    cols = lax.broadcasted_iota(jnp.int32, (128, channels), 1)
    low = heads * HEAD
    return jnp.where((cols >= low) & (cols < low + HEAD), 1.0, 0.0).astype(bf16)


def gather_matrix(channels):
    heads = lax.broadcasted_iota(jnp.int32, (channels, 128), 1)
    rows = lax.broadcasted_iota(jnp.int32, (channels, 128), 0)
    low = heads * HEAD
    return jnp.where((rows >= low) & (rows < low + HEAD), 1.0, 0.0).astype(bf16)


def lower_ones():
    rows = lax.broadcasted_iota(jnp.int32, (SPAN, SPAN), 0)
    cols = lax.broadcasted_iota(jnp.int32, (SPAN, SPAN), 1)
    return jnp.where(rows >= cols, 1.0, 0.0).astype(bf16)


def upper_ones():
    rows = lax.broadcasted_iota(jnp.int32, (SPAN, SPAN), 0)
    cols = lax.broadcasted_iota(jnp.int32, (SPAN, SPAN), 1)
    return jnp.where(rows <= cols, 1.0, 0.0).astype(bf16)


def sigmoid(v):
    return 1.0 / (1.0 + jnp.exp(-v))


def half_masks():
    lane = lax.broadcasted_iota(jnp.int32, (SPAN, 128), 1)
    return lane < HEAD


def rms_rows(tok, gain):
    wide = tok.astype(f32)
    inverse = lax.rsqrt(jnp.mean(wide * wide, -1, keepdims=True) + epsilon)
    return (wide * inverse * gain).astype(bf16)


def back_kernel(
    x, wr, gy_ref, r_ref, step_ref, sig_ref, meta, docrow, dr_ref, sprev, dsf, ds_in,
    pre, spre, sd, ssd, hpre, hspre, hmeta, head, par, spar,
    gx_o, gs_o, gz_o, hx_o, hs_o, accx_o, accs_o, acch_o,
    dmem, gbuf, hbuf, dxd,
):
    at = pl.program_id(0)
    channels = x.shape[1]

    @pl.when(at == 0)
    def _():
        dmem[...] = ds_in[...]
        accx_o[...] = jnp.zeros_like(accx_o)
        accs_o[...] = jnp.zeros_like(accs_o)
        acch_o[...] = jnp.zeros_like(acch_o)
        gbuf[...] = jnp.zeros_like(gbuf)
        hbuf[...] = jnp.zeros_like(hbuf)

    @pl.when(at > 0)
    def _():
        gbuf[SPAN + 8:SPAN + 16, :] = gbuf[8:16, :]
        hbuf[SPAN + 8:SPAN + 16, :] = hbuf[8:16, :]

    spread = spread_matrix(channels)
    gather = gather_matrix(channels)
    w_low = wr[:, 0:128]
    r_low = wr[:, 128:256]
    r = r_ref[...]
    r_t = jnp.transpose(r)
    step = step_ref[...]
    last = r[SPAN - 1:SPAN, :]
    rows = lax.broadcasted_iota(jnp.int32, (SPAN, SPAN), 0)
    cols = lax.broadcasted_iota(jnp.int32, (SPAN, SPAN), 1)
    allowed = (rows <= cols) & (meta[:, 0:1] == docrow[...])
    scores = jnp.where(allowed, mm_nt(w_low, r_low), 0.0)
    wide = x[...].astype(f32)
    step_wide = mm_split(step, spread)
    xd = (step_wide * wide).astype(bf16)
    gy = gy_ref[...]
    gyw = gy.astype(f32)
    ds = dmem[...]
    ds_low = ds.astype(bf16)
    te = mm_split(jnp.exp2(jnp.minimum(last - r, 0.0)) * meta[:, 5:6], spread)
    linked = mm_split(jnp.exp2(r) * meta[:, 4:5], spread)
    from_end = te * mm(w_low, ds_low)
    dxd[...] = from_end
    keep = mm_split(jnp.broadcast_to(jnp.exp2(last) * meta[0:1, 6:7], (8, 128)), spread)[0:1]
    ending = jnp.sum(xd.astype(f32) * from_end, 0, keepdims=True) + keep * jnp.sum(
        sprev[0].astype(f32) * ds, 0, keepdims=True
    )
    first = half_masks()
    dscores = jnp.zeros((SPAN, SPAN), f32)
    for pair in range(channels // 128):
        lanes = slice(pair * 128, pair * 128 + 128)
        xp = xd[:, lanes]
        gp = gy[:, lanes]
        total = dxd[:, lanes]
        for half in range(2):
            h = 2 * pair + half
            own = first if half == 0 else ~first
            decay = jnp.exp2(jnp.minimum(r_t[h:h + 1, :] - r[:, h:h + 1], 0.0))
            mixing = (scores * decay).astype(bf16)
            gown = jnp.where(own, gp, jnp.zeros_like(gp))
            total = total + mm(mixing, gown)
            dscores = dscores + mm_nt(xp, gown) * decay
        dxd[:, lanes] = total
    dscores = jnp.where(allowed, dscores, 0.0)
    dlow = dscores.astype(bf16)
    xdw = xd.astype(f32)
    g_write = mm(dlow, r_low) + mm_nt((te * xdw).astype(bf16), ds_low)
    g_read = mm(jnp.transpose(dscores).astype(bf16), w_low) + mm_nt(
        (linked * gyw).astype(bf16), sprev[0]
    )
    skip = mm_split(jnp.broadcast_to(head[2:3, :], (8, 128)), spread)[0:1]
    full = dxd[...]
    g_x = step_wide * full + skip * gyw
    dr = dr_ref[...] - mm_split(xdw * full, gather)
    at_end = mm_split(jnp.broadcast_to(ending, (8, channels)), gather, 3)[0:1]
    tail = lax.broadcasted_iota(jnp.int32, (SPAN, 128), 0) == SPAN - 1
    dr = dr + jnp.where(tail, at_end, 0.0)
    da = split_mm(upper_ones(), dr)
    dstep = mm_split(wide * full, gather) + head[3:4, :] * da
    gz = dstep * sig_ref[...]
    gz_o[...] = gz.astype(bf16)
    row = lax.broadcasted_iota(jnp.int32, (8, 128), 0)
    gbias = jnp.sum(gz, 0, keepdims=True)
    grate = jnp.sum(da * step, 0, keepdims=True)
    acch_o[...] += jnp.where(row == 0, gbias, jnp.where(row == 1, grate, 0.0))
    dmem[...] = keep * ds + dsf[0]

    def conv_back(buf, gv, base, taps, acc, halo_pre, out, halo_out):
        buf[8:SPAN + 8, :] = gv
        width = gv.shape[1]
        total = taps[0:1, :] * gv
        sums = [jnp.sum(gv * base, 0, keepdims=True)]
        halo = jnp.zeros((8, width), f32)
        hsum = []
        for k in range(1, 4):
            moved = meta[:, 7 + k:8 + k] * buf[8 + k:8 + k + SPAN, :]
            total = total + taps[k:k + 1, :] * moved
            sums.append(jnp.sum(moved * base, 0, keepdims=True))
            hmoved = hmeta[:, 7 + k:8 + k] * buf[k:8 + k, :]
            halo = halo + taps[k:k + 1, :] * hmoved
            hsum.append(jnp.sum(hmoved * halo_pre, 0, keepdims=True))
        sums.append(jnp.sum(gv, 0, keepdims=True))
        out[...] = total.astype(bf16)
        halo_out[...] = halo
        rows8 = lax.broadcasted_iota(jnp.int32, (8, width), 0)
        final = jnp.where(at == pl.num_programs(0) - 1, 1.0, 0.0)
        add = jnp.zeros((8, width), f32)
        for i, s in enumerate(sums):
            if 1 <= i <= 3:
                s = s + final * hsum[i - 1]
            add = add + jnp.where(rows8 == i, s, 0.0)
        acc[...] += add

    conv_back(gbuf, g_x * sd[...].astype(f32), pre[...].astype(f32), par, accx_o,
              hpre[...], gx_o, hx_o)
    g_wr = jnp.concatenate([g_write, g_read], 1)
    conv_back(hbuf, g_wr * ssd[...].astype(f32), spre[...].astype(f32), spar, accs_o,
              hspre[...], gs_o, hs_o)


PARAMS = dict(vmem_limit_bytes=56 * 1024 * 1024)


def whole(shape):
    return pl.BlockSpec(shape, lambda i: (0,) * len(shape))


def by_rows(cols, count=None):
    if count is None:
        return pl.BlockSpec((SPAN, cols), lambda i: (i, 0))
    return pl.BlockSpec((SPAN, cols), lambda i: (count - 1 - i, 0))


MESH = pl.DeviceIdType.MESH
SHARE = 4


def lane_block(index, width):
    return pl.ds(pl.multiple_of(index * width, 128), width)


class Links:
    def __init__(self, send, recv, local=None):
        self.send, self.recv, self.local = send, recv, local
        self.used, self.kept, self.sent = 0, 0, []
        dp = lax.axis_index("dp")
        self.groups = lax.axis_size("dp") // SHARE
        self.group = dp // SHARE
        self.x = lax.rem(dp, SHARE) // 2
        self.core = lax.rem(dp, 2)
        self.y = lax.axis_index("row")
        self.z = lax.axis_index("col")
        self.cols = lax.axis_size("col")

    def dp_of(self, group, x, core):
        return group * SHARE + x * 2 + core

    def mate(self):
        return {"dp": self.dp_of(self.group, self.x, 1 - self.core)}

    def across(self):
        return {"dp": self.dp_of(self.group, 1 - self.x, self.core)}

    def other_row(self):
        return {"row": 1 - self.y}

    def col_peer(self, off):
        return lax.rem(self.z + off, self.cols)

    def group_peer(self, off):
        return {"dp": self.dp_of(lax.rem(self.group + off, self.groups), self.x, self.core)}

    def meet(self, far_groups):
        barrier = pltpu.get_barrier_semaphore()
        peers = [self.mate(), self.across(), self.other_row()]
        peers += [{"col": self.col_peer(off)} for off in range(1, self.cols)]
        if far_groups:
            peers += [self.group_peer(off) for off in range(1, self.groups)]
        for peer in peers:
            pl.semaphore_signal(barrier, inc=1, device_id=peer, device_id_type=MESH)
        pl.semaphore_wait(barrier, len(peers))

    def make(self, src, dst, peer, when=None, track=True):
        at = self.used
        self.used += 1
        copy = pltpu.make_async_remote_copy(
            src_ref=src, dst_ref=dst, send_sem=self.send.at[at], recv_sem=self.recv.at[at],
            device_id=peer, device_id_type=MESH,
        )
        if track:
            self.sent.append((copy, when))
        return copy

    def go(self, src, dst, peer, track=True):
        copy = self.make(src, dst, peer, track=track)
        copy.start()
        return copy

    def keep(self, src, dst):
        copy = pltpu.make_async_copy(src, dst, self.local.at[self.kept])
        self.kept += 1
        return copy

    def finish(self):
        for copy, when in self.sent:
            if when is None:
                copy.wait_send()
            else:
                pl.when(when)(copy.wait_send)


class Steps:
    def __init__(self):
        self.stages = []

    def add(self, remote, local=()):
        self.stages.append((remote, list(local)))

    def run(self, s):
        if 0 < s <= len(self.stages):
            remote, local = self.stages[s - 1]
            for c in remote:
                c.wait_recv()
            for c in local:
                c.wait()
        if s < len(self.stages):
            remote, local = self.stages[s]
            for c in remote + local:
                c.start()


def spread_steps(t, dst_row, dst_x, dst_core, steps):
    steps.add([t.make(dst_row, dst_row, t.other_row())])
    steps.add([t.make(dst_x, dst_x, t.across())])
    steps.add([t.make(dst_core, dst_core, t.mate())])
    return steps


def column_steps(t, src, dst, width):
    part = src.shape[0] // SHARE
    x, y, z, core = t.x, t.y, t.z, t.core
    rows = pl.ds(pl.multiple_of((x * 2 + core) * part, 16), part)
    lanes = lane_block(y, width)
    steps = Steps()
    here = dst.at[z, x, core, :, lanes]
    remote = []
    for off in range(1, t.cols):
        to = t.col_peer(off)
        remote.append(t.make(src.at[rows, lane_block(to, width)], here, {"col": to}))
    steps.add(remote, [t.keep(src.at[rows, lane_block(z, width)], here)])
    return spread_steps(
        t, dst.at[:, x, core, :, lanes], dst.at[:, x, core], dst.at[:, :, core], steps
    )


def row_steps(t, src, dst, width):
    part = src.shape[0] // t.cols // SHARE
    x, y, z, core = t.x, t.y, t.z, t.core

    def rows(to):
        return pl.ds(pl.multiple_of((to * SHARE + x * 2 + core) * part, 16), part)

    steps = Steps()
    here = dst.at[y, x, core, :, lane_block(z, width)]
    remote = []
    for off in range(1, t.cols):
        to = t.col_peer(off)
        remote.append(t.make(src.at[rows(to), :], here, {"col": to}))
    steps.add(remote, [t.keep(src.at[rows(z), :], here)])
    return spread_steps(t, dst.at[y, x, core], dst.at[:, x, core], dst.at[:, :, core], steps)


class Relay:
    def __init__(self, t, own, whole):
        width = own.shape[1]
        z, last = t.z, t.cols - 1
        self.hops = []
        for hop in range(1, t.cols):
            pair = []
            for side in (1, -1):
                chunk = jnp.clip(z - side * (hop - 1), 0, last)
                there = whole.at[:, lane_block(chunk, width)]
                to = jnp.clip(z + side, 0, last)
                if side == 1:
                    sends = (z < last) & (z >= hop - 1)
                    gets = z >= hop
                else:
                    sends = (z > 0) & (z <= last - hop + 1)
                    gets = z <= last - hop
                copy = t.make(own if hop == 1 else there, there, {"col": to}, sends)
                pair.append((copy, sends, gets))
            self.hops.append(pair)

    def run(self, s):
        if s > 0:
            for copy, _, gets in self.hops[s - 1]:
                pl.when(gets)(copy.wait_recv)
        if s < len(self.hops):
            for copy, sends, _ in self.hops[s]:
                pl.when(sends)(copy.start)


def front_kernel(
    inner_total,
    tok, ngain, w_states, meta, docrow, spar, inner, gate, out, step_w, cot, par_own, head_own, halo,
    wi_o, wg_o, wo_o, ws_o, cots_o, par_o, head_o,
    normed_o, pre_o, spre_o, sd_o, ssd_o, x_o, wr_o, step_o, r_o, sig_o, hpre_o, hspre_o, sprev_o,
    gated_o, ggate_o, gy_o, dr_o, dsf_o, dsout_o, acc_o,
    wi, wg, wo, ws2, ws, cots, par, head, head_in, halo_in,
    normed_s, pre_s, spre_s, sd_s, ssd_s, x_s, wr_s, step_s, r_s, sig_s, hpre_s, hspre_s, sprev_s,
    gated_s, ggate_s, gy_s, dr_s, dsf_s, acc_s,
    fresh_s, y_s, gate_s, gg_s, sums_s, sums_in,
    xbuf, sbuf, mem, mem_in,
    send, recv, local,
):
    t = Links(send, recv, local)
    t.meet(False)
    x, y, z, core = t.x, t.y, t.z, t.core
    blocks = tok.shape[0] // SPAN
    channels = x_s.shape[1]
    half = channels // 2
    outputs = []

    def write(src, dst):
        copy = t.keep(src, dst)
        copy.start()
        outputs.append(copy)

    few = [
        t.go(par_own, par.at[:, lane_block(y, half)], t.other_row()),
        t.go(head_own, head_in, t.other_row()),
        t.go(halo, halo_in, t.other_row()),
    ]
    block = inner.shape[1] // t.cols
    get_inner = column_steps(t, inner, wi, block)
    get_step = column_steps(t, step_w, ws2, step_w.shape[1] // t.cols)
    get_gate = column_steps(t, gate, wg, block)
    get_out = row_steps(t, out, wo, out.shape[1])
    get_cot = Relay(t, cot, cots)
    own_cot = t.keep(cot, cots.at[:, lane_block(z, cot.shape[1])])
    pass_state = t.make(mem, mem_in, t.other_row(), track=False)
    pass_sums = [
        t.make(sums_s, sums_in.at[off - 1], {"col": t.col_peer(off)}) for off in range(1, t.cols)
    ]
    get_inner.run(0)
    get_step.run(0)
    get_gate.run(0)
    get_out.run(0)
    get_cot.run(0)
    own_cot.start()
    par[:, lane_block(y, half)] = par_own[...]
    for s in range(1, 5):
        get_inner.run(s)
        get_step.run(s)
        if s > 1:
            get_gate.run(s - 1)
        if s > 2:
            get_out.run(s - 2)
    for c in few:
        c.wait_recv()
    head[...] = head_own[...] + head_in[...]
    wide_in = normed_s.shape[1]
    ws[...] = (
        ws2[:, :, :, :, 0:128].reshape(wide_in, 128) + ws2[:, :, :, :, 128:256].reshape(wide_in, 128)
    )
    spread = spread_matrix(channels)
    gain = ngain[...]

    def w_of(ref):
        return ref[...].reshape(-1, ref.shape[-1])

    def rows_of(i):
        return pl.ds(pl.multiple_of(i * SPAN, SPAN), SPAN)

    hn = rms_rows(halo_in[...], gain)
    hp = mm(hn, w_of(wi))[8:16]
    hs = mm(hn, w_states[...])[8:16]
    xbuf[0:8, :] = hp
    sbuf[0:8, :] = hs
    hpre_s[...] = hp
    hspre_s[...] = hs
    mem[...] = jnp.zeros_like(mem)

    def entry(i, carry):
        at = rows_of(i)

        @pl.when(i > 0)
        def _():
            xbuf[0:8, :] = xbuf[SPAN:SPAN + 8, :]
            sbuf[0:8, :] = sbuf[SPAN:SPAN + 8, :]

        normed = rms_rows(tok[at, :], gain)
        normed_s[at, :] = normed
        x_pre = mm(normed, w_of(wi))
        s_pre = mm(normed, w_states[...])
        xbuf[8:SPAN + 8, :] = x_pre
        sbuf[8:SPAN + 8, :] = s_pre
        pre_s[at, :] = x_pre.astype(bf16)
        spre_s[at, :] = s_pre.astype(bf16)
        marks = meta[at, :]

        def conv_silu(buf, here, taps):
            v = taps[4:5, :] + taps[0:1, :] * here
            for k in range(1, 4):
                v = v + marks[:, k:k + 1] * (taps[k:k + 1, :] * buf[8 - k:8 - k + SPAN, :])
            sg = sigmoid(v)
            return v * sg, sg * (1.0 + v * (1.0 - sg))

        act, slope = conv_silu(xbuf, x_pre, par)
        x_low = act.astype(bf16)
        x_s[at, :] = x_low
        sd_s[at, :] = slope.astype(bf16)
        sact, sslope = conv_silu(sbuf, s_pre, spar)
        wr = sact.astype(bf16)
        wr_s[at, :] = wr
        ssd_s[at, :] = sslope.astype(bf16)

        raw = mm(normed, ws[...]) + head[0:1, :]
        step = jnp.maximum(raw, 0.0) + jnp.log1p(jnp.exp(-jnp.abs(raw)))
        sig_s[at, :] = sigmoid(raw)
        step_s[at, :] = step
        r = split_mm(lower_ones(), step * head[1:2, :])
        r_s[at, :] = r
        last = r[SPAN - 1:SPAN, :]
        to_end = jnp.exp2(jnp.minimum(last - r, 0.0)) * marks[:, 5:6]
        coef = mm_split(to_end * step, spread)
        w_t = jnp.transpose(wr[:, 0:128].astype(f32)).astype(bf16)
        fresh = mm(w_t, (coef * x_low.astype(f32)).astype(bf16))
        fresh_s[i] = fresh
        mem[...] = keep_of(last, marks) * mem[...] + fresh

        @pl.when(i == 0)
        def _():
            get_gate.run(4)
            get_out.run(3)
            get_cot.run(1)

        @pl.when(i == 2)
        def _():
            get_out.run(4)

        return carry

    def keep_of(last, marks):
        return mm_split(jnp.broadcast_to(jnp.exp2(last) * marks[0:1, 6:7], (8, 128)), spread)[0:1]

    lax.fori_loop(0, blocks, entry, 0)
    pass_state.start()
    get_cot.run(2)
    for src, dst in (
        (normed_s, normed_o), (pre_s, pre_o), (spre_s, spre_o), (sd_s, sd_o), (ssd_s, ssd_o),
        (x_s, x_o), (wr_s, wr_o), (step_s, step_o), (r_s, r_o), (sig_s, sig_o), (hpre_s, hpre_o),
        (hspre_s, hspre_o), (wi, wi_o), (wg, wg_o), (wo, wo_o), (ws, ws_o), (par, par_o),
        (head, head_o),
    ):
        write(src, dst)

    def gate_block(i, carry):
        at = rows_of(i)
        gate_s[at, :] = mm(normed_s[at, :], w_of(wg))
        return carry

    lax.fori_loop(0, blocks, gate_block, 0)

    pass_state.wait()
    mem[...] = mem_in[...] * jnp.where(y == 1, 1.0, 0.0)
    skip = mm_split(jnp.broadcast_to(head[2:3, :], (8, 128)), spread)[0:1]
    first = half_masks()

    def scan(i, carry):
        at = rows_of(i)
        marks = meta[at, :]
        w_low = wr_s[at, 0:128]
        r_low = wr_s[at, 128:256]
        r = r_s[at, :]
        r_t = jnp.transpose(r)
        rows = lax.broadcasted_iota(jnp.int32, (SPAN, SPAN), 0)
        cols = lax.broadcasted_iota(jnp.int32, (SPAN, SPAN), 1)
        allowed = (rows >= cols) & (marks[:, 0:1] == docrow[:, at])
        scores = jnp.where(allowed, mm_nt(r_low, w_low), 0.0)
        wide = x_s[at, :].astype(f32)
        xd = (mm_split(step_s[at, :], spread) * wide).astype(bf16)
        sprev = mem[...].astype(bf16)
        sprev_s[i] = sprev
        linked = jnp.exp2(r) * marks[:, 4:5]
        carried = mm(r_low, sprev) * mm_split(linked, spread)
        y_s[at, :] = carried + skip * wide
        for pair in range(channels // 128):
            lanes = slice(pair * 128, pair * 128 + 128)
            xp = xd[:, lanes]
            total = y_s[at, lanes]
            for part in range(2):
                h = 2 * pair + part
                decay = jnp.exp2(jnp.minimum(r[:, h:h + 1] - r_t[h:h + 1, :], 0.0))
                mixing = (scores * decay).astype(bf16)
                own = jnp.where(first if part == 0 else ~first, xp, jnp.zeros_like(xp))
                total = total + mm(mixing, own)
            y_s[at, lanes] = total
        last = r[SPAN - 1:SPAN, :]
        mem[...] = keep_of(last, marks) * mem[...] + fresh_s[i]
        return carry

    lax.fori_loop(0, blocks, scan, 0)
    write(sprev_s, sprev_o)

    get_cot.run(3)
    own_cot.wait()
    write(cots, cots_o)
    ones = jnp.ones((8, channels), bf16)

    def totals_of(i, carry):
        at = rows_of(i)
        gg = mm_nt(cots[at, :], w_of(wo))
        gg_s[at, :] = gg
        g = gate_s[at, :]
        mixed = y_s[at, :] * (g * sigmoid(g))
        sq = sum(mm_nt(ones, part) for part in split(mixed * mixed, 2))
        pr = sum(mm_nt(ones, part) for part in split(mixed * (par[5:6, :] * gg), 2))
        row = lax.broadcasted_iota(jnp.int32, (8, SPAN), 0)
        sums_s[:, at] = jnp.where(row == 0, sq, jnp.where(row == 1, pr, 0.0))
        return carry

    lax.fori_loop(0, blocks, totals_of, 0)
    for c in pass_sums:
        c.start()
    for c in pass_sums:
        c.wait_recv()
    mem[...] = jnp.zeros_like(mem)
    acc_s[...] = jnp.zeros_like(acc_s)
    gather = gather_matrix(channels)

    def turn(back_i, carry):
        i = blocks - 1 - back_i
        at = rows_of(i)
        marks = meta[at, :]
        both = sums_s[:, at]
        for off in range(1, t.cols):
            both = both + sums_in[off - 1, :, at]
        totals = jnp.transpose(both)
        scale = lax.rsqrt(totals[:, 0:1] / inner_total + epsilon)
        cross = totals[:, 1:2] / inner_total
        yv = y_s[at, :]
        g = gate_s[at, :]
        sg = sigmoid(g)
        sl = g * sg
        gg = gg_s[at, :]
        ngate = par[5:6, :]
        normal = yv * sl * scale
        gated_s[at, :] = (normal * ngate).astype(bf16)
        g_mixed = scale * (ngate * gg - normal * (scale * cross))
        ggate_s[at, :] = (g_mixed * yv * (sg * (1.0 + g * (1.0 - sg)))).astype(bf16)
        gy = (g_mixed * sl).astype(bf16)
        gy_s[at, :] = gy
        gyw = gy.astype(f32)
        wide = x_s[at, :].astype(f32)
        dr_s[at, :] = mm_split(gyw * (yv - skip * wide), gather)
        row = lax.broadcasted_iota(jnp.int32, (8, channels), 0)
        ggain = jnp.sum(gg * normal, 0, keepdims=True)
        gskip = jnp.sum(gyw * wide, 0, keepdims=True)
        acc_s[...] += jnp.where(row == 0, ggain, jnp.where(row == 1, gskip, 0.0))
        r = r_s[at, :]
        linked = mm_split(jnp.exp2(r) * marks[:, 4:5], spread)
        r_t = jnp.transpose(wr_s[at, 128:256].astype(f32)).astype(bf16)
        dfresh = mm(r_t, (linked * gyw).astype(bf16))
        dsf_s[i] = dfresh
        mem[...] = keep_of(r[SPAN - 1:SPAN, :], marks) * mem[...] + dfresh
        return carry

    lax.fori_loop(0, blocks, turn, 0)
    for src, dst in (
        (gated_s, gated_o), (ggate_s, ggate_o), (gy_s, gy_o), (dr_s, dr_o), (dsf_s, dsf_o),
        (mem, dsout_o), (acc_s, acc_o),
    ):
        write(src, dst)
    for copy in outputs:
        copy.wait()
    t.finish()


def front(inner_all, tok, ngain, w_states, meta, docrow, spar, inner, gate, out, step_w, cot, par_own,
          head_own, halo):
    tokens, width = tok.shape
    blocks = tokens // SPAN
    cols = lax.axis_size("col")
    part, half = inner.shape[0] // SHARE, inner.shape[1] // cols
    channels = 2 * half
    sds = jax.ShapeDtypeStruct
    V = pltpu.VMEM
    weights = [
        ((cols, 2, 2, part, channels), bf16), ((cols, 2, 2, part, channels), bf16),
        ((2, 2, 2, half // SHARE, width), bf16),
    ]
    entry_shapes = [
        ((tokens, width), bf16), ((tokens, channels), bf16), ((tokens, 256), bf16),
        ((tokens, channels), bf16), ((tokens, 256), bf16), ((tokens, channels), bf16),
        ((tokens, 256), bf16), ((tokens, 128), f32), ((tokens, 128), f32), ((tokens, 128), f32),
        ((8, channels), f32), ((8, 256), f32), ((blocks, 128, channels), bf16),
    ]
    turn_shapes = [
        ((tokens, channels), bf16), ((tokens, channels), bf16), ((tokens, channels), bf16),
        ((tokens, 128), f32), ((blocks, 128, channels), f32),
    ]
    state = ((128, channels), f32)
    acc = ((8, channels), f32)
    outs = (
        weights + [((width, 128), bf16), ((tokens, width), bf16), ((8, channels), f32), ((8, 128), f32)]
        + entry_shapes + turn_shapes + [state, acc]
    )
    scratch = (
        weights
        + [((cols, 2, 2, part, 256), bf16), ((width, 128), bf16), ((tokens, width), bf16),
           ((8, channels), f32), ((8, 128), f32), ((8, 128), f32), (halo.shape, bf16)]
        + entry_shapes + turn_shapes + [acc]
        + [((blocks, 128, channels), f32), ((tokens, channels), f32), ((tokens, channels), f32),
           ((tokens, channels), f32), ((8, tokens), f32), ((cols - 1, 8, tokens), f32),
           ((SPAN + 8, channels), f32), ((SPAN + 8, 256), f32), state, state]
    )
    vmem = pl.BlockSpec(memory_space=V)
    hbm = pl.BlockSpec(memory_space=pl.ANY)
    got = pl.pallas_call(
        functools.partial(front_kernel, float(inner_all)),
        out_shape=[sds(*o) for o in outs],
        in_specs=[vmem] * 6 + [hbm] * 5 + [vmem, vmem, hbm],
        out_specs=[hbm] * len(outs),
        scratch_shapes=[V(*s) for s in scratch] + [
            pltpu.SemaphoreType.DMA((48,)), pltpu.SemaphoreType.DMA((48,)),
            pltpu.SemaphoreType.DMA((48,)),
        ],
        compiler_params=pltpu.CompilerParams(
            collective_id=1, has_side_effects=True, vmem_limit_bytes=62 * 1024 * 1024
        ),
        name="front",
    )(tok, ngain, w_states, meta, docrow, spar, inner, gate, out, step_w, cot, par_own, head_own, halo)
    got = list(got)
    got[0] = got[0].reshape(width, channels)
    got[1] = got[1].reshape(width, channels)
    got[2] = got[2].reshape(channels, width)
    return got


def wavefront(stages, items):
    for turn in range(stages + len(items) - 1):
        for s in reversed(range(stages)):
            m = turn - s
            if 0 <= m < len(items):
                items[m](s)


def add_into(target, source, count, index_target, index_source):
    def body(i, carry):
        a, b = index_target(i), index_source(i)
        target[a] = (target[a].astype(f32) + source[b].astype(f32)).astype(target.dtype)
        return carry

    lax.fori_loop(0, count, body, 0)


def tail_kernel(
    part, ish, gi, gg, gz, go, gs, sm,
    own_o, ish_o, oi, og, oz, oo, os, sm_o,
    rpart, rish, i1, i2, i3, i4, g1, g2, g3, g4, z1, z2, z3, z4, o1, o2, o3, o4, s1, s2, s3, s4, s5,
    msum, mgot, far_i, far_g, far_o, far_z, far_s, send, recv,
):
    t = Links(send, recv)
    t.meet(True)
    x, y, z, core = t.x, t.y, t.z, t.core
    third = own_o.shape[1]
    rows = own_o.shape[0]

    sums = []
    for off in range(1, t.cols):
        to = t.col_peer(off)
        sums.append(t.go(ish, rish.at[off - 1], {"col": to}))
    parts = []

    def part_item(s):
        if s == 0:
            for off in range(1, t.cols):
                to = t.col_peer(off)
                parts.append(t.go(part.at[:, lane_block(to, third)], rpart.at[off - 1], {"col": to}))

    def matrix(g, a1, a2, a3, a4, far, o, by_col):
        width = a4.shape[-1] if by_col else a4.shape[-1] // t.cols
        copies = []
        lead = g.shape[0]

        def run(s):
            if s == 0:
                copies.append(t.go(g.at[:, :, 1 - core], a1, t.mate()))
            elif s == 1:
                copies[-1].wait_recv()

                def body(i, c):
                    for j in range(2):
                        a1[i, j] = (a1[i, j].astype(f32) + g[i, j, core].astype(f32)).astype(bf16)
                    return c

                lax.fori_loop(0, lead, body, 0)
                if by_col:
                    copies.append(t.go(a1.at[:, :, :, lane_block(1 - y, width)], a2, t.other_row()))
                else:
                    copies.append(t.go(a1.at[1 - y], a2, t.other_row()))
            elif s == 2:
                copies[-1].wait_recv()
                if by_col:
                    def body(i, c):
                        for j in range(2):
                            mine = a1[i, j, :, lane_block(y, width)]
                            a2[i, j] = (a2[i, j].astype(f32) + mine.astype(f32)).astype(bf16)
                        return c

                    lax.fori_loop(0, lead, body, 0)
                    copies.append(t.go(a2.at[:, 1 - x], a3, t.across()))
                else:
                    for j in range(2):
                        a2[j] = (a2[j].astype(f32) + a1[y, j].astype(f32)).astype(bf16)
                    copies.append(t.go(a2.at[1 - x], a3, t.across()))
            elif s == 3:
                copies[-1].wait_recv()
                if by_col:
                    def body(i, c):
                        a4[i] = (a3[i].astype(f32) + a2[i, x].astype(f32)).astype(bf16)
                        return c

                    lax.fori_loop(0, lead, body, 0)
                else:
                    a4[...] = (a3[...].astype(f32) + a2[x].astype(f32)).astype(bf16)
                if t.groups > 1:
                    more = [t.go(a4, far.at[off - 1], t.group_peer(off), False)
                            for off in range(1, t.groups)]
                    for c in more:
                        c.wait()
                    total = a4[...].astype(f32)
                    for off in range(1, t.groups):
                        total = total + far[off - 1].astype(f32)
                    a4[...] = total.astype(bf16)
                copies.clear()
                for off in range(1, t.cols):
                    to = t.col_peer(off)
                    if by_col:
                        copies.append(
                            t.go(a4.at[to], o.at[x, core, :, lane_block(z, width)], {"col": to})
                        )
                    else:
                        copies.append(
                            t.go(a4.at[:, lane_block(to, width)], o.at[z, x, core], {"col": to})
                        )
                if by_col:
                    o[x, core, :, lane_block(z, width)] = a4[z]
                else:
                    o[z, x, core] = a4[:, lane_block(z, width)]
            elif s == 4:
                for c in copies:
                    c.wait_recv()
                here = o.at[x, core] if by_col else o.at[:, x, core]
                copies.append(t.go(here, here, t.across()))
            elif s == 5:
                copies[-1].wait_recv()
                here = o.at[:, core] if by_col else o.at[:, :, core]
                copies.append(t.go(here, here, t.mate()))
            else:
                copies[-1].wait_recv()

        return run

    state_copies = []

    def states(s):
        copies = state_copies
        if s == 0:
            copies.append(t.go(gs.at[:, :, :, 1 - core], s1, t.mate()))
        elif s == 1:
            copies[-1].wait_recv()

            def body(i, c):
                for j in range(2):
                    for k in range(2):
                        s1[i, j, k] = (
                            s1[i, j, k].astype(f32) + gs[i, j, k, core].astype(f32)
                        ).astype(bf16)
                return c

            lax.fori_loop(0, t.cols, body, 0)
            copies.append(t.go(s1.at[:, 1 - y], s2, t.other_row()))
        elif s == 2:
            copies[-1].wait_recv()

            def body(i, c):
                for k in range(2):
                    s2[i, k] = (s2[i, k].astype(f32) + s1[i, y, k].astype(f32)).astype(bf16)
                return c

            lax.fori_loop(0, t.cols, body, 0)
            copies.append(t.go(s2.at[:, 1 - x], s3, t.across()))
        elif s == 3:
            copies[-1].wait_recv()

            def body(i, c):
                s4[i] = (s3[i].astype(f32) + s2[i, x].astype(f32)).astype(bf16)
                return c

            lax.fori_loop(0, t.cols, body, 0)
            if t.groups > 1:
                more = [t.go(s4, far_s.at[off - 1], t.group_peer(off), False)
                        for off in range(1, t.groups)]
                for c in more:
                    c.wait()
                total = s4[...].astype(f32)
                for off in range(1, t.groups):
                    total = total + far_s[off - 1].astype(f32)
                s4[...] = total.astype(bf16)
            copies.clear()
            for off in range(1, t.cols):
                to = t.col_peer(off)
                copies.append(t.go(s4.at[to], s5.at[off - 1], {"col": to}))
        elif s == 4:
            for c in copies:
                c.wait_recv()
            total = s4[z].astype(f32)
            for off in range(1, t.cols):
                total = total + s5[off - 1].astype(f32)
            os[z, y, x, core] = total.astype(bf16)
            copies.clear()
            here = os.at[z, y, x, core]
            for off in range(1, t.cols):
                copies.append(t.go(here, here, {"col": t.col_peer(off)}))
        elif s == 5:
            for c in copies:
                c.wait_recv()
            here = os.at[:, y, x, core]
            copies.append(t.go(here, here, t.other_row()))
        elif s == 6:
            copies[-1].wait_recv()
            here = os.at[:, :, x, core]
            copies.append(t.go(here, here, t.across()))
        elif s == 7:
            copies[-1].wait_recv()
            here = os.at[:, :, :, core]
            copies.append(t.go(here, here, t.mate()))
        else:
            copies[-1].wait_recv()

    few = []
    tail_rows = sm.shape[0] * 3 // 8

    def smalls(s):
        if s == 0:
            few.append(t.go(sm, mgot.at[0], t.mate()))
        elif s == 1:
            few[-1].wait_recv()
            msum[0] = sm[...] + mgot[0]
            few.append(t.go(msum.at[0], mgot.at[1], t.other_row()))
        elif s == 2:
            few[-1].wait_recv()
            msum[1] = msum[0] + mgot[1]
            few.append(t.go(msum.at[1], mgot.at[2], t.across()))
        elif s == 3:
            few[-1].wait_recv()
            msum[2] = msum[1] + mgot[2]
            if t.groups > 1:
                more = [t.go(msum.at[2], mgot.at[5 + off], t.group_peer(off), False)
                        for off in range(1, t.groups)]
                for c in more:
                    c.wait()
                total = msum[2]
                for off in range(1, t.groups):
                    total = total + mgot[5 + off]
                msum[2] = total
            few.clear()
            last = pl.ds(sm.shape[0] - tail_rows, tail_rows)
            for off in range(1, t.cols):
                few.append(t.go(msum.at[2, last], mgot.at[2 + off, last], {"col": t.col_peer(off)}))
        elif s == 4:
            for c in few:
                c.wait_recv()
            top = sm.shape[0] - tail_rows
            sm_o[0:top] = msum[2, 0:top]
            sm_o[top:] = msum[2, top:] + mgot[3, top:] + mgot[4, top:] + mgot[5, top:]

    def late(item, limit):
        return lambda s: item(s) if s <= limit else None

    wavefront(9, [
        late(matrix(go, o1, o2, o3, o4, far_o, oo, False), 6),
        late(part_item, 0),
        late(matrix(gi, i1, i2, i3, i4, far_i, oi, True), 6),
        late(matrix(gz, z1, z2, z3, z4, far_z, oz, True), 6),
        late(smalls, 4),
        states,
        late(matrix(gg, g1, g2, g3, g4, far_g, og, True), 6),
    ])
    for c in sums:
        c.wait_recv()
    ish_o[...] = ish[...] + rish[0] + rish[1] + rish[2]
    for c in parts:
        c.wait_recv()

    def add_rows(i, c):
        at = pl.ds(pl.multiple_of(i * 64, 64), 64)
        total = part[at, lane_block(z, third)].astype(f32)
        for j in range(t.cols - 1):
            total = total + rpart[j, at].astype(f32)
        own_o[at] = total
        return c

    lax.fori_loop(0, rows // 64, add_rows, 0)
    t.finish()


def tail(part, ish, gi, gg, gz, go, gs, sm):
    cols = lax.axis_size("col")
    groups = max(lax.axis_size("dp") // SHARE - 1, 1)
    rows, width = part.shape
    third = width // cols
    own = gi.shape[1] // 2
    q = third // SHARE
    qo = own // SHARE
    qs = width // (cols * 2 * SHARE)
    zl = gz.shape[1] // 2
    sds = jax.ShapeDtypeStruct
    V = pltpu.VMEM

    def col_scratch(w):
        return [
            V((cols, 2, q, 2 * w), bf16), V((cols, 2, q, w), bf16), V((cols, q, w), bf16),
            V((cols, q, w), bf16),
        ]

    got = pl.pallas_call(
        tail_kernel,
        out_shape=[
            sds((rows, third), f32), sds(ish.shape, f32),
            sds((2, 2, q, cols * own), bf16), sds((2, 2, q, cols * own), bf16),
            sds((2, 2, q, cols * zl), bf16), sds((cols, 2, 2, qo, third), bf16),
            sds((cols, 2, 2, 2, qs, gs.shape[1]), bf16), sds(sm.shape, f32),
        ],
        in_specs=[pl.BlockSpec(memory_space=V)] * 8,
        out_specs=[pl.BlockSpec(memory_space=V)] * 8,
        scratch_shapes=[
            V((cols - 1, rows, third), bf16), V((cols - 1,) + ish.shape, f32),
        ] + col_scratch(own) + col_scratch(own) + col_scratch(zl) + [
            V((2, 2, qo, width), bf16), V((2, qo, width), bf16), V((qo, width), bf16),
            V((qo, width), bf16),
            V((cols, 2, 2, qs, gs.shape[1]), bf16), V((cols, 2, qs, gs.shape[1]), bf16),
            V((cols, qs, gs.shape[1]), bf16), V((cols, qs, gs.shape[1]), bf16),
            V((cols - 1, qs, gs.shape[1]), bf16),
            V((3,) + sm.shape, f32), V((6 + groups,) + sm.shape, f32),
            V((groups, cols, q, own), bf16), V((groups, cols, q, own), bf16),
            V((groups, qo, width), bf16),
            V((groups, cols, q, zl), bf16), V((groups, cols, qs, gs.shape[1]), bf16),
            pltpu.SemaphoreType.DMA((80,)), pltpu.SemaphoreType.DMA((80,)),
        ],
        compiler_params=pltpu.CompilerParams(
            collective_id=3, has_side_effects=True, vmem_limit_bytes=56 * 1024 * 1024
        ),
        name="tail",
    )(
        part, ish, gi.reshape(cols, 2, 2, q, 2 * own), gg.reshape(cols, 2, 2, q, 2 * own),
        gz.reshape(cols, 2, 2, q, 2 * zl), go.reshape(2, 2, 2, qo, width),
        gs.reshape(cols, 2, 2, 2, qs, gs.shape[1]), sm,
    )
    own_o, ish_o, oi, og, oz, oo, os, sm_o = got
    return (
        own_o, ish_o, oi.reshape(third, -1), og.reshape(third, -1), oz.reshape(third, -1),
        oo.reshape(cols * own, third), os.reshape(width, -1), sm_o,
    )


def per_device(
    tokens_in, segment_ids, norm_gain, proj_gate, proj_inner, proj_step, proj_states,
    conv_inner, conv_inner_bias, conv_states, conv_states_bias, step_bias, decay_log,
    skip_gain, gate_gain, proj_out, cotangent,
):
    tokens, width = tokens_in.shape
    blocks = tokens // SPAN
    row = lax.axis_index("row")
    col = lax.axis_index("col")
    cols = lax.axis_size("col")
    own_ch = conv_inner.shape[1]
    own_heads = step_bias.shape[0]
    channels = 2 * own_ch
    inner_all = channels * cols
    col_width = width // cols

    own = jnp.concatenate(
        [conv_inner, conv_inner_bias[None], gate_gain[None], jnp.zeros((2, own_ch), f32)], 0
    )

    def at_row(values):
        pad = [(0, 0)] * (values.ndim - 1)
        low = jnp.pad(values, pad + [(0, 128 - own_heads)])
        high = jnp.pad(values, pad + [(own_heads, 128 - 2 * own_heads)])
        return jnp.where(row == 0, low, high)

    pieces = at_row(proj_step.reshape(col_width, cols, own_heads)).reshape(col_width, cols * 128)
    rate = -jnp.exp(decay_log)
    head_own = jnp.pad(
        at_row(jnp.stack([step_bias, rate * LOG2E, skip_gain, rate])), ((0, 4), (0, 0))
    )
    spar = jnp.concatenate([conv_states, conv_states_bias[None], jnp.zeros((3, 256), f32)], 0)

    docs = jnp.pad(segment_ids[0].astype(f32), (8, 8), constant_values=-1.0)
    docs = lax.dynamic_slice_in_dim(docs, row * tokens, tokens + 16, 0)
    here = docs[8:8 + tokens]
    spans = here.reshape(blocks, SPAN)
    before = jnp.concatenate([docs[7:8], spans[:-1, -1]])
    after = spans[:, -1]

    def flat(cond):
        return jnp.broadcast_to(cond, (blocks, SPAN)).reshape(tokens)

    def forward_same(start, count):
        own_docs = docs[start:start + count]
        return [own_docs == docs[start + k:start + k + count] for k in range(1, 4)]

    meta = jnp.stack(
        [here]
        + [(here == docs[8 - k:8 - k + tokens]) for k in range(1, 4)]
        + [
            flat(spans == before[:, None]),
            flat(spans == after[:, None]),
            flat((before == after)[:, None]),
            jnp.zeros_like(here),
        ]
        + forward_same(8, tokens)
        + [jnp.zeros_like(here)] * 5,
        1,
    ).astype(f32)
    hmeta = jnp.stack(
        [jnp.zeros((8,), f32)] * 8
        + forward_same(0, 8)
        + [jnp.zeros((8,), f32)] * 5,
        1,
    ).astype(f32)
    docrow = here[None, :]

    sds = jax.ShapeDtypeStruct
    back3 = pl.BlockSpec((1, 128, channels), lambda i: (blocks - 1 - i, 0, 0))
    (
        w_inner, w_gate, w_out, w_step, cot_all, par, head,
        normed, pre, spre, sd, ssd, x_low, wr, step, r, sig, hpre, hspre, sprev,
        gated, g_gate, gy, dr, dsf, dsout, acc1,
    ) = front(
        inner_all, tokens_in, norm_gain[None], proj_states, meta, docrow, spar,
        proj_inner, proj_gate, proj_out, pieces, cotangent, own, head_own, tokens_in[-16:],
    )

    ds_in = lax.ppermute(dsout, "row", [(1, 0)])
    out_part = mm(gated, w_out).astype(bf16)
    out_cols = lax.psum_scatter(out_part, "col", scatter_dimension=1, tiled=True)
    own_tokens = lax.dynamic_slice_in_dim(tokens_in, col * col_width, col_width, 1).astype(f32)
    mixed_out = (own_tokens + out_cols.astype(f32)).astype(bf16)
    grad_out_part = lax.dot_general(
        gated, cot_all, (((0,), (0,)), ((), ())), preferred_element_type=f32
    )

    gx, gs, gz, hx, hs, accx, accs, acch = pl.pallas_call(
        back_kernel,
        grid=(blocks,),
        in_specs=[
            by_rows(channels, blocks), by_rows(256, blocks), by_rows(channels, blocks),
            by_rows(128, blocks), by_rows(128, blocks), by_rows(128, blocks),
            by_rows(16, blocks), pl.BlockSpec((1, SPAN), lambda i: (0, blocks - 1 - i)),
            by_rows(128, blocks), back3, back3, whole((128, channels)),
            by_rows(channels, blocks), by_rows(256, blocks), by_rows(channels, blocks),
            by_rows(256, blocks), whole((8, channels)), whole((8, 256)), whole((8, 16)),
            whole((8, 128)), whole((8, channels)), whole((8, 256)),
        ],
        out_specs=[
            by_rows(channels, blocks), by_rows(256, blocks), by_rows(128, blocks),
            whole((8, channels)), whole((8, 256)), whole((8, channels)), whole((8, 256)),
            whole((8, 128)),
        ],
        out_shape=[
            sds((tokens, channels), bf16), sds((tokens, 256), bf16), sds((tokens, 128), bf16),
            sds((8, channels), f32), sds((8, 256), f32), sds((8, channels), f32),
            sds((8, 256), f32), sds((8, 128), f32),
        ],
        scratch_shapes=[
            pltpu.VMEM((128, channels), f32),
            pltpu.VMEM((SPAN + 16, channels), f32),
            pltpu.VMEM((SPAN + 16, 256), f32),
            pltpu.VMEM((SPAN, channels), f32),
        ],
        compiler_params=pltpu.CompilerParams(**PARAMS),
        name="back",
    )(
        x_low, wr, gy, r, step, sig, meta, docrow, dr, sprev, dsf, ds_in,
        pre, spre, sd, ssd, hpre, hspre, hmeta, head, par, spar,
    )

    hx_in, hs_in = lax.ppermute((hx, hs), "row", [(1, 0)])
    gx = gx.at[-8:].add(hx_in.astype(bf16))
    gs = gs.at[-8:].add(hs_in.astype(bf16))

    normed_grad = (
        mm_nt(g_gate, w_gate) + mm_nt(gx, w_inner) + mm_nt(gz, w_step) + mm_nt(gs, proj_states)
    )
    wide = tokens_in.astype(f32)
    inverse = lax.rsqrt(jnp.mean(wide * wide, -1, keepdims=True) + epsilon)
    input_share = jnp.sum(normed_grad * norm_gain * wide, -1)
    gain_share = jnp.sum(normed_grad * (wide * inverse), 0)

    def weight_grad(left, right):
        return lax.dot_general(
            left, right, (((0,), (0,)), ((), ())), preferred_element_type=f32
        ).astype(bf16)

    def head_sum(values):
        return values.reshape(2 * own_heads, HEAD).sum(-1)

    def lanes(values, multiple):
        values = values.reshape(-1)
        return jnp.pad(values, (0, multiple * 128 - values.shape[0])).reshape(multiple, 128)

    small = jnp.concatenate(
        [
            accx[0:5].reshape(5, 2, own_ch).transpose(1, 0, 2).reshape(2, -1),
            acc1[0].reshape(2, own_ch),
            acch[0, : 2 * own_heads].reshape(2, own_heads),
            (acch[1] * head[3])[: 2 * own_heads].reshape(2, own_heads),
            head_sum(acc1[1]).reshape(2, own_heads),
        ],
        1,
    )
    few = jnp.concatenate(
        [lanes(small, 40), lanes(jnp.concatenate([accs[0:5].reshape(-1), gain_share]), 24)], 0
    )
    gz_rows = jnp.concatenate(
        [
            jnp.pad(gz[:, i * own_heads:(i + 1) * own_heads], ((0, 0), (0, 128 - own_heads)))
            for i in range(2)
        ],
        1,
    )
    own_grad, input_total, oi, og, oz, oo, os, few = tail(
        normed_grad.astype(bf16), input_share.reshape(8, -1), weight_grad(normed, gx),
        weight_grad(normed, g_gate), weight_grad(normed, gz_rows), grad_out_part.astype(bf16),
        weight_grad(normed, gs), few,
    )
    input_total = input_total.reshape(tokens, 1)
    gain_cols = lax.dynamic_slice_in_dim(norm_gain, col * col_width, col_width, 0)
    grad_input = inverse * (own_grad * gain_cols) - own_tokens * inverse**3 * (input_total / width)
    grad_tokens = (grad_input + cotangent.astype(f32)).astype(bf16)
    grad_inner = oi.astype(f32)
    grad_gate = og.astype(f32)
    grad_out = oo.astype(f32)
    grad_states = os.astype(f32)
    grad_step = oz.reshape(col_width, cols, 128)[:, :, :own_heads].astype(f32)
    grad_step = grad_step.reshape(col_width, cols * own_heads)
    small = few[:40].reshape(-1)[: small.size].reshape(2, -1)
    small = lax.dynamic_index_in_dim(small, row, 0, keepdims=False)
    grad_conv_inner = small[: 4 * own_ch].reshape(4, own_ch)
    grad_conv_inner_bias = small[4 * own_ch:5 * own_ch]
    grad_gate_gain = small[5 * own_ch:6 * own_ch]
    rest = small[6 * own_ch:].reshape(3, own_heads)
    summed = few[40:].reshape(-1)
    accs = summed[: 5 * 256].reshape(5, 256)
    grad_norm_gain = lax.dynamic_slice_in_dim(
        summed, 5 * 256 + col * col_width, col_width, 0
    )

    return (
        mixed_out,
        grad_tokens,
        grad_norm_gain,
        grad_gate,
        grad_inner,
        grad_step,
        grad_states,
        grad_conv_inner,
        grad_conv_inner_bias,
        accs[0:4],
        accs[4],
        rest[0],
        rest[1],
        rest[2],
        grad_gate_gain,
        grad_out,
    )


def solution(mesh):
    in_specs = (
        P(("dp", "row"), None),
        P("dp", None),
        P(),
        P("col", "row"),
        P("col", "row"),
        P("col", "row"),
        P(),
        P(None, ("row", "col")),
        P(("row", "col")),
        P(),
        P(),
        P(("row", "col")),
        P(("row", "col")),
        P(("row", "col")),
        P(("row", "col")),
        P("row", "col"),
        P(("dp", "row"), "col"),
    )
    out_specs = (
        P(("dp", "row"), "col"),
        P(("dp", "row"), "col"),
        P("col"),
        P("col", "row"),
        P("col", "row"),
        P("col", "row"),
        P(),
        P(None, ("row", "col")),
        P(("row", "col")),
        P(),
        P(),
        P(("row", "col")),
        P(("row", "col")),
        P(("row", "col")),
        P(("row", "col")),
        P("row", "col"),
    )
    return jax.shard_map(
        per_device, mesh=mesh, in_specs=in_specs, out_specs=out_specs, check_vma=False
    )
```

```python
import functools

import jax
import jax.numpy as jnp
from jax import lax
from jax.experimental import pallas as pl
from jax.experimental.pallas import tpu as pltpu
from jax.sharding import PartitionSpec as P

SPAN = 256
HEAD = 64
epsilon = 1e-05
LOG2E = 1.4426950408889634
f32 = jnp.float32
bf16 = jnp.bfloat16
ANY = pl.ANY


def mm(a, b):
    return lax.dot_general(a, b, (((1,), (0,)), ((), ())), preferred_element_type=f32)


def mm_nt(a, b):
    return lax.dot_general(a, b, (((1,), (1,)), ((), ())), preferred_element_type=f32)


def split(v, terms):
    parts = []
    for _ in range(terms):
        part = v.astype(bf16)
        parts.append(part)
        v = v - part.astype(f32)
    return parts


def mm_split(a, exact, terms=2):
    return sum(mm(part, exact) for part in split(a, terms))


def split_mm(exact, b, terms=3):
    return sum(mm(exact, part) for part in split(b, terms))


def spread_matrix(channels):
    heads = lax.broadcasted_iota(jnp.int32, (128, channels), 0)
    cols = lax.broadcasted_iota(jnp.int32, (128, channels), 1)
    low = heads * HEAD
    return jnp.where((cols >= low) & (cols < low + HEAD), 1.0, 0.0).astype(bf16)


def gather_matrix(channels):
    heads = lax.broadcasted_iota(jnp.int32, (channels, 128), 1)
    rows = lax.broadcasted_iota(jnp.int32, (channels, 128), 0)
    low = heads * HEAD
    return jnp.where((rows >= low) & (rows < low + HEAD), 1.0, 0.0).astype(bf16)


def lower_ones():
    rows = lax.broadcasted_iota(jnp.int32, (SPAN, SPAN), 0)
    cols = lax.broadcasted_iota(jnp.int32, (SPAN, SPAN), 1)
    return jnp.where(rows >= cols, 1.0, 0.0).astype(bf16)


def upper_ones():
    rows = lax.broadcasted_iota(jnp.int32, (SPAN, SPAN), 0)
    cols = lax.broadcasted_iota(jnp.int32, (SPAN, SPAN), 1)
    return jnp.where(rows <= cols, 1.0, 0.0).astype(bf16)


def sigmoid(v):
    return 1.0 / (1.0 + jnp.exp(-v))


def half_masks():
    lane = lax.broadcasted_iota(jnp.int32, (SPAN, 128), 1)
    return lane < HEAD


def rms_rows(tok, gain):
    wide = tok.astype(f32)
    inverse = lax.rsqrt(jnp.mean(wide * wide, -1, keepdims=True) + epsilon)
    return (wide * inverse * gain).astype(bf16)


MESH = pl.DeviceIdType.MESH
SHARE = 4


def lane_block(index, width):
    return pl.ds(pl.multiple_of(index * width, 128), width)


class Links:
    def __init__(self, send, recv, local=None):
        self.send, self.recv, self.local = send, recv, local
        self.used, self.kept, self.sent = 0, 0, []
        dp = lax.axis_index("dp")
        self.groups = lax.axis_size("dp") // SHARE
        self.group = dp // SHARE
        self.x = lax.rem(dp, SHARE) // 2
        self.core = lax.rem(dp, 2)
        self.y = lax.axis_index("row")
        self.z = lax.axis_index("col")
        self.cols = lax.axis_size("col")

    def dp_of(self, group, x, core):
        return group * SHARE + x * 2 + core

    def mate(self):
        return {"dp": self.dp_of(self.group, self.x, 1 - self.core)}

    def across(self):
        return {"dp": self.dp_of(self.group, 1 - self.x, self.core)}

    def other_row(self):
        return {"row": 1 - self.y}

    def col_peer(self, off):
        return lax.rem(self.z + off, self.cols)

    def group_peer(self, off):
        return {"dp": self.dp_of(lax.rem(self.group + off, self.groups), self.x, self.core)}

    def meet(self, far_groups):
        barrier = pltpu.get_barrier_semaphore()
        peers = [self.mate(), self.across(), self.other_row()]
        peers += [{"col": self.col_peer(off)} for off in range(1, self.cols)]
        if far_groups:
            peers += [self.group_peer(off) for off in range(1, self.groups)]
        for peer in peers:
            pl.semaphore_signal(barrier, inc=1, device_id=peer, device_id_type=MESH)
        pl.semaphore_wait(barrier, len(peers))

    def make(self, src, dst, peer, when=None, track=True):
        at = self.used
        self.used += 1
        copy = pltpu.make_async_remote_copy(
            src_ref=src, dst_ref=dst, send_sem=self.send.at[at], recv_sem=self.recv.at[at],
            device_id=peer, device_id_type=MESH,
        )
        if track:
            self.sent.append((copy, when))
        return copy

    def go(self, src, dst, peer, track=True):
        copy = self.make(src, dst, peer, track=track)
        copy.start()
        return copy

    def keep(self, src, dst):
        copy = pltpu.make_async_copy(src, dst, self.local.at[self.kept])
        self.kept += 1
        return copy

    def finish(self):
        for copy, when in self.sent:
            if when is None:
                copy.wait_send()
            else:
                pl.when(when)(copy.wait_send)


class Steps:
    def __init__(self):
        self.stages = []

    def add(self, remote, local=(), before=None):
        self.stages.append((remote, list(local), before))

    def run(self, s):
        if 0 < s <= len(self.stages):
            remote, local, _ = self.stages[s - 1]
            for c in remote:
                c.wait_recv()
            for c in local:
                c.wait()
        if s < len(self.stages):
            remote, local, before = self.stages[s]
            if before is not None:
                before()
            for c in remote + local:
                c.start()


def spread_steps(t, dst_row, dst_x, dst_core, steps):
    steps.add([t.make(dst_row, dst_row, t.other_row())])
    steps.add([t.make(dst_x, dst_x, t.across())])
    steps.add([t.make(dst_core, dst_core, t.mate())])
    return steps


def column_steps(t, src, dst, width):
    part = src.shape[0] // SHARE
    x, y, z, core = t.x, t.y, t.z, t.core
    rows = pl.ds(pl.multiple_of((x * 2 + core) * part, 16), part)
    lanes = lane_block(y, width)
    steps = Steps()
    here = dst.at[z, x, core, :, lanes]
    remote = []
    for off in range(1, t.cols):
        to = t.col_peer(off)
        remote.append(t.make(src.at[rows, lane_block(to, width)], here, {"col": to}))
    steps.add(remote, [t.keep(src.at[rows, lane_block(z, width)], here)])
    return spread_steps(
        t, dst.at[:, x, core, :, lanes], dst.at[:, x, core], dst.at[:, :, core], steps
    )


def row_steps(t, src, dst, width):
    part = src.shape[0] // t.cols // SHARE
    x, y, z, core = t.x, t.y, t.z, t.core

    def rows(to):
        return pl.ds(pl.multiple_of((to * SHARE + x * 2 + core) * part, 16), part)

    steps = Steps()
    here = dst.at[y, x, core, :, lane_block(z, width)]
    remote = []
    for off in range(1, t.cols):
        to = t.col_peer(off)
        remote.append(t.make(src.at[rows(to), :], here, {"col": to}))
    steps.add(remote, [t.keep(src.at[rows(z), :], here)])
    return spread_steps(t, dst.at[y, x, core], dst.at[:, x, core], dst.at[:, :, core], steps)


def gather_steps(t, own, whole):
    width = own.shape[1]
    z = t.z
    mate, far = z + 1 - 2 * lax.rem(z, 2), lax.rem(z + 2, 4)
    here, there = whole.at[:, lane_block(z, width)], whole.at[:, lane_block(far, width)]
    steps = Steps()
    cross = t.make(own, here, {"col": far})
    near = t.make(own, here, {"col": mate})
    steps.add([cross], [t.keep(own, here)])
    steps.add([near, t.make(there, there, {"col": mate})])
    return steps


def front_kernel(
    inner_total,
    tok, ngain, w_states, meta, docrow, spar, inner, gate, out, step_w, cot, par_own, head_own, halo,
    wi_o, wg_o, wo_o, ws_o, cots_o, par_o, head_o,
    normed_o, pre_o, spre_o, sd_o, ssd_o, x_o, wr_o, step_o, r_o, sig_o, hpre_o, hspre_o, sprev_o,
    gated_o, ggate_o, gy_o, dr_o, dsf_o, dsout_o, acc_o,
    wi, wg, wo, ws2, ws, cots, par, head, head_in, halo_in,
    normed_s, pre_s, spre_s, sd_s, ssd_s, x_s, wr_s, step_s, r_s, sig_s, hpre_s, hspre_s, sprev_s,
    gated_s, ggate_s, gy_s, dr_s, dsf_s, acc_s,
    fresh_s, y_s, gate_s, gg_s, sums_s, sums_in,
    xbuf, sbuf, mem, mem_in,
    send, recv, local,
):
    t = Links(send, recv, local)
    t.meet(False)
    x, y, z, core = t.x, t.y, t.z, t.core
    blocks = tok.shape[0] // SPAN
    channels = x_s.shape[1]
    half = channels // 2
    outputs = []

    def write(src, dst):
        copy = t.keep(src, dst)
        copy.start()
        outputs.append(copy)

    few = [
        t.go(par_own, par.at[:, lane_block(y, half)], t.other_row()),
        t.go(head_own, head_in, t.other_row()),
        t.go(halo, halo_in, t.other_row()),
    ]
    block = inner.shape[1] // t.cols
    get_inner = column_steps(t, inner, wi, block)
    get_step = column_steps(t, step_w, ws2, step_w.shape[1] // t.cols)
    get_gate = column_steps(t, gate, wg, block)
    get_out = row_steps(t, out, wo, out.shape[1])
    get_cot = gather_steps(t, cot, cots)
    pass_state = t.make(mem, mem_in, t.other_row(), track=False)
    pass_sums = [
        t.make(sums_s, sums_in.at[off - 1], {"col": t.col_peer(off)}) for off in range(1, t.cols)
    ]
    get_inner.run(0)
    get_step.run(0)
    get_gate.run(0)
    get_out.run(0)
    get_cot.run(0)
    par[:, lane_block(y, half)] = par_own[...]
    for s in range(1, 5):
        get_inner.run(s)
        get_step.run(s)
        if s > 1:
            get_gate.run(s - 1)
        if s > 2:
            get_out.run(s - 2)
    for c in few:
        c.wait_recv()
    head[...] = head_own[...] + head_in[...]
    wide_in = normed_s.shape[1]
    ws[...] = (
        ws2[:, :, :, :, 0:128].reshape(wide_in, 128) + ws2[:, :, :, :, 128:256].reshape(wide_in, 128)
    )
    spread = spread_matrix(channels)
    gain = ngain[...]

    def w_of(ref):
        return ref[...].reshape(-1, ref.shape[-1])

    def rows_of(i):
        return pl.ds(pl.multiple_of(i * SPAN, SPAN), SPAN)

    hn = rms_rows(halo_in[...], gain)
    hp = mm(hn, w_of(wi))[8:16]
    hs = mm(hn, w_states[...])[8:16]
    xbuf[0:8, :] = hp
    sbuf[0:8, :] = hs
    hpre_s[...] = hp
    hspre_s[...] = hs
    mem[...] = jnp.zeros_like(mem)

    def entry(i, carry):
        at = rows_of(i)

        @pl.when(i > 0)
        def _():
            xbuf[0:8, :] = xbuf[SPAN:SPAN + 8, :]
            sbuf[0:8, :] = sbuf[SPAN:SPAN + 8, :]

        wide_tok = tok[at, :].astype(f32)
        inverse = lax.rsqrt(jnp.mean(wide_tok * wide_tok, -1, keepdims=True) + epsilon)
        normed = (wide_tok * inverse * gain).astype(bf16)
        normed_s[at, :] = normed
        x_pre = mm(normed, w_of(wi))
        s_pre = mm(normed, w_states[...])
        xbuf[8:SPAN + 8, :] = x_pre
        sbuf[8:SPAN + 8, :] = s_pre
        pre_s[at, :] = x_pre.astype(bf16)
        spre_s[at, :] = s_pre.astype(bf16)
        marks = meta[at, :]

        def conv_silu(buf, here, taps):
            v = taps[4:5, :] + taps[0:1, :] * here
            for k in range(1, 4):
                v = v + marks[:, k:k + 1] * (taps[k:k + 1, :] * buf[8 - k:8 - k + SPAN, :])
            sg = sigmoid(v)
            return v * sg, sg * (1.0 + v * (1.0 - sg))

        act, slope = conv_silu(xbuf, x_pre, par)
        x_low = act.astype(bf16)
        x_s[at, :] = x_low
        sd_s[at, :] = slope.astype(bf16)
        sact, sslope = conv_silu(sbuf, s_pre, spar)
        wr = sact.astype(bf16)
        wr_s[at, :] = wr
        ssd_s[at, :] = sslope.astype(bf16)

        raw = mm(normed, ws[...]) + head[0:1, :]
        step = jnp.maximum(raw, 0.0) + jnp.log1p(jnp.exp(-jnp.abs(raw)))
        lane = lax.broadcasted_iota(jnp.int32, (SPAN, 128), 1)
        sig_s[at, :] = jnp.where(lane == 127, inverse, sigmoid(raw))
        step_s[at, :] = step
        r = split_mm(lower_ones(), step * head[1:2, :])
        r_s[at, :] = r
        last = r[SPAN - 1:SPAN, :]
        to_end = jnp.exp2(jnp.minimum(last - r, 0.0)) * marks[:, 5:6]
        coef = mm_split(to_end * step, spread)
        w_t = jnp.transpose(wr[:, 0:128].astype(f32)).astype(bf16)
        fresh = mm(w_t, (coef * x_low.astype(f32)).astype(bf16))
        fresh_s[i] = fresh
        mem[...] = keep_of(last, marks) * mem[...] + fresh

        @pl.when(i == 0)
        def _():
            get_gate.run(4)
            get_out.run(3)
            get_cot.run(1)

        @pl.when(i == 2)
        def _():
            get_out.run(4)

        return carry

    def keep_of(last, marks):
        return mm_split(jnp.broadcast_to(jnp.exp2(last) * marks[0:1, 6:7], (8, 128)), spread)[0:1]

    lax.fori_loop(0, blocks, entry, 0)
    pass_state.start()
    for src, dst in (
        (normed_s, normed_o), (pre_s, pre_o), (spre_s, spre_o), (sd_s, sd_o), (ssd_s, ssd_o),
        (x_s, x_o), (wr_s, wr_o), (step_s, step_o), (r_s, r_o), (sig_s, sig_o), (hpre_s, hpre_o),
        (hspre_s, hspre_o), (wi, wi_o), (wg, wg_o), (wo, wo_o), (ws, ws_o), (par, par_o),
        (head, head_o),
    ):
        write(src, dst)

    def gate_block(i, carry):
        at = rows_of(i)
        gate_s[at, :] = mm(normed_s[at, :], w_of(wg))
        return carry

    lax.fori_loop(0, blocks, gate_block, 0)

    pass_state.wait()
    mem[...] = mem_in[...] * jnp.where(y == 1, 1.0, 0.0)
    skip = mm_split(jnp.broadcast_to(head[2:3, :], (8, 128)), spread)[0:1]
    first = half_masks()

    def scan(i, carry):
        at = rows_of(i)
        marks = meta[at, :]
        w_low = wr_s[at, 0:128]
        r_low = wr_s[at, 128:256]
        r = r_s[at, :]
        r_t = jnp.transpose(r)
        rows = lax.broadcasted_iota(jnp.int32, (SPAN, SPAN), 0)
        cols = lax.broadcasted_iota(jnp.int32, (SPAN, SPAN), 1)
        allowed = (rows >= cols) & (marks[:, 0:1] == docrow[:, at])
        scores = jnp.where(allowed, mm_nt(r_low, w_low), 0.0)
        wide = x_s[at, :].astype(f32)
        xd = (mm_split(step_s[at, :], spread) * wide).astype(bf16)
        sprev = mem[...].astype(bf16)
        sprev_s[i] = sprev
        linked = jnp.exp2(r) * marks[:, 4:5]
        carried = mm(r_low, sprev) * mm_split(linked, spread)
        y_s[at, :] = carried + skip * wide
        for pair in range(channels // 128):
            lanes = slice(pair * 128, pair * 128 + 128)
            xp = xd[:, lanes]
            total = y_s[at, lanes]
            for part in range(2):
                h = 2 * pair + part
                decay = jnp.exp2(jnp.minimum(r[:, h:h + 1] - r_t[h:h + 1, :], 0.0))
                mixing = (scores * decay).astype(bf16)
                own = jnp.where(first if part == 0 else ~first, xp, jnp.zeros_like(xp))
                total = total + mm(mixing, own)
            y_s[at, lanes] = total
        last = r[SPAN - 1:SPAN, :]
        mem[...] = keep_of(last, marks) * mem[...] + fresh_s[i]
        return carry

    lax.fori_loop(0, blocks, scan, 0)
    write(sprev_s, sprev_o)

    get_cot.run(2)
    write(cots, cots_o)
    ones = jnp.ones((8, channels), bf16)

    def totals_of(i, carry):
        at = rows_of(i)
        gg = mm_nt(cots[at, :], w_of(wo))
        gg_s[at, :] = gg
        g = gate_s[at, :]
        mixed = y_s[at, :] * (g * sigmoid(g))
        sq = sum(mm_nt(ones, part) for part in split(mixed * mixed, 2))
        pr = sum(mm_nt(ones, part) for part in split(mixed * (par[5:6, :] * gg), 2))
        row = lax.broadcasted_iota(jnp.int32, (8, SPAN), 0)
        sums_s[:, at] = jnp.where(row == 0, sq, jnp.where(row == 1, pr, 0.0))
        return carry

    lax.fori_loop(0, blocks, totals_of, 0)
    for c in pass_sums:
        c.start()
    for c in pass_sums:
        c.wait_recv()
    mem[...] = jnp.zeros_like(mem)
    acc_s[...] = jnp.zeros_like(acc_s)
    gather = gather_matrix(channels)

    def turn(back_i, carry):
        i = blocks - 1 - back_i
        at = rows_of(i)
        marks = meta[at, :]
        both = sums_s[:, at]
        for off in range(1, t.cols):
            both = both + sums_in[off - 1, :, at]
        totals = jnp.transpose(both)
        scale = lax.rsqrt(totals[:, 0:1] / inner_total + epsilon)
        cross = totals[:, 1:2] / inner_total
        yv = y_s[at, :]
        g = gate_s[at, :]
        sg = sigmoid(g)
        sl = g * sg
        gg = gg_s[at, :]
        ngate = par[5:6, :]
        normal = yv * sl * scale
        gated_s[at, :] = (normal * ngate).astype(bf16)
        g_mixed = scale * (ngate * gg - normal * (scale * cross))
        ggate_s[at, :] = (g_mixed * yv * (sg * (1.0 + g * (1.0 - sg)))).astype(bf16)
        gy = (g_mixed * sl).astype(bf16)
        gy_s[at, :] = gy
        gyw = gy.astype(f32)
        wide = x_s[at, :].astype(f32)
        dr_s[at, :] = mm_split(gyw * (yv - skip * wide), gather)
        row = lax.broadcasted_iota(jnp.int32, (8, channels), 0)
        ggain = jnp.sum(gg * normal, 0, keepdims=True)
        gskip = jnp.sum(gyw * wide, 0, keepdims=True)
        acc_s[...] += jnp.where(row == 0, ggain, jnp.where(row == 1, gskip, 0.0))
        r = r_s[at, :]
        linked = mm_split(jnp.exp2(r) * marks[:, 4:5], spread)
        r_t = jnp.transpose(wr_s[at, 128:256].astype(f32)).astype(bf16)
        dfresh = mm(r_t, (linked * gyw).astype(bf16))
        dsf_s[i] = dfresh
        mem[...] = keep_of(r[SPAN - 1:SPAN, :], marks) * mem[...] + dfresh
        return carry

    lax.fori_loop(0, blocks, turn, 0)
    for src, dst in (
        (gated_s, gated_o), (ggate_s, ggate_o), (gy_s, gy_o), (dr_s, dr_o), (dsf_s, dsf_o),
        (mem, dsout_o), (acc_s, acc_o),
    ):
        write(src, dst)
    for copy in outputs:
        copy.wait()
    t.finish()


def front(inner_all, tok, ngain, w_states, meta, docrow, spar, inner, gate, out, step_w, cot, par_own,
          head_own, halo):
    tokens, width = tok.shape
    blocks = tokens // SPAN
    cols = lax.axis_size("col")
    part, half = inner.shape[0] // SHARE, inner.shape[1] // cols
    channels = 2 * half
    sds = jax.ShapeDtypeStruct
    V = pltpu.VMEM
    weights = [
        ((cols, 2, 2, part, channels), bf16), ((cols, 2, 2, part, channels), bf16),
        ((2, 2, 2, half // SHARE, width), bf16),
    ]
    entry_shapes = [
        ((tokens, width), bf16), ((tokens, channels), bf16), ((tokens, 256), bf16),
        ((tokens, channels), bf16), ((tokens, 256), bf16), ((tokens, channels), bf16),
        ((tokens, 256), bf16), ((tokens, 128), f32), ((tokens, 128), f32), ((tokens, 128), f32),
        ((8, channels), f32), ((8, 256), f32), ((blocks, 128, channels), bf16),
    ]
    turn_shapes = [
        ((tokens, channels), bf16), ((tokens, channels), bf16), ((tokens, channels), bf16),
        ((tokens, 128), f32), ((blocks, 128, channels), f32),
    ]
    state = ((128, channels), f32)
    acc = ((8, channels), f32)
    outs = (
        weights + [((width, 128), bf16), ((tokens, width), bf16), ((8, channels), f32), ((8, 128), f32)]
        + entry_shapes + turn_shapes + [state, acc]
    )
    scratch = (
        weights
        + [((cols, 2, 2, part, 256), bf16), ((width, 128), bf16), ((tokens, width), bf16),
           ((8, channels), f32), ((8, 128), f32), ((8, 128), f32), (halo.shape, bf16)]
        + entry_shapes + turn_shapes + [acc]
        + [((blocks, 128, channels), f32), ((tokens, channels), f32), ((tokens, channels), f32),
           ((tokens, channels), f32), ((8, tokens), f32), ((cols - 1, 8, tokens), f32),
           ((SPAN + 8, channels), f32), ((SPAN + 8, 256), f32), state, state]
    )
    vmem = pl.BlockSpec(memory_space=V)
    hbm = pl.BlockSpec(memory_space=pl.ANY)
    got = pl.pallas_call(
        functools.partial(front_kernel, float(inner_all)),
        out_shape=[sds(*o) for o in outs],
        in_specs=[vmem] * 6 + [hbm] * 5 + [vmem, vmem, hbm],
        out_specs=[hbm] * len(outs),
        scratch_shapes=[V(*s) for s in scratch] + [
            pltpu.SemaphoreType.DMA((48,)), pltpu.SemaphoreType.DMA((48,)),
            pltpu.SemaphoreType.DMA((48,)),
        ],
        compiler_params=pltpu.CompilerParams(
            collective_id=1, has_side_effects=True, vmem_limit_bytes=62 * 1024 * 1024
        ),
        name="front",
    )(tok, ngain, w_states, meta, docrow, spar, inner, gate, out, step_w, cot, par_own, head_own, halo)
    got = list(got)
    got[0] = got[0].reshape(width, channels)
    got[1] = got[1].reshape(width, channels)
    got[2] = got[2].reshape(channels, width)
    return got


def mm_tn(a, b):
    return lax.dot_general(a, b, (((0,), (0,)), ((), ())), preferred_element_type=f32)


def add_bf16(a, b):
    return (a.astype(f32) + b.astype(f32)).astype(bf16)


def sum_far_groups(t, own, got, spare):
    if t.groups == 1:
        return
    more = [t.go(own, got.at[off - 1], t.group_peer(off), False) for off in range(1, t.groups)]
    for c in more:
        c.wait()
    for off in range(1, t.groups):
        back = t.keep(got.at[off - 1], spare)
        back.start()
        back.wait()
        own[...] = add_bf16(own[...], spare[...])


def column_sums(t, g, a1, a2, a3, a4, far, o):
    x, y, z, core = t.x, t.y, t.z, t.core
    width = a4.shape[-1]
    steps = Steps()
    steps.add([t.make(g.at[:, :, 1 - core], a1, t.mate())])

    def add_core():
        def body(i, c):
            for j in range(2):
                a1[i, j] = add_bf16(a1[i, j], g[i, j, core])
            return c

        lax.fori_loop(0, t.cols, body, 0)

    steps.add([t.make(a1.at[:, :, :, lane_block(1 - y, width)], a2, t.other_row())], (), add_core)
    mine = lane_block(y, width)

    def add_row():
        def body(i, c):
            for j in range(2):
                a2[i, j] = add_bf16(a2[i, j], a1[i, j, :, mine])
            return c

        lax.fori_loop(0, t.cols, body, 0)

    steps.add([t.make(a2.at[:, 1 - x], a3, t.across())], (), add_row)

    def add_x():
        def body(i, c):
            a4[i] = add_bf16(a3[i], a2[i, x])
            return c

        lax.fori_loop(0, t.cols, body, 0)
        sum_far_groups(t, a4, far, a3)

    here = o.at[x, core, :, lane_block(z, width)]
    steps.add(
        [t.make(a4.at[t.col_peer(off)], here, {"col": t.col_peer(off)}) for off in range(1, t.cols)],
        [t.keep(a4.at[z], here)], add_x,
    )
    steps.add([t.make(o.at[x, core], o.at[x, core], t.across())])
    steps.add([t.make(o.at[:, core], o.at[:, core], t.mate())])
    return steps


def row_sums(t, g, a1, a2, a3, a4, far, o):
    x, y, z, core = t.x, t.y, t.z, t.core
    width = o.shape[-1]
    steps = Steps()
    steps.add([t.make(g.at[:, :, 1 - core], a1, t.mate())])

    def add_core():
        def body(i, c):
            for j in range(2):
                a1[i, j] = add_bf16(a1[i, j], g[i, j, core])
            return c

        lax.fori_loop(0, 2, body, 0)

    steps.add([t.make(a1.at[1 - y], a2, t.other_row())], (), add_core)

    def add_row():
        for j in range(2):
            a2[j] = add_bf16(a2[j], a1[y, j])

    steps.add([t.make(a2.at[1 - x], a3, t.across())], (), add_row)

    def add_x():
        a4[...] = add_bf16(a3[...], a2[x])
        sum_far_groups(t, a4, far, a3)

    here = o.at[z, x, core]
    steps.add(
        [t.make(a4.at[:, lane_block(t.col_peer(off), width)], here, {"col": t.col_peer(off)})
         for off in range(1, t.cols)],
        [t.keep(a4.at[:, lane_block(z, width)], here)], add_x,
    )
    steps.add([t.make(o.at[:, x, core], o.at[:, x, core], t.across())])
    steps.add([t.make(o.at[:, :, core], o.at[:, :, core], t.mate())])
    return steps


def full_sums(t, g, s1, s2, s3, s4, s5, far, o):
    x, y, z, core = t.x, t.y, t.z, t.core
    steps = Steps()
    steps.add([t.make(g.at[:, :, :, 1 - core], s1, t.mate())])

    def add_core():
        def body(i, c):
            for j in range(2):
                for k in range(2):
                    s1[i, j, k] = add_bf16(s1[i, j, k], g[i, j, k, core])
            return c

        lax.fori_loop(0, t.cols, body, 0)

    steps.add([t.make(s1.at[:, 1 - y], s2, t.other_row())], (), add_core)

    def add_row():
        def body(i, c):
            for k in range(2):
                s2[i, k] = add_bf16(s2[i, k], s1[i, y, k])
            return c

        lax.fori_loop(0, t.cols, body, 0)

    steps.add([t.make(s2.at[:, 1 - x], s3, t.across())], (), add_row)

    def add_x():
        def body(i, c):
            s4[i] = add_bf16(s3[i], s2[i, x])
            return c

        lax.fori_loop(0, t.cols, body, 0)
        sum_far_groups(t, s4, far, s3)

    steps.add(
        [t.make(s4.at[t.col_peer(off)], s5.at[off - 1], {"col": t.col_peer(off)})
         for off in range(1, t.cols)], (), add_x,
    )

    def add_cols():
        total = s4[z].astype(f32)
        for off in range(1, t.cols):
            total = total + s5[off - 1].astype(f32)
        s4[z] = total.astype(bf16)

    here = o.at[z, y, x, core]
    steps.add(
        [t.make(s4.at[z], here, {"col": t.col_peer(off)}) for off in range(1, t.cols)],
        [t.keep(s4.at[z], here)], add_cols,
    )
    here = o.at[:, y, x, core]
    steps.add([t.make(here, here, t.other_row())])
    here = o.at[:, :, x, core]
    steps.add([t.make(here, here, t.across())])
    here = o.at[:, :, :, core]
    steps.add([t.make(here, here, t.mate())])
    return steps


def small_sums(t, sm, msum, mgot, out, rest):
    steps = Steps()
    steps.add([t.make(sm, mgot.at[0], t.mate())])

    def add_core():
        msum[0] = sm[...] + mgot[0]

    steps.add([t.make(msum.at[0], mgot.at[1], t.other_row())], (), add_core)

    def add_row():
        msum[1] = msum[0] + mgot[1]

    steps.add([t.make(msum.at[1], mgot.at[2], t.across())], (), add_row)

    def add_x():
        msum[2] = msum[1] + mgot[2]
        if t.groups > 1:
            more = [t.go(msum.at[2], mgot.at[5 + off], t.group_peer(off), False)
                    for off in range(1, t.groups)]
            for c in more:
                c.wait()
            total = msum[2]
            for off in range(1, t.groups):
                total = total + mgot[5 + off]
            msum[2] = total

    last = pl.ds(rest, sm.shape[0] - rest)
    steps.add(
        [t.make(msum.at[2, last], mgot.at[2 + off, last], {"col": t.col_peer(off)})
         for off in range(1, t.cols)], (), add_x,
    )

    def done():
        out[0:rest] = msum[2, 0:rest]
        out[rest:] = msum[2, rest:] + mgot[3, rest:] + mgot[4, rest:] + mgot[5, rest:]

    steps.add([], (), done)
    return steps


class PairSum:
    def __init__(self, t, part, near, far_in, rows):
        z = t.z
        mate = z + 1 - 2 * lax.rem(z, 2)
        far = lax.rem(z + 2, 4)
        mate_far = lax.rem(mate + 2, 4)
        width = near.shape[-1]
        self.part, self.near, self.far_in, self.rows = part, near, far_in, rows
        self.own, self.far = lane_block(z, width), lane_block(far, width)
        to_mate = [
            t.make(part.at[rows, lane_block(mate_far, width)], near.at[1, rows], {"col": mate}),
            t.make(part.at[rows, lane_block(mate, width)], near.at[0, rows], {"col": mate}),
        ]
        self.first, self.second = to_mate
        self.across = t.make(near.at[1, rows], far_in.at[rows], {"col": far})

    def start(self):
        self.first.start()
        self.second.start()

    def forward(self):
        self.first.wait_recv()
        count = self.rows.size // 64

        def body(i, c):
            at = pl.ds(pl.multiple_of(self.rows.start + i * 64, 16), 64)
            self.near[1, at] = add_bf16(self.near[1, at], self.part[at, self.far])
            return c

        lax.fori_loop(0, count, body, 0)
        self.across.start()

    def arrive(self):
        self.second.wait_recv()
        self.across.wait_recv()

    def total(self, at):
        return (
            self.part[at, self.own].astype(f32) + self.near[0, at].astype(f32)
            + self.far_in[at].astype(f32)
        )


def rear_kernel(
    meta, hmeta, docrow, head, par, spar, hpre, hspre, acc1, ngain_cols,
    tok_h, w_states_h, dsout_h, wi_h, wg_h, wo_h, ws_h, cots_h, normed_h, pre_h, spre_h, sd_h, ssd_h,
    x_h, wr_h, step_h, r_h, sig_h, sprev_h, gated_h, ggate_h, gy_h, dr_h, dsf_h,
    mixed_o, gtok_o, oi, og, oz, oo, os, sm_o, far_i, far_g, far_z, far_o, far_s,
    tok, wst, dsout, wi, wg, wo, ws, cots, normed, pre, spre, sd, ssd,
    x_s, wr_s, step_s, r_s, sig_s, sprev_s, gated, ggate, gy_s, dr_s, dsf_s,
    cot_own, dmem, gs_s, gz_s, gbuf, hbuf, hx, hs, hx_in, hs_in, accx, accs, acch, gshare,
    out_part, out_near, out_far, g_near, g_far, ish, ish_in,
    gi, i1, i2, i3, i4, gg, g1, g2, g3, g4, gz, z1, z2, z3, z4, o1, o2, o3, o4,
    gs, s1, s2, s3, s4, s5, sm, msum, mgot,
    send, recv, local,
):
    t = Links(send, recv, local)
    x, y, z, core = t.x, t.y, t.z, t.core
    tokens, width = normed.shape
    channels = gated.shape[1]
    third = width // t.cols
    blocks = tokens // SPAN
    own_cols = lane_block(z, third)

    def load(src, dst):
        copy = t.keep(src, dst)
        copy.start()
        return copy

    load_out = [load(gated_h, gated), load(wo_h, wo), load(dsout_h, dsout)]
    load_grad = [load(cots_h, cots), load(cots_h.at[:, own_cols], cot_own)]
    load_gate = [load(normed_h, normed), load(ggate_h, ggate)]
    load_back = [
        load(a, b) for a, b in (
            (x_h, x_s), (wr_h, wr_s), (gy_h, gy_s), (r_h, r_s), (step_h, step_s), (sig_h, sig_s),
            (dr_h, dr_s), (sprev_h, sprev_s), (dsf_h, dsf_s), (pre_h, pre), (spre_h, spre),
            (sd_h, sd), (ssd_h, ssd),
        )
    ]
    load_norm = [load(wg_h, wg), load(wi_h, wi), load(ws_h, ws), load(w_states_h, wst),
                 load(tok_h.at[:, own_cols], tok)]

    go = wo
    gx_s = gated
    part = cots
    pass_state = t.make(dsout, dmem, t.other_row())
    halo_x = t.make(hx, hx_in, t.other_row())
    halo_s = t.make(hs, hs_in, t.other_row())
    out_sum = PairSum(t, out_part, out_near, out_far, pl.ds(0, tokens))
    norm_sums = [PairSum(t, part, g_near, g_far, pl.ds(b * SPAN, SPAN)) for b in range(blocks)]
    sum_out = row_sums(t, go, o1, o2, o3, o4, far_o, oo)
    sum_gate = column_sums(t, gg, g1, g2, g3, g4, far_g, og)
    sum_inner = column_sums(t, gi, i1, i2, i3, i4, far_i, oi)
    sum_step = column_sums(t, gz, z1, z2, z3, z4, far_z, oz)
    sum_states = full_sums(t, gs, s1, s2, s3, s4, s5, far_s, os)
    sum_small = small_sums(t, sm, msum, mgot, sm_o, 16)
    send_ish = [t.make(ish, ish_in.at[off - 1], {"col": t.col_peer(off)}) for off in range(1, t.cols)]
    t.meet(True)

    def rows_of(i):
        return pl.ds(pl.multiple_of(i * SPAN, SPAN), SPAN)

    def w_of(ref):
        return ref[...].reshape(-1, ref.shape[-1])

    for c in load_out:
        c.wait()
    pass_state.start()

    def project(i, carry):
        at = rows_of(i)
        out_part[at, :] = mm(gated[at, :], w_of(wo)).astype(bf16)
        return carry

    lax.fori_loop(0, blocks, project, 0)
    out_sum.start()
    for c in load_grad:
        c.wait()

    def grad_out(i, carry):
        rows = pl.ds(pl.multiple_of(i * (channels // 2), 128), channels // 2)
        for n in range(2):
            lanes = slice(n * width // 2, (n + 1) * width // 2)
            value = mm_tn(gated[:, rows], cots[:, lanes]).astype(bf16)
            go[i, :, :, :, lanes] = value.reshape(go.shape[1:4] + (width // 2,))
        return carry

    lax.fori_loop(0, 2, grad_out, 0)
    sum_out.run(0)
    for c in load_gate:
        c.wait()

    def weight_grad(right, target):
        def body(i, carry):
            rows = pl.ds(pl.multiple_of(i * third, 128), third)
            target[i] = mm_tn(normed[:, rows], right[...]).astype(bf16).reshape(target.shape[1:])
            return carry

        lax.fori_loop(0, t.cols, body, 0)

    weight_grad(ggate, gg)
    sum_gate.run(0)
    for c in load_back + load_norm:
        c.wait()
    pass_state.wait_recv()
    dmem[...] = dmem[...] * jnp.where(y == 0, 1.0, 0.0)
    accx[...] = jnp.zeros_like(accx)
    accs[...] = jnp.zeros_like(accs)
    acch[...] = jnp.zeros_like(acch)
    gshare[...] = jnp.zeros_like(gshare)
    gbuf[...] = jnp.zeros_like(gbuf)
    hbuf[...] = jnp.zeros_like(hbuf)
    spread = spread_matrix(channels)
    gather = gather_matrix(channels)
    first = half_masks()
    skip = mm_split(jnp.broadcast_to(head[2:3, :], (8, 128)), spread)[0:1]

    def normed_grad(i):
        at = rows_of(i)

        def body(c, column):
            lanes = pl.ds(pl.multiple_of(c * third, 128), third)
            total = (
                mm_nt(ggate[at, :], wg[lanes, :]) + mm_nt(gx_s[at, :], wi[lanes, :])
                + mm_nt(gz_s[at, :], ws[lanes, :]) + mm_nt(gs_s[at, :], wst[lanes, :])
            )
            part[at, lanes] = total.astype(bf16)
            weighed = total * normed[at, lanes].astype(f32)
            gshare[0:1, lanes] += jnp.sum(weighed, 0, keepdims=True)
            return column + jnp.sum(weighed, -1, keepdims=True)

        column = lax.fori_loop(0, t.cols, body, jnp.zeros((SPAN, 1), f32))
        ish[:, at] = jnp.transpose(jnp.broadcast_to(column, (SPAN, 128)))[0:8]

    def back(back_i, carry):
        i = blocks - 1 - back_i
        at = rows_of(i)

        @pl.when(back_i > 0)
        def _():
            gbuf[SPAN + 8:SPAN + 16, :] = gbuf[8:16, :]
            hbuf[SPAN + 8:SPAN + 16, :] = hbuf[8:16, :]

        marks = meta[at, :]
        w_low = wr_s[at, 0:128]
        r_low = wr_s[at, 128:256]
        r = r_s[at, :]
        r_t = jnp.transpose(r)
        step = step_s[at, :]
        last = r[SPAN - 1:SPAN, :]
        rows = lax.broadcasted_iota(jnp.int32, (SPAN, SPAN), 0)
        cols = lax.broadcasted_iota(jnp.int32, (SPAN, SPAN), 1)
        allowed = (rows <= cols) & (marks[:, 0:1] == docrow[:, at])
        scores = jnp.where(allowed, mm_nt(w_low, r_low), 0.0)
        ds = dmem[...]
        ds_low = ds.astype(bf16)
        step_parts = split(step, 2)
        te_parts = split(jnp.exp2(jnp.minimum(last - r, 0.0)) * marks[:, 5:6], 2)
        linked_parts = split(jnp.exp2(r) * marks[:, 4:5], 2)
        keep = mm_split(jnp.broadcast_to(jnp.exp2(last) * marks[0:1, 6:7], (8, 128)), spread)[0:1]
        final = jnp.where(back_i == blocks - 1, 1.0, 0.0)

        def conv_back(buf, lanes, gv, base, taps, acc, halo_pre, out, halo_out):
            buf[8:SPAN + 8, lanes] = gv
            cols_here = gv.shape[1]
            total = taps[0:1, lanes] * gv
            sums = [jnp.sum(gv * base, 0, keepdims=True)]
            halo = jnp.zeros((8, cols_here), f32)
            hsum = []
            for k in range(1, 4):
                moved = marks[:, 7 + k:8 + k] * buf[8 + k:8 + k + SPAN, lanes]
                total = total + taps[k:k + 1, lanes] * moved
                sums.append(jnp.sum(moved * base, 0, keepdims=True))
                hmoved = hmeta[:, 7 + k:8 + k] * buf[k:8 + k, lanes]
                halo = halo + taps[k:k + 1, lanes] * hmoved
                hsum.append(jnp.sum(hmoved * halo_pre[:, lanes], 0, keepdims=True))
            sums.append(jnp.sum(gv, 0, keepdims=True))
            out[at, lanes] = total.astype(bf16)
            halo_out[:, lanes] = halo
            rows8 = lax.broadcasted_iota(jnp.int32, (8, cols_here), 0)
            add = jnp.zeros((8, cols_here), f32)
            for n, s in enumerate(sums):
                if 1 <= n <= 3:
                    s = s + final * hsum[n - 1]
                add = add + jnp.where(rows8 == n, s, 0.0)
            acc[:, lanes] += add

        zero = jnp.zeros((SPAN, 128), f32)
        dscores = jnp.zeros((SPAN, SPAN), f32)
        g_write, g_read, dr_cols, dstep = zero, zero, zero, zero
        at_end = jnp.zeros((8, 128), f32)
        for pair in range(channels // 128):
            lanes = slice(pair * 128, pair * 128 + 128)
            to_lanes, to_heads = spread[:, lanes], gather[lanes, :]

            def widen(parts):
                return sum(mm(p, to_lanes) for p in parts)

            wide = x_s[at, lanes].astype(f32)
            step_wide = widen(step_parts)
            xp = (step_wide * wide).astype(bf16)
            xdw = xp.astype(f32)
            gp = gy_s[at, lanes]
            gyw = gp.astype(f32)
            ds_pair = ds_low[:, lanes]
            sprev = sprev_s[i, :, lanes]
            te = widen(te_parts)
            total = te * mm(w_low, ds_pair)
            ending = jnp.sum(xdw * total, 0, keepdims=True) + keep[:, lanes] * jnp.sum(
                sprev.astype(f32) * ds[:, lanes], 0, keepdims=True
            )
            at_end = at_end + mm_split(jnp.broadcast_to(ending, (8, 128)), to_heads, 3)
            for half in range(2):
                h = 2 * pair + half
                own = first if half == 0 else ~first
                decay = jnp.exp2(jnp.minimum(r_t[h:h + 1, :] - r[:, h:h + 1], 0.0))
                mixing = (scores * decay).astype(bf16)
                gown = jnp.where(own, gp, jnp.zeros_like(gp))
                total = total + mm(mixing, gown)
                dscores = dscores + mm_nt(xp, gown) * decay
            g_write = g_write + mm_nt((te * xdw).astype(bf16), ds_pair)
            g_read = g_read + mm_nt((widen(linked_parts) * gyw).astype(bf16), sprev)
            dr_cols = dr_cols + mm_split(xdw * total, to_heads)
            dstep = dstep + mm_split(wide * total, to_heads)
            g_x = step_wide * total + skip[:, lanes] * gyw
            conv_back(gbuf, lanes, g_x * sd[at, lanes].astype(f32), pre[at, lanes].astype(f32), par,
                      accx, hpre, gx_s, hx)
        dscores = jnp.where(allowed, dscores, 0.0)
        g_write = g_write + mm(dscores.astype(bf16), r_low)
        g_read = g_read + mm(jnp.transpose(dscores).astype(bf16), w_low)
        both = slice(0, 256)
        g_wr = jnp.concatenate([g_write, g_read], 1)
        conv_back(hbuf, both, g_wr * ssd[at, :].astype(f32), spre[at, :].astype(f32), spar, accs,
                  hspre, gs_s, hs)
        tail_row = lax.broadcasted_iota(jnp.int32, (SPAN, 128), 0) == SPAN - 1
        dr = dr_s[at, :] - dr_cols + jnp.where(tail_row, at_end[0:1], 0.0)
        da = split_mm(upper_ones(), dr)
        dstep = dstep + head[3:4, :] * da
        gzv = dstep * sig_s[at, :]
        gz_s[at, :] = gzv.astype(bf16)
        row = lax.broadcasted_iota(jnp.int32, (8, 128), 0)
        gbias = jnp.sum(gzv, 0, keepdims=True)
        grate = jnp.sum(da * step, 0, keepdims=True)
        acch[...] += jnp.where(row == 0, gbias, jnp.where(row == 1, grate, 0.0))
        dmem[...] = keep * ds + dsf_s[i]

        @pl.when(back_i > 0)
        def _():
            normed_grad(i)

        @pl.when(back_i == 0)
        def _():
            sum_out.run(1)
            sum_gate.run(1)

        @pl.when(back_i == 1)
        def _():
            norm_sums[2].start()
            sum_out.run(2)
            sum_gate.run(2)
            out_sum.forward()

        @pl.when(back_i == 2)
        def _():
            norm_sums[1].start()
            sum_out.run(3)
            sum_gate.run(3)
            norm_sums[2].forward()

        return carry

    lax.fori_loop(0, blocks, back, 0)
    halo_x.start()
    halo_s.start()
    norm_sums[0].start()
    sum_out.run(4)
    sum_gate.run(4)
    norm_sums[1].forward()
    halo_x.wait_recv()
    halo_s.wait_recv()
    use = jnp.where(y == 0, 1.0, 0.0)
    end = pl.ds(tokens - 16, 16)
    zeros = jnp.zeros((8, channels), f32)
    gx_s[end, :] = (
        gx_s[end, :].astype(f32) + jnp.concatenate([zeros, use * hx_in[...]], 0)
    ).astype(bf16)
    zeros = jnp.zeros((8, 256), f32)
    gs_s[end, :] = (
        gs_s[end, :].astype(f32) + jnp.concatenate([zeros, use * hs_in[...]], 0)
    ).astype(bf16)
    normed_grad(blocks - 1)
    norm_sums[3].start()
    for c in send_ish:
        c.start()
    weight_grad(gx_s, gi)
    sum_inner.run(0)
    norm_sums[0].forward()
    sum_out.run(5)
    sum_gate.run(5)

    def gz_body(i, carry):
        rows = pl.ds(pl.multiple_of(i * third, 128), third)
        value = mm_tn(normed[:, rows], gz_s[...]).astype(bf16)
        gz[i] = jnp.concatenate([value, value], 1).reshape(gz.shape[1:])
        return carry

    lax.fori_loop(0, t.cols, gz_body, 0)
    sum_step.run(0)
    sum_inner.run(1)

    def gs_body(i, carry):
        rows = pl.ds(pl.multiple_of(i * third, 128), third)
        gs[i] = mm_tn(normed[:, rows], gs_s[...]).astype(bf16).reshape(gs.shape[1:])
        return carry

    lax.fori_loop(0, t.cols, gs_body, 0)
    sum_states.run(0)
    sm[0:8, :] = accx[...]
    sm[8:16, :] = acc1[...]
    sm[16:24, 0:256] = accs[...]
    sm[10:12, 0:128] = acch[0:2, :]
    sm[16:24, 256:] = jnp.zeros((8, channels - 256), f32)
    sm[24:32, :] = gshare[:, 0:channels]
    sm[32:40, :] = gshare[:, channels:]
    sum_small.run(0)
    norm_sums[3].forward()
    sum_out.run(6)
    sum_gate.run(6)
    chain = [sum_inner, sum_step, sum_small, sum_states]
    at_stage = [2, 1, 1, 1]
    for _ in range(9):
        for n, item in enumerate(chain):
            if at_stage[n] <= len(item.stages):
                item.run(at_stage[n])
                at_stage[n] += 1

    out_sum.arrive()
    for c in send_ish:
        c.wait_recv()
    for n in norm_sums:
        n.arrive()

    def finish(i, carry):
        at = rows_of(i)
        own = tok[at, :].astype(f32)
        out_far[at, :] = (own + out_sum.total(at)).astype(bf16)
        both = ish[:, at]
        for off in range(1, t.cols):
            both = both + ish_in[off - 1, :, at]
        along = jnp.transpose(both)[:, 0:1] / width
        inverse = sig_s[at, 127:128]
        grad = inverse * (norm_sums[0].total(at) * ngain_cols[...] - own * (inverse * along))
        g_far[at, :] = (grad + cot_own[at, :].astype(f32)).astype(bf16)
        return carry

    lax.fori_loop(0, blocks, finish, 0)
    results = [load(out_far, mixed_o), load(g_far, gtok_o)]
    for c in results:
        c.wait()
    t.finish()


def rear(meta, hmeta, docrow, head, par, spar, hpre, hspre, acc1, ngain_cols, tok, w_states, dsout,
         weights, cots, normed, pre, spre, sd, ssd, x, wr, step, r, sig, sprev, gated, ggate, gy, dr, dsf):
    wi, wg, wo, ws = weights
    tokens, width = normed.shape
    channels = gated.shape[1]
    blocks = tokens // SPAN
    cols = lax.axis_size("col")
    groups = lax.axis_size("dp") // SHARE - 1
    third, own = width // cols, channels // 2
    q, qo, qs = third // SHARE, own // SHARE, width // (cols * 2 * SHARE)
    sds = jax.ShapeDtypeStruct
    V = pltpu.VMEM
    big = [tok, w_states, dsout, wi, wg, wo.reshape(2, 2, 2, qo, width), ws, cots, normed, pre, spre,
           sd, ssd, x, wr, step, r, sig, sprev, gated, ggate, gy, dr, dsf]
    scratch = [((tokens, third), bf16)] + [(b.shape, b.dtype) for b in big[1:]]

    def col_scratch(w):
        return [((cols, 2, 2, q, 2 * w), bf16), ((cols, 2, q, 2 * w), bf16), ((cols, 2, q, w), bf16),
                ((cols, q, w), bf16), ((cols, q, w), bf16)]

    scratch += [
        ((tokens, third), bf16), ((128, channels), f32),
        ((tokens, 256), bf16), ((tokens, 128), bf16),
        ((SPAN + 16, channels), f32), ((SPAN + 16, 256), f32), ((8, channels), f32), ((8, 256), f32),
        ((8, channels), f32), ((8, 256), f32), ((8, channels), f32), ((8, 256), f32), ((8, 128), f32),
        ((8, width), f32),
        ((tokens, width), bf16), ((2, tokens, third), bf16), ((tokens, third), bf16),
        ((2, tokens, third), bf16), ((tokens, third), bf16), ((8, tokens), f32),
        ((cols - 1, 8, tokens), f32),
    ]
    scratch += col_scratch(own) + col_scratch(own) + col_scratch(128)
    scratch += [
        ((2, 2, qo, width), bf16), ((2, qo, width), bf16), ((qo, width), bf16), ((qo, width), bf16),
        ((cols, 2, 2, 2, qs, 256), bf16), ((cols, 2, 2, qs, 256), bf16), ((cols, 2, qs, 256), bf16),
        ((cols, qs, 256), bf16), ((cols, qs, 256), bf16), ((cols - 1, qs, 256), bf16),
        ((40, channels), f32), ((3, 40, channels), f32), ((6 + groups, 40, channels), f32),
    ]
    if groups:
        far = [(groups, cols, q, own), (groups, cols, q, own), (groups, cols, q, 128),
               (groups, qo, width), (groups, cols, qs, 256)]
    else:
        far = [(16, 128)] * 5
    vmem = pl.BlockSpec(memory_space=V)
    hbm = pl.BlockSpec(memory_space=pl.ANY)
    small = [meta, hmeta, docrow, head, par, spar, hpre, hspre, acc1, ngain_cols]
    got = pl.pallas_call(
        rear_kernel,
        out_shape=[
            sds((tokens, third), bf16), sds((tokens, third), bf16),
            sds((2, 2, q, cols * own), bf16), sds((2, 2, q, cols * own), bf16),
            sds((2, 2, q, cols * 128), bf16), sds((cols, 2, 2, qo, third), bf16),
            sds((cols, 2, 2, 2, qs, 256), bf16), sds((40, channels), f32),
        ] + [sds(f, bf16) for f in far],
        in_specs=[vmem] * len(small) + [hbm] * len(big),
        out_specs=[hbm] * 7 + [vmem] + [hbm] * 5,
        scratch_shapes=[V(*s) for s in scratch] + [
            pltpu.SemaphoreType.DMA((100,)), pltpu.SemaphoreType.DMA((100,)),
            pltpu.SemaphoreType.DMA((48,)),
        ],
        compiler_params=pltpu.CompilerParams(
            collective_id=2, has_side_effects=True, vmem_limit_bytes=64 * 1024 * 1024
        ),
        name="rear",
    )(*small, *big)
    mixed, gtok, oi, og, oz, oo, os, sm = got[:8]
    return (
        mixed, gtok, oi.reshape(third, -1), og.reshape(third, -1), oz.reshape(third, -1),
        oo.reshape(cols * own, third), os.reshape(width, -1), sm,
    )


def per_device(
    tokens_in, segment_ids, norm_gain, proj_gate, proj_inner, proj_step, proj_states,
    conv_inner, conv_inner_bias, conv_states, conv_states_bias, step_bias, decay_log,
    skip_gain, gate_gain, proj_out, cotangent,
):
    tokens, width = tokens_in.shape
    blocks = tokens // SPAN
    row = lax.axis_index("row")
    col = lax.axis_index("col")
    cols = lax.axis_size("col")
    own_ch = conv_inner.shape[1]
    own_heads = step_bias.shape[0]
    channels = 2 * own_ch
    inner_all = channels * cols
    col_width = width // cols

    own = jnp.concatenate(
        [conv_inner, conv_inner_bias[None], gate_gain[None], jnp.zeros((2, own_ch), f32)], 0
    )

    def at_row(values):
        pad = [(0, 0)] * (values.ndim - 1)
        low = jnp.pad(values, pad + [(0, 128 - own_heads)])
        high = jnp.pad(values, pad + [(own_heads, 128 - 2 * own_heads)])
        return jnp.where(row == 0, low, high)

    pieces = at_row(proj_step.reshape(col_width, cols, own_heads)).reshape(col_width, cols * 128)
    rate = -jnp.exp(decay_log)
    head_own = jnp.pad(
        at_row(jnp.stack([step_bias, rate * LOG2E, skip_gain, rate])), ((0, 4), (0, 0))
    )
    spar = jnp.concatenate([conv_states, conv_states_bias[None], jnp.zeros((3, 256), f32)], 0)

    docs = jnp.pad(segment_ids[0].astype(f32), (8, 8), constant_values=-1.0)
    docs = lax.dynamic_slice_in_dim(docs, row * tokens, tokens + 16, 0)
    here = docs[8:8 + tokens]
    spans = here.reshape(blocks, SPAN)
    before = jnp.concatenate([docs[7:8], spans[:-1, -1]])
    after = spans[:, -1]

    def flat(cond):
        return jnp.broadcast_to(cond, (blocks, SPAN)).reshape(tokens)

    def forward_same(start, count):
        own_docs = docs[start:start + count]
        return [own_docs == docs[start + k:start + k + count] for k in range(1, 4)]

    meta = jnp.stack(
        [here]
        + [(here == docs[8 - k:8 - k + tokens]) for k in range(1, 4)]
        + [
            flat(spans == before[:, None]),
            flat(spans == after[:, None]),
            flat((before == after)[:, None]),
            jnp.zeros_like(here),
        ]
        + forward_same(8, tokens)
        + [jnp.zeros_like(here)] * 5,
        1,
    ).astype(f32)
    hmeta = jnp.stack(
        [jnp.zeros((8,), f32)] * 8
        + forward_same(0, 8)
        + [jnp.zeros((8,), f32)] * 5,
        1,
    ).astype(f32)
    docrow = here[None, :]

    sds = jax.ShapeDtypeStruct
    (
        w_inner, w_gate, w_out, w_step, cot_all, par, head,
        normed, pre, spre, sd, ssd, x_low, wr, step, r, sig, hpre, hspre, sprev,
        gated, g_gate, gy, dr, dsf, dsout, acc1,
    ) = front(
        inner_all, tokens_in, norm_gain[None], proj_states, meta, docrow, spar,
        proj_inner, proj_gate, proj_out, pieces, cotangent, own, head_own, tokens_in[-16:],
    )

    gain_cols = lax.dynamic_slice_in_dim(norm_gain, col * col_width, col_width, 0)
    mixed_out, grad_tokens, oi, og, oz, oo, os, few = rear(
        meta, hmeta, docrow, head, par, spar, hpre, hspre, acc1, gain_cols[None], tokens_in,
        proj_states, dsout, (w_inner, w_gate, w_out, w_step), cot_all, normed, pre, spre, sd, ssd,
        x_low, wr, step, r, sig, sprev, gated, g_gate, gy, dr, dsf,
    )
    grad_inner = oi.astype(f32)
    grad_gate = og.astype(f32)
    grad_out = oo.astype(f32)
    grad_states = os.astype(f32)
    oz = lax.dynamic_slice_in_dim(oz.reshape(col_width, cols, 128), row * own_heads, own_heads, 2)
    grad_step = oz.astype(f32).reshape(col_width, cols * own_heads)
    own_few = lax.dynamic_slice_in_dim(few, row * own_ch, own_ch, 1)

    def head_row(values):
        return lax.dynamic_slice_in_dim(values, row * own_heads, own_heads, 0)

    grad_conv_inner = own_few[0:4]
    grad_conv_inner_bias = own_few[4]
    grad_gate_gain = own_few[8]
    grad_skip = own_few[9].reshape(own_heads, HEAD).sum(-1)
    grad_step_bias = head_row(few[10, 0:128])
    grad_decay = head_row(few[11, 0:128]) * rate
    grad_norm_gain = few[24:40:8].reshape(-1)
    grad_norm_gain = lax.dynamic_slice_in_dim(
        grad_norm_gain, col * col_width, col_width, 0
    ) / gain_cols

    return (
        mixed_out,
        grad_tokens,
        grad_norm_gain,
        grad_gate,
        grad_inner,
        grad_step,
        grad_states,
        grad_conv_inner,
        grad_conv_inner_bias,
        few[16:20, 0:256],
        few[20, 0:256],
        grad_step_bias,
        grad_decay,
        grad_skip,
        grad_gate_gain,
        grad_out,
    )


def solution(mesh):
    in_specs = (
        P(("dp", "row"), None),
        P("dp", None),
        P(),
        P("col", "row"),
        P("col", "row"),
        P("col", "row"),
        P(),
        P(None, ("row", "col")),
        P(("row", "col")),
        P(),
        P(),
        P(("row", "col")),
        P(("row", "col")),
        P(("row", "col")),
        P(("row", "col")),
        P("row", "col"),
        P(("dp", "row"), "col"),
    )
    out_specs = (
        P(("dp", "row"), "col"),
        P(("dp", "row"), "col"),
        P("col"),
        P("col", "row"),
        P("col", "row"),
        P("col", "row"),
        P(),
        P(None, ("row", "col")),
        P(("row", "col")),
        P(),
        P(),
        P(("row", "col")),
        P(("row", "col")),
        P(("row", "col")),
        P(("row", "col")),
        P("row", "col"),
    )
    return jax.shard_map(
        per_device, mesh=mesh, in_specs=in_specs, out_specs=out_specs, check_vma=False
    )
```

```python
import functools

import jax
import jax.numpy as jnp
from jax import lax
from jax.experimental import pallas as pl
from jax.experimental.pallas import tpu as pltpu
from jax.sharding import PartitionSpec as P

SPAN = 256
HEAD = 64
epsilon = 1e-05
LOG2E = 1.4426950408889634
f32 = jnp.float32
bf16 = jnp.bfloat16
ANY = pl.ANY


def mm(a, b):
    return lax.dot_general(a, b, (((1,), (0,)), ((), ())), preferred_element_type=f32)


def mm_nt(a, b):
    return lax.dot_general(a, b, (((1,), (1,)), ((), ())), preferred_element_type=f32)


def split(v, terms):
    parts = []
    for _ in range(terms):
        part = v.astype(bf16)
        parts.append(part)
        v = v - part.astype(f32)
    return parts


def mm_split(a, exact, terms=2):
    return sum(mm(part, exact) for part in split(a, terms))


def split_mm(exact, b, terms=3):
    return sum(mm(exact, part) for part in split(b, terms))


def spread_matrix(channels):
    heads = lax.broadcasted_iota(jnp.int32, (128, channels), 0)
    cols = lax.broadcasted_iota(jnp.int32, (128, channels), 1)
    low = heads * HEAD
    return jnp.where((cols >= low) & (cols < low + HEAD), 1.0, 0.0).astype(bf16)


def gather_matrix(channels):
    heads = lax.broadcasted_iota(jnp.int32, (channels, 128), 1)
    rows = lax.broadcasted_iota(jnp.int32, (channels, 128), 0)
    low = heads * HEAD
    return jnp.where((rows >= low) & (rows < low + HEAD), 1.0, 0.0).astype(bf16)


def lower_ones():
    rows = lax.broadcasted_iota(jnp.int32, (SPAN, SPAN), 0)
    cols = lax.broadcasted_iota(jnp.int32, (SPAN, SPAN), 1)
    return jnp.where(rows >= cols, 1.0, 0.0).astype(bf16)


def upper_ones():
    rows = lax.broadcasted_iota(jnp.int32, (SPAN, SPAN), 0)
    cols = lax.broadcasted_iota(jnp.int32, (SPAN, SPAN), 1)
    return jnp.where(rows <= cols, 1.0, 0.0).astype(bf16)


def sigmoid(v):
    return 1.0 / (1.0 + jnp.exp(-v))


def half_masks():
    lane = lax.broadcasted_iota(jnp.int32, (SPAN, 128), 1)
    return lane < HEAD


def rms_rows(tok, gain):
    wide = tok.astype(f32)
    inverse = lax.rsqrt(jnp.mean(wide * wide, -1, keepdims=True) + epsilon)
    return (wide * inverse * gain).astype(bf16)


MESH = pl.DeviceIdType.MESH
SHARE = 4


def lane_block(index, width):
    return pl.ds(pl.multiple_of(index * width, 128), width)


class Links:
    def __init__(self, send, recv, local=None):
        self.send, self.recv, self.local = send, recv, local
        self.used, self.kept, self.sent = 0, 0, []
        dp = lax.axis_index("dp")
        self.groups = lax.axis_size("dp") // SHARE
        self.group = dp // SHARE
        self.x = lax.rem(dp, SHARE) // 2
        self.core = lax.rem(dp, 2)
        self.y = lax.axis_index("row")
        self.z = lax.axis_index("col")
        self.cols = lax.axis_size("col")

    def dp_of(self, group, x, core):
        return group * SHARE + x * 2 + core

    def mate(self):
        return {"dp": self.dp_of(self.group, self.x, 1 - self.core)}

    def across(self):
        return {"dp": self.dp_of(self.group, 1 - self.x, self.core)}

    def other_row(self):
        return {"row": 1 - self.y}

    def col_peer(self, off):
        return lax.rem(self.z + off, self.cols)

    def group_peer(self, off):
        return {"dp": self.dp_of(lax.rem(self.group + off, self.groups), self.x, self.core)}

    def meet(self, far_groups):
        barrier = pltpu.get_barrier_semaphore()
        peers = [self.mate(), self.across(), self.other_row()]
        peers += [{"col": self.col_peer(off)} for off in range(1, self.cols)]
        if far_groups:
            peers += [self.group_peer(off) for off in range(1, self.groups)]
        for peer in peers:
            pl.semaphore_signal(barrier, inc=1, device_id=peer, device_id_type=MESH)
        pl.semaphore_wait(barrier, len(peers))

    def make(self, src, dst, peer, when=None, track=True):
        at = self.used
        self.used += 1
        copy = pltpu.make_async_remote_copy(
            src_ref=src, dst_ref=dst, send_sem=self.send.at[at], recv_sem=self.recv.at[at],
            device_id=peer, device_id_type=MESH,
        )
        if track:
            self.sent.append((copy, when))
        return copy

    def go(self, src, dst, peer, track=True):
        copy = self.make(src, dst, peer, track=track)
        copy.start()
        return copy

    def keep(self, src, dst):
        copy = pltpu.make_async_copy(src, dst, self.local.at[self.kept])
        self.kept += 1
        return copy

    def finish(self):
        for copy, when in self.sent:
            if when is None:
                copy.wait_send()
            else:
                pl.when(when)(copy.wait_send)


class Steps:
    def __init__(self):
        self.stages = []

    def add(self, remote, local=(), before=None):
        self.stages.append((remote, list(local), before))

    def drain(self, t):
        for remote, _, _ in self.stages:
            for c in remote:
                c.wait_send()
                t.sent = [(copy, when) for copy, when in t.sent if copy is not c]

    def run(self, s):
        if 0 < s <= len(self.stages):
            remote, local, _ = self.stages[s - 1]
            for c in remote:
                c.wait_recv()
            for c in local:
                c.wait()
        if s < len(self.stages):
            remote, local, before = self.stages[s]
            if before is not None:
                before()
            for c in remote + local:
                c.start()


def spread_steps(t, view, steps):
    x, y = t.x, t.y
    first, second = view(x, y, 0), view(x, y, 1)
    steps.add([t.make(first, first, t.other_row()), t.make(second, second, t.across())])
    first, second = view(x, None, 0), view(None, y, 1)
    steps.add([t.make(first, first, t.across()), t.make(second, second, t.other_row())])
    every = view(None, None, None)
    steps.add([t.make(every, every, t.mate())])
    return steps


def half_lines(part, half):
    return slice(None) if half is None else pl.ds(half * (part // 2), part // 2)


def column_steps(t, src, dst, width):
    part = src.shape[0] // SHARE
    x, y, z, core = t.x, t.y, t.z, t.core
    rows = pl.ds(pl.multiple_of((x * 2 + core) * part, 16), part)
    lanes = lane_block(y, width)
    steps = Steps()
    here = dst.at[z, x, core, :, lanes]
    remote = []
    for off in range(1, t.cols):
        to = t.col_peer(off)
        remote.append(t.make(src.at[rows, lane_block(to, width)], here, {"col": to}))
    steps.add(remote, [t.keep(src.at[rows, lane_block(z, width)], here)])

    def view(at_x, at_y, half):
        return dst.at[:, slice(None) if at_x is None else at_x, core, half_lines(part, half),
                      slice(None) if at_y is None else lanes]

    return spread_steps(t, view, steps)


def row_steps(t, src, dst, width):
    part = src.shape[0] // t.cols // SHARE
    x, y, z, core = t.x, t.y, t.z, t.core

    def rows(to):
        return pl.ds(pl.multiple_of((to * SHARE + x * 2 + core) * part, 16), part)

    steps = Steps()
    here = dst.at[y, x, core, :, lane_block(z, width)]
    remote = []
    for off in range(1, t.cols):
        to = t.col_peer(off)
        remote.append(t.make(src.at[rows(to), :], here, {"col": to}))
    steps.add(remote, [t.keep(src.at[rows(z), :], here)])

    def view(at_x, at_y, half):
        return dst.at[slice(None) if at_y is None else at_y, slice(None) if at_x is None else at_x,
                      core, half_lines(part, half), :]

    return spread_steps(t, view, steps)


def gather_steps(t, own, whole, rows):
    width = own.shape[1]
    z = t.z
    mate, far = z + 1 - 2 * lax.rem(z, 2), lax.rem(z + 2, 4)
    here, there = whole.at[rows, lane_block(z, width)], whole.at[rows, lane_block(far, width)]
    steps = Steps()
    cross = t.make(own.at[rows, :], here, {"col": far})
    near = t.make(own.at[rows, :], here, {"col": mate})
    steps.add([cross, near], [t.keep(own.at[rows, :], here)])
    steps.add([t.make(there, there, {"col": mate})])
    return steps


def mm_tn(a, b):
    return lax.dot_general(a, b, (((0,), (0,)), ((), ())), preferred_element_type=f32)


def add_bf16(a, b):
    return (a.astype(f32) + b.astype(f32)).astype(bf16)


class PairSum:
    def __init__(self, t, part, near, far_in, rows):
        z = t.z
        mate = z + 1 - 2 * lax.rem(z, 2)
        far = lax.rem(z + 2, 4)
        mate_far = lax.rem(mate + 2, 4)
        width = near.shape[-1]
        self.part, self.near, self.far_in, self.rows = part, near, far_in, rows
        self.own, self.far = lane_block(z, width), lane_block(far, width)
        to_mate = [
            t.make(part.at[rows, lane_block(mate_far, width)], near.at[1, rows], {"col": mate}),
            t.make(part.at[rows, lane_block(mate, width)], near.at[0, rows], {"col": mate}),
        ]
        self.first, self.second = to_mate
        self.across = t.make(near.at[1, rows], far_in.at[rows], {"col": far})

    def start(self):
        self.first.start()

    def forward(self):
        self.first.wait_recv()
        count = self.rows.size // 64

        def body(i, c):
            at = pl.ds(pl.multiple_of(self.rows.start + i * 64, 16), 64)
            self.near[1, at] = add_bf16(self.near[1, at], self.part[at, self.far])
            return c

        lax.fori_loop(0, count, body, 0)
        self.across.start()
        self.second.start()

    def arrive(self):
        self.second.wait_recv()
        self.across.wait_recv()

    def total(self, at):
        return (
            self.part[at, self.own].astype(f32) + self.near[0, at].astype(f32)
            + self.far_in[at].astype(f32)
        )


def sum_far_groups(t, own, got):
    if t.groups == 1:
        return
    more = [t.go(own, got.at[off - 1], t.group_peer(off), False) for off in range(1, t.groups)]
    for c in more:
        c.wait()

    def total(spare):
        for off in range(1, t.groups):
            back = t.keep(got.at[off - 1], spare)
            back.start()
            back.wait()
            own[...] = add_bf16(own[...], spare[...])

    pl.run_scoped(total, pltpu.VMEM(own.shape, own.dtype))


def column_sums(t, g, a1, yx, xy, yx2, xy2, a4, far):
    x, y, core = t.x, t.y, t.core
    width = a4.shape[-1]
    h = a4.shape[1] // 2
    mine, other = lane_block(y, width), lane_block(1 - y, width)
    top, low = pl.ds(0, h), pl.ds(h, h)
    steps = Steps()
    steps.add([t.make(g.at[:, :, 1 - core], a1, t.mate())])

    def add_core():
        def body(i, c):
            for j in range(2):
                a1[i, j] = add_bf16(a1[i, j], g[i, j, core])
            return c

        lax.fori_loop(0, t.cols, body, 0)

    steps.add([
        t.make(a1.at[:, :, top, other], yx, t.other_row()),
        t.make(a1.at[:, 1 - x, low, :], xy, t.across()),
    ], (), add_core)

    def add_first():
        def body(i, c):
            for j in range(2):
                yx[i, j] = add_bf16(yx[i, j], a1[i, j, top, mine])
            xy[i] = add_bf16(xy[i], a1[i, x, low, :])
            return c

        lax.fori_loop(0, t.cols, body, 0)

    steps.add([
        t.make(yx.at[:, 1 - x], yx2, t.across()),
        t.make(xy.at[:, :, other], xy2, t.other_row()),
    ], (), add_first)

    def add_second():
        def body(i, c):
            a4[i, top] = add_bf16(yx2[i], yx[i, x])
            a4[i, low] = add_bf16(xy2[i], xy[i, :, mine])
            return c

        lax.fori_loop(0, t.cols, body, 0)
        sum_far_groups(t, a4, far)

    steps.add([], (), add_second)
    return steps


def column_sum_shapes(cols, q, w):
    h = q // 2
    return [((cols, 2, q, 2 * w), bf16), ((cols, 2, h, w), bf16), ((cols, h, 2 * w), bf16),
            ((cols, h, w), bf16), ((cols, h, w), bf16), ((cols, q, w), bf16)]


def column_home(t, a4, o, steps):
    x, z, core = t.x, t.z, t.core
    here = o.at[x, core, :, lane_block(z, a4.shape[-1])]
    steps.add(
        [t.make(a4.at[t.col_peer(off)], here, {"col": t.col_peer(off)}) for off in range(1, t.cols)],
        [t.keep(a4.at[z], here)],
    )
    steps.add([t.make(o.at[x, core], o.at[x, core], t.across())])
    steps.add([t.make(o.at[:, core], o.at[:, core], t.mate())])
    return steps


def row_sums(t, g, a1, yx, xy, yx2, xy2, a4, far):
    x, y, core = t.x, t.y, t.core
    h = a4.shape[0] // 2
    top, low = pl.ds(0, h), pl.ds(h, h)
    steps = Steps()
    steps.add([t.make(g.at[:, :, 1 - core], a1, t.mate())])

    def add_core():
        def body(i, c):
            for j in range(2):
                a1[i, j] = add_bf16(a1[i, j], g[i, j, core])
            return c

        lax.fori_loop(0, 2, body, 0)

    steps.add([
        t.make(a1.at[1 - y, :, top], yx, t.other_row()),
        t.make(a1.at[:, 1 - x, low], xy, t.across()),
    ], (), add_core)

    def add_first():
        for j in range(2):
            yx[j] = add_bf16(yx[j], a1[y, j, top])
            xy[j] = add_bf16(xy[j], a1[j, x, low])

    steps.add([
        t.make(yx.at[1 - x], yx2, t.across()), t.make(xy.at[1 - y], xy2, t.other_row()),
    ], (), add_first)

    def add_second():
        a4[top] = add_bf16(yx2[...], yx[x])
        a4[low] = add_bf16(xy2[...], xy[y])
        sum_far_groups(t, a4, far)

    steps.add([], (), add_second)
    return steps


def row_sum_shapes(q, width):
    h = q // 2
    return [((2, 2, q, width), bf16), ((2, h, width), bf16), ((2, h, width), bf16),
            ((h, width), bf16), ((h, width), bf16), ((q, width), bf16)]


def row_home(t, a4, o, steps):
    x, z, core = t.x, t.z, t.core
    width = o.shape[-1]
    here = o.at[z, x, core]
    steps.add(
        [t.make(a4.at[:, lane_block(t.col_peer(off), width)], here, {"col": t.col_peer(off)})
         for off in range(1, t.cols)],
        [t.keep(a4.at[:, lane_block(z, width)], here)],
    )
    steps.add([t.make(o.at[:, x, core], o.at[:, x, core], t.across())])
    steps.add([t.make(o.at[:, :, core], o.at[:, :, core], t.mate())])
    return steps


def full_sums(t, g, s1, s2, s3, s4, s5, far, o):
    x, y, z, core = t.x, t.y, t.z, t.core
    steps = Steps()
    steps.add([t.make(g.at[:, :, :, 1 - core], s1, t.mate())])

    def add_core():
        def body(i, c):
            for j in range(2):
                for k in range(2):
                    s1[i, j, k] = add_bf16(s1[i, j, k], g[i, j, k, core])
            return c

        lax.fori_loop(0, t.cols, body, 0)

    steps.add([t.make(s1.at[:, 1 - y], s2, t.other_row())], (), add_core)

    def add_row():
        def body(i, c):
            for k in range(2):
                s2[i, k] = add_bf16(s2[i, k], s1[i, y, k])
            return c

        lax.fori_loop(0, t.cols, body, 0)

    steps.add([t.make(s2.at[:, 1 - x], s3, t.across())], (), add_row)

    def add_x():
        def body(i, c):
            s4[i] = add_bf16(s3[i], s2[i, x])
            return c

        lax.fori_loop(0, t.cols, body, 0)
        sum_far_groups(t, s4, far)

    steps.add(
        [t.make(s4.at[t.col_peer(off)], s5.at[off - 1], {"col": t.col_peer(off)})
         for off in range(1, t.cols)], (), add_x,
    )

    def add_cols():
        total = s4[z].astype(f32)
        for off in range(1, t.cols):
            total = total + s5[off - 1].astype(f32)
        s4[z] = total.astype(bf16)

    here = o.at[z, y, x, core]
    steps.add(
        [t.make(s4.at[z], here, {"col": t.col_peer(off)}) for off in range(1, t.cols)],
        [t.keep(s4.at[z], here)], add_cols,
    )
    here = o.at[:, y, x, core]
    steps.add([t.make(here, here, t.other_row())])
    here = o.at[:, :, x, core]
    steps.add([t.make(here, here, t.across())])
    here = o.at[:, :, :, core]
    steps.add([t.make(here, here, t.mate())])
    return steps


def small_sums(t, sm, msum, mgot, out, rest):
    steps = Steps()
    steps.add([t.make(sm, mgot.at[0], t.mate())])

    def add_core():
        msum[0] = sm[...] + mgot[0]

    steps.add([t.make(msum.at[0], mgot.at[1], t.other_row())], (), add_core)

    def add_row():
        msum[1] = msum[0] + mgot[1]

    steps.add([t.make(msum.at[1], mgot.at[2], t.across())], (), add_row)

    def add_x():
        msum[2] = msum[1] + mgot[2]
        if t.groups > 1:
            more = [t.go(msum.at[2], mgot.at[5 + off], t.group_peer(off), False)
                    for off in range(1, t.groups)]
            for c in more:
                c.wait()
            total = msum[2]
            for off in range(1, t.groups):
                total = total + mgot[5 + off]
            msum[2] = total

    last = pl.ds(rest, sm.shape[0] - rest)
    steps.add(
        [t.make(msum.at[2, last], mgot.at[2 + off, last], {"col": t.col_peer(off)})
         for off in range(1, t.cols)], (), add_x,
    )

    def done():
        out[0:rest] = msum[2, 0:rest]
        out[rest:] = msum[2, rest:] + mgot[3, rest:] + mgot[4, rest:] + mgot[5, rest:]

    steps.add([], (), done)
    return steps


def front_kernel(
    inner_total,
    ngain_v, w_states, segments, taps_inner, bias_inner, gain_gate, taps_states, bias_states, step_all,
    step_bias, decay_log, skip_gain,
    tok_h, inner, gate, out, cot,
    mixed_o, wi_o, wg_o, ws_o, normed_o, sig_o, gx_o, gs_o, gz_o, accx_o, accs_o, acch_o, acc_o,
    gg4_o, go4_o, ggate_o, far_g, far_o,
    wi, wg, wo, ws2, ws, step_w, cots, par, spar, head, head_own, head_in, halo_in, tok, tok_own,
    meta, hmeta, docrow, docs,
    normed_s, pre_s, spre_s, sd_s, ssd_s, x_s, wr_s, step_s, r_s, sig_s, hpre_s, hspre_s, sprev_s,
    gated_s, ggate_s, gy_s, dr_s, fresh_s, y_s, gate_s, gg_s, gs_s, gz_s,
    out_near, out_far, sums_s, sums_in, xbuf, sbuf, mem, pass_out, state_in, dstate_in, pass_back,
    hx, hs, hx_in, hs_in, accx, accs, acch, acc_s, gg, g1, g2, g3, g5, g6, g4, o1, o2, o3, o5, o6, o4,
    send, recv, local,
):
    t = Links(send, recv, local)
    x, y, z, core = t.x, t.y, t.z, t.core
    blocks = tok.shape[0] // SPAN
    channels = x_s.shape[1]
    half = channels // 2
    outputs = []

    def write(src, dst):
        copy = t.keep(src, dst)
        copy.start()
        outputs.append(copy)

    def load(src, dst):
        copy = t.keep(src, dst)
        copy.start()
        return copy

    loads = [load(tok_h, tok), load(tok_h.at[:, lane_block(z, cot.shape[1])], tok_own)]
    own_lanes = lane_block(y, half)
    few = [
        t.make(par.at[:, own_lanes], par.at[:, own_lanes], t.other_row()),
        t.make(head_own, head_in, t.other_row()),
        t.make(tok_h.at[pl.ds(tok.shape[0] - 16, 16), :], halo_in, t.other_row()),
    ]
    block = inner.shape[1] // t.cols
    get_inner = column_steps(t, inner, wi, block)
    get_step = column_steps(t, step_w, ws2, step_w.shape[1] // t.cols)
    get_gate = column_steps(t, gate, wg, block)
    get_out = row_steps(t, out, wo, out.shape[1])
    half_rows = tok.shape[0] // 2
    get_cot = [gather_steps(t, cot, cots, pl.ds(n * half_rows, half_rows)) for n in range(2)]
    pass_state = t.make(pass_out, state_in, t.other_row())
    pass_back_state = t.make(pass_back, dstate_in, t.other_row())
    halo_x = t.make(hx, hx_in, t.other_row())
    halo_s = t.make(hs, hs_in, t.other_row())
    out_part = tok
    sum_gate = column_sums(t, gg, g1, g2, g3, g5, g6, g4, far_g)
    go = wo
    sum_out = row_sums(t, go, o1, o2, o3, o5, o6, o4, far_o)
    out_sums = [PairSum(t, out_part, out_near, out_far, pl.ds(b * SPAN, SPAN)) for b in range(blocks)]
    pass_sums = [
        t.make(sums_s, sums_in.at[off - 1], {"col": t.col_peer(off)}) for off in range(1, t.cols)
    ]
    t.meet(True)
    get_inner.run(0)

    own_heads = step_bias.shape[0]
    lane8 = lax.broadcasted_iota(jnp.int32, (8, 128), 1)
    row8 = lax.broadcasted_iota(jnp.int32, (8, 128), 0)
    scalars = jnp.zeros((8, 128), f32)
    for j in range(own_heads):
        here = lane8 == y * own_heads + j
        scalars = scalars + jnp.where(here & (row8 == 0), step_bias[j], 0.0)
        scalars = scalars + jnp.where(here & ((row8 == 1) | (row8 == 3)), decay_log[j], 0.0)
        scalars = scalars + jnp.where(here & (row8 == 2), skip_gain[j], 0.0)
    own_lane = (lane8 >= y * own_heads) & (lane8 < (y + 1) * own_heads)
    rate = jnp.where(own_lane, -jnp.exp(scalars), 0.0)
    head_own[...] = jnp.where(row8 == 1, rate * LOG2E, jnp.where(row8 == 3, rate, scalars))
    par[:, own_lanes] = jnp.zeros((8, half), f32)
    par[0:4, own_lanes] = taps_inner[...]
    par[4:5, own_lanes] = bias_inner[...].reshape(1, half)
    par[5:6, own_lanes] = gain_gate[...].reshape(1, half)
    spar[...] = jnp.zeros_like(spar)
    spar[0:4, :] = taps_states[...]
    spar[4:5, :] = bias_states[...].reshape(1, 256)
    every = step_all.shape[1]
    src = lax.broadcasted_iota(jnp.int32, (every, t.cols * 128), 0)
    dst = lax.broadcasted_iota(jnp.int32, (every, t.cols * 128), 1)
    place = jnp.zeros((every, t.cols * 128), f32)
    for c in range(t.cols):
        low = c * 128 + y * own_heads - c * own_heads
        mine = (src >= c * own_heads) & (src < (c + 1) * own_heads)
        place = place + jnp.where(mine & (dst - src == low), 1.0, 0.0)
    step_w[...] = mm(step_all[...], place.astype(bf16)).astype(bf16)
    get_step.run(0)
    for c in few:
        c.start()

    length = tok.shape[0]
    docs[:, 0:128] = jnp.full((8, 128), -1.0, f32)
    docs[:, 128:128 + 2 * length] = jnp.broadcast_to(segments[...].astype(f32), (8, 2 * length))
    docs[:, 128 + 2 * length:] = jnp.full((8, 128), -1.0, f32)
    window = docs[:, pl.ds(pl.multiple_of(y * length, 128), length + 256)]
    span_w = length + 256
    docrow[...] = window[:, 128:128 + length]
    same_before = [(window == pltpu.roll(window, k, 1)).astype(f32) for k in range(1, 4)]
    same_after = [(window == pltpu.roll(window, span_w - k, 1)).astype(f32) for k in range(1, 4)]
    row16 = lax.broadcasted_iota(jnp.int32, (8, SPAN), 0)
    for i in range(blocks):
        at = slice(128 + i * SPAN, 128 + (i + 1) * SPAN)
        here = window[:, at]
        before = window[0:1, 127 + i * SPAN:128 + i * SPAN]
        last = window[0:1, 127 + (i + 1) * SPAN:128 + (i + 1) * SPAN]
        low = jnp.where(row16 == 0, here, 0.0)
        for k in range(1, 4):
            low = low + jnp.where(row16 == k, same_before[k - 1][:, at], 0.0)
        low = low + jnp.where((row16 == 4) & (here == before), 1.0, 0.0)
        low = low + jnp.where((row16 == 5) & (here == last), 1.0, 0.0)
        low = low + jnp.where((row16 == 6) & (before == last), 1.0, 0.0)
        high = jnp.zeros((8, SPAN), f32)
        for k in range(1, 4):
            high = high + jnp.where(row16 == k - 1, same_after[k - 1][:, at], 0.0)
        rows128 = jnp.concatenate([low, high, jnp.zeros((112, SPAN), f32)], 0)
        meta[i * SPAN:(i + 1) * SPAN, :] = jnp.transpose(rows128)
    row16 = lax.broadcasted_iota(jnp.int32, (8, 128), 0)
    high = jnp.zeros((8, 128), f32)
    for k in range(1, 4):
        high = high + jnp.where(row16 == k - 1, same_after[k - 1][:, 0:128], 0.0)
    rows128 = jnp.concatenate([jnp.zeros((8, 128), f32), high, jnp.zeros((112, 128), f32)], 0)
    hmeta[...] = jnp.transpose(rows128)[120:128]

    gain = ngain_v[...].reshape(1, -1)
    for c in loads:
        c.wait()

    def rows_of(i):
        return pl.ds(pl.multiple_of(i * SPAN, SPAN), SPAN)

    def conv_silu(buf, lanes, here, taps, marks):
        v = taps[4:5, lanes] + taps[0:1, lanes] * here
        for k in range(1, 4):
            v = v + marks[:, k:k + 1] * (taps[k:k + 1, lanes] * buf[8 - k:8 - k + SPAN, lanes])
        sg = sigmoid(v)
        return v * sg, sg * (1.0 + v * (1.0 - sg))

    for c in few:
        c.wait_recv()
    hn = rms_rows(halo_in[...], gain)
    h_states = mm(hn, w_states[...])[8:16]
    sbuf[0:8, :] = h_states
    hspre_s[...] = h_states

    def norm_block(i, carry):
        at = rows_of(i)

        @pl.when(i > 0)
        def _():
            sbuf[0:8, :] = sbuf[SPAN:SPAN + 8, :]

        wide_tok = tok[at, :].astype(f32)
        inverse = lax.rsqrt(jnp.mean(wide_tok * wide_tok, -1, keepdims=True) + epsilon)
        normed = (wide_tok * inverse * gain).astype(bf16)
        normed_s[at, :] = normed
        s_pre = mm(normed, w_states[...])
        sbuf[8:SPAN + 8, :] = s_pre
        spre_s[at, :] = s_pre.astype(bf16)
        sact, sslope = conv_silu(sbuf, slice(0, 256), s_pre, spar, meta[at, :])
        wr_s[at, :] = sact.astype(bf16)
        ssd_s[at, :] = sslope.astype(bf16)
        sig_s[at, :] = jnp.broadcast_to(inverse, (SPAN, 128))
        pl.when(i == 0)(lambda: (get_inner.run(1), get_step.run(1), get_gate.run(0)) and None)
        return carry

    lax.fori_loop(0, blocks, norm_block, 0)
    head[...] = head_own[...] + head_in[...]
    get_inner.run(2)
    get_step.run(2)
    get_out.run(0)
    get_cot[0].run(0)
    get_inner.run(3)
    get_step.run(3)
    get_gate.run(1)
    get_inner.run(4)
    get_step.run(4)
    wide_in = normed_s.shape[1]
    ws[...] = (
        ws2[:, :, :, :, 0:128].reshape(wide_in, 128) + ws2[:, :, :, :, 128:256].reshape(wide_in, 128)
    )
    spread = spread_matrix(channels)

    def w_of(ref):
        return ref[...].reshape(-1, ref.shape[-1])

    h_inner = mm(hn, w_of(wi))[8:16]
    xbuf[0:8, :] = h_inner
    hpre_s[...] = h_inner
    mem[...] = jnp.zeros_like(mem)

    def entry(i, carry):
        at = rows_of(i)

        @pl.when(i > 0)
        def _():
            xbuf[0:8, :] = xbuf[SPAN:SPAN + 8, :]

        normed = normed_s[at, :]
        x_pre = mm(normed, w_of(wi))
        xbuf[8:SPAN + 8, :] = x_pre
        pre_s[at, :] = x_pre.astype(bf16)
        marks = meta[at, :]
        wr = wr_s[at, :]
        for pair in range(channels // 128):
            lanes = slice(pair * 128, pair * 128 + 128)
            act, slope = conv_silu(xbuf, lanes, xbuf[8:SPAN + 8, lanes], par, marks)
            x_s[at, lanes] = act.astype(bf16)
            sd_s[at, lanes] = slope.astype(bf16)
        x_low = x_s[at, :]

        raw = mm(normed, ws[...]) + head[0:1, :]
        step = jnp.maximum(raw, 0.0) + jnp.log1p(jnp.exp(-jnp.abs(raw)))
        lane = lax.broadcasted_iota(jnp.int32, (SPAN, 128), 1)
        sig_s[at, :] = jnp.where(lane == 127, sig_s[at, :], sigmoid(raw))
        step_s[at, :] = step
        r = split_mm(lower_ones(), step * head[1:2, :])
        r_s[at, :] = r
        last = r[SPAN - 1:SPAN, :]
        to_end = jnp.exp2(jnp.minimum(last - r, 0.0)) * marks[:, 5:6]
        coef = mm_split(to_end * step, spread)
        w_t = jnp.transpose(wr[:, 0:128].astype(f32)).astype(bf16)
        fresh = mm(w_t, (coef * x_low.astype(f32)).astype(bf16))
        fresh_s[i] = fresh
        mem[...] = keep_of(last, marks) * mem[...] + fresh

        @pl.when(i == 0)
        def _():
            get_gate.run(2)
            get_out.run(1)

        @pl.when(i == 2)
        def _():
            get_gate.run(3)
            get_out.run(2)
            get_cot[0].run(1)
            get_cot[1].run(0)

        return carry

    def keep_of(last, marks):
        return mm_split(jnp.broadcast_to(jnp.exp2(last) * marks[0:1, 6:7], (8, 128)), spread)[0:1]

    lax.fori_loop(0, blocks, entry, 0)
    pass_out[...] = mem[...].astype(bf16)
    pass_state.start()
    get_gate.run(4)
    for src, dst in (
        (normed_s, normed_o), (sig_s, sig_o), (wi, wi_o), (wg, wg_o), (ws, ws_o),
    ):
        write(src, dst)

    def gate_block(i, carry):
        at = rows_of(i)
        gate_s[at, :] = mm(normed_s[at, :], w_of(wg))
        return carry

    lax.fori_loop(0, blocks, gate_block, 0)

    pass_state.wait_recv()
    mem[...] = state_in[...].astype(f32) * jnp.where(y == 1, 1.0, 0.0)
    get_out.run(3)
    skip = mm_split(jnp.broadcast_to(head[2:3, :], (8, 128)), spread)[0:1]
    first = half_masks()

    def scan(i, carry):
        at = rows_of(i)
        marks = meta[at, :]
        w_low = wr_s[at, 0:128]
        r_low = wr_s[at, 128:256]
        r = r_s[at, :]
        r_t = jnp.transpose(r)
        rows = lax.broadcasted_iota(jnp.int32, (SPAN, SPAN), 0)
        cols = lax.broadcasted_iota(jnp.int32, (SPAN, SPAN), 1)
        allowed = (rows >= cols) & (marks[:, 0:1] == docrow[0:1, at])
        scores = jnp.where(allowed, mm_nt(r_low, w_low), 0.0)
        wide = x_s[at, :].astype(f32)
        xd = (mm_split(step_s[at, :], spread) * wide).astype(bf16)
        sprev = mem[...].astype(bf16)
        sprev_s[i] = sprev
        linked = jnp.exp2(r) * marks[:, 4:5]
        carried = mm(r_low, sprev) * mm_split(linked, spread)
        y_s[at, :] = carried + skip * wide
        for pair in range(channels // 128):
            lanes = slice(pair * 128, pair * 128 + 128)
            xp = xd[:, lanes]
            total = y_s[at, lanes]
            for part in range(2):
                h = 2 * pair + part
                decay = jnp.exp2(jnp.minimum(r[:, h:h + 1] - r_t[h:h + 1, :], 0.0))
                mixing = (scores * decay).astype(bf16)
                own = jnp.where(first if part == 0 else ~first, xp, jnp.zeros_like(xp))
                total = total + mm(mixing, own)
            y_s[at, lanes] = total
        last = r[SPAN - 1:SPAN, :]
        mem[...] = keep_of(last, marks) * mem[...] + fresh_s[i]

        @pl.when(i == 2)
        def _():
            get_cot[1].run(1)

        return carry

    lax.fori_loop(0, blocks, scan, 0)
    get_out.run(4)

    def project(i, carry):
        at = rows_of(i)
        g = gate_s[at, :]
        mixed = y_s[at, :] * (g * sigmoid(g))
        out_part[at, :] = mm((mixed * par[5:6, :]).astype(bf16), w_of(wo)).astype(bf16)
        return carry

    lax.fori_loop(0, blocks, project, 0)
    get_cot[0].run(2)
    ones = jnp.ones((8, channels), bf16)

    def totals_of(i, carry):
        at = rows_of(i)
        gg = mm_nt(cots[at, :], w_of(wo))
        gg_s[at, :] = gg.astype(bf16)
        g = gate_s[at, :]
        mixed = y_s[at, :] * (g * sigmoid(g))
        sq = sum(mm_nt(ones, part) for part in split(mixed * mixed, 2))
        pr = sum(mm_nt(ones, part) for part in split(mixed * (par[5:6, :] * gg), 2))
        row = lax.broadcasted_iota(jnp.int32, (8, SPAN), 0)
        sums_s[:, at] = jnp.where(row == 0, sq, jnp.where(row == 1, pr, 0.0))
        return carry

    lax.fori_loop(0, blocks // 2, totals_of, 0)
    get_cot[1].run(2)
    for s in out_sums:
        s.start()
    lax.fori_loop(blocks // 2, blocks, totals_of, 0)
    for c in pass_sums:
        c.start()
    out_sums[0].forward()
    for c in pass_sums:
        c.wait_recv()
    mem[...] = jnp.zeros_like(mem)
    acc_s[...] = jnp.zeros_like(acc_s)
    gather = gather_matrix(channels)

    def scale_of(at):
        both = sums_s[:, at]
        for off in range(1, t.cols):
            both = both + sums_in[off - 1, :, at]
        totals = jnp.transpose(both)
        return lax.rsqrt(totals[:, 0:1] / inner_total + epsilon), totals[:, 1:2] / inner_total

    def turn(back_i, carry):
        i = blocks - 1 - back_i
        at = rows_of(i)
        marks = meta[at, :]
        scale, cross = scale_of(at)
        yv = y_s[at, :]
        g = gate_s[at, :]
        sg = sigmoid(g)
        sl = g * sg
        gg = gg_s[at, :].astype(f32)
        ngate = par[5:6, :]
        normal = yv * sl * scale
        gated_s[at, :] = (normal * ngate).astype(bf16)
        g_mixed = scale * (ngate * gg - normal * (scale * cross))
        ggate_s[at, :] = (g_mixed * yv * (sg * (1.0 + g * (1.0 - sg)))).astype(bf16)
        gy = (g_mixed * sl).astype(bf16)
        gy_s[at, :] = gy
        gyw = gy.astype(f32)
        wide = x_s[at, :].astype(f32)
        dr_s[at, :] = mm_split(gyw * (yv - skip * wide), gather)
        row = lax.broadcasted_iota(jnp.int32, (8, channels), 0)
        ggain = jnp.sum(gg * normal, 0, keepdims=True)
        gskip = jnp.sum(gyw * wide, 0, keepdims=True)
        acc_s[...] += jnp.where(row == 0, ggain, jnp.where(row == 1, gskip, 0.0))
        r = r_s[at, :]
        linked = mm_split(jnp.exp2(r) * marks[:, 4:5], spread)
        r_t = jnp.transpose(wr_s[at, 128:256].astype(f32)).astype(bf16)
        dfresh = mm(r_t, (linked * gyw).astype(bf16))
        fresh_s[i] = dfresh
        mem[...] = keep_of(r[SPAN - 1:SPAN, :], marks) * mem[...] + dfresh

        @pl.when(back_i == 2)
        def _():
            out_sums[1].forward()

        return carry

    lax.fori_loop(0, blocks, turn, 0)
    pass_back[...] = mem[...].astype(bf16)
    pass_back_state.start()
    out_sums[2].forward()

    def grad_out(i, carry):
        rows = pl.ds(pl.multiple_of(i * half, 128), half)
        for n in range(2):
            lanes = slice(n * wide_in // 2, (n + 1) * wide_in // 2)
            value = mm_tn(gated_s[:, rows], cots[:, lanes]).astype(bf16)
            go[i, :, :, :, lanes] = value.reshape(go.shape[1:4] + (wide_in // 2,))
        return carry

    get_out.drain(t)
    lax.fori_loop(0, 2, grad_out, 0)
    sum_out.run(0)

    def grad_gate(i, carry):
        rows = pl.ds(pl.multiple_of(i * (wide_in // t.cols), 128), wide_in // t.cols)
        gg[i] = mm_tn(normed_s[:, rows], ggate_s[...]).astype(bf16).reshape(gg.shape[1:])
        return carry

    lax.fori_loop(0, t.cols, grad_gate, 0)
    sum_gate.run(0)
    sum_out.run(1)
    write(ggate_s, ggate_o)
    accx[...] = jnp.zeros_like(accx)
    accs[...] = jnp.zeros_like(accs)
    acch[...] = jnp.zeros_like(acch)
    xbuf[...] = jnp.zeros_like(xbuf)
    sbuf[...] = jnp.zeros_like(sbuf)
    pass_back_state.wait_recv()
    mem[...] = dstate_in[...].astype(f32) * jnp.where(y == 0, 1.0, 0.0)
    gx_s = gg_s

    def back(back_i, carry):
        i = blocks - 1 - back_i
        at = rows_of(i)

        @pl.when(back_i > 0)
        def _():
            xbuf[SPAN + 8:SPAN + 16, :] = xbuf[8:16, :]
            sbuf[SPAN + 8:SPAN + 16, :] = sbuf[8:16, :]

        marks = meta[at, :]
        w_low = wr_s[at, 0:128]
        r_low = wr_s[at, 128:256]
        r = r_s[at, :]
        r_t = jnp.transpose(r)
        step = step_s[at, :]
        last = r[SPAN - 1:SPAN, :]
        rows = lax.broadcasted_iota(jnp.int32, (SPAN, SPAN), 0)
        cols = lax.broadcasted_iota(jnp.int32, (SPAN, SPAN), 1)
        allowed = (rows <= cols) & (marks[:, 0:1] == docrow[0:1, at])
        scores = jnp.where(allowed, mm_nt(w_low, r_low), 0.0)
        ds = mem[...]
        ds_low = ds.astype(bf16)
        step_parts = split(step, 2)
        te_parts = split(jnp.exp2(jnp.minimum(last - r, 0.0)) * marks[:, 5:6], 2)
        linked_parts = split(jnp.exp2(r) * marks[:, 4:5], 2)
        keep = mm_split(jnp.broadcast_to(jnp.exp2(last) * marks[0:1, 6:7], (8, 128)), spread)[0:1]
        final = jnp.where(back_i == blocks - 1, 1.0, 0.0)

        def conv_back(buf, lanes, gv, base, taps, acc, halo_pre, out, halo_out):
            buf[8:SPAN + 8, lanes] = gv
            cols_here = gv.shape[1]
            total = taps[0:1, lanes] * gv
            sums = [jnp.sum(gv * base, 0, keepdims=True)]
            halo = jnp.zeros((8, cols_here), f32)
            hsum = []
            for k in range(1, 4):
                moved = marks[:, 7 + k:8 + k] * buf[8 + k:8 + k + SPAN, lanes]
                total = total + taps[k:k + 1, lanes] * moved
                sums.append(jnp.sum(moved * base, 0, keepdims=True))
                hmoved = hmeta[:, 7 + k:8 + k] * buf[k:8 + k, lanes]
                halo = halo + taps[k:k + 1, lanes] * hmoved
                hsum.append(jnp.sum(hmoved * halo_pre[:, lanes], 0, keepdims=True))
            sums.append(jnp.sum(gv, 0, keepdims=True))
            out[at, lanes] = total.astype(bf16)
            halo_out[:, lanes] = halo
            rows8 = lax.broadcasted_iota(jnp.int32, (8, cols_here), 0)
            add = jnp.zeros((8, cols_here), f32)
            for n, s in enumerate(sums):
                if 1 <= n <= 3:
                    s = s + final * hsum[n - 1]
                add = add + jnp.where(rows8 == n, s, 0.0)
            acc[:, lanes] += add

        zero = jnp.zeros((SPAN, 128), f32)
        dscores = jnp.zeros((SPAN, SPAN), f32)
        g_write, g_read, dr_cols, dstep = zero, zero, zero, zero
        at_end = jnp.zeros((8, 128), f32)
        for pair in range(channels // 128):
            lanes = slice(pair * 128, pair * 128 + 128)
            to_lanes, to_heads = spread[:, lanes], gather[lanes, :]

            def widen(parts):
                return sum(mm(p, to_lanes) for p in parts)

            wide = x_s[at, lanes].astype(f32)
            step_wide = widen(step_parts)
            xp = (step_wide * wide).astype(bf16)
            xdw = xp.astype(f32)
            gp = gy_s[at, lanes]
            gyw = gp.astype(f32)
            ds_pair = ds_low[:, lanes]
            sprev = sprev_s[i, :, lanes]
            te = widen(te_parts)
            total = te * mm(w_low, ds_pair)
            ending = jnp.sum(xdw * total, 0, keepdims=True) + keep[:, lanes] * jnp.sum(
                sprev.astype(f32) * ds[:, lanes], 0, keepdims=True
            )
            at_end = at_end + mm_split(jnp.broadcast_to(ending, (8, 128)), to_heads, 3)
            for half in range(2):
                h = 2 * pair + half
                own = first if half == 0 else ~first
                decay = jnp.exp2(jnp.minimum(r_t[h:h + 1, :] - r[:, h:h + 1], 0.0))
                mixing = (scores * decay).astype(bf16)
                gown = jnp.where(own, gp, jnp.zeros_like(gp))
                total = total + mm(mixing, gown)
                dscores = dscores + mm_nt(xp, gown) * decay
            g_write = g_write + mm_nt((te * xdw).astype(bf16), ds_pair)
            g_read = g_read + mm_nt((widen(linked_parts) * gyw).astype(bf16), sprev)
            dr_cols = dr_cols + mm_split(xdw * total, to_heads)
            dstep = dstep + mm_split(wide * total, to_heads)
            g_x = step_wide * total + skip[:, lanes] * gyw
            conv_back(xbuf, lanes, g_x * sd_s[at, lanes].astype(f32), pre_s[at, lanes].astype(f32), par,
                      accx, hpre_s, gg_s, hx)
        dscores = jnp.where(allowed, dscores, 0.0)
        g_write = g_write + mm(dscores.astype(bf16), r_low)
        g_read = g_read + mm(jnp.transpose(dscores).astype(bf16), w_low)
        both = slice(0, 256)
        g_wr = jnp.concatenate([g_write, g_read], 1)
        conv_back(sbuf, both, g_wr * ssd_s[at, :].astype(f32), spre_s[at, :].astype(f32), spar, accs,
                  hspre_s, gs_s, hs)
        tail_row = lax.broadcasted_iota(jnp.int32, (SPAN, 128), 0) == SPAN - 1
        dr = dr_s[at, :] - dr_cols + jnp.where(tail_row, at_end[0:1], 0.0)
        da = split_mm(upper_ones(), dr)
        dstep = dstep + head[3:4, :] * da
        gzv = dstep * sig_s[at, :]
        gz_s[at, :] = gzv.astype(bf16)
        row = lax.broadcasted_iota(jnp.int32, (8, 128), 0)
        gbias = jnp.sum(gzv, 0, keepdims=True)
        grate = jnp.sum(da * step, 0, keepdims=True)
        acch[...] += jnp.where(row == 0, gbias, jnp.where(row == 1, grate, 0.0))
        mem[...] = keep * ds + fresh_s[i]

        @pl.when(back_i == 0)
        def _():
            out_sums[3].forward()
            sum_gate.run(1)

        @pl.when(back_i == 1)
        def _():
            sum_out.run(2)

        @pl.when(back_i == 2)
        def _():
            sum_gate.run(2)

        return carry

    lax.fori_loop(0, blocks, back, 0)
    halo_x.start()
    halo_s.start()
    write(gz_s, gz_o)
    write(accx, accx_o)
    write(accs, accs_o)
    write(acch, acch_o)
    write(acc_s, acc_o)
    sum_out.run(3)
    sum_gate.run(3)
    write(o4, go4_o)
    write(g4, gg4_o)
    halo_x.wait_recv()
    halo_s.wait_recv()
    use = jnp.where(y == 0, 1.0, 0.0)
    end = pl.ds(tok.shape[0] - 16, 16)
    zeros = jnp.zeros((8, channels), f32)
    gx_s[end, :] = (
        gx_s[end, :].astype(f32) + jnp.concatenate([zeros, use * hx_in[...]], 0)
    ).astype(bf16)
    zeros = jnp.zeros((8, 256), f32)
    gs_s[end, :] = (
        gs_s[end, :].astype(f32) + jnp.concatenate([zeros, use * hs_in[...]], 0)
    ).astype(bf16)
    write(gx_s, gx_o)
    write(gs_s, gs_o)

    for s in out_sums:
        s.arrive()

    def finish(i, carry):
        at = rows_of(i)
        scale = scale_of(at)[0]
        out_far[at, :] = (
            tok_own[at, :].astype(f32) + scale * out_sums[0].total(at)
        ).astype(bf16)
        return carry

    lax.fori_loop(0, blocks, finish, 0)
    write(out_far, mixed_o)
    for copy in outputs:
        copy.wait()
    t.finish()


def front(inner_all, ngain, w_states, segments, taps_inner, bias_inner, gain_gate, taps_states,
          bias_states, step_all, step_bias, decay_log, skip_gain, tok, inner, gate, out, cot):
    tokens, width = tok.shape
    blocks = tokens // SPAN
    cols = lax.axis_size("col")
    groups = lax.axis_size("dp") // SHARE - 1
    part, half = inner.shape[0] // SHARE, inner.shape[1] // cols
    channels = 2 * half
    third = width // cols
    q, qo = third // SHARE, half // SHARE
    sds = jax.ShapeDtypeStruct
    V = pltpu.VMEM
    wide = ((cols, 2, 2, part, channels), bf16)
    by_channel = ((tokens, channels), bf16)
    by_state = ((tokens, 256), bf16)
    by_head = ((tokens, 128), f32)
    acc, sacc, hacc = ((8, channels), f32), ((8, 256), f32), ((8, 128), f32)
    passed = ((128, channels), bf16)
    far = [(groups, cols, q, half), (groups, qo, width)] if groups else [(16, 128)] * 2
    outs = [
        ((tokens, third), bf16), wide, wide, ((width, 128), bf16), ((tokens, width), bf16), by_head,
        by_channel, by_state, ((tokens, 128), bf16), acc, sacc, hacc, acc,
        ((cols, q, half), bf16), ((qo, width), bf16), by_channel,
    ] + [(shape, bf16) for shape in far]
    scratch = [
        wide, wide, ((2, 2, 2, half // SHARE, width), bf16), ((cols, 2, 2, part, 256), bf16),
        ((width, 128), bf16), ((part * SHARE, cols * 128), bf16), ((tokens, width), bf16), acc, sacc,
        hacc, hacc, hacc, ((16, width), bf16), ((tokens, width), bf16), ((tokens, third), bf16),
        by_head, hacc, ((8, tokens), f32), ((8, 2 * tokens + 256), f32),
        ((tokens, width), bf16), by_channel, by_state, by_channel, by_state, by_channel, by_state,
        by_head, by_head, by_head, acc, sacc, ((blocks, 128, channels), bf16),
        by_channel, by_channel, by_channel, by_head, ((blocks, 128, channels), f32),
        ((tokens, channels), f32), ((tokens, channels), f32), by_channel, by_state,
        ((tokens, 128), bf16),
        ((2, tokens, third), bf16), ((tokens, third), bf16), ((8, tokens), f32),
        ((cols - 1, 8, tokens), f32), ((SPAN + 16, channels), f32), ((SPAN + 16, 256), f32),
        ((128, channels), f32), passed, passed, passed, passed,
        acc, sacc, acc, sacc, acc, sacc, hacc, acc,
        ((cols, 2, 2, q, channels), bf16),
    ] + column_sum_shapes(cols, q, half) + row_sum_shapes(qo, width)
    vmem = pl.BlockSpec(memory_space=V)
    hbm = pl.BlockSpec(memory_space=pl.ANY)
    smem = pl.BlockSpec(memory_space=pltpu.SMEM)
    got = pl.pallas_call(
        functools.partial(front_kernel, float(inner_all)),
        out_shape=[sds(*o) for o in outs],
        in_specs=[vmem] * 9 + [smem] * 3 + [hbm] * 5,
        out_specs=[hbm] * len(outs),
        scratch_shapes=[V(*s) for s in scratch] + [
            pltpu.SemaphoreType.DMA((72,)), pltpu.SemaphoreType.DMA((72,)),
            pltpu.SemaphoreType.DMA((40,)),
        ],
        compiler_params=pltpu.CompilerParams(
            collective_id=1, has_side_effects=True, vmem_limit_bytes=63 * 1024 * 1024
        ),
        name="front",
    )(ngain, w_states, segments, taps_inner, bias_inner, gain_gate, taps_states, bias_states, step_all,
      step_bias, decay_log, skip_gain, tok, inner, gate, out, cot)
    got = list(got[:16])
    got[1] = got[1].reshape(width, channels)
    got[2] = got[2].reshape(width, channels)
    return got


def rear_kernel(
    accx, accs, acch, acc1, ngain_v,
    tok_h, w_states_h, wi_h, wg_h, ws_h, cot_h, normed_h, sig_h, ggate_h, gx_h, gs_h, gz_h, g4_h, o4_h,
    gtok_o, oi, og, oz, oo, os, sm_o, far_i, far_z, far_s,
    tok, wst, wi, wg, ws, cot_own, normed, sig_s, ggate, gx_s, gs_s, gz_s, g4, o4,
    ngain, part, gshare, g_near, g_far, ish, ish_in,
    gi, i1, i2, i3, i5, i6, i4, gz, z1, z2, z3, z5, z6, z4,
    gs, s1, s2, s3, s4, s5, sm, msum, mgot,
    send, recv, local,
):
    t = Links(send, recv, local)
    x, y, z, core = t.x, t.y, t.z, t.core
    tokens, width = normed.shape
    channels = ggate.shape[1]
    third = width // t.cols
    blocks = tokens // SPAN
    own_cols = lane_block(z, third)

    def load(src, dst):
        copy = t.keep(src, dst)
        copy.start()
        return copy

    first = [load(g4_h, g4), load(o4_h, o4)]
    loads = [load(a, b) for a, b in (
        (ggate_h, ggate), (wg_h, wg), (gx_h, gx_s), (wi_h, wi), (gz_h, gz_s), (ws_h, ws), (gs_h, gs_s),
        (w_states_h, wst), (normed_h, normed),
    )]
    later = [load(a, b) for a, b in (
        (cot_h, cot_own), (sig_h, sig_s), (tok_h.at[:, own_cols], tok),
    )]
    norm_sums = [PairSum(t, part, g_near, g_far, pl.ds(b * SPAN, SPAN)) for b in range(blocks)]
    home_out = row_home(t, o4, oo, Steps())
    home_gate = column_home(t, g4, og, Steps())
    sum_inner = column_home(t, i4, oi, column_sums(t, gi, i1, i2, i3, i5, i6, i4, far_i))
    sum_step = column_home(t, z4, oz, column_sums(t, gz, z1, z2, z3, z5, z6, z4, far_z))
    sum_states = full_sums(t, gs, s1, s2, s3, s4, s5, far_s, os)
    sum_small = small_sums(t, sm, msum, mgot, sm_o, 16)
    send_ish = [t.make(ish, ish_in.at[off - 1], {"col": t.col_peer(off)}) for off in range(1, t.cols)]
    t.meet(True)

    def rows_of(i):
        return pl.ds(pl.multiple_of(i * SPAN, SPAN), SPAN)

    for c in first:
        c.wait()
    home_out.run(0)
    home_gate.run(0)
    gshare[...] = jnp.zeros_like(gshare)
    ngain[...] = jnp.broadcast_to(ngain_v[...].reshape(1, width), (8, width))
    for c in loads:
        c.wait()

    def normed_grad(i, carry):
        at = rows_of(i)

        def body(c, column):
            lanes = pl.ds(pl.multiple_of(c * third, 128), third)
            total = (
                mm_nt(ggate[at, :], wg[lanes, :]) + mm_nt(gx_s[at, :], wi[lanes, :])
                + mm_nt(gz_s[at, :], ws[lanes, :]) + mm_nt(gs_s[at, :], wst[lanes, :])
            )
            part[at, lanes] = total.astype(bf16)
            weighed = total * normed[at, lanes].astype(f32)
            gshare[0:1, lanes] += jnp.sum(weighed, 0, keepdims=True)
            return column + jnp.sum(weighed, -1, keepdims=True)

        column = lax.fori_loop(0, t.cols, body, jnp.zeros((SPAN, 1), f32))
        ish[:, at] = jnp.transpose(jnp.broadcast_to(column, (SPAN, 128)))[0:8]
        for b in range(blocks):
            pl.when(i == b)(norm_sums[b].start)
        return carry

    def weight_grad(right, target):
        def body(i, carry):
            rows = pl.ds(pl.multiple_of(i * third, 128), third)
            target[i] = mm_tn(normed[:, rows], right[...]).astype(bf16).reshape(target.shape[1:])
            return carry

        lax.fori_loop(0, t.cols, body, 0)

    def gz_body(i, carry):
        rows = pl.ds(pl.multiple_of(i * third, 128), third)
        value = mm_tn(normed[:, rows], gz_s[...]).astype(bf16)
        gz[i] = jnp.concatenate([value, value], 1).reshape(gz.shape[1:])
        return carry

    def gs_body(i, carry):
        rows = pl.ds(pl.multiple_of(i * third, 128), third)
        gs[i] = mm_tn(normed[:, rows], gs_s[...]).astype(bf16).reshape(gs.shape[1:])
        return carry

    lax.fori_loop(0, 1, normed_grad, 0)
    weight_grad(gx_s, gi)
    sum_inner.run(0)
    lax.fori_loop(1, blocks, normed_grad, 0)
    sum_inner.run(1)
    lax.fori_loop(0, t.cols, gs_body, 0)
    sum_states.run(0)
    lax.fori_loop(0, t.cols, gz_body, 0)
    sum_step.run(0)
    sm[0:8, :] = accx[...]
    sm[8:16, :] = acc1[...]
    sm[10:12, 0:128] = acch[0:2, :]
    sm[16:24, 0:256] = accs[...]
    sm[16:24, 256:] = jnp.zeros((8, channels - 256), f32)
    sm[24:32, :] = gshare[:, 0:channels]
    sm[32:40, :] = gshare[:, channels:]
    sum_small.run(0)
    for c in send_ish:
        c.start()
    norm_sums[0].forward()
    home_out.run(1)
    home_gate.run(1)
    norm_sums[1].forward()
    sum_states.run(1)
    sum_step.run(1)
    sum_small.run(1)
    norm_sums[2].forward()
    sum_inner.run(2)
    norm_sums[3].forward()
    sum_states.run(2)
    sum_step.run(2)
    sum_small.run(2)
    sum_inner.run(3)
    sum_inner.run(4)
    sum_states.run(3)
    sum_step.run(3)
    sum_step.run(4)
    sum_small.run(3)
    home_out.run(2)
    home_gate.run(2)
    sum_states.run(4)
    sum_small.run(4)
    sum_step.run(5)
    sum_inner.run(5)
    sum_states.run(5)
    sum_step.run(6)
    sum_states.run(6)
    sum_inner.run(6)
    sum_states.run(7)
    for c in later:
        c.wait()

    for c in send_ish:
        c.wait_recv()
    for n in norm_sums:
        n.arrive()

    def finish(i, carry):
        at = rows_of(i)
        own = tok[at, :].astype(f32)
        both = ish[:, at]
        for off in range(1, t.cols):
            both = both + ish_in[off - 1, :, at]
        along = jnp.transpose(both)[:, 0:1] / width
        inverse = sig_s[at, 127:128]
        grad = inverse * (norm_sums[0].total(at) * ngain[0:1, own_cols] - own * (inverse * along))
        g_far[at, :] = (grad + cot_own[at, :].astype(f32)).astype(bf16)
        return carry

    lax.fori_loop(0, blocks, finish, 0)
    last = load(g_far, gtok_o)
    home_out.run(3)
    home_gate.run(3)
    sum_step.run(7)
    sum_inner.run(7)
    sum_states.run(8)
    sum_small.run(5)
    last.wait()
    t.finish()


def rear(accx, accs, acch, acc1, ngain, tok, w_states, wi, wg, ws, cot, normed, sig, ggate, gx, gs, gz,
         g4, o4):
    tokens, width = normed.shape
    channels = ggate.shape[1]
    cols = lax.axis_size("col")
    groups = lax.axis_size("dp") // SHARE - 1
    third, own = width // cols, channels // 2
    q, qo, qs = third // SHARE, own // SHARE, width // (cols * 2 * SHARE)
    sds = jax.ShapeDtypeStruct
    V = pltpu.VMEM
    small = [accx, accs, acch, acc1, ngain]
    big = [tok, w_states, wi, wg, ws, cot, normed, sig, ggate, gx, gs, gz, g4, o4]
    scratch = [((tokens, third), bf16)] + [(b.shape, b.dtype) for b in big[1:]]

    scratch += [
        ((8, width), f32), ((tokens, width), bf16), ((8, width), f32),
        ((2, tokens, third), bf16), ((tokens, third), bf16), ((8, tokens), f32),
        ((cols - 1, 8, tokens), f32),
    ]
    scratch += [((cols, 2, 2, q, 2 * own), bf16)] + column_sum_shapes(cols, q, own)
    scratch += [((cols, 2, 2, q, 256), bf16)] + column_sum_shapes(cols, q, 128)
    scratch += [
        ((cols, 2, 2, 2, qs, 256), bf16), ((cols, 2, 2, qs, 256), bf16), ((cols, 2, qs, 256), bf16),
        ((cols, qs, 256), bf16), ((cols, qs, 256), bf16), ((cols - 1, qs, 256), bf16),
        ((40, channels), f32), ((3, 40, channels), f32), ((6 + groups, 40, channels), f32),
    ]
    if groups:
        far = [(groups, cols, q, own), (groups, cols, q, 128), (groups, cols, qs, 256)]
    else:
        far = [(16, 128)] * 3
    vmem = pl.BlockSpec(memory_space=V)
    hbm = pl.BlockSpec(memory_space=pl.ANY)
    got = pl.pallas_call(
        rear_kernel,
        out_shape=[
            sds((tokens, third), bf16),
            sds((2, 2, q, cols * own), bf16), sds((2, 2, q, cols * own), bf16),
            sds((2, 2, q, cols * 128), bf16), sds((cols, 2, 2, qo, third), bf16),
            sds((cols, 2, 2, 2, qs, 256), bf16), sds((40, channels), f32),
        ] + [sds(f, bf16) for f in far],
        in_specs=[vmem] * len(small) + [hbm] * len(big),
        out_specs=[hbm] * 6 + [vmem] + [hbm] * 3,
        scratch_shapes=[V(*s) for s in scratch] + [
            pltpu.SemaphoreType.DMA((100,)), pltpu.SemaphoreType.DMA((100,)),
            pltpu.SemaphoreType.DMA((48,)),
        ],
        compiler_params=pltpu.CompilerParams(
            collective_id=2, has_side_effects=True, vmem_limit_bytes=62 * 1024 * 1024
        ),
        name="rear",
    )(*small, *big)
    gtok, oi, og, oz, oo, os, sm = got[:7]
    return (
        gtok, oi.reshape(third, -1), og.reshape(third, -1), oz.reshape(third, -1),
        oo.reshape(cols * own, third), os.reshape(width, -1), sm,
    )


def unpack_kernel(
    oi, og, oz, oo, os, sm, ngain, decay_log,
    inner_o, gate_o, step_o, out_o, states_o, taps_o, bias_o, staps_o, sbias_o, step_bias_o, decay_o,
    skip_o, gain_o, norm_o,
    wide,
):
    y, z = lax.axis_index("row"), lax.axis_index("col")
    inner_o[...] = oi[...].astype(f32)
    gate_o[...] = og[...].astype(f32)
    out_o[...] = oo[...].astype(f32)
    states_o[...] = os[...].astype(f32)
    heads = decay_log.shape[0]
    lanes, steps = oz.shape[1], step_o.shape[1]
    src = lax.broadcasted_iota(jnp.int32, (lanes, steps), 0)
    dst = lax.broadcasted_iota(jnp.int32, (lanes, steps), 1)
    pick = jnp.zeros((lanes, steps), f32)
    for c in range(steps // heads):
        mine = (dst >= c * heads) & (dst < (c + 1) * heads)
        pick = pick + jnp.where(mine & (src - dst == c * 128 + y * heads - c * heads), 1.0, 0.0)
    step_o[...] = mm(oz[...], pick.astype(bf16))

    @pl.when(pl.program_id(0) == 0)
    def _():
        own_ch, third = taps_o.shape[1], norm_o.shape[0]
        own = lane_block(y, own_ch)
        taps_o[...] = sm[0:4, own]
        bias_o[...] = sm[4:5, own].reshape(own_ch)
        gain_o[...] = sm[8:9, own].reshape(own_ch)
        staps_o[...] = sm[16:20, 0:256]
        sbias_o[...] = sm[20:21, 0:256].reshape(256)
        skip = mm_split(sm[8:16, own], gather_matrix(own_ch), 3)
        skip_o[...] = skip[1:2, 0:heads].reshape(heads)

        def own_head(row):
            both = sm[row:row + 1, 0:128]
            return jnp.where(y == 0, both[:, 0:heads], both[:, heads:2 * heads])

        step_bias_o[...] = own_head(10).reshape(heads)
        rate = -jnp.exp(decay_log[...].reshape(1, heads))
        decay_o[...] = (own_head(11) * rate).reshape(heads)
        half = sm.shape[1]
        wide[0:8, 0:half] = sm[24:32, :]
        wide[0:8, half:] = sm[32:40, :]
        wide[8:16, :] = jnp.broadcast_to(ngain[...].reshape(1, 2 * half), (8, 2 * half))
        cols = lane_block(z, third)
        norm_o[...] = (wide[0:1, cols] / wide[8:9, cols]).reshape(third)


def unpack(oi, og, oz, oo, os, sm, ngain, decay_log, own_ch):
    sds = jax.ShapeDtypeStruct
    heads, parts = decay_log.shape[0], 4
    third, block = oi.shape

    def rows(shape):
        return pl.BlockSpec((shape[0] // parts, shape[1]), lambda i: (i, 0))

    def whole(shape):
        return pl.BlockSpec(shape, lambda i: (0,) * len(shape))

    steps = (third, block // own_ch * heads)
    small = [(4, own_ch), (own_ch,), (4, 256), (256,), (heads,), (heads,), (heads,), (own_ch,),
             (third,)]
    big = [oi.shape, og.shape, steps, oo.shape, os.shape]
    ins = [rows(v.shape) for v in (oi, og, oz, oo, os)]
    return pl.pallas_call(
        unpack_kernel,
        grid=(parts,),
        out_shape=[sds(s, f32) for s in big + small],
        in_specs=ins + [whole(sm.shape), whole(ngain.shape), whole(decay_log.shape)],
        out_specs=[rows(s) for s in big] + [whole(s) for s in small],
        scratch_shapes=[pltpu.VMEM((16, 2 * sm.shape[1]), f32)],
        compiler_params=pltpu.CompilerParams(vmem_limit_bytes=62 * 1024 * 1024),
        name="unpack",
    )(oi, og, oz, oo, os, sm, ngain, decay_log)


def per_device(
    tokens_in, segment_ids, norm_gain, proj_gate, proj_inner, proj_step, proj_states,
    conv_inner, conv_inner_bias, conv_states, conv_states_bias, step_bias, decay_log,
    skip_gain, gate_gain, proj_out, cotangent,
):
    inner_all = proj_gate.shape[1] * lax.axis_size("row")
    (
        mixed_out, w_inner, w_gate, w_step, normed, sig, gx, gs, gz, accx, accs, acch, acc1, g4, o4,
        g_gate,
    ) = front(
        inner_all, norm_gain, proj_states, segment_ids, conv_inner, conv_inner_bias, gate_gain,
        conv_states, conv_states_bias, proj_step, step_bias, decay_log, skip_gain,
        tokens_in, proj_inner, proj_gate, proj_out, cotangent,
    )
    grad_tokens, oi, og, oz, oo, os, sums = rear(
        accx, accs, acch, acc1, norm_gain, tokens_in, proj_states, w_inner, w_gate, w_step, cotangent,
        normed, sig, g_gate, gx, gs, gz, g4, o4,
    )
    (
        grad_inner, grad_gate, grad_step, grad_out, grad_states, grad_conv_inner,
        grad_conv_inner_bias, grad_conv_states, grad_conv_states_bias, grad_step_bias, grad_decay,
        grad_skip, grad_gate_gain, grad_norm_gain,
    ) = unpack(oi, og, oz, oo, os, sums, norm_gain, decay_log, conv_inner.shape[1])
    return (
        mixed_out, grad_tokens, grad_norm_gain, grad_gate, grad_inner, grad_step, grad_states,
        grad_conv_inner, grad_conv_inner_bias, grad_conv_states, grad_conv_states_bias,
        grad_step_bias, grad_decay, grad_skip, grad_gate_gain, grad_out,
    )


def solution(mesh):
    in_specs = (
        P(("dp", "row"), None),
        P("dp", None),
        P(),
        P("col", "row"),
        P("col", "row"),
        P("col", "row"),
        P(),
        P(None, ("row", "col")),
        P(("row", "col")),
        P(),
        P(),
        P(("row", "col")),
        P(("row", "col")),
        P(("row", "col")),
        P(("row", "col")),
        P("row", "col"),
        P(("dp", "row"), "col"),
    )
    out_specs = (
        P(("dp", "row"), "col"),
        P(("dp", "row"), "col"),
        P("col"),
        P("col", "row"),
        P("col", "row"),
        P("col", "row"),
        P(),
        P(None, ("row", "col")),
        P(("row", "col")),
        P(),
        P(),
        P(("row", "col")),
        P(("row", "col")),
        P(("row", "col")),
        P(("row", "col")),
        P("row", "col"),
    )
    return jax.shard_map(
        per_device, mesh=mesh, in_specs=in_specs, out_specs=out_specs, check_vma=False
    )
```

```python
import functools

import jax
import jax.numpy as jnp
from jax import lax
from jax.experimental import pallas as pl
from jax.experimental.pallas import tpu as pltpu
from jax.sharding import PartitionSpec as P

SPAN = 256
HEAD = 64
epsilon = 1e-05
LOG2E = 1.4426950408889634
f32 = jnp.float32
bf16 = jnp.bfloat16
ANY = pl.ANY


def mm(a, b):
    return lax.dot_general(a, b, (((1,), (0,)), ((), ())), preferred_element_type=f32)


def mm_nt(a, b):
    return lax.dot_general(a, b, (((1,), (1,)), ((), ())), preferred_element_type=f32)


def split(v, terms):
    parts = []
    for _ in range(terms):
        part = v.astype(bf16)
        parts.append(part)
        v = v - part.astype(f32)
    return parts


def mm_split(a, exact, terms=2):
    return sum(mm(part, exact) for part in split(a, terms))


def split_mm(exact, b, terms=3):
    return sum(mm(exact, part) for part in split(b, terms))


def spread_matrix(channels):
    heads = lax.broadcasted_iota(jnp.int32, (128, channels), 0)
    cols = lax.broadcasted_iota(jnp.int32, (128, channels), 1)
    low = heads * HEAD
    return jnp.where((cols >= low) & (cols < low + HEAD), 1.0, 0.0).astype(bf16)


def gather_matrix(channels):
    heads = lax.broadcasted_iota(jnp.int32, (channels, 128), 1)
    rows = lax.broadcasted_iota(jnp.int32, (channels, 128), 0)
    low = heads * HEAD
    return jnp.where((rows >= low) & (rows < low + HEAD), 1.0, 0.0).astype(bf16)


def lower_ones():
    rows = lax.broadcasted_iota(jnp.int32, (SPAN, SPAN), 0)
    cols = lax.broadcasted_iota(jnp.int32, (SPAN, SPAN), 1)
    return jnp.where(rows >= cols, 1.0, 0.0).astype(bf16)


def upper_ones():
    rows = lax.broadcasted_iota(jnp.int32, (SPAN, SPAN), 0)
    cols = lax.broadcasted_iota(jnp.int32, (SPAN, SPAN), 1)
    return jnp.where(rows <= cols, 1.0, 0.0).astype(bf16)


def sigmoid(v):
    return 1.0 / (1.0 + jnp.exp(-v))


def widen(first, values, pair):
    return jnp.where(first, values[:, 2 * pair:2 * pair + 1], values[:, 2 * pair + 1:2 * pair + 2])


def head_totals(values, to_heads):
    high = values.astype(bf16)
    low = (values - high.astype(f32)).astype(bf16)
    return mm(jnp.concatenate([high, low], 1), jnp.concatenate([to_heads, to_heads], 0))


def half_masks():
    lane = lax.broadcasted_iota(jnp.int32, (SPAN, 128), 1)
    return lane < HEAD


def rms_rows(tok, gain):
    wide = tok.astype(f32)
    inverse = lax.rsqrt(jnp.mean(wide * wide, -1, keepdims=True) + epsilon)
    return (wide * inverse * gain).astype(bf16)


MESH = pl.DeviceIdType.MESH
SHARE = 4


def lane_block(index, width):
    return pl.ds(pl.multiple_of(index * width, 128), width)


class Links:
    def __init__(self, send, recv, local=None):
        self.send, self.recv, self.local = send, recv, local
        self.used, self.kept, self.sent = 0, 0, []
        dp = lax.axis_index("dp")
        self.groups = lax.axis_size("dp") // SHARE
        self.group = dp // SHARE
        self.x = lax.rem(dp, SHARE) // 2
        self.core = lax.rem(dp, 2)
        self.y = lax.axis_index("row")
        self.z = lax.axis_index("col")
        self.cols = lax.axis_size("col")

    def dp_of(self, group, x, core):
        return group * SHARE + x * 2 + core

    def mate(self):
        return {"dp": self.dp_of(self.group, self.x, 1 - self.core)}

    def across(self):
        return {"dp": self.dp_of(self.group, 1 - self.x, self.core)}

    def other_row(self):
        return {"row": 1 - self.y}

    def col_peer(self, off):
        return lax.rem(self.z + off, self.cols)

    def group_peer(self, off):
        return {"dp": self.dp_of(lax.rem(self.group + off, self.groups), self.x, self.core)}

    def meet(self, far_groups):
        barrier = pltpu.get_barrier_semaphore()
        peers = [self.mate(), self.across(), self.other_row()]
        peers += [{"col": self.col_peer(off)} for off in range(1, self.cols)]
        if far_groups:
            peers += [self.group_peer(off) for off in range(1, self.groups)]
        for peer in peers:
            pl.semaphore_signal(barrier, inc=1, device_id=peer, device_id_type=MESH)
        pl.semaphore_wait(barrier, len(peers))

    def make(self, src, dst, peer, when=None, track=True):
        at = self.used
        self.used += 1
        copy = pltpu.make_async_remote_copy(
            src_ref=src, dst_ref=dst, send_sem=self.send.at[at], recv_sem=self.recv.at[at],
            device_id=peer, device_id_type=MESH,
        )
        if track:
            self.sent.append((copy, when))
        return copy

    def go(self, src, dst, peer, track=True):
        copy = self.make(src, dst, peer, track=track)
        copy.start()
        return copy

    def keep(self, src, dst):
        copy = pltpu.make_async_copy(src, dst, self.local.at[self.kept])
        self.kept += 1
        return copy

    def finish(self):
        for copy, when in self.sent:
            if when is None:
                copy.wait_send()
            else:
                pl.when(when)(copy.wait_send)


class Steps:
    def __init__(self):
        self.stages = []

    def add(self, remote, local=(), before=None):
        self.stages.append((remote, list(local), before))

    def drain(self, t):
        for remote, _, _ in self.stages:
            for c in remote:
                c.wait_send()
                t.sent = [(copy, when) for copy, when in t.sent if copy is not c]

    def run(self, s):
        if 0 < s <= len(self.stages):
            remote, local, _ = self.stages[s - 1]
            for c in remote:
                c.wait_recv()
            for c in local:
                c.wait()
        if s < len(self.stages):
            remote, local, before = self.stages[s]
            if before is not None:
                before()
            for c in remote + local:
                c.start()


def spread_steps(t, view, steps):
    x, y = t.x, t.y
    first, second = view(x, y, 0), view(x, y, 1)
    steps.add([t.make(first, first, t.other_row()), t.make(second, second, t.across())])
    first, second = view(x, None, 0), view(None, y, 1)
    steps.add([t.make(first, first, t.across()), t.make(second, second, t.other_row())])
    every = view(None, None, None)
    steps.add([t.make(every, every, t.mate())])
    return steps


def half_lines(part, half):
    return slice(None) if half is None else pl.ds(half * (part // 2), part // 2)


def column_steps(t, src, dst, width):
    part = src.shape[0] // SHARE
    x, y, z, core = t.x, t.y, t.z, t.core
    rows = pl.ds(pl.multiple_of((x * 2 + core) * part, 16), part)
    lanes = lane_block(y, width)
    steps = Steps()
    here = dst.at[z, x, core, :, lanes]
    remote = []
    for off in range(1, t.cols):
        to = t.col_peer(off)
        remote.append(t.make(src.at[rows, lane_block(to, width)], here, {"col": to}))
    steps.add(remote, [t.keep(src.at[rows, lane_block(z, width)], here)])

    def view(at_x, at_y, half):
        return dst.at[:, slice(None) if at_x is None else at_x, core, half_lines(part, half),
                      slice(None) if at_y is None else lanes]

    return spread_steps(t, view, steps)


def row_steps(t, src, dst, width):
    part = src.shape[0] // t.cols // SHARE
    x, y, z, core = t.x, t.y, t.z, t.core

    def rows(to):
        return pl.ds(pl.multiple_of((to * SHARE + x * 2 + core) * part, 16), part)

    steps = Steps()
    here = dst.at[y, x, core, :, lane_block(z, width)]
    remote = []
    for off in range(1, t.cols):
        to = t.col_peer(off)
        remote.append(t.make(src.at[rows(to), :], here, {"col": to}))
    steps.add(remote, [t.keep(src.at[rows(z), :], here)])

    def view(at_x, at_y, half):
        return dst.at[slice(None) if at_y is None else at_y, slice(None) if at_x is None else at_x,
                      core, half_lines(part, half), :]

    return spread_steps(t, view, steps)


def gather_steps(t, own, whole, rows):
    width = own.shape[1]
    z = t.z
    mate, far = z + 1 - 2 * lax.rem(z, 2), lax.rem(z + 2, 4)
    here, there = whole.at[rows, lane_block(z, width)], whole.at[rows, lane_block(far, width)]
    steps = Steps()
    cross = t.make(own.at[rows, :], here, {"col": far})
    near = t.make(own.at[rows, :], here, {"col": mate})
    steps.add([cross, near], [t.keep(own.at[rows, :], here)])
    steps.add([t.make(there, there, {"col": mate})])
    return steps


def mm_tn(a, b):
    return lax.dot_general(a, b, (((0,), (0,)), ((), ())), preferred_element_type=f32)


def add_bf16(a, b):
    return (a.astype(f32) + b.astype(f32)).astype(bf16)


class PairSum:
    def __init__(self, t, part, near, far_in, rows):
        z = t.z
        mate = z + 1 - 2 * lax.rem(z, 2)
        far = lax.rem(z + 2, 4)
        mate_far = lax.rem(mate + 2, 4)
        width = near.shape[-1]
        self.part, self.near, self.far_in, self.rows = part, near, far_in, rows
        self.own, self.far = lane_block(z, width), lane_block(far, width)
        to_mate = [
            t.make(part.at[rows, lane_block(mate_far, width)], near.at[1, rows], {"col": mate}),
            t.make(part.at[rows, lane_block(mate, width)], near.at[0, rows], {"col": mate}),
        ]
        self.first, self.second = to_mate
        self.across = t.make(near.at[1, rows], far_in.at[rows], {"col": far})

    def start(self):
        self.first.start()

    def forward(self, both=True):
        self.first.wait_recv()
        count = self.rows.size // 64

        def body(i, c):
            at = pl.ds(pl.multiple_of(self.rows.start + i * 64, 16), 64)
            self.near[1, at] = add_bf16(self.near[1, at], self.part[at, self.far])
            return c

        lax.fori_loop(0, count, body, 0)
        self.across.start()
        if both:
            self.second.start()

    def arrive(self):
        self.second.wait_recv()
        self.across.wait_recv()

    def total(self, at):
        return (
            self.part[at, self.own].astype(f32) + self.near[0, at].astype(f32)
            + self.far_in[at].astype(f32)
        )


def sum_far_groups(t, own, got):
    if t.groups == 1:
        return
    more = [t.go(own, got.at[off - 1], t.group_peer(off), False) for off in range(1, t.groups)]
    for c in more:
        c.wait()

    def total(spare):
        for off in range(1, t.groups):
            back = t.keep(got.at[off - 1], spare)
            back.start()
            back.wait()
            own[...] = add_bf16(own[...], spare[...])

    pl.run_scoped(total, pltpu.VMEM(own.shape, own.dtype))


def column_sums(t, g, a1, yx, xy, yx2, xy2, a4, far):
    x, y, core = t.x, t.y, t.core
    width = a4.shape[-1]
    h = a4.shape[1] // 2
    mine, other = lane_block(y, width), lane_block(1 - y, width)
    top, low = pl.ds(0, h), pl.ds(h, h)
    steps = Steps()
    steps.add([t.make(g.at[:, :, 1 - core], a1, t.mate())])

    def add_core():
        def body(i, c):
            for j in range(2):
                a1[i, j] = add_bf16(a1[i, j], g[i, j, core])
            return c

        lax.fori_loop(0, t.cols, body, 0)

    steps.add([
        t.make(a1.at[:, :, top, other], yx, t.other_row()),
        t.make(a1.at[:, 1 - x, low, :], xy, t.across()),
    ], (), add_core)

    def add_first():
        def body(i, c):
            for j in range(2):
                yx[i, j] = add_bf16(yx[i, j], a1[i, j, top, mine])
            xy[i] = add_bf16(xy[i], a1[i, x, low, :])
            return c

        lax.fori_loop(0, t.cols, body, 0)

    steps.add([
        t.make(yx.at[:, 1 - x], yx2, t.across()),
        t.make(xy.at[:, :, other], xy2, t.other_row()),
    ], (), add_first)

    def add_second():
        def body(i, c):
            a4[i, top] = add_bf16(yx2[i], yx[i, x])
            a4[i, low] = add_bf16(xy2[i], xy[i, :, mine])
            return c

        lax.fori_loop(0, t.cols, body, 0)
        sum_far_groups(t, a4, far)

    steps.add([], (), add_second)
    return steps


def column_sum_shapes(cols, q, w):
    h = q // 2
    return [((cols, 2, q, 2 * w), bf16), ((cols, 2, h, w), bf16), ((cols, h, 2 * w), bf16),
            ((cols, h, w), bf16), ((cols, h, w), bf16), ((cols, q, w), bf16)]


def column_home(t, a4, o, steps):
    x, z, core = t.x, t.z, t.core
    here = o.at[x, core, :, lane_block(z, a4.shape[-1])]
    steps.add(
        [t.make(a4.at[t.col_peer(off)], here, {"col": t.col_peer(off)}) for off in range(1, t.cols)],
        [t.keep(a4.at[z], here)],
    )
    steps.add([t.make(o.at[x, core], o.at[x, core], t.across())])
    steps.add([t.make(o.at[:, core], o.at[:, core], t.mate())])
    return steps


def row_sums(t, g, a1, yx, xy, yx2, xy2, a4, far):
    x, y, core = t.x, t.y, t.core
    h = a4.shape[0] // 2
    top, low = pl.ds(0, h), pl.ds(h, h)
    steps = Steps()
    steps.add([t.make(g.at[:, :, 1 - core], a1, t.mate())])

    def add_core():
        def body(i, c):
            for j in range(2):
                a1[i, j] = add_bf16(a1[i, j], g[i, j, core])
            return c

        lax.fori_loop(0, 2, body, 0)

    steps.add([
        t.make(a1.at[1 - y, :, top], yx, t.other_row()),
        t.make(a1.at[:, 1 - x, low], xy, t.across()),
    ], (), add_core)

    def add_first():
        for j in range(2):
            yx[j] = add_bf16(yx[j], a1[y, j, top])
            xy[j] = add_bf16(xy[j], a1[j, x, low])

    steps.add([
        t.make(yx.at[1 - x], yx2, t.across()), t.make(xy.at[1 - y], xy2, t.other_row()),
    ], (), add_first)

    def add_second():
        a4[top] = add_bf16(yx2[...], yx[x])
        a4[low] = add_bf16(xy2[...], xy[y])
        sum_far_groups(t, a4, far)

    steps.add([], (), add_second)
    return steps


def row_sum_shapes(q, width):
    h = q // 2
    return [((2, 2, q, width), bf16), ((2, h, width), bf16), ((2, h, width), bf16),
            ((h, width), bf16), ((h, width), bf16), ((q, width), bf16)]


def row_home(t, a4, o, steps):
    x, z, core = t.x, t.z, t.core
    width = o.shape[-1]
    here = o.at[z, x, core]
    steps.add(
        [t.make(a4.at[:, lane_block(t.col_peer(off), width)], here, {"col": t.col_peer(off)})
         for off in range(1, t.cols)],
        [t.keep(a4.at[:, lane_block(z, width)], here)],
    )
    steps.add([t.make(o.at[:, x, core], o.at[:, x, core], t.across())])
    steps.add([t.make(o.at[:, :, core], o.at[:, :, core], t.mate())])
    return steps


def full_sums(t, g, s1, s2, s3, s4, s5, far, o):
    x, y, z, core = t.x, t.y, t.z, t.core
    steps = Steps()
    steps.add([t.make(g.at[:, :, :, 1 - core], s1, t.mate())])

    def add_core():
        def body(i, c):
            for j in range(2):
                for k in range(2):
                    s1[i, j, k] = add_bf16(s1[i, j, k], g[i, j, k, core])
            return c

        lax.fori_loop(0, t.cols, body, 0)

    steps.add([t.make(s1.at[:, 1 - y], s2, t.other_row())], (), add_core)

    def add_row():
        def body(i, c):
            for k in range(2):
                s2[i, k] = add_bf16(s2[i, k], s1[i, y, k])
            return c

        lax.fori_loop(0, t.cols, body, 0)

    steps.add([t.make(s2.at[:, 1 - x], s3, t.across())], (), add_row)

    def add_x():
        def body(i, c):
            s4[i] = add_bf16(s3[i], s2[i, x])
            return c

        lax.fori_loop(0, t.cols, body, 0)
        sum_far_groups(t, s4, far)

    steps.add(
        [t.make(s4.at[t.col_peer(off)], s5.at[off - 1], {"col": t.col_peer(off)})
         for off in range(1, t.cols)], (), add_x,
    )

    def add_cols():
        total = s4[z].astype(f32)
        for off in range(1, t.cols):
            total = total + s5[off - 1].astype(f32)
        s4[z] = total.astype(bf16)

    here = o.at[z, y, x, core]
    steps.add(
        [t.make(s4.at[z], here, {"col": t.col_peer(off)}) for off in range(1, t.cols)],
        [t.keep(s4.at[z], here)], add_cols,
    )
    here = o.at[:, y, x, core]
    steps.add([t.make(here, here, t.other_row())])
    here = o.at[:, :, x, core]
    steps.add([t.make(here, here, t.across())])
    here = o.at[:, :, :, core]
    steps.add([t.make(here, here, t.mate())])
    return steps


def small_sums(t, sm, msum, mgot, out, rest):
    steps = Steps()
    steps.add([t.make(sm, mgot.at[0], t.mate())])

    def add_core():
        msum[0] = sm[...] + mgot[0]

    steps.add([t.make(msum.at[0], mgot.at[1], t.other_row())], (), add_core)

    def add_row():
        msum[1] = msum[0] + mgot[1]

    steps.add([t.make(msum.at[1], mgot.at[2], t.across())], (), add_row)

    def add_x():
        msum[2] = msum[1] + mgot[2]
        if t.groups > 1:
            more = [t.go(msum.at[2], mgot.at[5 + off], t.group_peer(off), False)
                    for off in range(1, t.groups)]
            for c in more:
                c.wait()
            total = msum[2]
            for off in range(1, t.groups):
                total = total + mgot[5 + off]
            msum[2] = total

    last = pl.ds(rest, sm.shape[0] - rest)
    steps.add(
        [t.make(msum.at[2, last], mgot.at[2 + off, last], {"col": t.col_peer(off)})
         for off in range(1, t.cols)], (), add_x,
    )

    def done():
        out[0:rest] = msum[2, 0:rest]
        out[rest:] = msum[2, rest:] + mgot[3, rest:] + mgot[4, rest:] + mgot[5, rest:]

    steps.add([], (), done)
    return steps


def front_kernel(
    inner_total,
    ngain_v, w_states, segments, taps_inner, bias_inner, gain_gate, taps_states, bias_states, step_all,
    step_bias, decay_log, skip_gain,
    tok_h, inner, gate, out, cot,
    mixed_o, wi_o, wg_o, ws_o, normed_o, sig_o, gx_o, gs_o, gz_o, accx_o, accs_o, acch_o, acc_o,
    gg4_o, go4_o, ggate_o, far_g, far_o,
    wi, wg, wo, ws2, ws, step_w, cots, par, spar, head, head_own, head_in, halo_in, tok, tok_own,
    meta, hmeta, docrow, docs,
    normed_s, pre_s, spre_s, sd_s, ssd_s, x_s, wr_s, step_s, r_s, sig_s, hpre_s, hspre_s, sprev_s,
    gated_s, ggate_s, gy_s, dr_s, fresh_s, y_s, gate_s, gg_s, gs_s, gz_s,
    out_near, out_far, sums_s, sums_in, xbuf, sbuf, mem, pass_out, state_in, dstate_in, pass_back,
    hx, hs, hx_in, hs_in, accx, accs, acch, acc_s, gg, g1, g2, g3, g5, g6, g4, o1, o2, o3, o5, o6, o4,
    tile_a, tile_b, wide_tile,
    send, recv, local,
):
    t = Links(send, recv, local)
    x, y, z, core = t.x, t.y, t.z, t.core
    blocks = tok.shape[0] // SPAN
    channels = x_s.shape[1]
    half = channels // 2
    outputs = []

    def write(src, dst):
        copy = t.keep(src, dst)
        copy.start()
        outputs.append(copy)

    def load(src, dst):
        copy = t.keep(src, dst)
        copy.start()
        return copy

    loads = [load(tok_h, tok), load(tok_h.at[:, lane_block(z, cot.shape[1])], tok_own)]
    own_lanes = lane_block(y, half)
    few = [
        t.make(par.at[:, own_lanes], par.at[:, own_lanes], t.other_row()),
        t.make(head_own, head_in, t.other_row()),
        t.make(tok_h.at[pl.ds(tok.shape[0] - 16, 16), :], halo_in, t.other_row()),
    ]
    block = inner.shape[1] // t.cols
    get_inner = column_steps(t, inner, wi, block)
    get_step = column_steps(t, step_w, ws2, step_w.shape[1] // t.cols)
    get_gate = column_steps(t, gate, wg, block)
    get_out = row_steps(t, out, wo, out.shape[1])
    half_rows = tok.shape[0] // 2
    get_cot = [gather_steps(t, cot, cots, pl.ds(n * half_rows, half_rows)) for n in range(2)]
    pass_state = t.make(pass_out, state_in, t.other_row())
    pass_back_state = t.make(pass_back, dstate_in, t.other_row())
    halo_x = t.make(hx, hx_in, t.other_row())
    halo_s = t.make(hs, hs_in, t.other_row())
    out_part = tok
    sum_gate = column_sums(t, gg, g1, g2, g3, g5, g6, g4, far_g)
    go = wo
    sum_out = row_sums(t, go, o1, o2, o3, o5, o6, o4, far_o)
    out_sums = [PairSum(t, out_part, out_near, out_far, pl.ds(b * SPAN, SPAN)) for b in range(blocks)]
    pass_sums = [
        t.make(sums_s, sums_in.at[off - 1], {"col": t.col_peer(off)}) for off in range(1, t.cols)
    ]
    t.meet(True)
    get_inner.run(0)

    own_heads = step_bias.shape[0]
    lane8 = lax.broadcasted_iota(jnp.int32, (8, 128), 1)
    row8 = lax.broadcasted_iota(jnp.int32, (8, 128), 0)
    scalars = jnp.zeros((8, 128), f32)
    for j in range(own_heads):
        here = lane8 == y * own_heads + j
        scalars = scalars + jnp.where(here & (row8 == 0), step_bias[j], 0.0)
        scalars = scalars + jnp.where(here & ((row8 == 1) | (row8 == 3)), decay_log[j], 0.0)
        scalars = scalars + jnp.where(here & (row8 == 2), skip_gain[j], 0.0)
    own_lane = (lane8 >= y * own_heads) & (lane8 < (y + 1) * own_heads)
    rate = jnp.where(own_lane, -jnp.exp(scalars), 0.0)
    head_own[...] = jnp.where(row8 == 1, rate * LOG2E, jnp.where(row8 == 3, rate, scalars))
    par[:, own_lanes] = jnp.zeros((8, half), f32)
    par[0:4, own_lanes] = taps_inner[...]
    par[4:5, own_lanes] = bias_inner[...].reshape(1, half)
    par[5:6, own_lanes] = gain_gate[...].reshape(1, half)
    spar[...] = jnp.zeros_like(spar)
    spar[0:4, :] = taps_states[...]
    spar[4:5, :] = bias_states[...].reshape(1, 256)
    every = step_all.shape[0]
    src = lax.broadcasted_iota(jnp.int32, (every, t.cols * 128), 0)
    dst = lax.broadcasted_iota(jnp.int32, (every, t.cols * 128), 1)
    place = jnp.zeros((every, t.cols * 128), f32)
    for c in range(t.cols):
        low = c * 128 + y * own_heads - c * own_heads
        mine = (src >= c * own_heads) & (src < (c + 1) * own_heads)
        place = place + jnp.where(mine & (dst - src == low), 1.0, 0.0)
    step_w[...] = mm_tn(step_all[...], place.astype(bf16)).astype(bf16)
    get_step.run(0)
    for c in few:
        c.start()

    length = tok.shape[0]
    docs[:, 0:128] = jnp.full((8, 128), -1.0, f32)
    docs[:, 128:128 + 2 * length] = jnp.broadcast_to(segments[...].astype(f32), (8, 2 * length))
    docs[:, 128 + 2 * length:] = jnp.full((8, 128), -1.0, f32)
    window = docs[:, pl.ds(pl.multiple_of(y * length, 128), length + 256)]
    span_w = length + 256
    docrow[...] = window[:, 128:128 + length]
    same_before = [(window == pltpu.roll(window, k, 1)).astype(f32) for k in range(1, 4)]
    same_after = [(window == pltpu.roll(window, span_w - k, 1)).astype(f32) for k in range(1, 4)]
    row16 = lax.broadcasted_iota(jnp.int32, (8, SPAN), 0)
    for i in range(blocks):
        at = slice(128 + i * SPAN, 128 + (i + 1) * SPAN)
        here = window[:, at]
        before = window[0:1, 127 + i * SPAN:128 + i * SPAN]
        last = window[0:1, 127 + (i + 1) * SPAN:128 + (i + 1) * SPAN]
        low = jnp.where(row16 == 0, here, 0.0)
        for k in range(1, 4):
            low = low + jnp.where(row16 == k, same_before[k - 1][:, at], 0.0)
        low = low + jnp.where((row16 == 4) & (here == before), 1.0, 0.0)
        low = low + jnp.where((row16 == 5) & (here == last), 1.0, 0.0)
        low = low + jnp.where((row16 == 6) & (before == last), 1.0, 0.0)
        high = jnp.zeros((8, SPAN), f32)
        for k in range(1, 4):
            high = high + jnp.where(row16 == k - 1, same_after[k - 1][:, at], 0.0)
        rows128 = jnp.concatenate([low, high, jnp.zeros((112, SPAN), f32)], 0)
        meta[i * SPAN:(i + 1) * SPAN, :] = jnp.transpose(rows128)
    row16 = lax.broadcasted_iota(jnp.int32, (8, 128), 0)
    high = jnp.zeros((8, 128), f32)
    for k in range(1, 4):
        high = high + jnp.where(row16 == k - 1, same_after[k - 1][:, 0:128], 0.0)
    rows128 = jnp.concatenate([jnp.zeros((8, 128), f32), high, jnp.zeros((112, 128), f32)], 0)
    hmeta[...] = jnp.transpose(rows128)[120:128]

    gain = ngain_v[...].reshape(1, -1)
    for c in loads:
        c.wait()

    def rows_of(i):
        return pl.ds(pl.multiple_of(i * SPAN, SPAN), SPAN)

    def conv_silu(buf, lanes, here, taps, marks):
        v = taps[4:5, lanes] + taps[0:1, lanes] * here
        for k in range(1, 4):
            v = v + marks[:, k:k + 1] * (taps[k:k + 1, lanes] * buf[8 - k:8 - k + SPAN, lanes])
        sg = sigmoid(v)
        return v * sg, sg * (1.0 + v * (1.0 - sg))

    for c in few:
        c.wait_recv()
    hn = rms_rows(halo_in[...], gain)
    h_states = mm(hn, w_states[...])[8:16]
    sbuf[0:8, :] = h_states
    hspre_s[...] = h_states

    def norm_block(i, carry):
        at = rows_of(i)

        @pl.when(i > 0)
        def _():
            sbuf[0:8, :] = sbuf[SPAN:SPAN + 8, :]

        wide_tok = tok[at, :].astype(f32)
        inverse = lax.rsqrt(jnp.mean(wide_tok * wide_tok, -1, keepdims=True) + epsilon)
        normed = (wide_tok * inverse * gain).astype(bf16)
        normed_s[at, :] = normed
        s_pre = mm(normed, w_states[...])
        sbuf[8:SPAN + 8, :] = s_pre
        spre_s[at, :] = s_pre.astype(bf16)
        sact, sslope = conv_silu(sbuf, slice(0, 256), s_pre, spar, meta[at, :])
        wr_s[at, :] = sact.astype(bf16)
        ssd_s[at, :] = sslope.astype(bf16)
        sig_s[at, :] = jnp.broadcast_to(inverse, (SPAN, 128))

        @pl.when(i == 0)
        def _():
            get_inner.run(1)
            get_step.run(1)
            get_gate.run(0)
            get_out.run(0)
            get_cot[0].run(0)

        return carry

    lax.fori_loop(0, blocks, norm_block, 0)
    head[...] = head_own[...] + head_in[...]
    get_inner.run(2)
    get_step.run(2)
    get_inner.run(3)
    get_step.run(3)
    get_gate.run(1)
    get_inner.run(4)
    get_step.run(4)
    wide_in = normed_s.shape[1]
    ws[...] = (
        ws2[:, :, :, :, 0:128].reshape(wide_in, 128) + ws2[:, :, :, :, 128:256].reshape(wide_in, 128)
    )
    spread = spread_matrix(channels)

    def w_of(ref):
        return ref[...].reshape(-1, ref.shape[-1])

    first = half_masks()
    h_inner = mm(hn, w_of(wi))[8:16]
    xbuf[0:8, :] = h_inner
    hpre_s[...] = h_inner
    mem[...] = jnp.zeros_like(mem)

    def entry(i, carry):
        at = rows_of(i)

        @pl.when(i > 0)
        def _():
            xbuf[0:8, :] = xbuf[SPAN:SPAN + 8, :]

        normed = normed_s[at, :]
        x_pre = mm(normed, w_of(wi))
        xbuf[8:SPAN + 8, :] = x_pre
        pre_s[at, :] = x_pre.astype(bf16)
        marks = meta[at, :]
        wr = wr_s[at, :]
        for pair in range(channels // 128):
            lanes = slice(pair * 128, pair * 128 + 128)
            act, slope = conv_silu(xbuf, lanes, xbuf[8:SPAN + 8, lanes], par, marks)
            x_s[at, lanes] = act.astype(bf16)
            sd_s[at, lanes] = slope.astype(bf16)

        raw = mm(normed, ws[...]) + head[0:1, :]
        step = jnp.maximum(raw, 0.0) + jnp.log1p(jnp.exp(-jnp.abs(raw)))
        lane = lax.broadcasted_iota(jnp.int32, (SPAN, 128), 1)
        sig_s[at, :] = jnp.where(lane == 127, sig_s[at, :], sigmoid(raw))
        step_s[at, :] = step
        r = split_mm(lower_ones(), step * head[1:2, :])
        r_s[at, :] = r
        last = r[SPAN - 1:SPAN, :]
        to_end = jnp.exp2(jnp.minimum(last - r, 0.0)) * marks[:, 5:6]
        coef = to_end * step
        for pair in range(channels // 128):
            lanes = slice(pair * 128, pair * 128 + 128)
            tile_a[:, lanes] = (widen(first, coef, pair) * x_s[at, lanes].astype(f32)).astype(bf16)
        w_t = jnp.transpose(wr[:, 0:128].astype(f32)).astype(bf16)
        fresh = mm(w_t, tile_a[...])
        fresh_s[i] = fresh
        mem[...] = keep_of(last, marks) * mem[...] + fresh

        @pl.when(i == 0)
        def _():
            get_gate.run(2)
            get_out.run(1)

        @pl.when(i == 2)
        def _():
            get_gate.run(3)
            get_out.run(2)
            get_cot[0].run(1)
            get_cot[1].run(0)

        return carry

    def keep_of(last, marks):
        return mm_split(jnp.broadcast_to(jnp.exp2(last) * marks[0:1, 6:7], (8, 128)), spread)[0:1]

    lax.fori_loop(0, blocks, entry, 0)
    pass_out[...] = mem[...].astype(bf16)
    pass_state.start()
    get_gate.run(4)
    for src, dst in (
        (normed_s, normed_o), (sig_s, sig_o), (wi, wi_o), (wg, wg_o), (ws, ws_o),
    ):
        write(src, dst)

    def gate_block(i, carry):
        at = rows_of(i)
        gate_s[at, :] = mm(normed_s[at, :], w_of(wg))
        return carry

    lax.fori_loop(0, blocks, gate_block, 0)

    pass_state.wait_recv()
    mem[...] = state_in[...].astype(f32) * jnp.where(y == 1, 1.0, 0.0)
    get_out.run(3)
    skip = mm_split(jnp.broadcast_to(head[2:3, :], (8, 128)), spread)[0:1]

    def scan(i, carry):
        at = rows_of(i)
        marks = meta[at, :]
        w_low = wr_s[at, 0:128]
        r_low = wr_s[at, 128:256]
        r = r_s[at, :]
        r_t = jnp.transpose(r)
        rows = lax.broadcasted_iota(jnp.int32, (SPAN, SPAN), 0)
        cols = lax.broadcasted_iota(jnp.int32, (SPAN, SPAN), 1)
        allowed = (rows >= cols) & (marks[:, 0:1] == docrow[0:1, at])
        scores = jnp.where(allowed, mm_nt(r_low, w_low), 0.0)
        step = step_s[at, :]
        sprev = mem[...].astype(bf16)
        sprev_s[i] = sprev
        linked = jnp.exp2(r) * marks[:, 4:5]
        y_s[at, :] = mm(r_low, sprev)
        for pair in range(channels // 128):
            lanes = slice(pair * 128, pair * 128 + 128)
            wide = x_s[at, lanes].astype(f32)
            xp = (widen(first, step, pair) * wide).astype(bf16)
            total = y_s[at, lanes] * widen(first, linked, pair) + skip[:, lanes] * wide
            for part in range(2):
                h = 2 * pair + part
                decay = jnp.exp2(jnp.minimum(r[:, h:h + 1] - r_t[h:h + 1, :], 0.0))
                mixing = (scores * decay).astype(bf16)
                own = jnp.where(first if part == 0 else ~first, xp, jnp.zeros_like(xp))
                total = total + mm(mixing, own)
            y_s[at, lanes] = total
        last = r[SPAN - 1:SPAN, :]
        mem[...] = keep_of(last, marks) * mem[...] + fresh_s[i]

        @pl.when(i == 2)
        def _():
            get_cot[1].run(1)

        return carry

    lax.fori_loop(0, blocks, scan, 0)
    get_out.run(4)

    def project(i, carry):
        at = rows_of(i)
        g = gate_s[at, :]
        mixed = y_s[at, :] * (g * sigmoid(g))
        out_part[at, :] = mm((mixed * par[5:6, :]).astype(bf16), w_of(wo)).astype(bf16)
        return carry

    lax.fori_loop(0, blocks, project, 0)
    get_cot[0].run(2)
    ones = jnp.ones((8, channels), bf16)

    def totals_of(i, carry):
        at = rows_of(i)
        gg = mm_nt(cots[at, :], w_of(wo))
        gg_s[at, :] = gg.astype(bf16)
        g = gate_s[at, :]
        mixed = y_s[at, :] * (g * sigmoid(g))
        sq = sum(mm_nt(ones, part) for part in split(mixed * mixed, 2))
        pr = sum(mm_nt(ones, part) for part in split(mixed * (par[5:6, :] * gg), 2))
        for n in range(2):
            lanes = slice(n * 128, n * 128 + 128)
            sums_s[pl.ds(2 * i + n, 1), :] = sq[0:1, lanes]
            sums_s[pl.ds(2 * blocks + 2 * i + n, 1), :] = pr[0:1, lanes]
        return carry

    lax.fori_loop(0, blocks // 2, totals_of, 0)
    get_cot[1].run(2)
    for s in out_sums:
        s.start()
    lax.fori_loop(blocks // 2, blocks, totals_of, 0)
    for c in pass_sums:
        c.start()
    for c in pass_sums:
        c.wait_recv()
    mem[...] = jnp.zeros_like(mem)
    acc_s[...] = jnp.zeros_like(acc_s)
    gather = gather_matrix(channels)

    def scale_of(i):
        columns = []
        for base in (0, 2 * blocks):
            rows = pl.ds(base + 2 * i, 2)
            pair = sums_s[rows, :]
            for off in range(1, t.cols):
                pair = pair + sums_in[off - 1, rows, :]
            columns.append(jnp.concatenate([pair[0:1], pair[1:2]], 1))
        row = lax.broadcasted_iota(jnp.int32, (8, SPAN), 0)
        both = jnp.where(row == 0, jnp.broadcast_to(columns[0], (8, SPAN)),
                         jnp.broadcast_to(columns[1], (8, SPAN)))
        totals = jnp.transpose(both)
        return lax.rsqrt(totals[:, 0:1] / inner_total + epsilon), totals[:, 1:2] / inner_total

    def turn(back_i, carry):
        i = blocks - 1 - back_i
        at = rows_of(i)
        marks = meta[at, :]
        scale, cross = scale_of(i)
        r = r_s[at, :]
        linked = jnp.exp2(r) * marks[:, 4:5]
        row = lax.broadcasted_iota(jnp.int32, (8, 128), 0)
        dr = jnp.zeros((SPAN, 128), f32)
        for pair in range(channels // 128):
            lanes = slice(pair * 128, pair * 128 + 128)
            yv = y_s[at, lanes]
            g = gate_s[at, lanes]
            sg = sigmoid(g)
            sl = g * sg
            gg = gg_s[at, lanes].astype(f32)
            ngate = par[5:6, lanes]
            normal = yv * sl * scale
            gated_s[at, lanes] = (normal * ngate).astype(bf16)
            g_mixed = scale * (ngate * gg - normal * (scale * cross))
            ggate_s[at, lanes] = (g_mixed * yv * (sg * (1.0 + g * (1.0 - sg)))).astype(bf16)
            gy = (g_mixed * sl).astype(bf16)
            gy_s[at, lanes] = gy
            gyw = gy.astype(f32)
            wide = x_s[at, lanes].astype(f32)
            dr = dr + head_totals(gyw * (yv - skip[:, lanes] * wide), gather[lanes, :])
            ggain = jnp.sum(gg * normal, 0, keepdims=True)
            gskip = jnp.sum(gyw * wide, 0, keepdims=True)
            acc_s[:, lanes] += jnp.where(row == 0, ggain, jnp.where(row == 1, gskip, 0.0))
            tile_a[:, lanes] = (widen(first, linked, pair) * gyw).astype(bf16)
        dr_s[at, :] = dr
        r_t = jnp.transpose(wr_s[at, 128:256].astype(f32)).astype(bf16)
        dfresh = mm(r_t, tile_a[...])
        fresh_s[i] = dfresh
        for b in range(blocks):
            pl.when(back_i == b)(out_sums[b].forward)
        mem[...] = keep_of(r[SPAN - 1:SPAN, :], marks) * mem[...] + dfresh
        return carry

    lax.fori_loop(0, blocks, turn, 0)
    pass_back[...] = mem[...].astype(bf16)
    pass_back_state.start()

    def grad_out(i, carry):
        rows = pl.ds(pl.multiple_of(i * half, 128), half)
        for n in range(2):
            lanes = slice(n * wide_in // 2, (n + 1) * wide_in // 2)
            value = mm_tn(gated_s[:, rows], cots[:, lanes]).astype(bf16)
            go[i, :, :, :, lanes] = value.reshape(go.shape[1:4] + (wide_in // 2,))
        return carry

    get_out.drain(t)
    lax.fori_loop(0, 2, grad_out, 0)
    sum_out.run(0)

    def grad_gate(i, carry):
        rows = pl.ds(pl.multiple_of(i * (wide_in // t.cols), 128), wide_in // t.cols)
        gg[i] = mm_tn(normed_s[:, rows], ggate_s[...]).astype(bf16).reshape(gg.shape[1:])
        return carry

    lax.fori_loop(0, t.cols, grad_gate, 0)
    sum_gate.run(0)
    sum_out.run(1)
    write(ggate_s, ggate_o)
    accx[...] = jnp.zeros_like(accx)
    accs[...] = jnp.zeros_like(accs)
    acch[...] = jnp.zeros_like(acch)
    xbuf[...] = jnp.zeros_like(xbuf)
    sbuf[...] = jnp.zeros_like(sbuf)
    pass_back_state.wait_recv()
    mem[...] = dstate_in[...].astype(f32) * jnp.where(y == 0, 1.0, 0.0)
    gx_s = gg_s

    def back(back_i, carry):
        i = blocks - 1 - back_i
        at = rows_of(i)

        @pl.when(back_i > 0)
        def _():
            xbuf[SPAN + 8:SPAN + 16, :] = xbuf[8:16, :]
            sbuf[SPAN + 8:SPAN + 16, :] = sbuf[8:16, :]

        marks = meta[at, :]
        w_low = wr_s[at, 0:128]
        r_low = wr_s[at, 128:256]
        r = r_s[at, :]
        r_t = jnp.transpose(r)
        step = step_s[at, :]
        last = r[SPAN - 1:SPAN, :]
        rows = lax.broadcasted_iota(jnp.int32, (SPAN, SPAN), 0)
        cols = lax.broadcasted_iota(jnp.int32, (SPAN, SPAN), 1)
        allowed = (rows <= cols) & (marks[:, 0:1] == docrow[0:1, at])
        scores = jnp.where(allowed, mm_nt(w_low, r_low), 0.0)
        ds = mem[...]
        ds_low = ds.astype(bf16)
        to_end = jnp.exp2(jnp.minimum(last - r, 0.0)) * marks[:, 5:6]
        linked = jnp.exp2(r) * marks[:, 4:5]
        wide_tile[...] = mm(w_low, ds_low)
        keep = mm_split(jnp.broadcast_to(jnp.exp2(last) * marks[0:1, 6:7], (8, 128)), spread)[0:1]
        final = jnp.where(back_i == blocks - 1, 1.0, 0.0)

        def conv_back(buf, lanes, gv, base, taps, acc, halo_pre, out, halo_out):
            buf[8:SPAN + 8, lanes] = gv
            cols_here = gv.shape[1]
            total = taps[0:1, lanes] * gv
            sums = [jnp.sum(gv * base, 0, keepdims=True)]
            halo = jnp.zeros((8, cols_here), f32)
            hsum = []
            for k in range(1, 4):
                moved = marks[:, 7 + k:8 + k] * buf[8 + k:8 + k + SPAN, lanes]
                total = total + taps[k:k + 1, lanes] * moved
                sums.append(jnp.sum(moved * base, 0, keepdims=True))
                hmoved = hmeta[:, 7 + k:8 + k] * buf[k:8 + k, lanes]
                halo = halo + taps[k:k + 1, lanes] * hmoved
                hsum.append(jnp.sum(hmoved * halo_pre[:, lanes], 0, keepdims=True))
            sums.append(jnp.sum(gv, 0, keepdims=True))
            out[at, lanes] = total.astype(bf16)
            halo_out[:, lanes] = halo
            rows8 = lax.broadcasted_iota(jnp.int32, (8, cols_here), 0)
            add = jnp.zeros((8, cols_here), f32)
            for n, s in enumerate(sums):
                if 1 <= n <= 3:
                    s = s + final * hsum[n - 1]
                add = add + jnp.where(rows8 == n, s, 0.0)
            acc[:, lanes] += add

        zero = jnp.zeros((SPAN, 128), f32)
        dscores = jnp.zeros((SPAN, SPAN), f32)
        dr_cols, dstep = zero, zero
        endings = []
        for pair in range(channels // 128):
            lanes = slice(pair * 128, pair * 128 + 128)
            to_heads = gather[lanes, :]
            wide = x_s[at, lanes].astype(f32)
            step_wide = widen(first, step, pair)
            xp = (step_wide * wide).astype(bf16)
            xdw = xp.astype(f32)
            gp = gy_s[at, lanes]
            gyw = gp.astype(f32)
            sprev = sprev_s[i, :, lanes]
            te = widen(first, to_end, pair)
            total = te * wide_tile[:, lanes]
            ending = jnp.sum(xdw * total, 0, keepdims=True) + keep[:, lanes] * jnp.sum(
                sprev.astype(f32) * ds[:, lanes], 0, keepdims=True
            )
            endings.append(ending)
            for half in range(2):
                h = 2 * pair + half
                own = first if half == 0 else ~first
                decay = jnp.exp2(jnp.minimum(r_t[h:h + 1, :] - r[:, h:h + 1], 0.0))
                mixing = (scores * decay).astype(bf16)
                gown = jnp.where(own, gp, jnp.zeros_like(gp))
                total = total + mm(mixing, gown)
                dscores = dscores + mm_nt(xp, gown) * decay
            tile_a[:, lanes] = (te * xdw).astype(bf16)
            tile_b[:, lanes] = (widen(first, linked, pair) * gyw).astype(bf16)
            dr_cols = dr_cols + head_totals(xdw * total, to_heads)
            dstep = dstep + head_totals(wide * total, to_heads)
            g_x = step_wide * total + skip[:, lanes] * gyw
            conv_back(xbuf, lanes, g_x * sd_s[at, lanes].astype(f32), pre_s[at, lanes].astype(f32), par,
                      accx, hpre_s, gg_s, hx)
        ending = jnp.broadcast_to(jnp.concatenate(endings, 1), (8, channels))
        at_end = mm_split(ending, gather, 3)
        dscores = jnp.where(allowed, dscores, 0.0)
        g_write = mm(dscores.astype(bf16), r_low) + mm_nt(tile_a[...], ds_low)
        g_read = mm(jnp.transpose(dscores).astype(bf16), w_low) + mm_nt(tile_b[...], sprev_s[i])
        both = slice(0, 256)
        g_wr = jnp.concatenate([g_write, g_read], 1)
        conv_back(sbuf, both, g_wr * ssd_s[at, :].astype(f32), spre_s[at, :].astype(f32), spar, accs,
                  hspre_s, gs_s, hs)
        tail_row = lax.broadcasted_iota(jnp.int32, (SPAN, 128), 0) == SPAN - 1
        dr = dr_s[at, :] - dr_cols + jnp.where(tail_row, at_end[0:1], 0.0)
        da = split_mm(upper_ones(), dr)
        dstep = dstep + head[3:4, :] * da
        gzv = dstep * sig_s[at, :]
        gz_s[at, :] = gzv.astype(bf16)
        row = lax.broadcasted_iota(jnp.int32, (8, 128), 0)
        gbias = jnp.sum(gzv, 0, keepdims=True)
        grate = jnp.sum(da * step, 0, keepdims=True)
        acch[...] += jnp.where(row == 0, gbias, jnp.where(row == 1, grate, 0.0))
        mem[...] = keep * ds + fresh_s[i]

        @pl.when(back_i == 0)
        def _():
            sum_gate.run(1)

        @pl.when(back_i == 1)
        def _():
            sum_out.run(2)

        @pl.when(back_i == 2)
        def _():
            sum_gate.run(2)

        return carry

    lax.fori_loop(0, blocks, back, 0)
    halo_x.start()
    halo_s.start()
    write(gz_s, gz_o)
    write(accx, accx_o)
    write(accs, accs_o)
    write(acch, acch_o)
    write(acc_s, acc_o)
    sum_out.run(3)
    sum_gate.run(3)
    write(o4, go4_o)
    write(g4, gg4_o)
    halo_x.wait_recv()
    halo_s.wait_recv()
    use = jnp.where(y == 0, 1.0, 0.0)
    end = pl.ds(tok.shape[0] - 16, 16)
    zeros = jnp.zeros((8, channels), f32)
    gx_s[end, :] = (
        gx_s[end, :].astype(f32) + jnp.concatenate([zeros, use * hx_in[...]], 0)
    ).astype(bf16)
    zeros = jnp.zeros((8, 256), f32)
    gs_s[end, :] = (
        gs_s[end, :].astype(f32) + jnp.concatenate([zeros, use * hs_in[...]], 0)
    ).astype(bf16)
    write(gx_s, gx_o)
    write(gs_s, gs_o)

    for s in out_sums:
        s.arrive()

    def finish(i, carry):
        at = rows_of(i)
        scale = scale_of(i)[0]
        out_far[at, :] = (
            tok_own[at, :].astype(f32) + scale * out_sums[0].total(at)
        ).astype(bf16)
        return carry

    lax.fori_loop(0, blocks, finish, 0)
    write(out_far, mixed_o)
    for copy in outputs:
        copy.wait()
    t.finish()


def front(inner_all, ngain, w_states, segments, taps_inner, bias_inner, gain_gate, taps_states,
          bias_states, step_all, step_bias, decay_log, skip_gain, tok, inner, gate, out, cot):
    tokens, width = tok.shape
    blocks = tokens // SPAN
    cols = lax.axis_size("col")
    groups = lax.axis_size("dp") // SHARE - 1
    part, half = inner.shape[0] // SHARE, inner.shape[1] // cols
    channels = 2 * half
    third = width // cols
    q, qo = third // SHARE, half // SHARE
    sds = jax.ShapeDtypeStruct
    V = pltpu.VMEM
    wide = ((cols, 2, 2, part, channels), bf16)
    by_channel = ((tokens, channels), bf16)
    by_state = ((tokens, 256), bf16)
    by_head = ((tokens, 128), f32)
    acc, sacc, hacc = ((8, channels), f32), ((8, 256), f32), ((8, 128), f32)
    passed = ((128, channels), bf16)
    far = [(groups, cols, q, half), (groups, qo, width)] if groups else [(16, 128)] * 2
    outs = [
        ((tokens, third), bf16), wide, wide, ((width, 128), bf16), ((tokens, width), bf16), by_head,
        by_channel, by_state, ((tokens, 128), bf16), acc, sacc, hacc, acc,
        ((cols, q, half), bf16), ((qo, width), bf16), by_channel,
    ] + [(shape, bf16) for shape in far]
    scratch = [
        wide, wide, ((2, 2, 2, half // SHARE, width), bf16), ((cols, 2, 2, part, 256), bf16),
        ((width, 128), bf16), ((part * SHARE, cols * 128), bf16), ((tokens, width), bf16), acc, sacc,
        hacc, hacc, hacc, ((16, width), bf16), ((tokens, width), bf16), ((tokens, third), bf16),
        by_head, hacc, ((8, tokens), f32), ((8, 2 * tokens + 256), f32),
        ((tokens, width), bf16), by_channel, by_state, by_channel, by_state, by_channel, by_state,
        by_head, by_head, by_head, acc, sacc, ((blocks, 128, channels), bf16),
        by_channel, by_channel, by_channel, by_head, ((blocks, 128, channels), f32),
        ((tokens, channels), f32), ((tokens, channels), f32), by_channel, by_state,
        ((tokens, 128), bf16),
        ((2, tokens, third), bf16), ((tokens, third), bf16), ((tokens // 64, 128), f32),
        ((cols - 1, tokens // 64, 128), f32), ((SPAN + 16, channels), f32), ((SPAN + 16, 256), f32),
        ((128, channels), f32), passed, passed, passed, passed,
        acc, sacc, acc, sacc, acc, sacc, hacc, acc,
        ((cols, 2, 2, q, channels), bf16),
    ] + column_sum_shapes(cols, q, half) + row_sum_shapes(qo, width) + [
        ((SPAN, channels), bf16), ((SPAN, channels), bf16), ((SPAN, channels), f32),
    ]
    vmem = pl.BlockSpec(memory_space=V)
    hbm = pl.BlockSpec(memory_space=pl.ANY)
    smem = pl.BlockSpec(memory_space=pltpu.SMEM)
    got = pl.pallas_call(
        functools.partial(front_kernel, float(inner_all)),
        out_shape=[sds(*o) for o in outs],
        in_specs=[vmem] * 9 + [smem] * 3 + [hbm] * 5,
        out_specs=[hbm] * len(outs),
        scratch_shapes=[V(*s) for s in scratch] + [
            pltpu.SemaphoreType.DMA((72,)), pltpu.SemaphoreType.DMA((72,)),
            pltpu.SemaphoreType.DMA((40,)),
        ],
        compiler_params=pltpu.CompilerParams(
            collective_id=1, has_side_effects=True, vmem_limit_bytes=63 * 1024 * 1024
        ),
        name="front",
    )(ngain, w_states, segments, taps_inner, bias_inner, gain_gate, taps_states, bias_states, step_all,
      step_bias, decay_log, skip_gain, tok, inner, gate, out, cot)
    got = list(got[:16])
    got[1] = got[1].reshape(width, channels)
    got[2] = got[2].reshape(width, channels)
    return got


def rear_kernel(
    accx, accs, acch, acc1, ngain_v,
    tok_h, w_states_h, wi_h, wg_h, ws_h, cot_h, normed_h, sig_h, ggate_h, gx_h, gs_h, gz_h, g4_h, o4_h,
    gtok_o, oi, og, oz, oo, os, sm_o, far_i, far_z, far_s,
    tok, wst, wi, wg, ws, cot_own, normed, sig_s, ggate, gx_s, gs_s, gz_s, g4, o4,
    ngain, part, gshare, g_near, g_far, ish, ish_in,
    gi, i1, i2, i3, i5, i6, i4, gz, z1, z2, z3, z5, z6, z4,
    gs, s1, s2, s3, s4, s5, sm, msum, mgot,
    send, recv, local,
):
    t = Links(send, recv, local)
    x, y, z, core = t.x, t.y, t.z, t.core
    tokens, width = normed.shape
    channels = ggate.shape[1]
    third = width // t.cols
    blocks = tokens // SPAN
    own_cols = lane_block(z, third)

    def load(src, dst):
        copy = t.keep(src, dst)
        copy.start()
        return copy

    first = [load(g4_h, g4), load(o4_h, o4)]
    early = [load(normed_h, normed), load(gx_h, gx_s)]
    loads = [load(a, b) for a, b in (
        (ggate_h, ggate), (wg_h, wg), (wi_h, wi), (ws_h, ws), (w_states_h, wst), (gs_h, gs_s),
        (gz_h, gz_s),
    )]
    later = [load(a, b) for a, b in (
        (cot_h, cot_own), (sig_h, sig_s), (tok_h.at[:, own_cols], tok),
    )]
    norm_sums = [PairSum(t, part, g_near, g_far, pl.ds(b * SPAN, SPAN)) for b in range(blocks)]
    home_out = row_home(t, o4, oo, Steps())
    home_gate = column_home(t, g4, og, Steps())
    sum_inner = column_home(t, i4, oi, column_sums(t, gi, i1, i2, i3, i5, i6, i4, far_i))
    sum_step = column_home(t, z4, oz, column_sums(t, gz, z1, z2, z3, z5, z6, z4, far_z))
    sum_states = full_sums(t, gs, s1, s2, s3, s4, s5, far_s, os)
    sum_small = small_sums(t, sm, msum, mgot, sm_o, 8)
    send_ish = [t.make(ish, ish_in.at[off - 1], {"col": t.col_peer(off)}) for off in range(1, t.cols)]
    t.meet(True)

    def rows_of(i):
        return pl.ds(pl.multiple_of(i * SPAN, SPAN), SPAN)

    for c in first:
        c.wait()
    home_out.run(0)
    home_gate.run(0)
    gshare[...] = jnp.zeros_like(gshare)
    ngain[...] = jnp.broadcast_to(ngain_v[...].reshape(1, width), (8, width))

    def normed_grad(i, carry):
        at = rows_of(i)

        def body(c, column):
            lanes = pl.ds(pl.multiple_of(c * third, 128), third)
            total = (
                mm_nt(ggate[at, :], wg[lanes, :]) + mm_nt(gx_s[at, :], wi[lanes, :])
                + mm_nt(gz_s[at, :], ws[lanes, :]) + mm_nt(gs_s[at, :], wst[lanes, :])
            )
            part[at, lanes] = total.astype(bf16)
            weighed = total * normed[at, lanes].astype(f32)
            gshare[0:1, lanes] += jnp.sum(weighed, 0, keepdims=True)
            return column + jnp.sum(weighed, -1, keepdims=True)

        column = lax.fori_loop(0, t.cols, body, jnp.zeros((SPAN, 1), f32))
        along = jnp.transpose(jnp.broadcast_to(column, (SPAN, 128)))
        for n in range(2):
            ish[pl.ds(2 * i + n, 1), :] = along[0:1, n * 128:n * 128 + 128]
        for b in range(blocks):
            pl.when(i == b)(norm_sums[b].start)
        return carry

    def weight_grad(right, target):
        def body(i, carry):
            rows = pl.ds(pl.multiple_of(i * third, 128), third)
            target[i] = mm_tn(normed[:, rows], right[...]).astype(bf16).reshape(target.shape[1:])
            return carry

        lax.fori_loop(0, t.cols, body, 0)

    def gz_body(i, carry):
        rows = pl.ds(pl.multiple_of(i * third, 128), third)
        value = mm_tn(normed[:, rows], gz_s[...]).astype(bf16)
        gz[i] = jnp.concatenate([value, value], 1).reshape(gz.shape[1:])
        return carry

    def gs_body(i, carry):
        rows = pl.ds(pl.multiple_of(i * third, 128), third)
        gs[i] = mm_tn(normed[:, rows], gs_s[...]).astype(bf16).reshape(gs.shape[1:])
        return carry

    for c in early:
        c.wait()
    weight_grad(gx_s, gi)
    sum_inner.run(0)
    for c in loads:
        c.wait()
    lax.fori_loop(0, 1, normed_grad, 0)
    sum_inner.run(1)
    lax.fori_loop(1, 2, normed_grad, 0)
    lax.fori_loop(0, t.cols, gs_body, 0)
    sum_states.run(0)
    lax.fori_loop(0, t.cols, gz_body, 0)
    sum_step.run(0)
    lax.fori_loop(2, 3, normed_grad, 0)
    norm_sums[0].forward()
    lax.fori_loop(3, blocks, normed_grad, 0)
    norm_sums[1].forward()
    sm[...] = jnp.zeros_like(sm)
    sm[0:5, :] = accx[0:5, :]
    sm[5:7, :] = acc1[0:2, :]
    for n in range(2):
        sm[7:8, n * 128:n * 128 + 128] = acch[n:n + 1, :]
        sm[8 + n:9 + n, :] = gshare[0:1, n * channels:(n + 1) * channels]
    for n in range(5):
        sm[10 + n // 3:11 + n // 3, n % 3 * 256:n % 3 * 256 + 256] = accs[n:n + 1, :]
    sum_small.run(0)
    for c in send_ish:
        c.start()
    sum_states.run(1)
    sum_step.run(1)
    sum_small.run(1)
    home_out.run(1)
    home_gate.run(1)
    sum_inner.run(2)
    sum_states.run(2)
    sum_step.run(2)
    sum_small.run(2)
    norm_sums[2].forward()
    norm_sums[3].forward()
    sum_inner.run(3)
    sum_inner.run(4)
    sum_states.run(3)
    sum_step.run(3)
    sum_step.run(4)
    sum_small.run(3)
    home_out.run(2)
    home_gate.run(2)
    sum_states.run(4)
    sum_inner.run(5)
    sum_states.run(5)
    sum_step.run(5)
    sum_small.run(4)
    sum_states.run(6)
    sum_step.run(6)
    sum_inner.run(6)
    sum_states.run(7)
    for c in later:
        c.wait()

    for c in send_ish:
        c.wait_recv()
    for n in norm_sums:
        n.arrive()

    def finish(i, carry):
        at = rows_of(i)
        own = tok[at, :].astype(f32)
        rows = pl.ds(2 * i, 2)
        pair = ish[rows, :]
        for off in range(1, t.cols):
            pair = pair + ish_in[off - 1, rows, :]
        line = jnp.concatenate([pair[0:1], pair[1:2]], 1)
        along = jnp.transpose(jnp.broadcast_to(line, (8, SPAN)))[:, 0:1] / width
        inverse = sig_s[at, 127:128]
        grad = inverse * (norm_sums[0].total(at) * ngain[0:1, own_cols] - own * (inverse * along))
        g_far[at, :] = (grad + cot_own[at, :].astype(f32)).astype(bf16)
        return carry

    lax.fori_loop(0, blocks, finish, 0)
    last = load(g_far, gtok_o)
    home_out.run(3)
    home_gate.run(3)
    sum_step.run(7)
    sum_inner.run(7)
    sum_states.run(8)
    sum_small.run(5)
    last.wait()
    t.finish()


def rear(accx, accs, acch, acc1, ngain, tok, w_states, wi, wg, ws, cot, normed, sig, ggate, gx, gs, gz,
         g4, o4):
    tokens, width = normed.shape
    channels = ggate.shape[1]
    cols = lax.axis_size("col")
    groups = lax.axis_size("dp") // SHARE - 1
    third, own = width // cols, channels // 2
    q, qo, qs = third // SHARE, own // SHARE, width // (cols * 2 * SHARE)
    sds = jax.ShapeDtypeStruct
    V = pltpu.VMEM
    small = [accx, accs, acch, acc1, ngain]
    big = [tok, w_states, wi, wg, ws, cot, normed, sig, ggate, gx, gs, gz, g4, o4]
    scratch = [((tokens, third), bf16)] + [(b.shape, b.dtype) for b in big[1:]]

    scratch += [
        ((8, width), f32), ((tokens, width), bf16), ((8, width), f32),
        ((2, tokens, third), bf16), ((tokens, third), bf16), ((tokens // 128, 128), f32),
        ((cols - 1, tokens // 128, 128), f32),
    ]
    scratch += [((cols, 2, 2, q, 2 * own), bf16)] + column_sum_shapes(cols, q, own)
    scratch += [((cols, 2, 2, q, 256), bf16)] + column_sum_shapes(cols, q, 128)
    scratch += [
        ((cols, 2, 2, 2, qs, 256), bf16), ((cols, 2, 2, qs, 256), bf16), ((cols, 2, qs, 256), bf16),
        ((cols, qs, 256), bf16), ((cols, qs, 256), bf16), ((cols - 1, qs, 256), bf16),
        ((16, channels), f32), ((3, 16, channels), f32), ((6 + groups, 16, channels), f32),
    ]
    if groups:
        far = [(groups, cols, q, own), (groups, cols, q, 128), (groups, cols, qs, 256)]
    else:
        far = [(16, 128)] * 3
    vmem = pl.BlockSpec(memory_space=V)
    hbm = pl.BlockSpec(memory_space=pl.ANY)
    got = pl.pallas_call(
        rear_kernel,
        out_shape=[
            sds((tokens, third), bf16),
            sds((2, 2, q, cols * own), bf16), sds((2, 2, q, cols * own), bf16),
            sds((2, 2, q, cols * 128), bf16), sds((cols, 2, 2, qo, third), bf16),
            sds((cols, 2, 2, 2, qs, 256), bf16), sds((16, channels), f32),
        ] + [sds(f, bf16) for f in far],
        in_specs=[vmem] * len(small) + [hbm] * len(big),
        out_specs=[hbm] * 6 + [vmem] + [hbm] * 3,
        scratch_shapes=[V(*s) for s in scratch] + [
            pltpu.SemaphoreType.DMA((100,)), pltpu.SemaphoreType.DMA((100,)),
            pltpu.SemaphoreType.DMA((48,)),
        ],
        compiler_params=pltpu.CompilerParams(
            collective_id=2, has_side_effects=True, vmem_limit_bytes=62 * 1024 * 1024
        ),
        name="rear",
    )(*small, *big)
    gtok, oi, og, oz, oo, os, sm = got[:7]
    return (
        gtok, oi.reshape(third, -1), og.reshape(third, -1), oz.reshape(third, -1),
        oo.reshape(cols * own, third), os.reshape(width, -1), sm,
    )


def unpack_kernel(
    oi, og, oz, oo, os, sm, ngain, decay_log,
    inner_o, gate_o, step_o, out_o, states_o, taps_o, bias_o, staps_o, sbias_o, step_bias_o, decay_o,
    skip_o, gain_o, norm_o,
    wide,
):
    y, z = lax.axis_index("row"), lax.axis_index("col")
    inner_o[...] = oi[...].astype(f32)
    gate_o[...] = og[...].astype(f32)
    out_o[...] = oo[...].astype(f32)
    states_o[...] = os[...].astype(f32)
    heads = decay_log.shape[0]

    @pl.when(pl.program_id(0) == 0)
    def _():
        own_ch, third = taps_o.shape[1], norm_o.shape[0]
        steps, lanes = step_o.shape[0], oz.shape[1]
        dst = lax.broadcasted_iota(jnp.int32, (steps, lanes), 0)
        src = lax.broadcasted_iota(jnp.int32, (steps, lanes), 1)
        pick = jnp.zeros((steps, lanes), f32)
        for c in range(steps // heads):
            mine = (dst >= c * heads) & (dst < (c + 1) * heads)
            place = src - dst == c * 128 + y * heads - c * heads
            pick = pick + jnp.where(mine & place, 1.0, 0.0)
        step_o[...] = mm_nt(pick.astype(bf16), oz[...])
        own = lane_block(y, own_ch)
        taps_o[...] = sm[0:4, own]
        bias_o[...] = sm[4:5, own].reshape(own_ch)
        gain_o[...] = sm[5:6, own].reshape(own_ch)
        for n in range(4):
            staps_o[n:n + 1, :] = sm[10 + n // 3:11 + n // 3, n % 3 * 256:n % 3 * 256 + 256]
        sbias_o[...] = sm[11:12, 256:512].reshape(256)
        skip = mm_split(sm[0:8, own], gather_matrix(own_ch), 3)
        skip_o[...] = skip[6:7, 0:heads].reshape(heads)

        def own_head(n):
            both = sm[7:8, n * 128:n * 128 + 128]
            return jnp.where(y == 0, both[:, 0:heads], both[:, heads:2 * heads])

        step_bias_o[...] = own_head(0).reshape(heads)
        rate = -jnp.exp(decay_log[...].reshape(1, heads))
        decay_o[...] = (own_head(1) * rate).reshape(heads)
        half = sm.shape[1]
        wide[0:1, 0:half] = sm[8:9, :]
        wide[0:1, half:] = sm[9:10, :]
        wide[8:16, :] = jnp.broadcast_to(ngain[...].reshape(1, 2 * half), (8, 2 * half))
        cols = lane_block(z, third)
        norm_o[...] = (wide[0:1, cols] / wide[8:9, cols]).reshape(third)


def unpack(oi, og, oz, oo, os, sm, ngain, decay_log, own_ch):
    sds = jax.ShapeDtypeStruct
    heads, parts = decay_log.shape[0], 4
    third, block = oi.shape

    def rows(shape):
        return pl.BlockSpec((shape[0] // parts, shape[1]), lambda i: (i, 0))

    def whole(shape):
        return pl.BlockSpec(shape, lambda i: (0,) * len(shape))

    steps = (block // own_ch * heads, third)
    small = [(4, own_ch), (own_ch,), (4, 256), (256,), (heads,), (heads,), (heads,), (own_ch,),
             (third,)]
    big = [oi.shape, og.shape, steps, oo.shape, os.shape]
    ins = [rows(oi.shape), rows(og.shape), whole(oz.shape), rows(oo.shape), rows(os.shape)]
    return pl.pallas_call(
        unpack_kernel,
        grid=(parts,),
        out_shape=[sds(s, f32) for s in big + small],
        in_specs=ins + [whole(sm.shape), whole(ngain.shape), whole(decay_log.shape)],
        out_specs=[whole(s) if s == steps else rows(s) for s in big] + [whole(s) for s in small],
        scratch_shapes=[pltpu.VMEM((16, 2 * sm.shape[1]), f32)],
        compiler_params=pltpu.CompilerParams(vmem_limit_bytes=62 * 1024 * 1024),
        name="unpack",
    )(oi, og, oz, oo, os, sm, ngain, decay_log)


def per_device(
    tokens_in, segment_ids, norm_gain, proj_gate, proj_inner, proj_step, proj_states,
    conv_inner, conv_inner_bias, conv_states, conv_states_bias, step_bias, decay_log,
    skip_gain, gate_gain, proj_out, cotangent,
):
    inner_all = proj_gate.shape[1] * lax.axis_size("row")
    (
        mixed_out, w_inner, w_gate, w_step, normed, sig, gx, gs, gz, accx, accs, acch, acc1, g4, o4,
        g_gate,
    ) = front(
        inner_all, norm_gain, proj_states, segment_ids, conv_inner, conv_inner_bias, gate_gain,
        conv_states, conv_states_bias, proj_step.T, step_bias, decay_log, skip_gain,
        tokens_in, proj_inner, proj_gate, proj_out, cotangent,
    )
    grad_tokens, oi, og, oz, oo, os, sums = rear(
        accx, accs, acch, acc1, norm_gain, tokens_in, proj_states, w_inner, w_gate, w_step, cotangent,
        normed, sig, g_gate, gx, gs, gz, g4, o4,
    )
    (
        grad_inner, grad_gate, grad_step, grad_out, grad_states, grad_conv_inner,
        grad_conv_inner_bias, grad_conv_states, grad_conv_states_bias, grad_step_bias, grad_decay,
        grad_skip, grad_gate_gain, grad_norm_gain,
    ) = unpack(oi, og, oz, oo, os, sums, norm_gain, decay_log, conv_inner.shape[1])
    return (
        mixed_out, grad_tokens, grad_norm_gain, grad_gate, grad_inner, grad_step.T, grad_states,
        grad_conv_inner, grad_conv_inner_bias, grad_conv_states, grad_conv_states_bias,
        grad_step_bias, grad_decay, grad_skip, grad_gate_gain, grad_out,
    )


def solution(mesh):
    in_specs = (
        P(("dp", "row"), None),
        P("dp", None),
        P(),
        P("col", "row"),
        P("col", "row"),
        P("col", "row"),
        P(),
        P(None, ("row", "col")),
        P(("row", "col")),
        P(),
        P(),
        P(("row", "col")),
        P(("row", "col")),
        P(("row", "col")),
        P(("row", "col")),
        P("row", "col"),
        P(("dp", "row"), "col"),
    )
    out_specs = (
        P(("dp", "row"), "col"),
        P(("dp", "row"), "col"),
        P("col"),
        P("col", "row"),
        P("col", "row"),
        P("col", "row"),
        P(),
        P(None, ("row", "col")),
        P(("row", "col")),
        P(),
        P(),
        P(("row", "col")),
        P(("row", "col")),
        P(("row", "col")),
        P(("row", "col")),
        P("row", "col"),
    )
    return jax.shard_map(
        per_device, mesh=mesh, in_specs=in_specs, out_specs=out_specs, check_vma=False
    )
```

```python
import functools

import jax
import jax.numpy as jnp
from jax import lax
from jax.experimental import pallas as pl
from jax.experimental.pallas import tpu as pltpu
from jax.sharding import PartitionSpec as P

SPAN = 256
HEAD = 64
epsilon = 1e-05
LOG2E = 1.4426950408889634
f32 = jnp.float32
bf16 = jnp.bfloat16
ANY = pl.ANY


def mm(a, b):
    return lax.dot_general(a, b, (((1,), (0,)), ((), ())), preferred_element_type=f32)


def mm_nt(a, b):
    return lax.dot_general(a, b, (((1,), (1,)), ((), ())), preferred_element_type=f32)


def split(v, terms):
    parts = []
    for _ in range(terms):
        part = v.astype(bf16)
        parts.append(part)
        v = v - part.astype(f32)
    return parts


def mm_split(a, exact, terms=2):
    return sum(mm(part, exact) for part in split(a, terms))


def split_mm(exact, b, terms=3):
    return sum(mm(exact, part) for part in split(b, terms))


def spread_matrix(channels):
    heads = lax.broadcasted_iota(jnp.int32, (128, channels), 0)
    cols = lax.broadcasted_iota(jnp.int32, (128, channels), 1)
    low = heads * HEAD
    return jnp.where((cols >= low) & (cols < low + HEAD), 1.0, 0.0).astype(bf16)


def gather_matrix(channels):
    heads = lax.broadcasted_iota(jnp.int32, (channels, 128), 1)
    rows = lax.broadcasted_iota(jnp.int32, (channels, 128), 0)
    low = heads * HEAD
    return jnp.where((rows >= low) & (rows < low + HEAD), 1.0, 0.0).astype(bf16)


def lower_ones():
    rows = lax.broadcasted_iota(jnp.int32, (SPAN, SPAN), 0)
    cols = lax.broadcasted_iota(jnp.int32, (SPAN, SPAN), 1)
    return jnp.where(rows >= cols, 1.0, 0.0).astype(bf16)


def upper_ones():
    rows = lax.broadcasted_iota(jnp.int32, (SPAN, SPAN), 0)
    cols = lax.broadcasted_iota(jnp.int32, (SPAN, SPAN), 1)
    return jnp.where(rows <= cols, 1.0, 0.0).astype(bf16)


def sigmoid(v):
    return 1.0 / (1.0 + jnp.exp(-v))


def widen(first, values, pair):
    return jnp.where(first, values[:, 2 * pair:2 * pair + 1], values[:, 2 * pair + 1:2 * pair + 2])


def head_totals(values, to_heads):
    high = values.astype(bf16)
    low = (values - high.astype(f32)).astype(bf16)
    return mm(jnp.concatenate([high, low], 1), jnp.concatenate([to_heads, to_heads], 0))


def half_masks():
    lane = lax.broadcasted_iota(jnp.int32, (SPAN, 128), 1)
    return lane < HEAD


def rms_rows(tok, gain):
    wide = tok.astype(f32)
    inverse = lax.rsqrt(jnp.mean(wide * wide, -1, keepdims=True) + epsilon)
    return (wide * inverse * gain).astype(bf16)


MESH = pl.DeviceIdType.MESH
SHARE = 4


def lane_block(index, width):
    return pl.ds(pl.multiple_of(index * width, 128), width)


class Links:
    def __init__(self, send, recv, local=None):
        self.send, self.recv, self.local = send, recv, local
        self.used, self.kept, self.sent = 0, 0, []
        dp = lax.axis_index("dp")
        self.groups = lax.axis_size("dp") // SHARE
        self.group = dp // SHARE
        self.x = lax.rem(dp, SHARE) // 2
        self.core = lax.rem(dp, 2)
        self.y = lax.axis_index("row")
        self.z = lax.axis_index("col")
        self.cols = lax.axis_size("col")

    def dp_of(self, group, x, core):
        return group * SHARE + x * 2 + core

    def mate(self):
        return {"dp": self.dp_of(self.group, self.x, 1 - self.core)}

    def across(self):
        return {"dp": self.dp_of(self.group, 1 - self.x, self.core)}

    def other_row(self):
        return {"row": 1 - self.y}

    def col_peer(self, off):
        return lax.rem(self.z + off, self.cols)

    def group_peer(self, off):
        return {"dp": self.dp_of(lax.rem(self.group + off, self.groups), self.x, self.core)}

    def meet(self, far_groups):
        barrier = pltpu.get_barrier_semaphore()
        peers = [self.mate(), self.across(), self.other_row()]
        peers += [{"col": self.col_peer(off)} for off in range(1, self.cols)]
        if far_groups:
            peers += [self.group_peer(off) for off in range(1, self.groups)]
        for peer in peers:
            pl.semaphore_signal(barrier, inc=1, device_id=peer, device_id_type=MESH)
        pl.semaphore_wait(barrier, len(peers))

    def make(self, src, dst, peer, when=None, track=True):
        at = self.used
        self.used += 1
        copy = pltpu.make_async_remote_copy(
            src_ref=src, dst_ref=dst, send_sem=self.send.at[at], recv_sem=self.recv.at[at],
            device_id=peer, device_id_type=MESH,
        )
        if track:
            self.sent.append((copy, when))
        return copy

    def go(self, src, dst, peer, track=True):
        copy = self.make(src, dst, peer, track=track)
        copy.start()
        return copy

    def keep(self, src, dst):
        copy = pltpu.make_async_copy(src, dst, self.local.at[self.kept])
        self.kept += 1
        return copy

    def finish(self):
        for copy, when in self.sent:
            if when is None:
                copy.wait_send()
            else:
                pl.when(when)(copy.wait_send)


class Steps:
    def __init__(self):
        self.stages = []

    def add(self, remote, local=(), before=None):
        self.stages.append((remote, list(local), before))

    def drain(self, t):
        for remote, _, _ in self.stages:
            for c in remote:
                c.wait_send()
                t.sent = [(copy, when) for copy, when in t.sent if copy is not c]

    def run(self, s):
        if 0 < s <= len(self.stages):
            remote, local, _ = self.stages[s - 1]
            for c in remote:
                c.wait_recv()
            for c in local:
                c.wait()
        if s < len(self.stages):
            remote, local, before = self.stages[s]
            if before is not None:
                before()
            for c in remote + local:
                c.start()


def spread_steps(t, view, steps):
    x, y = t.x, t.y
    first, second = view(x, y, 0), view(x, y, 1)
    steps.add([t.make(first, first, t.other_row()), t.make(second, second, t.across())])
    first, second = view(x, None, 0), view(None, y, 1)
    steps.add([t.make(first, first, t.across()), t.make(second, second, t.other_row())])
    every = view(None, None, None)
    steps.add([t.make(every, every, t.mate())])
    return steps


def half_lines(part, half):
    return slice(None) if half is None else pl.ds(half * (part // 2), part // 2)


def column_steps(t, src, dst, width):
    part = src.shape[0] // SHARE
    x, y, z, core = t.x, t.y, t.z, t.core
    rows = pl.ds(pl.multiple_of((x * 2 + core) * part, 16), part)
    lanes = lane_block(y, width)
    steps = Steps()
    here = dst.at[z, x, core, :, lanes]
    remote = []
    for off in range(1, t.cols):
        to = t.col_peer(off)
        remote.append(t.make(src.at[rows, lane_block(to, width)], here, {"col": to}))
    steps.add(remote, [t.keep(src.at[rows, lane_block(z, width)], here)])

    def view(at_x, at_y, half):
        return dst.at[:, slice(None) if at_x is None else at_x, core, half_lines(part, half),
                      slice(None) if at_y is None else lanes]

    return spread_steps(t, view, steps)


def row_steps(t, src, dst, width):
    part = src.shape[0] // t.cols // SHARE
    x, y, z, core = t.x, t.y, t.z, t.core

    def rows(to):
        return pl.ds(pl.multiple_of((to * SHARE + x * 2 + core) * part, 16), part)

    steps = Steps()
    here = dst.at[y, x, core, :, lane_block(z, width)]
    remote = []
    for off in range(1, t.cols):
        to = t.col_peer(off)
        remote.append(t.make(src.at[rows(to), :], here, {"col": to}))
    steps.add(remote, [t.keep(src.at[rows(z), :], here)])

    def view(at_x, at_y, half):
        return dst.at[slice(None) if at_y is None else at_y, slice(None) if at_x is None else at_x,
                      core, half_lines(part, half), :]

    return spread_steps(t, view, steps)


def gather_steps(t, own, whole, rows):
    width = own.shape[1]
    z = t.z
    mate, far = z + 1 - 2 * lax.rem(z, 2), lax.rem(z + 2, 4)
    here, there = whole.at[rows, lane_block(z, width)], whole.at[rows, lane_block(far, width)]
    steps = Steps()
    cross = t.make(own.at[rows, :], here, {"col": far})
    near = t.make(own.at[rows, :], here, {"col": mate})
    steps.add([cross, near], [t.keep(own.at[rows, :], here)])
    steps.add([t.make(there, there, {"col": mate})])
    return steps


def mm_tn(a, b):
    return lax.dot_general(a, b, (((0,), (0,)), ((), ())), preferred_element_type=f32)


def add_bf16(a, b):
    return (a.astype(f32) + b.astype(f32)).astype(bf16)


class PairSum:
    def __init__(self, t, part, near, far_in, rows):
        z = t.z
        mate = z + 1 - 2 * lax.rem(z, 2)
        far = lax.rem(z + 2, 4)
        mate_far = lax.rem(mate + 2, 4)
        width = near.shape[-1]
        self.part, self.near, self.far_in, self.rows = part, near, far_in, rows
        self.own, self.far = lane_block(z, width), lane_block(far, width)
        to_mate = [
            t.make(part.at[rows, lane_block(mate_far, width)], near.at[1, rows], {"col": mate}),
            t.make(part.at[rows, lane_block(mate, width)], near.at[0, rows], {"col": mate}),
        ]
        self.first, self.second = to_mate
        self.across = t.make(near.at[1, rows], far_in.at[rows], {"col": far})

    def start(self):
        self.first.start()

    def forward(self, both=True):
        self.first.wait_recv()
        count = self.rows.size // 64

        def body(i, c):
            at = pl.ds(pl.multiple_of(self.rows.start + i * 64, 16), 64)
            self.near[1, at] = add_bf16(self.near[1, at], self.part[at, self.far])
            return c

        lax.fori_loop(0, count, body, 0)
        self.across.start()
        if both:
            self.second.start()

    def arrive(self):
        self.second.wait_recv()
        self.across.wait_recv()

    def total(self, at):
        return (
            self.part[at, self.own].astype(f32) + self.near[0, at].astype(f32)
            + self.far_in[at].astype(f32)
        )


def sum_far_groups(t, own, got):
    if t.groups == 1:
        return
    more = [t.go(own, got.at[off - 1], t.group_peer(off), False) for off in range(1, t.groups)]
    for c in more:
        c.wait()

    def total(spare):
        for off in range(1, t.groups):
            back = t.keep(got.at[off - 1], spare)
            back.start()
            back.wait()
            own[...] = add_bf16(own[...], spare[...])

    pl.run_scoped(total, pltpu.VMEM(own.shape, own.dtype))


def column_sums(t, g, a1, yx, xy, yx2, xy2, a4, far):
    x, y, core = t.x, t.y, t.core
    width = a4.shape[-1]
    h = a4.shape[1] // 2
    mine, other = lane_block(y, width), lane_block(1 - y, width)
    top, low = pl.ds(0, h), pl.ds(h, h)
    steps = Steps()
    steps.add([t.make(g.at[:, :, 1 - core], a1, t.mate())])

    def add_core():
        def body(i, c):
            for j in range(2):
                a1[i, j] = add_bf16(a1[i, j], g[i, j, core])
            return c

        lax.fori_loop(0, t.cols, body, 0)

    steps.add([
        t.make(a1.at[:, :, top, other], yx, t.other_row()),
        t.make(a1.at[:, 1 - x, low, :], xy, t.across()),
    ], (), add_core)

    def add_first():
        def body(i, c):
            for j in range(2):
                yx[i, j] = add_bf16(yx[i, j], a1[i, j, top, mine])
            xy[i] = add_bf16(xy[i], a1[i, x, low, :])
            return c

        lax.fori_loop(0, t.cols, body, 0)

    steps.add([
        t.make(yx.at[:, 1 - x], yx2, t.across()),
        t.make(xy.at[:, :, other], xy2, t.other_row()),
    ], (), add_first)

    def add_second():
        def body(i, c):
            a4[i, top] = add_bf16(yx2[i], yx[i, x])
            a4[i, low] = add_bf16(xy2[i], xy[i, :, mine])
            return c

        lax.fori_loop(0, t.cols, body, 0)
        sum_far_groups(t, a4, far)

    steps.add([], (), add_second)
    return steps


def column_sum_shapes(cols, q, w):
    h = q // 2
    return [((cols, 2, q, 2 * w), bf16), ((cols, 2, h, w), bf16), ((cols, h, 2 * w), bf16),
            ((cols, h, w), bf16), ((cols, h, w), bf16), ((cols, q, w), bf16)]


def column_home(t, a4, o, steps):
    x, z, core = t.x, t.z, t.core
    here = o.at[x, core, :, lane_block(z, a4.shape[-1])]
    steps.add(
        [t.make(a4.at[t.col_peer(off)], here, {"col": t.col_peer(off)}) for off in range(1, t.cols)],
        [t.keep(a4.at[z], here)],
    )
    steps.add([t.make(o.at[x, core], o.at[x, core], t.across())])
    steps.add([t.make(o.at[:, core], o.at[:, core], t.mate())])
    return steps


def row_sums(t, g, a1, yx, xy, yx2, xy2, a4, far):
    x, y, core = t.x, t.y, t.core
    h = a4.shape[0] // 2
    top, low = pl.ds(0, h), pl.ds(h, h)
    steps = Steps()
    steps.add([t.make(g.at[:, :, 1 - core], a1, t.mate())])

    def add_core():
        def body(i, c):
            for j in range(2):
                a1[i, j] = add_bf16(a1[i, j], g[i, j, core])
            return c

        lax.fori_loop(0, 2, body, 0)

    steps.add([
        t.make(a1.at[1 - y, :, top], yx, t.other_row()),
        t.make(a1.at[:, 1 - x, low], xy, t.across()),
    ], (), add_core)

    def add_first():
        for j in range(2):
            yx[j] = add_bf16(yx[j], a1[y, j, top])
            xy[j] = add_bf16(xy[j], a1[j, x, low])

    steps.add([
        t.make(yx.at[1 - x], yx2, t.across()), t.make(xy.at[1 - y], xy2, t.other_row()),
    ], (), add_first)

    def add_second():
        a4[top] = add_bf16(yx2[...], yx[x])
        a4[low] = add_bf16(xy2[...], xy[y])
        sum_far_groups(t, a4, far)

    steps.add([], (), add_second)
    return steps


def row_sum_shapes(q, width):
    h = q // 2
    return [((2, 2, q, width), bf16), ((2, h, width), bf16), ((2, h, width), bf16),
            ((h, width), bf16), ((h, width), bf16), ((q, width), bf16)]


def row_home(t, a4, o, steps):
    x, z, core = t.x, t.z, t.core
    width = o.shape[-1]
    here = o.at[z, x, core]
    steps.add(
        [t.make(a4.at[:, lane_block(t.col_peer(off), width)], here, {"col": t.col_peer(off)})
         for off in range(1, t.cols)],
        [t.keep(a4.at[:, lane_block(z, width)], here)],
    )
    steps.add([t.make(o.at[:, x, core], o.at[:, x, core], t.across())])
    steps.add([t.make(o.at[:, :, core], o.at[:, :, core], t.mate())])
    return steps


def full_sums(t, g, s1, s2, s3, s4, s5, far, o):
    x, y, z, core = t.x, t.y, t.z, t.core
    steps = Steps()
    steps.add([t.make(g.at[:, :, :, 1 - core], s1, t.mate())])

    def add_core():
        def body(i, c):
            for j in range(2):
                for k in range(2):
                    s1[i, j, k] = add_bf16(s1[i, j, k], g[i, j, k, core])
            return c

        lax.fori_loop(0, t.cols, body, 0)

    steps.add([t.make(s1.at[:, 1 - y], s2, t.other_row())], (), add_core)

    def add_row():
        def body(i, c):
            for k in range(2):
                s2[i, k] = add_bf16(s2[i, k], s1[i, y, k])
            return c

        lax.fori_loop(0, t.cols, body, 0)

    steps.add([t.make(s2.at[:, 1 - x], s3, t.across())], (), add_row)

    def add_x():
        def body(i, c):
            s4[i] = add_bf16(s3[i], s2[i, x])
            return c

        lax.fori_loop(0, t.cols, body, 0)
        sum_far_groups(t, s4, far)

    steps.add(
        [t.make(s4.at[t.col_peer(off)], s5.at[off - 1], {"col": t.col_peer(off)})
         for off in range(1, t.cols)], (), add_x,
    )

    def add_cols():
        total = s4[z].astype(f32)
        for off in range(1, t.cols):
            total = total + s5[off - 1].astype(f32)
        s4[z] = total.astype(bf16)

    here = o.at[z, y, x, core]
    steps.add(
        [t.make(s4.at[z], here, {"col": t.col_peer(off)}) for off in range(1, t.cols)],
        [t.keep(s4.at[z], here)], add_cols,
    )
    here = o.at[:, y, x, core]
    steps.add([t.make(here, here, t.other_row())])
    here = o.at[:, :, x, core]
    steps.add([t.make(here, here, t.across())])
    here = o.at[:, :, :, core]
    steps.add([t.make(here, here, t.mate())])
    return steps


def small_sums(t, sm, msum, mgot, out, rest):
    steps = Steps()
    steps.add([t.make(sm, mgot.at[0], t.mate())])

    def add_core():
        msum[0] = sm[...] + mgot[0]

    steps.add([t.make(msum.at[0], mgot.at[1], t.other_row())], (), add_core)

    def add_row():
        msum[1] = msum[0] + mgot[1]

    steps.add([t.make(msum.at[1], mgot.at[2], t.across())], (), add_row)

    def add_x():
        msum[2] = msum[1] + mgot[2]
        if t.groups > 1:
            more = [t.go(msum.at[2], mgot.at[5 + off], t.group_peer(off), False)
                    for off in range(1, t.groups)]
            for c in more:
                c.wait()
            total = msum[2]
            for off in range(1, t.groups):
                total = total + mgot[5 + off]
            msum[2] = total

    last = pl.ds(rest, sm.shape[0] - rest)
    steps.add(
        [t.make(msum.at[2, last], mgot.at[2 + off, last], {"col": t.col_peer(off)})
         for off in range(1, t.cols)], (), add_x,
    )

    def done():
        out[0:rest] = msum[2, 0:rest]
        out[rest:] = msum[2, rest:] + mgot[3, rest:] + mgot[4, rest:] + mgot[5, rest:]

    steps.add([], (), done)
    return steps


def front_kernel(
    inner_total,
    ngain_v, w_states, segments, taps_inner, bias_inner, gain_gate, taps_states, bias_states, step_all,
    step_bias, decay_log, skip_gain,
    tok_h, inner, gate, out, cot,
    mixed_o, wi_o, wg_o, ws_o, normed_o, sig_o, gx_o, gs_o, gz_o, accx_o, accs_o, acch_o, acc_o,
    gg4_o, go4_o, ggate_o, far_g, far_o,
    wi, wg, wo, ws2, ws, step_w, cots, par, spar, head, head_own, head_in, halo_in, tok, tok_own,
    meta, hmeta, docrow, docs,
    normed_s, pre_s, spre_s, sd_s, ssd_s, x_s, wr_s, step_s, r_s, sig_s, hpre_s, hspre_s, sprev_s,
    gated_s, ggate_s, gy_s, dr_s, fresh_s, y_s, gate_s, gg_s, gs_s, gz_s,
    out_near, out_far, sums_s, sums_in, xbuf, sbuf, mem, pass_out, state_in, dstate_in, pass_back,
    hx, hs, hx_in, hs_in, accx, accs, acch, acc_s, gg, g1, g2, g3, g5, g6, g4, o1, o2, o3, o5, o6, o4,
    tile_a, tile_b, wide_tile,
    send, recv, local,
):
    t = Links(send, recv, local)
    x, y, z, core = t.x, t.y, t.z, t.core
    blocks = tok.shape[0] // SPAN
    channels = x_s.shape[1]
    half = channels // 2
    outputs = []

    def write(src, dst):
        copy = t.keep(src, dst)
        copy.start()
        outputs.append(copy)

    def load(src, dst):
        copy = t.keep(src, dst)
        copy.start()
        return copy

    loads = [load(tok_h, tok), load(tok_h.at[:, lane_block(z, cot.shape[1])], tok_own)]
    own_lanes = lane_block(y, half)
    few = [
        t.make(par.at[:, own_lanes], par.at[:, own_lanes], t.other_row()),
        t.make(head_own, head_in, t.other_row()),
        t.make(tok_h.at[pl.ds(tok.shape[0] - 16, 16), :], halo_in, t.other_row()),
    ]
    block = inner.shape[1] // t.cols
    get_inner = column_steps(t, inner, wi, block)
    get_step = column_steps(t, step_w, ws2, step_w.shape[1] // t.cols)
    get_gate = column_steps(t, gate, wg, block)
    get_out = row_steps(t, out, wo, out.shape[1])
    half_rows = tok.shape[0] // 2
    get_cot = [gather_steps(t, cot, cots, pl.ds(n * half_rows, half_rows)) for n in range(2)]
    pass_state = t.make(pass_out, state_in, t.other_row())
    pass_back_state = t.make(pass_back, dstate_in, t.other_row())
    halo_x = t.make(hx, hx_in, t.other_row())
    halo_s = t.make(hs, hs_in, t.other_row())
    out_part = tok
    sum_gate = column_sums(t, gg, g1, g2, g3, g5, g6, g4, far_g)
    go = wo
    sum_out = row_sums(t, go, o1, o2, o3, o5, o6, o4, far_o)
    out_sums = [PairSum(t, out_part, out_near, out_far, pl.ds(b * SPAN, SPAN)) for b in range(blocks)]
    pass_sums = [
        t.make(sums_s, sums_in.at[off - 1], {"col": t.col_peer(off)}) for off in range(1, t.cols)
    ]
    t.meet(True)
    get_inner.run(0)

    own_heads = step_bias.shape[0]
    lane8 = lax.broadcasted_iota(jnp.int32, (8, 128), 1)
    row8 = lax.broadcasted_iota(jnp.int32, (8, 128), 0)
    scalars = jnp.zeros((8, 128), f32)
    for j in range(own_heads):
        here = lane8 == y * own_heads + j
        scalars = scalars + jnp.where(here & (row8 == 0), step_bias[j], 0.0)
        scalars = scalars + jnp.where(here & ((row8 == 1) | (row8 == 3)), decay_log[j], 0.0)
        scalars = scalars + jnp.where(here & (row8 == 2), skip_gain[j], 0.0)
    own_lane = (lane8 >= y * own_heads) & (lane8 < (y + 1) * own_heads)
    rate = jnp.where(own_lane, -jnp.exp(scalars), 0.0)
    head_own[...] = jnp.where(row8 == 1, rate * LOG2E, jnp.where(row8 == 3, rate, scalars))
    par[:, own_lanes] = jnp.zeros((8, half), f32)
    par[0:4, own_lanes] = taps_inner[...]
    par[4:5, own_lanes] = bias_inner[...].reshape(1, half)
    par[5:6, own_lanes] = gain_gate[...].reshape(1, half)
    spar[...] = jnp.zeros_like(spar)
    spar[0:4, :] = taps_states[...]
    spar[4:5, :] = bias_states[...].reshape(1, 256)
    every = step_all.shape[0]
    src = lax.broadcasted_iota(jnp.int32, (every, t.cols * 128), 0)
    dst = lax.broadcasted_iota(jnp.int32, (every, t.cols * 128), 1)
    place = jnp.zeros((every, t.cols * 128), f32)
    for c in range(t.cols):
        low = c * 128 + y * own_heads - c * own_heads
        mine = (src >= c * own_heads) & (src < (c + 1) * own_heads)
        place = place + jnp.where(mine & (dst - src == low), 1.0, 0.0)
    step_w[...] = mm_tn(step_all[...], place.astype(bf16)).astype(bf16)
    get_step.run(0)
    for c in few:
        c.start()

    length = tok.shape[0]
    docs[:, 0:128] = jnp.full((8, 128), -1.0, f32)
    docs[:, 128:128 + 2 * length] = jnp.broadcast_to(segments[...].astype(f32), (8, 2 * length))
    docs[:, 128 + 2 * length:] = jnp.full((8, 128), -1.0, f32)
    window = docs[:, pl.ds(pl.multiple_of(y * length, 128), length + 256)]
    span_w = length + 256
    docrow[...] = window[:, 128:128 + length]
    same_before = [(window == pltpu.roll(window, k, 1)).astype(f32) for k in range(1, 4)]
    same_after = [(window == pltpu.roll(window, span_w - k, 1)).astype(f32) for k in range(1, 4)]
    row16 = lax.broadcasted_iota(jnp.int32, (8, SPAN), 0)
    for i in range(blocks):
        at = slice(128 + i * SPAN, 128 + (i + 1) * SPAN)
        here = window[:, at]
        before = window[0:1, 127 + i * SPAN:128 + i * SPAN]
        last = window[0:1, 127 + (i + 1) * SPAN:128 + (i + 1) * SPAN]
        low = jnp.where(row16 == 0, here, 0.0)
        for k in range(1, 4):
            low = low + jnp.where(row16 == k, same_before[k - 1][:, at], 0.0)
        low = low + jnp.where((row16 == 4) & (here == before), 1.0, 0.0)
        low = low + jnp.where((row16 == 5) & (here == last), 1.0, 0.0)
        low = low + jnp.where((row16 == 6) & (before == last), 1.0, 0.0)
        high = jnp.zeros((8, SPAN), f32)
        for k in range(1, 4):
            high = high + jnp.where(row16 == k - 1, same_after[k - 1][:, at], 0.0)
        rows128 = jnp.concatenate([low, high, jnp.zeros((112, SPAN), f32)], 0)
        meta[i * SPAN:(i + 1) * SPAN, :] = jnp.transpose(rows128)
    row16 = lax.broadcasted_iota(jnp.int32, (8, 128), 0)
    high = jnp.zeros((8, 128), f32)
    for k in range(1, 4):
        high = high + jnp.where(row16 == k - 1, same_after[k - 1][:, 0:128], 0.0)
    rows128 = jnp.concatenate([jnp.zeros((8, 128), f32), high, jnp.zeros((112, 128), f32)], 0)
    hmeta[...] = jnp.transpose(rows128)[120:128]

    gain = ngain_v[...].reshape(1, -1)
    for c in loads:
        c.wait()

    def rows_of(i):
        return pl.ds(pl.multiple_of(i * SPAN, SPAN), SPAN)

    def over_lanes(column):
        return jnp.broadcast_to(column, (SPAN, 128))

    def conv_silu(buf, lanes, here, taps, marks):
        v = taps[4:5, lanes] + taps[0:1, lanes] * here
        for k in range(1, 4):
            v = v + marks[k - 1] * (taps[k:k + 1, lanes] * buf[8 - k:8 - k + SPAN, lanes])
        sg = sigmoid(v)
        return v * sg, sg * (1.0 + v * (1.0 - sg))

    for c in few:
        c.wait_recv()
    hn = rms_rows(halo_in[...], gain)
    h_states = mm(hn, w_states[...])[8:16]
    sbuf[0:8, :] = h_states
    hspre_s[...] = h_states

    def norm_block(i, carry):
        at = rows_of(i)

        @pl.when(i > 0)
        def _():
            sbuf[0:8, :] = sbuf[SPAN:SPAN + 8, :]

        wide_tok = tok[at, :].astype(f32)
        inverse = lax.rsqrt(jnp.mean(wide_tok * wide_tok, -1, keepdims=True) + epsilon)
        normed = (wide_tok * inverse * gain).astype(bf16)
        normed_s[at, :] = normed
        s_pre = mm(normed, w_states[...])
        sbuf[8:SPAN + 8, :] = s_pre
        spre_s[at, :] = s_pre.astype(bf16)
        earlier = [over_lanes(meta[at, k:k + 1]) for k in range(1, 4)]
        for lanes in (slice(0, 128), slice(128, 256)):
            sact, sslope = conv_silu(sbuf, lanes, sbuf[8:SPAN + 8, lanes], spar, earlier)
            wr_s[at, lanes] = sact.astype(bf16)
            ssd_s[at, lanes] = sslope.astype(bf16)
        sig_s[at, :] = jnp.broadcast_to(inverse, (SPAN, 128))

        @pl.when(i == 0)
        def _():
            get_inner.run(1)
            get_step.run(1)
            get_gate.run(0)
            get_out.run(0)
            get_cot[0].run(0)

        return carry

    lax.fori_loop(0, blocks, norm_block, 0)
    head[...] = head_own[...] + head_in[...]
    get_inner.run(2)
    get_step.run(2)
    get_inner.run(3)
    get_step.run(3)
    get_gate.run(1)
    get_inner.run(4)
    get_step.run(4)
    wide_in = normed_s.shape[1]
    ws[...] = (
        ws2[:, :, :, :, 0:128].reshape(wide_in, 128) + ws2[:, :, :, :, 128:256].reshape(wide_in, 128)
    )
    spread = spread_matrix(channels)

    def w_of(ref):
        return ref[...].reshape(-1, ref.shape[-1])

    first = half_masks()
    h_inner = mm(hn, w_of(wi))[8:16]
    xbuf[0:8, :] = h_inner
    hpre_s[...] = h_inner
    mem[...] = jnp.zeros_like(mem)

    def entry(i, carry):
        at = rows_of(i)

        @pl.when(i > 0)
        def _():
            xbuf[0:8, :] = xbuf[SPAN:SPAN + 8, :]

        normed = normed_s[at, :]
        x_pre = mm(normed, w_of(wi))
        xbuf[8:SPAN + 8, :] = x_pre
        pre_s[at, :] = x_pre.astype(bf16)
        marks = meta[at, :]
        wr = wr_s[at, :]
        earlier = [over_lanes(marks[:, k:k + 1]) for k in range(1, 4)]
        for pair in range(channels // 128):
            lanes = slice(pair * 128, pair * 128 + 128)
            act, slope = conv_silu(xbuf, lanes, xbuf[8:SPAN + 8, lanes], par, earlier)
            x_s[at, lanes] = act.astype(bf16)
            sd_s[at, lanes] = slope.astype(bf16)

        raw = mm(normed, ws[...]) + head[0:1, :]
        step = jnp.maximum(raw, 0.0) + jnp.log1p(jnp.exp(-jnp.abs(raw)))
        lane = lax.broadcasted_iota(jnp.int32, (SPAN, 128), 1)
        sig_s[at, :] = jnp.where(lane == 127, sig_s[at, :], sigmoid(raw))
        step_s[at, :] = step
        r = split_mm(lower_ones(), step * head[1:2, :])
        r_s[at, :] = r
        last = r[SPAN - 1:SPAN, :]
        to_end = jnp.exp2(jnp.minimum(last - r, 0.0)) * marks[:, 5:6]
        coef = to_end * step
        for pair in range(channels // 128):
            lanes = slice(pair * 128, pair * 128 + 128)
            tile_a[:, lanes] = (widen(first, coef, pair) * x_s[at, lanes].astype(f32)).astype(bf16)
        w_t = jnp.transpose(wr[:, 0:128].astype(f32)).astype(bf16)
        fresh = mm(w_t, tile_a[...])
        fresh_s[i] = fresh
        mem[...] = keep_of(last, marks) * mem[...] + fresh

        @pl.when(i == 0)
        def _():
            get_gate.run(2)
            get_out.run(1)
            get_cot[1].run(0)

        @pl.when(i == 2)
        def _():
            get_gate.run(3)
            get_out.run(2)
            get_cot[0].run(1)

        return carry

    def keep_of(last, marks):
        return mm_split(jnp.broadcast_to(jnp.exp2(last) * marks[0:1, 6:7], (8, 128)), spread)[0:1]

    lax.fori_loop(0, blocks, entry, 0)
    pass_out[...] = mem[...].astype(bf16)
    pass_state.start()
    get_gate.run(4)
    for src, dst in (
        (normed_s, normed_o), (sig_s, sig_o), (wi, wi_o), (wg, wg_o), (ws, ws_o),
    ):
        write(src, dst)

    def gate_block(i, carry):
        at = rows_of(i)
        gate_s[at, :] = mm(normed_s[at, :], w_of(wg))
        return carry

    lax.fori_loop(0, blocks, gate_block, 0)

    pass_state.wait_recv()
    mem[...] = state_in[...].astype(f32) * jnp.where(y == 1, 1.0, 0.0)
    get_out.run(3)
    skip = mm_split(jnp.broadcast_to(head[2:3, :], (8, 128)), spread)[0:1]

    def scan(i, carry):
        at = rows_of(i)
        marks = meta[at, :]
        w_low = wr_s[at, 0:128]
        r_low = wr_s[at, 128:256]
        r = r_s[at, :]
        r_t = jnp.transpose(r)
        rows = lax.broadcasted_iota(jnp.int32, (SPAN, SPAN), 0)
        cols = lax.broadcasted_iota(jnp.int32, (SPAN, SPAN), 1)
        allowed = (rows >= cols) & (marks[:, 0:1] == docrow[0:1, at])
        scores = jnp.where(allowed, mm_nt(r_low, w_low), 0.0)
        step = step_s[at, :]
        sprev = mem[...].astype(bf16)
        sprev_s[i] = sprev
        linked = jnp.exp2(r) * marks[:, 4:5]
        y_s[at, :] = mm(r_low, sprev)
        for pair in range(channels // 128):
            lanes = slice(pair * 128, pair * 128 + 128)
            wide = x_s[at, lanes].astype(f32)
            xp = (widen(first, step, pair) * wide).astype(bf16)
            total = y_s[at, lanes] * widen(first, linked, pair) + skip[:, lanes] * wide
            for part in range(2):
                h = 2 * pair + part
                decay = jnp.exp2(jnp.minimum(r[:, h:h + 1] - r_t[h:h + 1, :], 0.0))
                mixing = (scores * decay).astype(bf16)
                own = jnp.where(first if part == 0 else ~first, xp, jnp.zeros_like(xp))
                total = total + mm(mixing, own)
            y_s[at, lanes] = total
        last = r[SPAN - 1:SPAN, :]
        mem[...] = keep_of(last, marks) * mem[...] + fresh_s[i]

        @pl.when(i == 3)
        def _():
            get_cot[1].run(1)

        return carry

    lax.fori_loop(0, blocks, scan, 0)
    get_out.run(4)

    def project(i, carry):
        at = rows_of(i)
        g = gate_s[at, :]
        mixed = y_s[at, :] * (g * sigmoid(g))
        out_part[at, :] = mm((mixed * par[5:6, :]).astype(bf16), w_of(wo)).astype(bf16)
        return carry

    lax.fori_loop(0, blocks, project, 0)
    for s in out_sums:
        s.start()
    get_cot[0].run(2)
    ones = jnp.ones((8, channels), bf16)

    def totals_of(i, carry):
        at = rows_of(i)
        gg = mm_nt(cots[at, :], w_of(wo))
        gg_s[at, :] = gg.astype(bf16)
        g = gate_s[at, :]
        mixed = y_s[at, :] * (g * sigmoid(g))
        sq = sum(mm_nt(ones, part) for part in split(mixed * mixed, 2))
        pr = sum(mm_nt(ones, part) for part in split(mixed * (par[5:6, :] * gg), 2))
        for n in range(2):
            lanes = slice(n * 128, n * 128 + 128)
            sums_s[pl.ds(2 * i + n, 1), :] = sq[0:1, lanes]
            sums_s[pl.ds(2 * blocks + 2 * i + n, 1), :] = pr[0:1, lanes]
        return carry

    lax.fori_loop(0, blocks // 2, totals_of, 0)
    get_cot[1].run(2)
    lax.fori_loop(blocks // 2, blocks, totals_of, 0)
    for c in pass_sums:
        c.start()
    for c in pass_sums:
        c.wait_recv()
    mem[...] = jnp.zeros_like(mem)
    acc_s[...] = jnp.zeros_like(acc_s)
    gather = gather_matrix(channels)

    def scale_of(i):
        columns = []
        for base in (0, 2 * blocks):
            rows = pl.ds(base + 2 * i, 2)
            pair = sums_s[rows, :]
            for off in range(1, t.cols):
                pair = pair + sums_in[off - 1, rows, :]
            columns.append(jnp.concatenate([pair[0:1], pair[1:2]], 1))
        row = lax.broadcasted_iota(jnp.int32, (8, SPAN), 0)
        both = jnp.where(row == 0, jnp.broadcast_to(columns[0], (8, SPAN)),
                         jnp.broadcast_to(columns[1], (8, SPAN)))
        totals = jnp.transpose(both)
        return lax.rsqrt(totals[:, 0:1] / inner_total + epsilon), totals[:, 1:2] / inner_total

    def turn(back_i, carry):
        i = blocks - 1 - back_i
        at = rows_of(i)
        marks = meta[at, :]
        scale, cross = scale_of(i)
        r = r_s[at, :]
        linked = jnp.exp2(r) * marks[:, 4:5]
        row = lax.broadcasted_iota(jnp.int32, (8, 128), 0)
        dr = jnp.zeros((SPAN, 128), f32)
        for pair in range(channels // 128):
            lanes = slice(pair * 128, pair * 128 + 128)
            yv = y_s[at, lanes]
            g = gate_s[at, lanes]
            sg = sigmoid(g)
            sl = g * sg
            gg = gg_s[at, lanes].astype(f32)
            ngate = par[5:6, lanes]
            normal = yv * sl * scale
            gated_s[at, lanes] = (normal * ngate).astype(bf16)
            g_mixed = scale * (ngate * gg - normal * (scale * cross))
            ggate_s[at, lanes] = (g_mixed * yv * (sg * (1.0 + g * (1.0 - sg)))).astype(bf16)
            gy = (g_mixed * sl).astype(bf16)
            gy_s[at, lanes] = gy
            gyw = gy.astype(f32)
            wide = x_s[at, lanes].astype(f32)
            dr = dr + head_totals(gyw * (yv - skip[:, lanes] * wide), gather[lanes, :])
            ggain = jnp.sum(gg * normal, 0, keepdims=True)
            gskip = jnp.sum(gyw * wide, 0, keepdims=True)
            acc_s[:, lanes] += jnp.where(row == 0, ggain, jnp.where(row == 1, gskip, 0.0))
            tile_a[:, lanes] = (widen(first, linked, pair) * gyw).astype(bf16)
        dr_s[at, :] = dr
        r_t = jnp.transpose(wr_s[at, 128:256].astype(f32)).astype(bf16)
        dfresh = mm(r_t, tile_a[...])
        fresh_s[i] = dfresh
        for b in range(blocks):
            pl.when(back_i == b)(out_sums[b].forward)
        mem[...] = keep_of(r[SPAN - 1:SPAN, :], marks) * mem[...] + dfresh
        return carry

    lax.fori_loop(0, blocks, turn, 0)
    pass_back[...] = mem[...].astype(bf16)
    pass_back_state.start()

    def grad_out(i, carry):
        rows = pl.ds(pl.multiple_of(i * half, 128), half)
        for n in range(2):
            lanes = slice(n * wide_in // 2, (n + 1) * wide_in // 2)
            value = mm_tn(gated_s[:, rows], cots[:, lanes]).astype(bf16)
            go[i, :, :, :, lanes] = value.reshape(go.shape[1:4] + (wide_in // 2,))
        return carry

    get_out.drain(t)
    lax.fori_loop(0, 2, grad_out, 0)
    sum_out.run(0)

    def grad_gate(i, carry):
        rows = pl.ds(pl.multiple_of(i * (wide_in // t.cols), 128), wide_in // t.cols)
        gg[i] = mm_tn(normed_s[:, rows], ggate_s[...]).astype(bf16).reshape(gg.shape[1:])
        return carry

    lax.fori_loop(0, t.cols, grad_gate, 0)
    sum_gate.run(0)
    sum_out.run(1)
    write(ggate_s, ggate_o)
    accx[...] = jnp.zeros_like(accx)
    accs[...] = jnp.zeros_like(accs)
    acch[...] = jnp.zeros_like(acch)
    xbuf[...] = jnp.zeros_like(xbuf)
    sbuf[...] = jnp.zeros_like(sbuf)
    pass_back_state.wait_recv()
    mem[...] = dstate_in[...].astype(f32) * jnp.where(y == 0, 1.0, 0.0)
    gx_s = gg_s

    def back(back_i, carry):
        i = blocks - 1 - back_i
        at = rows_of(i)

        @pl.when(back_i > 0)
        def _():
            xbuf[SPAN + 8:SPAN + 16, :] = xbuf[8:16, :]
            sbuf[SPAN + 8:SPAN + 16, :] = sbuf[8:16, :]

        marks = meta[at, :]
        w_low = wr_s[at, 0:128]
        r_low = wr_s[at, 128:256]
        r = r_s[at, :]
        r_t = jnp.transpose(r)
        step = step_s[at, :]
        last = r[SPAN - 1:SPAN, :]
        rows = lax.broadcasted_iota(jnp.int32, (SPAN, SPAN), 0)
        cols = lax.broadcasted_iota(jnp.int32, (SPAN, SPAN), 1)
        allowed = (rows <= cols) & (marks[:, 0:1] == docrow[0:1, at])
        scores = jnp.where(allowed, mm_nt(w_low, r_low), 0.0)
        ds = mem[...]
        ds_low = ds.astype(bf16)
        to_end = jnp.exp2(jnp.minimum(last - r, 0.0)) * marks[:, 5:6]
        linked = jnp.exp2(r) * marks[:, 4:5]
        wide_tile[...] = mm(w_low, ds_low)
        after = [over_lanes(marks[:, 7 + k:8 + k]) for k in range(1, 4)]
        keep = mm_split(jnp.broadcast_to(jnp.exp2(last) * marks[0:1, 6:7], (8, 128)), spread)[0:1]
        final = jnp.where(back_i == blocks - 1, 1.0, 0.0)

        def conv_back(buf, lanes, gv, base, taps, acc, halo_pre, out, halo_out):
            buf[8:SPAN + 8, lanes] = gv
            cols_here = gv.shape[1]
            total = taps[0:1, lanes] * gv
            sums = [jnp.sum(gv * base, 0, keepdims=True)]
            halo = jnp.zeros((8, cols_here), f32)
            hsum = []
            for k in range(1, 4):
                moved = after[k - 1] * buf[8 + k:8 + k + SPAN, lanes]
                total = total + taps[k:k + 1, lanes] * moved
                sums.append(jnp.sum(moved * base, 0, keepdims=True))
                hmoved = hmeta[:, 7 + k:8 + k] * buf[k:8 + k, lanes]
                halo = halo + taps[k:k + 1, lanes] * hmoved
                hsum.append(jnp.sum(hmoved * halo_pre[:, lanes], 0, keepdims=True))
            sums.append(jnp.sum(gv, 0, keepdims=True))
            out[at, lanes] = total.astype(bf16)
            halo_out[:, lanes] = halo
            rows8 = lax.broadcasted_iota(jnp.int32, (8, cols_here), 0)
            add = jnp.zeros((8, cols_here), f32)
            for n, s in enumerate(sums):
                if 1 <= n <= 3:
                    s = s + final * hsum[n - 1]
                add = add + jnp.where(rows8 == n, s, 0.0)
            acc[:, lanes] += add

        zero = jnp.zeros((SPAN, 128), f32)
        dscores = jnp.zeros((SPAN, SPAN), f32)
        dr_cols, dstep = zero, zero
        endings = []
        for pair in range(channels // 128):
            lanes = slice(pair * 128, pair * 128 + 128)
            to_heads = gather[lanes, :]
            wide = x_s[at, lanes].astype(f32)
            step_wide = widen(first, step, pair)
            xp = (step_wide * wide).astype(bf16)
            xdw = xp.astype(f32)
            gp = gy_s[at, lanes]
            gyw = gp.astype(f32)
            sprev = sprev_s[i, :, lanes]
            te = widen(first, to_end, pair)
            total = te * wide_tile[:, lanes]
            ending = jnp.sum(xdw * total, 0, keepdims=True) + keep[:, lanes] * jnp.sum(
                sprev.astype(f32) * ds[:, lanes], 0, keepdims=True
            )
            endings.append(ending)
            for half in range(2):
                h = 2 * pair + half
                own = first if half == 0 else ~first
                decay = jnp.exp2(jnp.minimum(r_t[h:h + 1, :] - r[:, h:h + 1], 0.0))
                mixing = (scores * decay).astype(bf16)
                gown = jnp.where(own, gp, jnp.zeros_like(gp))
                total = total + mm(mixing, gown)
                dscores = dscores + mm_nt(xp, gown) * decay
            tile_a[:, lanes] = (te * xdw).astype(bf16)
            tile_b[:, lanes] = (widen(first, linked, pair) * gyw).astype(bf16)
            dr_cols = dr_cols + head_totals(xdw * total, to_heads)
            dstep = dstep + head_totals(wide * total, to_heads)
            g_x = step_wide * total + skip[:, lanes] * gyw
            conv_back(xbuf, lanes, g_x * sd_s[at, lanes].astype(f32), pre_s[at, lanes].astype(f32), par,
                      accx, hpre_s, gg_s, hx)
        ending = jnp.broadcast_to(jnp.concatenate(endings, 1), (8, channels))
        at_end = mm_split(ending, gather, 3)
        dscores = jnp.where(allowed, dscores, 0.0)
        g_write = mm(dscores.astype(bf16), r_low) + mm_nt(tile_a[...], ds_low)
        g_read = mm(jnp.transpose(dscores).astype(bf16), w_low) + mm_nt(tile_b[...], sprev_s[i])
        for lanes, grad in ((slice(0, 128), g_write), (slice(128, 256), g_read)):
            conv_back(sbuf, lanes, grad * ssd_s[at, lanes].astype(f32), spre_s[at, lanes].astype(f32),
                      spar, accs, hspre_s, gs_s, hs)
        tail_row = lax.broadcasted_iota(jnp.int32, (SPAN, 128), 0) == SPAN - 1
        dr = dr_s[at, :] - dr_cols + jnp.where(tail_row, at_end[0:1], 0.0)
        da = split_mm(upper_ones(), dr)
        dstep = dstep + head[3:4, :] * da
        gzv = dstep * sig_s[at, :]
        gz_s[at, :] = gzv.astype(bf16)
        row = lax.broadcasted_iota(jnp.int32, (8, 128), 0)
        gbias = jnp.sum(gzv, 0, keepdims=True)
        grate = jnp.sum(da * step, 0, keepdims=True)
        acch[...] += jnp.where(row == 0, gbias, jnp.where(row == 1, grate, 0.0))
        mem[...] = keep * ds + fresh_s[i]

        @pl.when(back_i == 0)
        def _():
            sum_gate.run(1)

        @pl.when(back_i == 1)
        def _():
            sum_out.run(2)

        @pl.when(back_i == 2)
        def _():
            sum_gate.run(2)

        return carry

    lax.fori_loop(0, blocks, back, 0)
    halo_x.start()
    halo_s.start()
    write(gz_s, gz_o)
    write(accx, accx_o)
    write(accs, accs_o)
    write(acch, acch_o)
    write(acc_s, acc_o)
    sum_out.run(3)
    sum_gate.run(3)
    write(o4, go4_o)
    write(g4, gg4_o)
    halo_x.wait_recv()
    halo_s.wait_recv()
    use = jnp.where(y == 0, 1.0, 0.0)
    end = pl.ds(tok.shape[0] - 16, 16)
    zeros = jnp.zeros((8, channels), f32)
    gx_s[end, :] = (
        gx_s[end, :].astype(f32) + jnp.concatenate([zeros, use * hx_in[...]], 0)
    ).astype(bf16)
    zeros = jnp.zeros((8, 256), f32)
    gs_s[end, :] = (
        gs_s[end, :].astype(f32) + jnp.concatenate([zeros, use * hs_in[...]], 0)
    ).astype(bf16)
    write(gx_s, gx_o)
    write(gs_s, gs_o)

    for b in range(blocks):
        out_sums[b].arrive()
        at = slice(b * SPAN, (b + 1) * SPAN)
        out_far[at, :] = (
            tok_own[at, :].astype(f32) + scale_of(b)[0] * out_sums[b].total(at)
        ).astype(bf16)
    write(out_far, mixed_o)
    for copy in outputs:
        copy.wait()
    t.finish()


def front(inner_all, ngain, w_states, segments, taps_inner, bias_inner, gain_gate, taps_states,
          bias_states, step_all, step_bias, decay_log, skip_gain, tok, inner, gate, out, cot):
    tokens, width = tok.shape
    blocks = tokens // SPAN
    cols = lax.axis_size("col")
    groups = lax.axis_size("dp") // SHARE - 1
    part, half = inner.shape[0] // SHARE, inner.shape[1] // cols
    channels = 2 * half
    third = width // cols
    q, qo = third // SHARE, half // SHARE
    sds = jax.ShapeDtypeStruct
    V = pltpu.VMEM
    wide = ((cols, 2, 2, part, channels), bf16)
    by_channel = ((tokens, channels), bf16)
    by_state = ((tokens, 256), bf16)
    by_head = ((tokens, 128), f32)
    acc, sacc, hacc = ((8, channels), f32), ((8, 256), f32), ((8, 128), f32)
    passed = ((128, channels), bf16)
    far = [(groups, cols, q, half), (groups, qo, width)] if groups else [(16, 128)] * 2
    outs = [
        ((tokens, third), bf16), wide, wide, ((width, 128), bf16), ((tokens, width), bf16), by_head,
        by_channel, by_state, ((tokens, 128), bf16), acc, sacc, hacc, acc,
        ((cols, q, half), bf16), ((qo, width), bf16), by_channel,
    ] + [(shape, bf16) for shape in far]
    scratch = [
        wide, wide, ((2, 2, 2, half // SHARE, width), bf16), ((cols, 2, 2, part, 256), bf16),
        ((width, 128), bf16), ((part * SHARE, cols * 128), bf16), ((tokens, width), bf16), acc, sacc,
        hacc, hacc, hacc, ((16, width), bf16), ((tokens, width), bf16), ((tokens, third), bf16),
        by_head, hacc, ((8, tokens), f32), ((8, 2 * tokens + 256), f32),
        ((tokens, width), bf16), by_channel, by_state, by_channel, by_state, by_channel, by_state,
        by_head, by_head, by_head, acc, sacc, ((blocks, 128, channels), bf16),
        by_channel, by_channel, by_channel, by_head, ((blocks, 128, channels), f32),
        ((tokens, channels), f32), ((tokens, channels), f32), by_channel, by_state,
        ((tokens, 128), bf16),
        ((2, tokens, third), bf16), ((tokens, third), bf16), ((tokens // 64, 128), f32),
        ((cols - 1, tokens // 64, 128), f32), ((SPAN + 16, channels), f32), ((SPAN + 16, 256), f32),
        ((128, channels), f32), passed, passed, passed, passed,
        acc, sacc, acc, sacc, acc, sacc, hacc, acc,
        ((cols, 2, 2, q, channels), bf16),
    ] + column_sum_shapes(cols, q, half) + row_sum_shapes(qo, width) + [
        ((SPAN, channels), bf16), ((SPAN, channels), bf16), ((SPAN, channels), f32),
    ]
    vmem = pl.BlockSpec(memory_space=V)
    hbm = pl.BlockSpec(memory_space=pl.ANY)
    smem = pl.BlockSpec(memory_space=pltpu.SMEM)
    got = pl.pallas_call(
        functools.partial(front_kernel, float(inner_all)),
        out_shape=[sds(*o) for o in outs],
        in_specs=[vmem] * 9 + [smem] * 3 + [hbm] * 5,
        out_specs=[hbm] * len(outs),
        scratch_shapes=[V(*s) for s in scratch] + [
            pltpu.SemaphoreType.DMA((72,)), pltpu.SemaphoreType.DMA((72,)),
            pltpu.SemaphoreType.DMA((40,)),
        ],
        compiler_params=pltpu.CompilerParams(
            collective_id=1, has_side_effects=True, vmem_limit_bytes=63 * 1024 * 1024
        ),
        name="front",
    )(ngain, w_states, segments, taps_inner, bias_inner, gain_gate, taps_states, bias_states, step_all,
      step_bias, decay_log, skip_gain, tok, inner, gate, out, cot)
    got = list(got[:16])
    got[1] = got[1].reshape(width, channels)
    got[2] = got[2].reshape(width, channels)
    return got


def rear_kernel(
    accx, accs, acch, acc1, ngain_v,
    tok_h, w_states_h, wi_h, wg_h, ws_h, cot_h, normed_h, sig_h, ggate_h, gx_h, gs_h, gz_h, g4_h, o4_h,
    gtok_o, oi, og, oz, oo, os, sm_o, far_i, far_z, far_s,
    tok, wst, wi, wg, ws, cot_own, normed, sig_s, ggate, gx_s, gs_s, gz_s, g4, o4,
    ngain, part, gshare, g_near, g_far, ish, ish_in,
    gi, i1, i2, i3, i5, i6, i4, gz, z1, z2, z3, z5, z6, z4,
    gs, s1, s2, s3, s4, s5, sm, msum, mgot,
    send, recv, local,
):
    t = Links(send, recv, local)
    x, y, z, core = t.x, t.y, t.z, t.core
    tokens, width = normed.shape
    channels = ggate.shape[1]
    third = width // t.cols
    blocks = tokens // SPAN
    own_cols = lane_block(z, third)

    def load(src, dst):
        copy = t.keep(src, dst)
        copy.start()
        return copy

    first = [load(g4_h, g4), load(o4_h, o4)]
    early = [load(normed_h, normed), load(gx_h, gx_s)]
    loads = [load(a, b) for a, b in (
        (ggate_h, ggate), (wg_h, wg), (wi_h, wi), (ws_h, ws), (w_states_h, wst), (gs_h, gs_s),
        (gz_h, gz_s),
    )]
    later = [load(a, b) for a, b in (
        (cot_h, cot_own), (sig_h, sig_s), (tok_h.at[:, own_cols], tok),
    )]
    norm_sums = [PairSum(t, part, g_near, g_far, pl.ds(b * SPAN, SPAN)) for b in range(blocks)]
    home_out = row_home(t, o4, oo, Steps())
    home_gate = column_home(t, g4, og, Steps())
    sum_inner = column_home(t, i4, oi, column_sums(t, gi, i1, i2, i3, i5, i6, i4, far_i))
    sum_step = column_home(t, z4, oz, column_sums(t, gz, z1, z2, z3, z5, z6, z4, far_z))
    sum_states = full_sums(t, gs, s1, s2, s3, s4, s5, far_s, os)
    sum_small = small_sums(t, sm, msum, mgot, sm_o, 8)
    send_ish = [t.make(ish, ish_in.at[off - 1], {"col": t.col_peer(off)}) for off in range(1, t.cols)]
    t.meet(True)

    def rows_of(i):
        return pl.ds(pl.multiple_of(i * SPAN, SPAN), SPAN)

    for c in first:
        c.wait()
    home_out.run(0)
    home_gate.run(0)
    gshare[...] = jnp.zeros_like(gshare)
    ngain[...] = jnp.broadcast_to(ngain_v[...].reshape(1, width), (8, width))

    def normed_grad(i, carry):
        at = rows_of(i)

        def body(c, column):
            lanes = pl.ds(pl.multiple_of(c * third, 128), third)
            total = (
                mm_nt(ggate[at, :], wg[lanes, :]) + mm_nt(gx_s[at, :], wi[lanes, :])
                + mm_nt(gz_s[at, :], ws[lanes, :]) + mm_nt(gs_s[at, :], wst[lanes, :])
            )
            part[at, lanes] = total.astype(bf16)
            weighed = total * normed[at, lanes].astype(f32)
            gshare[0:1, lanes] += jnp.sum(weighed, 0, keepdims=True)
            return column + jnp.sum(weighed, -1, keepdims=True)

        column = lax.fori_loop(0, t.cols, body, jnp.zeros((SPAN, 1), f32))
        along = jnp.transpose(jnp.broadcast_to(column, (SPAN, 128)))
        for n in range(2):
            ish[pl.ds(2 * i + n, 1), :] = along[0:1, n * 128:n * 128 + 128]
        for b in range(blocks):
            pl.when(i == b)(norm_sums[b].start)
        return carry

    def weight_grad(right, target):
        def body(i, carry):
            rows = pl.ds(pl.multiple_of(i * third, 128), third)
            target[i] = mm_tn(normed[:, rows], right[...]).astype(bf16).reshape(target.shape[1:])
            return carry

        lax.fori_loop(0, t.cols, body, 0)

    def gz_body(i, carry):
        rows = pl.ds(pl.multiple_of(i * third, 128), third)
        value = mm_tn(normed[:, rows], gz_s[...]).astype(bf16)
        gz[i] = jnp.concatenate([value, value], 1).reshape(gz.shape[1:])
        return carry

    def gs_body(i, carry):
        rows = pl.ds(pl.multiple_of(i * third, 128), third)
        gs[i] = mm_tn(normed[:, rows], gs_s[...]).astype(bf16).reshape(gs.shape[1:])
        return carry

    for c in early + loads:
        c.wait()
    lax.fori_loop(0, 1, normed_grad, 0)
    weight_grad(gx_s, gi)
    sum_inner.run(0)
    lax.fori_loop(0, t.cols, gs_body, 0)
    sum_states.run(0)
    lax.fori_loop(1, 2, normed_grad, 0)
    sum_inner.run(1)
    lax.fori_loop(0, t.cols, gz_body, 0)
    sum_step.run(0)
    sum_states.run(1)
    lax.fori_loop(2, 3, normed_grad, 0)
    sum_step.run(1)
    norm_sums[0].forward(False)
    sum_inner.run(2)
    sum_states.run(2)
    lax.fori_loop(3, blocks, normed_grad, 0)
    sm[...] = jnp.zeros_like(sm)
    sm[0:5, :] = accx[0:5, :]
    sm[5:7, :] = acc1[0:2, :]
    for n in range(2):
        sm[7:8, n * 128:n * 128 + 128] = acch[n:n + 1, :]
        sm[8 + n:9 + n, :] = gshare[0:1, n * channels:(n + 1) * channels]
    for n in range(5):
        sm[10 + n // 3:11 + n // 3, n % 3 * 256:n % 3 * 256 + 256] = accs[n:n + 1, :]
    sum_small.run(0)
    for c in send_ish:
        c.start()
    norm_sums[1].forward(False)
    sum_states.run(3)
    sum_step.run(2)
    sum_inner.run(3)
    sum_inner.run(4)
    norm_sums[2].forward(False)
    norm_sums[3].forward(False)
    sum_small.run(1)
    home_out.run(1)
    home_gate.run(1)
    sum_step.run(3)
    sum_step.run(4)
    sum_states.run(4)
    sum_small.run(2)
    sum_inner.run(5)
    for n in norm_sums:
        n.second.start()
    sum_states.run(5)
    home_out.run(2)
    home_gate.run(2)
    sum_small.run(3)
    sum_states.run(6)
    sum_step.run(5)
    sum_small.run(4)
    sum_inner.run(6)
    sum_states.run(7)
    sum_step.run(6)
    for c in later:
        c.wait()

    for c in send_ish:
        c.wait_recv()
    for b in range(blocks):
        norm_sums[b].arrive()
        at = slice(b * SPAN, (b + 1) * SPAN)
        own = tok[at, :].astype(f32)
        rows = slice(2 * b, 2 * b + 2)
        pair = ish[rows, :]
        for off in range(1, t.cols):
            pair = pair + ish_in[off - 1, rows, :]
        line = jnp.concatenate([pair[0:1], pair[1:2]], 1)
        along = jnp.transpose(jnp.broadcast_to(line, (8, SPAN)))[:, 0:1] / width
        inverse = sig_s[at, 127:128]
        grad = inverse * (norm_sums[b].total(at) * ngain[0:1, own_cols] - own * (inverse * along))
        g_far[at, :] = (grad + cot_own[at, :].astype(f32)).astype(bf16)
    last = load(g_far, gtok_o)
    home_out.run(3)
    home_gate.run(3)
    sum_step.run(7)
    sum_inner.run(7)
    sum_states.run(8)
    sum_small.run(5)
    last.wait()
    t.finish()


def rear(accx, accs, acch, acc1, ngain, tok, w_states, wi, wg, ws, cot, normed, sig, ggate, gx, gs, gz,
         g4, o4):
    tokens, width = normed.shape
    channels = ggate.shape[1]
    cols = lax.axis_size("col")
    groups = lax.axis_size("dp") // SHARE - 1
    third, own = width // cols, channels // 2
    q, qo, qs = third // SHARE, own // SHARE, width // (cols * 2 * SHARE)
    sds = jax.ShapeDtypeStruct
    V = pltpu.VMEM
    small = [accx, accs, acch, acc1, ngain]
    big = [tok, w_states, wi, wg, ws, cot, normed, sig, ggate, gx, gs, gz, g4, o4]
    scratch = [((tokens, third), bf16)] + [(b.shape, b.dtype) for b in big[1:]]

    scratch += [
        ((8, width), f32), ((tokens, width), bf16), ((8, width), f32),
        ((2, tokens, third), bf16), ((tokens, third), bf16), ((tokens // 128, 128), f32),
        ((cols - 1, tokens // 128, 128), f32),
    ]
    scratch += [((cols, 2, 2, q, 2 * own), bf16)] + column_sum_shapes(cols, q, own)
    scratch += [((cols, 2, 2, q, 256), bf16)] + column_sum_shapes(cols, q, 128)
    scratch += [
        ((cols, 2, 2, 2, qs, 256), bf16), ((cols, 2, 2, qs, 256), bf16), ((cols, 2, qs, 256), bf16),
        ((cols, qs, 256), bf16), ((cols, qs, 256), bf16), ((cols - 1, qs, 256), bf16),
        ((16, channels), f32), ((3, 16, channels), f32), ((6 + groups, 16, channels), f32),
    ]
    if groups:
        far = [(groups, cols, q, own), (groups, cols, q, 128), (groups, cols, qs, 256)]
    else:
        far = [(16, 128)] * 3
    vmem = pl.BlockSpec(memory_space=V)
    hbm = pl.BlockSpec(memory_space=pl.ANY)
    got = pl.pallas_call(
        rear_kernel,
        out_shape=[
            sds((tokens, third), bf16),
            sds((2, 2, q, cols * own), bf16), sds((2, 2, q, cols * own), bf16),
            sds((2, 2, q, cols * 128), bf16), sds((cols, 2, 2, qo, third), bf16),
            sds((cols, 2, 2, 2, qs, 256), bf16), sds((16, channels), f32),
        ] + [sds(f, bf16) for f in far],
        in_specs=[vmem] * len(small) + [hbm] * len(big),
        out_specs=[hbm] * 6 + [vmem] + [hbm] * 3,
        scratch_shapes=[V(*s) for s in scratch] + [
            pltpu.SemaphoreType.DMA((100,)), pltpu.SemaphoreType.DMA((100,)),
            pltpu.SemaphoreType.DMA((48,)),
        ],
        compiler_params=pltpu.CompilerParams(
            collective_id=2, has_side_effects=True, vmem_limit_bytes=62 * 1024 * 1024
        ),
        name="rear",
    )(*small, *big)
    gtok, oi, og, oz, oo, os, sm = got[:7]
    return (
        gtok, oi.reshape(third, -1), og.reshape(third, -1), oz.reshape(third, -1),
        oo.reshape(cols * own, third), os.reshape(width, -1), sm,
    )


def unpack_kernel(
    oi, og, oz, oo, os, sm, ngain, decay_log,
    inner_o, gate_o, step_o, out_o, states_o, taps_o, bias_o, staps_o, sbias_o, step_bias_o, decay_o,
    skip_o, gain_o, norm_o,
    wide,
):
    y, z = lax.axis_index("row"), lax.axis_index("col")
    inner_o[...] = oi[...].astype(f32)
    gate_o[...] = og[...].astype(f32)
    out_o[...] = oo[...].astype(f32)
    states_o[...] = os[...].astype(f32)
    heads = decay_log.shape[0]

    @pl.when(pl.program_id(0) == 0)
    def _():
        own_ch, third = taps_o.shape[1], norm_o.shape[0]
        steps, lanes = step_o.shape[0], oz.shape[1]
        dst = lax.broadcasted_iota(jnp.int32, (steps, lanes), 0)
        src = lax.broadcasted_iota(jnp.int32, (steps, lanes), 1)
        pick = jnp.zeros((steps, lanes), f32)
        for c in range(steps // heads):
            mine = (dst >= c * heads) & (dst < (c + 1) * heads)
            place = src - dst == c * 128 + y * heads - c * heads
            pick = pick + jnp.where(mine & place, 1.0, 0.0)
        step_o[...] = mm_nt(pick.astype(bf16), oz[...])
        own = lane_block(y, own_ch)
        taps_o[...] = sm[0:4, own]
        bias_o[...] = sm[4:5, own].reshape(own_ch)
        gain_o[...] = sm[5:6, own].reshape(own_ch)
        for n in range(4):
            staps_o[n:n + 1, :] = sm[10 + n // 3:11 + n // 3, n % 3 * 256:n % 3 * 256 + 256]
        sbias_o[...] = sm[11:12, 256:512].reshape(256)
        skip = mm_split(sm[0:8, own], gather_matrix(own_ch), 3)
        skip_o[...] = skip[6:7, 0:heads].reshape(heads)

        def own_head(n):
            both = sm[7:8, n * 128:n * 128 + 128]
            return jnp.where(y == 0, both[:, 0:heads], both[:, heads:2 * heads])

        step_bias_o[...] = own_head(0).reshape(heads)
        rate = -jnp.exp(decay_log[...].reshape(1, heads))
        decay_o[...] = (own_head(1) * rate).reshape(heads)
        half = sm.shape[1]
        wide[0:1, 0:half] = sm[8:9, :]
        wide[0:1, half:] = sm[9:10, :]
        wide[8:16, :] = jnp.broadcast_to(ngain[...].reshape(1, 2 * half), (8, 2 * half))
        cols = lane_block(z, third)
        norm_o[...] = (wide[0:1, cols] / wide[8:9, cols]).reshape(third)


def unpack(oi, og, oz, oo, os, sm, ngain, decay_log, own_ch):
    sds = jax.ShapeDtypeStruct
    heads, parts = decay_log.shape[0], 4
    third, block = oi.shape

    def rows(shape):
        return pl.BlockSpec((shape[0] // parts, shape[1]), lambda i: (i, 0))

    def whole(shape):
        return pl.BlockSpec(shape, lambda i: (0,) * len(shape))

    steps = (block // own_ch * heads, third)
    small = [(4, own_ch), (own_ch,), (4, 256), (256,), (heads,), (heads,), (heads,), (own_ch,),
             (third,)]
    big = [oi.shape, og.shape, steps, oo.shape, os.shape]
    ins = [rows(oi.shape), rows(og.shape), whole(oz.shape), rows(oo.shape), rows(os.shape)]
    return pl.pallas_call(
        unpack_kernel,
        grid=(parts,),
        out_shape=[sds(s, f32) for s in big + small],
        in_specs=ins + [whole(sm.shape), whole(ngain.shape), whole(decay_log.shape)],
        out_specs=[whole(s) if s == steps else rows(s) for s in big] + [whole(s) for s in small],
        scratch_shapes=[pltpu.VMEM((16, 2 * sm.shape[1]), f32)],
        compiler_params=pltpu.CompilerParams(vmem_limit_bytes=62 * 1024 * 1024),
        name="unpack",
    )(oi, og, oz, oo, os, sm, ngain, decay_log)


def per_device(
    tokens_in, segment_ids, norm_gain, proj_gate, proj_inner, proj_step, proj_states,
    conv_inner, conv_inner_bias, conv_states, conv_states_bias, step_bias, decay_log,
    skip_gain, gate_gain, proj_out, cotangent,
):
    inner_all = proj_gate.shape[1] * lax.axis_size("row")
    (
        mixed_out, w_inner, w_gate, w_step, normed, sig, gx, gs, gz, accx, accs, acch, acc1, g4, o4,
        g_gate,
    ) = front(
        inner_all, norm_gain, proj_states, segment_ids, conv_inner, conv_inner_bias, gate_gain,
        conv_states, conv_states_bias, proj_step.T, step_bias, decay_log, skip_gain,
        tokens_in, proj_inner, proj_gate, proj_out, cotangent,
    )
    grad_tokens, oi, og, oz, oo, os, sums = rear(
        accx, accs, acch, acc1, norm_gain, tokens_in, proj_states, w_inner, w_gate, w_step, cotangent,
        normed, sig, g_gate, gx, gs, gz, g4, o4,
    )
    (
        grad_inner, grad_gate, grad_step, grad_out, grad_states, grad_conv_inner,
        grad_conv_inner_bias, grad_conv_states, grad_conv_states_bias, grad_step_bias, grad_decay,
        grad_skip, grad_gate_gain, grad_norm_gain,
    ) = unpack(oi, og, oz, oo, os, sums, norm_gain, decay_log, conv_inner.shape[1])
    return (
        mixed_out, grad_tokens, grad_norm_gain, grad_gate, grad_inner, grad_step.T, grad_states,
        grad_conv_inner, grad_conv_inner_bias, grad_conv_states, grad_conv_states_bias,
        grad_step_bias, grad_decay, grad_skip, grad_gate_gain, grad_out,
    )


def solution(mesh):
    in_specs = (
        P(("dp", "row"), None),
        P("dp", None),
        P(),
        P("col", "row"),
        P("col", "row"),
        P("col", "row"),
        P(),
        P(None, ("row", "col")),
        P(("row", "col")),
        P(),
        P(),
        P(("row", "col")),
        P(("row", "col")),
        P(("row", "col")),
        P(("row", "col")),
        P("row", "col"),
        P(("dp", "row"), "col"),
    )
    out_specs = (
        P(("dp", "row"), "col"),
        P(("dp", "row"), "col"),
        P("col"),
        P("col", "row"),
        P("col", "row"),
        P("col", "row"),
        P(),
        P(None, ("row", "col")),
        P(("row", "col")),
        P(),
        P(),
        P(("row", "col")),
        P(("row", "col")),
        P(("row", "col")),
        P(("row", "col")),
        P("row", "col"),
    )
    return jax.shard_map(
        per_device, mesh=mesh, in_specs=in_specs, out_specs=out_specs, check_vma=False
    )
```

```python
import functools

import jax
import jax.numpy as jnp
from jax import lax
from jax.experimental import pallas as pl
from jax.experimental.pallas import tpu as pltpu
from jax.sharding import PartitionSpec as P

SPAN = 256
HEAD = 64
epsilon = 1e-05
LOG2E = 1.4426950408889634
f32 = jnp.float32
bf16 = jnp.bfloat16
ANY = pl.ANY


def mm(a, b):
    return lax.dot_general(a, b, (((1,), (0,)), ((), ())), preferred_element_type=f32)


def mm_nt(a, b):
    return lax.dot_general(a, b, (((1,), (1,)), ((), ())), preferred_element_type=f32)


def split(v, terms):
    parts = []
    for _ in range(terms):
        part = v.astype(bf16)
        parts.append(part)
        v = v - part.astype(f32)
    return parts


def mm_split(a, exact, terms=2):
    return sum(mm(part, exact) for part in split(a, terms))


def split_mm(exact, b, terms=3):
    return sum(mm(exact, part) for part in split(b, terms))


def spread_matrix(channels):
    heads = lax.broadcasted_iota(jnp.int32, (128, channels), 0)
    cols = lax.broadcasted_iota(jnp.int32, (128, channels), 1)
    low = heads * HEAD
    return jnp.where((cols >= low) & (cols < low + HEAD), 1.0, 0.0).astype(bf16)


def gather_matrix(channels):
    heads = lax.broadcasted_iota(jnp.int32, (channels, 128), 1)
    rows = lax.broadcasted_iota(jnp.int32, (channels, 128), 0)
    low = heads * HEAD
    return jnp.where((rows >= low) & (rows < low + HEAD), 1.0, 0.0).astype(bf16)


def lower_ones():
    rows = lax.broadcasted_iota(jnp.int32, (SPAN, SPAN), 0)
    cols = lax.broadcasted_iota(jnp.int32, (SPAN, SPAN), 1)
    return jnp.where(rows >= cols, 1.0, 0.0).astype(bf16)


def upper_ones():
    rows = lax.broadcasted_iota(jnp.int32, (SPAN, SPAN), 0)
    cols = lax.broadcasted_iota(jnp.int32, (SPAN, SPAN), 1)
    return jnp.where(rows <= cols, 1.0, 0.0).astype(bf16)


def sigmoid(v):
    return 1.0 / (1.0 + jnp.exp(-v))


def widen(first, values, pair):
    return jnp.where(first, values[:, 2 * pair:2 * pair + 1], values[:, 2 * pair + 1:2 * pair + 2])


def head_totals(values, to_heads):
    high = values.astype(bf16)
    low = (values - high.astype(f32)).astype(bf16)
    return mm(jnp.concatenate([high, low], 1), jnp.concatenate([to_heads, to_heads], 0))


def half_masks():
    lane = lax.broadcasted_iota(jnp.int32, (SPAN, 128), 1)
    return lane < HEAD


def rms_rows(tok, gain):
    wide = tok.astype(f32)
    inverse = lax.rsqrt(jnp.mean(wide * wide, -1, keepdims=True) + epsilon)
    return (wide * inverse * gain).astype(bf16)


MESH = pl.DeviceIdType.MESH
SHARE = 4


def lane_block(index, width):
    return pl.ds(pl.multiple_of(index * width, 128), width)


class Links:
    def __init__(self, send, recv, local=None):
        self.send, self.recv, self.local = send, recv, local
        self.used, self.kept, self.sent = 0, 0, []
        dp = lax.axis_index("dp")
        self.groups = lax.axis_size("dp") // SHARE
        self.group = dp // SHARE
        self.x = lax.rem(dp, SHARE) // 2
        self.core = lax.rem(dp, 2)
        self.y = lax.axis_index("row")
        self.z = lax.axis_index("col")
        self.cols = lax.axis_size("col")

    def dp_of(self, group, x, core):
        return group * SHARE + x * 2 + core

    def mate(self):
        return {"dp": self.dp_of(self.group, self.x, 1 - self.core)}

    def across(self):
        return {"dp": self.dp_of(self.group, 1 - self.x, self.core)}

    def other_row(self):
        return {"row": 1 - self.y}

    def col_peer(self, off):
        return lax.rem(self.z + off, self.cols)

    def group_peer(self, off):
        return {"dp": self.dp_of(lax.rem(self.group + off, self.groups), self.x, self.core)}

    def meet(self, far_groups):
        barrier = pltpu.get_barrier_semaphore()
        peers = [self.mate(), self.across(), self.other_row()]
        peers += [{"col": self.col_peer(off)} for off in range(1, self.cols)]
        if far_groups:
            peers += [self.group_peer(off) for off in range(1, self.groups)]
        for peer in peers:
            pl.semaphore_signal(barrier, inc=1, device_id=peer, device_id_type=MESH)
        pl.semaphore_wait(barrier, len(peers))

    def make(self, src, dst, peer, when=None, track=True):
        at = self.used
        self.used += 1
        copy = pltpu.make_async_remote_copy(
            src_ref=src, dst_ref=dst, send_sem=self.send.at[at], recv_sem=self.recv.at[at],
            device_id=peer, device_id_type=MESH,
        )
        if track:
            self.sent.append((copy, when))
        return copy

    def go(self, src, dst, peer, track=True):
        copy = self.make(src, dst, peer, track=track)
        copy.start()
        return copy

    def keep(self, src, dst):
        copy = pltpu.make_async_copy(src, dst, self.local.at[self.kept])
        self.kept += 1
        return copy

    def finish(self):
        for copy, when in self.sent:
            if when is None:
                copy.wait_send()
            else:
                pl.when(when)(copy.wait_send)


class Steps:
    def __init__(self):
        self.stages = []

    def add(self, remote, local=(), before=None):
        self.stages.append((remote, list(local), before))

    def drain(self, t):
        for remote, _, _ in self.stages:
            for c in remote:
                c.wait_send()
                t.sent = [(copy, when) for copy, when in t.sent if copy is not c]

    def run(self, s):
        if 0 < s <= len(self.stages):
            remote, local, _ = self.stages[s - 1]
            for c in remote:
                c.wait_recv()
            for c in local:
                c.wait()
        if s < len(self.stages):
            remote, local, before = self.stages[s]
            if before is not None:
                before()
            for c in remote + local:
                c.start()


def spread_steps(t, view, steps):
    x, y = t.x, t.y
    first, second = view(x, y, 0), view(x, y, 1)
    steps.add([t.make(first, first, t.other_row()), t.make(second, second, t.across())])
    first, second = view(x, None, 0), view(None, y, 1)
    steps.add([t.make(first, first, t.across()), t.make(second, second, t.other_row())])
    every = view(None, None, None)
    steps.add([t.make(every, every, t.mate())])
    return steps


def half_lines(part, half):
    return slice(None) if half is None else pl.ds(half * (part // 2), part // 2)


def column_steps(t, src, dst, width):
    part = src.shape[0] // SHARE
    x, y, z, core = t.x, t.y, t.z, t.core
    rows = pl.ds(pl.multiple_of((x * 2 + core) * part, 16), part)
    lanes = lane_block(y, width)
    steps = Steps()
    here = dst.at[z, x, core, :, lanes]
    remote = []
    for off in range(1, t.cols):
        to = t.col_peer(off)
        remote.append(t.make(src.at[rows, lane_block(to, width)], here, {"col": to}))
    steps.add(remote, [t.keep(src.at[rows, lane_block(z, width)], here)])

    def view(at_x, at_y, half):
        return dst.at[:, slice(None) if at_x is None else at_x, core, half_lines(part, half),
                      slice(None) if at_y is None else lanes]

    return spread_steps(t, view, steps)


def row_steps(t, src, dst, width):
    part = src.shape[0] // t.cols // SHARE
    x, y, z, core = t.x, t.y, t.z, t.core

    def rows(to):
        return pl.ds(pl.multiple_of((to * SHARE + x * 2 + core) * part, 16), part)

    steps = Steps()
    here = dst.at[y, x, core, :, lane_block(z, width)]
    remote = []
    for off in range(1, t.cols):
        to = t.col_peer(off)
        remote.append(t.make(src.at[rows(to), :], here, {"col": to}))
    steps.add(remote, [t.keep(src.at[rows(z), :], here)])

    def view(at_x, at_y, half):
        return dst.at[slice(None) if at_y is None else at_y, slice(None) if at_x is None else at_x,
                      core, half_lines(part, half), :]

    return spread_steps(t, view, steps)


def gather_steps(t, own, whole, rows):
    width = own.shape[1]
    z = t.z
    mate, far = z + 1 - 2 * lax.rem(z, 2), lax.rem(z + 2, 4)
    here, there = whole.at[rows, lane_block(z, width)], whole.at[rows, lane_block(far, width)]
    steps = Steps()
    cross = t.make(own.at[rows, :], here, {"col": far})
    near = t.make(own.at[rows, :], here, {"col": mate})
    steps.add([cross, near], [t.keep(own.at[rows, :], here)])
    steps.add([t.make(there, there, {"col": mate})])
    return steps


def mm_tn(a, b):
    return lax.dot_general(a, b, (((0,), (0,)), ((), ())), preferred_element_type=f32)


def add_bf16(a, b):
    return (a.astype(f32) + b.astype(f32)).astype(bf16)


class PairSum:
    def __init__(self, t, part, near, far_in, rows):
        z = t.z
        mate = z + 1 - 2 * lax.rem(z, 2)
        far = lax.rem(z + 2, 4)
        mate_far = lax.rem(mate + 2, 4)
        width = near.shape[-1]
        self.part, self.near, self.far_in, self.rows = part, near, far_in, rows
        self.own, self.far = lane_block(z, width), lane_block(far, width)
        to_mate = [
            t.make(part.at[rows, lane_block(mate_far, width)], near.at[1, rows], {"col": mate}),
            t.make(part.at[rows, lane_block(mate, width)], near.at[0, rows], {"col": mate}),
        ]
        self.first, self.second = to_mate
        self.across = t.make(near.at[1, rows], far_in.at[rows], {"col": far})

    def start(self):
        self.first.start()

    def forward(self, both=True):
        self.first.wait_recv()
        count = self.rows.size // 64

        def body(i, c):
            at = pl.ds(pl.multiple_of(self.rows.start + i * 64, 16), 64)
            self.near[1, at] = add_bf16(self.near[1, at], self.part[at, self.far])
            return c

        lax.fori_loop(0, count, body, 0)
        self.across.start()
        if both:
            self.second.start()

    def arrive(self):
        self.second.wait_recv()
        self.across.wait_recv()

    def total(self, at):
        return (
            self.part[at, self.own].astype(f32) + self.near[0, at].astype(f32)
            + self.far_in[at].astype(f32)
        )


def sum_far_groups(t, own, got):
    if t.groups == 1:
        return
    more = [t.go(own, got.at[off - 1], t.group_peer(off), False) for off in range(1, t.groups)]
    for c in more:
        c.wait()

    def total(spare):
        for off in range(1, t.groups):
            back = t.keep(got.at[off - 1], spare)
            back.start()
            back.wait()
            own[...] = add_bf16(own[...], spare[...])

    pl.run_scoped(total, pltpu.VMEM(own.shape, own.dtype))


def column_sums(t, g, a1, yx, xy, yx2, xy2, a4, far):
    x, y, core = t.x, t.y, t.core
    width = a4.shape[-1]
    h = a4.shape[1] // 2
    mine, other = lane_block(y, width), lane_block(1 - y, width)
    top, low = pl.ds(0, h), pl.ds(h, h)
    steps = Steps()
    steps.add([t.make(g.at[:, :, 1 - core], a1, t.mate())])

    def add_core():
        def body(i, c):
            for j in range(2):
                a1[i, j] = add_bf16(a1[i, j], g[i, j, core])
            return c

        lax.fori_loop(0, t.cols, body, 0)

    steps.add([
        t.make(a1.at[:, :, top, other], yx, t.other_row()),
        t.make(a1.at[:, 1 - x, low, :], xy, t.across()),
    ], (), add_core)

    def add_first():
        def body(i, c):
            for j in range(2):
                yx[i, j] = add_bf16(yx[i, j], a1[i, j, top, mine])
            xy[i] = add_bf16(xy[i], a1[i, x, low, :])
            return c

        lax.fori_loop(0, t.cols, body, 0)

    steps.add([
        t.make(yx.at[:, 1 - x], yx2, t.across()),
        t.make(xy.at[:, :, other], xy2, t.other_row()),
    ], (), add_first)

    def add_second():
        def body(i, c):
            a4[i, top] = add_bf16(yx2[i], yx[i, x])
            a4[i, low] = add_bf16(xy2[i], xy[i, :, mine])
            return c

        lax.fori_loop(0, t.cols, body, 0)
        sum_far_groups(t, a4, far)

    steps.add([], (), add_second)
    return steps


def column_sum_shapes(cols, q, w):
    h = q // 2
    return [((cols, 2, q, 2 * w), bf16), ((cols, 2, h, w), bf16), ((cols, h, 2 * w), bf16),
            ((cols, h, w), bf16), ((cols, h, w), bf16), ((cols, q, w), bf16)]


def column_home(t, a4, o, steps):
    x, z, core = t.x, t.z, t.core
    here = o.at[x, core, :, lane_block(z, a4.shape[-1])]
    steps.add(
        [t.make(a4.at[t.col_peer(off)], here, {"col": t.col_peer(off)}) for off in range(1, t.cols)],
        [t.keep(a4.at[z], here)],
    )
    steps.add([t.make(o.at[x, core], o.at[x, core], t.across())])
    steps.add([t.make(o.at[:, core], o.at[:, core], t.mate())])
    return steps


def row_sums(t, g, a1, yx, xy, yx2, xy2, a4, far):
    x, y, core = t.x, t.y, t.core
    h = a4.shape[0] // 2
    top, low = pl.ds(0, h), pl.ds(h, h)
    steps = Steps()
    steps.add([t.make(g.at[:, :, 1 - core], a1, t.mate())])

    def add_core():
        def body(i, c):
            for j in range(2):
                a1[i, j] = add_bf16(a1[i, j], g[i, j, core])
            return c

        lax.fori_loop(0, 2, body, 0)

    steps.add([
        t.make(a1.at[1 - y, :, top], yx, t.other_row()),
        t.make(a1.at[:, 1 - x, low], xy, t.across()),
    ], (), add_core)

    def add_first():
        for j in range(2):
            yx[j] = add_bf16(yx[j], a1[y, j, top])
            xy[j] = add_bf16(xy[j], a1[j, x, low])

    steps.add([
        t.make(yx.at[1 - x], yx2, t.across()), t.make(xy.at[1 - y], xy2, t.other_row()),
    ], (), add_first)

    def add_second():
        a4[top] = add_bf16(yx2[...], yx[x])
        a4[low] = add_bf16(xy2[...], xy[y])
        sum_far_groups(t, a4, far)

    steps.add([], (), add_second)
    return steps


def row_sum_shapes(q, width):
    h = q // 2
    return [((2, 2, q, width), bf16), ((2, h, width), bf16), ((2, h, width), bf16),
            ((h, width), bf16), ((h, width), bf16), ((q, width), bf16)]


def row_home(t, a4, o, steps):
    x, z, core = t.x, t.z, t.core
    width = o.shape[-1]
    here = o.at[z, x, core]
    steps.add(
        [t.make(a4.at[:, lane_block(t.col_peer(off), width)], here, {"col": t.col_peer(off)})
         for off in range(1, t.cols)],
        [t.keep(a4.at[:, lane_block(z, width)], here)],
    )
    steps.add([t.make(o.at[:, x, core], o.at[:, x, core], t.across())])
    steps.add([t.make(o.at[:, :, core], o.at[:, :, core], t.mate())])
    return steps


def full_sums(t, g, s1, s2, s3, s4, s5, far, o):
    x, y, z, core = t.x, t.y, t.z, t.core
    steps = Steps()
    steps.add([t.make(g.at[:, :, :, 1 - core], s1, t.mate())])

    def add_core():
        def body(i, c):
            for j in range(2):
                for k in range(2):
                    s1[i, j, k] = add_bf16(s1[i, j, k], g[i, j, k, core])
            return c

        lax.fori_loop(0, t.cols, body, 0)

    steps.add([t.make(s1.at[:, 1 - y], s2, t.other_row())], (), add_core)

    def add_row():
        def body(i, c):
            for k in range(2):
                s2[i, k] = add_bf16(s2[i, k], s1[i, y, k])
            return c

        lax.fori_loop(0, t.cols, body, 0)

    steps.add([t.make(s2.at[:, 1 - x], s3, t.across())], (), add_row)

    def add_x():
        def body(i, c):
            s4[i] = add_bf16(s3[i], s2[i, x])
            return c

        lax.fori_loop(0, t.cols, body, 0)
        sum_far_groups(t, s4, far)

    steps.add(
        [t.make(s4.at[t.col_peer(off)], s5.at[off - 1], {"col": t.col_peer(off)})
         for off in range(1, t.cols)], (), add_x,
    )

    def add_cols():
        total = s4[z].astype(f32)
        for off in range(1, t.cols):
            total = total + s5[off - 1].astype(f32)
        s4[z] = total.astype(bf16)

    here = o.at[z, y, x, core]
    steps.add(
        [t.make(s4.at[z], here, {"col": t.col_peer(off)}) for off in range(1, t.cols)],
        [t.keep(s4.at[z], here)], add_cols,
    )
    here = o.at[:, y, x, core]
    steps.add([t.make(here, here, t.other_row())])
    here = o.at[:, :, x, core]
    steps.add([t.make(here, here, t.across())])
    here = o.at[:, :, :, core]
    steps.add([t.make(here, here, t.mate())])
    return steps


def small_sums(t, sm, msum, mgot, out, rest):
    steps = Steps()
    steps.add([t.make(sm, mgot.at[0], t.mate())])

    def add_core():
        msum[0] = sm[...] + mgot[0]

    steps.add([t.make(msum.at[0], mgot.at[1], t.other_row())], (), add_core)

    def add_row():
        msum[1] = msum[0] + mgot[1]

    steps.add([t.make(msum.at[1], mgot.at[2], t.across())], (), add_row)

    def add_x():
        msum[2] = msum[1] + mgot[2]
        if t.groups > 1:
            more = [t.go(msum.at[2], mgot.at[5 + off], t.group_peer(off), False)
                    for off in range(1, t.groups)]
            for c in more:
                c.wait()
            total = msum[2]
            for off in range(1, t.groups):
                total = total + mgot[5 + off]
            msum[2] = total

    last = pl.ds(rest, sm.shape[0] - rest)
    steps.add(
        [t.make(msum.at[2, last], mgot.at[2 + off, last], {"col": t.col_peer(off)})
         for off in range(1, t.cols)], (), add_x,
    )

    def done():
        out[0:rest] = msum[2, 0:rest]
        out[rest:] = msum[2, rest:] + mgot[3, rest:] + mgot[4, rest:] + mgot[5, rest:]

    steps.add([], (), done)
    return steps


def front_kernel(
    inner_total,
    ngain_v, w_states, segments, taps_inner, bias_inner, gain_gate, taps_states, bias_states, step_all,
    step_bias, decay_log, skip_gain,
    tok_h, inner, gate, out, cot,
    mixed_o, wi_o, wg_o, ws_o, normed_o, sig_o, gx_o, gs_o, gz_o, accx_o, accs_o, acch_o, acc_o,
    gg4_o, go4_o, ggate_o, far_g, far_o,
    wi, wg, wo, ws2, ws, step_w, cots, par, spar, head, head_own, head_in, halo_in, tok, tok_own,
    meta, hmeta, docrow, docs,
    normed_s, pre_s, spre_s, sd_s, ssd_s, x_s, wr_s, step_s, r_s, sig_s, hpre_s, hspre_s, sprev_s,
    gated_s, ggate_s, gy_s, dr_s, fresh_s, y_s, gate_s, gg_s, gs_s, gz_s,
    out_near, out_far, sums_s, sums_in, xbuf, sbuf, mem, pass_out, state_in, dstate_in, pass_back,
    hx, hs, hx_in, hs_in, accx, accs, acch, acc_s, gg, g1, g2, g3, g5, g6, g4, o1, o2, o3, o5, o6, o4,
    tile_a, tile_b, wide_tile,
    send, recv, local,
):
    t = Links(send, recv, local)
    x, y, z, core = t.x, t.y, t.z, t.core
    blocks = tok.shape[0] // SPAN
    channels = x_s.shape[1]
    half = channels // 2
    outputs = []

    def write(src, dst):
        copy = t.keep(src, dst)
        copy.start()
        outputs.append(copy)

    def load(src, dst):
        copy = t.keep(src, dst)
        copy.start()
        return copy

    loads = [load(tok_h, tok), load(tok_h.at[:, lane_block(z, cot.shape[1])], tok_own)]
    own_lanes = lane_block(y, half)
    few = [
        t.make(par.at[:, own_lanes], par.at[:, own_lanes], t.other_row()),
        t.make(head_own, head_in, t.other_row()),
        t.make(tok_h.at[pl.ds(tok.shape[0] - 16, 16), :], halo_in, t.other_row()),
    ]
    block = inner.shape[1] // t.cols
    get_inner = column_steps(t, inner, wi, block)
    get_step = column_steps(t, step_w, ws2, step_w.shape[1] // t.cols)
    get_gate = column_steps(t, gate, wg, block)
    get_out = row_steps(t, out, wo, out.shape[1])
    half_rows = tok.shape[0] // 2
    get_cot = [gather_steps(t, cot, cots, pl.ds(n * half_rows, half_rows)) for n in range(2)]
    pass_state = t.make(pass_out, state_in, t.other_row())
    pass_back_state = t.make(pass_back, dstate_in, t.other_row())
    halo_x = t.make(hx, hx_in, t.other_row())
    halo_s = t.make(hs, hs_in, t.other_row())
    out_part = tok
    sum_gate = column_sums(t, gg, g1, g2, g3, g5, g6, g4, far_g)
    go = wo
    sum_out = row_sums(t, go, o1, o2, o3, o5, o6, o4, far_o)
    out_sums = [PairSum(t, out_part, out_near, out_far, pl.ds(b * SPAN, SPAN)) for b in range(blocks)]
    pass_sums = [
        t.make(sums_s, sums_in.at[off - 1], {"col": t.col_peer(off)}) for off in range(1, t.cols)
    ]
    t.meet(True)
    get_inner.run(0)

    own_heads = step_bias.shape[0]
    lane8 = lax.broadcasted_iota(jnp.int32, (8, 128), 1)
    row8 = lax.broadcasted_iota(jnp.int32, (8, 128), 0)
    scalars = jnp.zeros((8, 128), f32)
    for j in range(own_heads):
        here = lane8 == y * own_heads + j
        scalars = scalars + jnp.where(here & (row8 == 0), step_bias[j], 0.0)
        scalars = scalars + jnp.where(here & ((row8 == 1) | (row8 == 3)), decay_log[j], 0.0)
        scalars = scalars + jnp.where(here & (row8 == 2), skip_gain[j], 0.0)
    own_lane = (lane8 >= y * own_heads) & (lane8 < (y + 1) * own_heads)
    rate = jnp.where(own_lane, -jnp.exp(scalars), 0.0)
    head_own[...] = jnp.where(row8 == 1, rate * LOG2E, jnp.where(row8 == 3, rate, scalars))
    par[:, own_lanes] = jnp.zeros((8, half), f32)
    par[0:4, own_lanes] = taps_inner[...]
    par[4:5, own_lanes] = bias_inner[...].reshape(1, half)
    par[5:6, own_lanes] = gain_gate[...].reshape(1, half)
    spar[...] = jnp.zeros_like(spar)
    spar[0:4, :] = taps_states[...]
    spar[4:5, :] = bias_states[...].reshape(1, 256)
    every = step_all.shape[0]
    src = lax.broadcasted_iota(jnp.int32, (every, t.cols * 128), 0)
    dst = lax.broadcasted_iota(jnp.int32, (every, t.cols * 128), 1)
    place = jnp.zeros((every, t.cols * 128), f32)
    for c in range(t.cols):
        low = c * 128 + y * own_heads - c * own_heads
        mine = (src >= c * own_heads) & (src < (c + 1) * own_heads)
        place = place + jnp.where(mine & (dst - src == low), 1.0, 0.0)
    step_w[...] = mm_tn(step_all[...], place.astype(bf16)).astype(bf16)
    get_step.run(0)
    for c in few:
        c.start()

    length = tok.shape[0]
    docs[:, 0:128] = jnp.full((8, 128), -1.0, f32)
    docs[:, 128:128 + 2 * length] = jnp.broadcast_to(segments[...].astype(f32), (8, 2 * length))
    docs[:, 128 + 2 * length:] = jnp.full((8, 128), -1.0, f32)
    window = docs[:, pl.ds(pl.multiple_of(y * length, 128), length + 256)]
    span_w = length + 256
    docrow[...] = window[:, 128:128 + length]
    same_before = [(window == pltpu.roll(window, k, 1)).astype(f32) for k in range(1, 4)]
    same_after = [(window == pltpu.roll(window, span_w - k, 1)).astype(f32) for k in range(1, 4)]
    row16 = lax.broadcasted_iota(jnp.int32, (8, SPAN), 0)
    for i in range(blocks):
        at = slice(128 + i * SPAN, 128 + (i + 1) * SPAN)
        here = window[:, at]
        before = window[0:1, 127 + i * SPAN:128 + i * SPAN]
        last = window[0:1, 127 + (i + 1) * SPAN:128 + (i + 1) * SPAN]
        low = jnp.where(row16 == 0, here, 0.0)
        for k in range(1, 4):
            low = low + jnp.where(row16 == k, same_before[k - 1][:, at], 0.0)
        low = low + jnp.where((row16 == 4) & (here == before), 1.0, 0.0)
        low = low + jnp.where((row16 == 5) & (here == last), 1.0, 0.0)
        low = low + jnp.where((row16 == 6) & (before == last), 1.0, 0.0)
        high = jnp.zeros((8, SPAN), f32)
        for k in range(1, 4):
            high = high + jnp.where(row16 == k - 1, same_after[k - 1][:, at], 0.0)
        rows128 = jnp.concatenate([low, high, jnp.zeros((112, SPAN), f32)], 0)
        meta[i * SPAN:(i + 1) * SPAN, :] = jnp.transpose(rows128)
    row16 = lax.broadcasted_iota(jnp.int32, (8, 128), 0)
    high = jnp.zeros((8, 128), f32)
    for k in range(1, 4):
        high = high + jnp.where(row16 == k - 1, same_after[k - 1][:, 0:128], 0.0)
    rows128 = jnp.concatenate([jnp.zeros((8, 128), f32), high, jnp.zeros((112, 128), f32)], 0)
    hmeta[...] = jnp.transpose(rows128)[120:128]

    gain = ngain_v[...].reshape(1, -1)
    for c in loads:
        c.wait()

    def rows_of(i):
        return pl.ds(pl.multiple_of(i * SPAN, SPAN), SPAN)

    def over_lanes(column):
        return jnp.broadcast_to(column, (SPAN, 128))

    def conv_silu(buf, lanes, here, taps, marks):
        v = taps[4:5, lanes] + taps[0:1, lanes] * here
        for k in range(1, 4):
            v = v + marks[k - 1] * (taps[k:k + 1, lanes] * buf[8 - k:8 - k + SPAN, lanes])
        sg = sigmoid(v)
        return v * sg, sg * (1.0 + v * (1.0 - sg))

    for c in few:
        c.wait_recv()
    hn = rms_rows(halo_in[...], gain)
    h_states = mm(hn, w_states[...])[8:16]
    sbuf[0:8, :] = h_states
    hspre_s[...] = h_states

    def norm_block(i, carry):
        at = rows_of(i)

        @pl.when(i > 0)
        def _():
            sbuf[0:8, :] = sbuf[SPAN:SPAN + 8, :]

        wide_tok = tok[at, :].astype(f32)
        inverse = lax.rsqrt(jnp.mean(wide_tok * wide_tok, -1, keepdims=True) + epsilon)
        normed = (wide_tok * inverse * gain).astype(bf16)
        normed_s[at, :] = normed
        s_pre = mm(normed, w_states[...])
        sbuf[8:SPAN + 8, :] = s_pre
        spre_s[at, :] = s_pre.astype(bf16)
        earlier = [over_lanes(meta[at, k:k + 1]) for k in range(1, 4)]
        for lanes in (slice(0, 128), slice(128, 256)):
            sact, sslope = conv_silu(sbuf, lanes, sbuf[8:SPAN + 8, lanes], spar, earlier)
            wr_s[at, lanes] = sact.astype(bf16)
            ssd_s[at, lanes] = sslope.astype(bf16)
        sig_s[at, :] = jnp.broadcast_to(inverse, (SPAN, 128))

        @pl.when(i == 0)
        def _():
            get_inner.run(1)
            get_step.run(1)
            get_gate.run(0)
            get_out.run(0)
            get_cot[0].run(0)

        return carry

    lax.fori_loop(0, blocks, norm_block, 0)
    head[...] = head_own[...] + head_in[...]
    get_inner.run(2)
    get_step.run(2)
    get_inner.run(3)
    get_step.run(3)
    get_gate.run(1)
    get_inner.run(4)
    get_step.run(4)
    wide_in = normed_s.shape[1]
    ws[...] = (
        ws2[:, :, :, :, 0:128].reshape(wide_in, 128) + ws2[:, :, :, :, 128:256].reshape(wide_in, 128)
    )
    spread = spread_matrix(channels)

    def w_of(ref):
        return ref[...].reshape(-1, ref.shape[-1])

    first = half_masks()
    h_inner = mm(hn, w_of(wi))[8:16]
    xbuf[0:8, :] = h_inner
    hpre_s[...] = h_inner
    mem[...] = jnp.zeros_like(mem)

    def entry(i, carry):
        at = rows_of(i)

        @pl.when(i > 0)
        def _():
            xbuf[0:8, :] = xbuf[SPAN:SPAN + 8, :]

        normed = normed_s[at, :]
        x_pre = mm(normed, w_of(wi))
        xbuf[8:SPAN + 8, :] = x_pre
        pre_s[at, :] = x_pre.astype(bf16)
        marks = meta[at, :]
        wr = wr_s[at, :]
        earlier = [over_lanes(marks[:, k:k + 1]) for k in range(1, 4)]
        for pair in range(channels // 128):
            lanes = slice(pair * 128, pair * 128 + 128)
            act, slope = conv_silu(xbuf, lanes, xbuf[8:SPAN + 8, lanes], par, earlier)
            x_s[at, lanes] = act.astype(bf16)
            sd_s[at, lanes] = slope.astype(bf16)

        raw = mm(normed, ws[...]) + head[0:1, :]
        step = jnp.maximum(raw, 0.0) + jnp.log1p(jnp.exp(-jnp.abs(raw)))
        lane = lax.broadcasted_iota(jnp.int32, (SPAN, 128), 1)
        sig_s[at, :] = jnp.where(lane == 127, sig_s[at, :], sigmoid(raw))
        step_s[at, :] = step
        r = split_mm(lower_ones(), step * head[1:2, :])
        r_s[at, :] = r
        last = r[SPAN - 1:SPAN, :]
        to_end = jnp.exp2(jnp.minimum(last - r, 0.0)) * marks[:, 5:6]
        coef = to_end * step
        for pair in range(channels // 128):
            lanes = slice(pair * 128, pair * 128 + 128)
            tile_a[:, lanes] = (widen(first, coef, pair) * x_s[at, lanes].astype(f32)).astype(bf16)
        w_t = jnp.transpose(wr[:, 0:128].astype(f32)).astype(bf16)
        fresh = mm(w_t, tile_a[...])
        fresh_s[i] = fresh
        mem[...] = keep_of(last, marks) * mem[...] + fresh

        @pl.when(i == 0)
        def _():
            get_gate.run(2)
            get_out.run(1)
            get_cot[1].run(0)

        @pl.when(i == 2)
        def _():
            get_gate.run(3)
            get_out.run(2)
            get_cot[0].run(1)

        return carry

    def keep_of(last, marks):
        return mm_split(jnp.broadcast_to(jnp.exp2(last) * marks[0:1, 6:7], (8, 128)), spread)[0:1]

    lax.fori_loop(0, blocks, entry, 0)
    pass_out[...] = mem[...].astype(bf16)
    pass_state.start()
    get_gate.run(4)
    for src, dst in (
        (normed_s, normed_o), (sig_s, sig_o), (wi, wi_o), (wg, wg_o), (ws, ws_o),
    ):
        write(src, dst)

    def gate_block(i, carry):
        at = rows_of(i)
        gate_s[at, :] = mm(normed_s[at, :], w_of(wg))
        return carry

    lax.fori_loop(0, blocks, gate_block, 0)

    pass_state.wait_recv()
    mem[...] = state_in[...].astype(f32) * jnp.where(y == 1, 1.0, 0.0)
    get_out.run(3)
    skip = mm_split(jnp.broadcast_to(head[2:3, :], (8, 128)), spread)[0:1]

    def scan(i, carry):
        at = rows_of(i)
        marks = meta[at, :]
        w_low = wr_s[at, 0:128]
        r_low = wr_s[at, 128:256]
        r = r_s[at, :]
        r_t = jnp.transpose(r)
        rows = lax.broadcasted_iota(jnp.int32, (SPAN, SPAN), 0)
        cols = lax.broadcasted_iota(jnp.int32, (SPAN, SPAN), 1)
        allowed = (rows >= cols) & (marks[:, 0:1] == docrow[0:1, at])
        scores = jnp.where(allowed, mm_nt(r_low, w_low), 0.0)
        step = step_s[at, :]
        sprev = mem[...].astype(bf16)
        sprev_s[i] = sprev
        linked = jnp.exp2(r) * marks[:, 4:5]
        y_s[at, :] = mm(r_low, sprev)
        for pair in range(channels // 128):
            lanes = slice(pair * 128, pair * 128 + 128)
            wide = x_s[at, lanes].astype(f32)
            xp = (widen(first, step, pair) * wide).astype(bf16)
            total = y_s[at, lanes] * widen(first, linked, pair) + skip[:, lanes] * wide
            for part in range(2):
                h = 2 * pair + part
                decay = jnp.exp2(jnp.minimum(r[:, h:h + 1] - r_t[h:h + 1, :], 0.0))
                mixing = (scores * decay).astype(bf16)
                own = jnp.where(first if part == 0 else ~first, xp, jnp.zeros_like(xp))
                total = total + mm(mixing, own)
            y_s[at, lanes] = total
        last = r[SPAN - 1:SPAN, :]
        mem[...] = keep_of(last, marks) * mem[...] + fresh_s[i]

        @pl.when(i == 3)
        def _():
            get_cot[1].run(1)

        return carry

    lax.fori_loop(0, blocks, scan, 0)
    get_out.run(4)

    def project(i, carry):
        at = rows_of(i)
        g = gate_s[at, :]
        mixed = y_s[at, :] * (g * sigmoid(g))
        out_part[at, :] = mm((mixed * par[5:6, :]).astype(bf16), w_of(wo)).astype(bf16)
        return carry

    lax.fori_loop(0, blocks, project, 0)
    for s in out_sums:
        s.start()
    get_cot[0].run(2)
    ones = jnp.ones((8, channels), bf16)

    def totals_of(i, carry):
        at = rows_of(i)
        gg = mm_nt(cots[at, :], w_of(wo))
        gg_s[at, :] = gg.astype(bf16)
        g = gate_s[at, :]
        mixed = y_s[at, :] * (g * sigmoid(g))
        sq = sum(mm_nt(ones, part) for part in split(mixed * mixed, 2))
        pr = sum(mm_nt(ones, part) for part in split(mixed * (par[5:6, :] * gg), 2))
        for n in range(2):
            lanes = slice(n * 128, n * 128 + 128)
            sums_s[pl.ds(2 * i + n, 1), :] = sq[0:1, lanes]
            sums_s[pl.ds(2 * blocks + 2 * i + n, 1), :] = pr[0:1, lanes]
        return carry

    lax.fori_loop(0, blocks // 2, totals_of, 0)
    get_cot[1].run(2)
    lax.fori_loop(blocks // 2, blocks, totals_of, 0)
    for c in pass_sums:
        c.start()
    for c in pass_sums:
        c.wait_recv()
    mem[...] = jnp.zeros_like(mem)
    acc_s[...] = jnp.zeros_like(acc_s)
    gather = gather_matrix(channels)

    def scale_of(i):
        columns = []
        for base in (0, 2 * blocks):
            rows = pl.ds(base + 2 * i, 2)
            pair = sums_s[rows, :]
            for off in range(1, t.cols):
                pair = pair + sums_in[off - 1, rows, :]
            columns.append(jnp.concatenate([pair[0:1], pair[1:2]], 1))
        row = lax.broadcasted_iota(jnp.int32, (8, SPAN), 0)
        both = jnp.where(row == 0, jnp.broadcast_to(columns[0], (8, SPAN)),
                         jnp.broadcast_to(columns[1], (8, SPAN)))
        totals = jnp.transpose(both)
        return lax.rsqrt(totals[:, 0:1] / inner_total + epsilon), totals[:, 1:2] / inner_total

    def turn(back_i, carry):
        i = blocks - 1 - back_i
        at = rows_of(i)
        marks = meta[at, :]
        scale, cross = scale_of(i)
        r = r_s[at, :]
        linked = jnp.exp2(r) * marks[:, 4:5]
        row = lax.broadcasted_iota(jnp.int32, (8, 128), 0)
        dr = jnp.zeros((SPAN, 128), f32)
        for pair in range(channels // 128):
            lanes = slice(pair * 128, pair * 128 + 128)
            yv = y_s[at, lanes]
            g = gate_s[at, lanes]
            sg = sigmoid(g)
            sl = g * sg
            gg = gg_s[at, lanes].astype(f32)
            ngate = par[5:6, lanes]
            normal = yv * sl * scale
            gated_s[at, lanes] = (normal * ngate).astype(bf16)
            g_mixed = scale * (ngate * gg - normal * (scale * cross))
            ggate_s[at, lanes] = (g_mixed * yv * (sg * (1.0 + g * (1.0 - sg)))).astype(bf16)
            gy = (g_mixed * sl).astype(bf16)
            gy_s[at, lanes] = gy
            gyw = gy.astype(f32)
            wide = x_s[at, lanes].astype(f32)
            dr = dr + head_totals(gyw * (yv - skip[:, lanes] * wide), gather[lanes, :])
            ggain = jnp.sum(gg * normal, 0, keepdims=True)
            gskip = jnp.sum(gyw * wide, 0, keepdims=True)
            acc_s[:, lanes] += jnp.where(row == 0, ggain, jnp.where(row == 1, gskip, 0.0))
            tile_a[:, lanes] = (widen(first, linked, pair) * gyw).astype(bf16)
        dr_s[at, :] = dr
        r_t = jnp.transpose(wr_s[at, 128:256].astype(f32)).astype(bf16)
        dfresh = mm(r_t, tile_a[...])
        fresh_s[i] = dfresh
        for b in range(blocks):
            pl.when(back_i == b)(out_sums[b].forward)
        mem[...] = keep_of(r[SPAN - 1:SPAN, :], marks) * mem[...] + dfresh
        return carry

    lax.fori_loop(0, blocks, turn, 0)
    pass_back[...] = mem[...].astype(bf16)
    pass_back_state.start()

    def grad_out(i, carry):
        rows = pl.ds(pl.multiple_of(i * half, 128), half)
        for n in range(2):
            lanes = slice(n * wide_in // 2, (n + 1) * wide_in // 2)
            value = mm_tn(gated_s[:, rows], cots[:, lanes]).astype(bf16)
            go[i, :, :, :, lanes] = value.reshape(go.shape[1:4] + (wide_in // 2,))
        return carry

    get_out.drain(t)
    lax.fori_loop(0, 2, grad_out, 0)
    sum_out.run(0)

    def grad_gate(i, carry):
        rows = pl.ds(pl.multiple_of(i * (wide_in // t.cols), 128), wide_in // t.cols)
        gg[i] = mm_tn(normed_s[:, rows], ggate_s[...]).astype(bf16).reshape(gg.shape[1:])
        return carry

    lax.fori_loop(0, t.cols, grad_gate, 0)
    sum_gate.run(0)
    sum_out.run(1)
    write(ggate_s, ggate_o)
    accx[...] = jnp.zeros_like(accx)
    accs[...] = jnp.zeros_like(accs)
    acch[...] = jnp.zeros_like(acch)
    xbuf[...] = jnp.zeros_like(xbuf)
    sbuf[...] = jnp.zeros_like(sbuf)
    pass_back_state.wait_recv()
    mem[...] = dstate_in[...].astype(f32) * jnp.where(y == 0, 1.0, 0.0)
    gx_s = gg_s

    def back(back_i, carry):
        i = blocks - 1 - back_i
        at = rows_of(i)

        @pl.when(back_i > 0)
        def _():
            xbuf[SPAN + 8:SPAN + 16, :] = xbuf[8:16, :]
            sbuf[SPAN + 8:SPAN + 16, :] = sbuf[8:16, :]

        marks = meta[at, :]
        w_low = wr_s[at, 0:128]
        r_low = wr_s[at, 128:256]
        r = r_s[at, :]
        r_t = jnp.transpose(r)
        step = step_s[at, :]
        last = r[SPAN - 1:SPAN, :]
        rows = lax.broadcasted_iota(jnp.int32, (SPAN, SPAN), 0)
        cols = lax.broadcasted_iota(jnp.int32, (SPAN, SPAN), 1)
        allowed = (rows <= cols) & (marks[:, 0:1] == docrow[0:1, at])
        scores = jnp.where(allowed, mm_nt(w_low, r_low), 0.0)
        ds = mem[...]
        ds_low = ds.astype(bf16)
        to_end = jnp.exp2(jnp.minimum(last - r, 0.0)) * marks[:, 5:6]
        linked = jnp.exp2(r) * marks[:, 4:5]
        wide_tile[...] = mm(w_low, ds_low)
        after = [over_lanes(marks[:, 7 + k:8 + k]) for k in range(1, 4)]
        keep = mm_split(jnp.broadcast_to(jnp.exp2(last) * marks[0:1, 6:7], (8, 128)), spread)[0:1]
        final = jnp.where(back_i == blocks - 1, 1.0, 0.0)

        def conv_back(buf, lanes, gv, base, taps, acc, halo_pre, out, halo_out):
            buf[8:SPAN + 8, lanes] = gv
            cols_here = gv.shape[1]
            total = taps[0:1, lanes] * gv
            sums = [jnp.sum(gv * base, 0, keepdims=True)]
            halo = jnp.zeros((8, cols_here), f32)
            hsum = []
            for k in range(1, 4):
                moved = after[k - 1] * buf[8 + k:8 + k + SPAN, lanes]
                total = total + taps[k:k + 1, lanes] * moved
                sums.append(jnp.sum(moved * base, 0, keepdims=True))
                hmoved = hmeta[:, 7 + k:8 + k] * buf[k:8 + k, lanes]
                halo = halo + taps[k:k + 1, lanes] * hmoved
                hsum.append(jnp.sum(hmoved * halo_pre[:, lanes], 0, keepdims=True))
            sums.append(jnp.sum(gv, 0, keepdims=True))
            out[at, lanes] = total.astype(bf16)
            halo_out[:, lanes] = halo
            rows8 = lax.broadcasted_iota(jnp.int32, (8, cols_here), 0)
            add = jnp.zeros((8, cols_here), f32)
            for n, s in enumerate(sums):
                if 1 <= n <= 3:
                    s = s + final * hsum[n - 1]
                add = add + jnp.where(rows8 == n, s, 0.0)
            acc[:, lanes] += add

        zero = jnp.zeros((SPAN, 128), f32)
        dscores = jnp.zeros((SPAN, SPAN), f32)
        dr_cols, dstep = zero, zero
        endings = []
        for pair in range(channels // 128):
            lanes = slice(pair * 128, pair * 128 + 128)
            to_heads = gather[lanes, :]
            wide = x_s[at, lanes].astype(f32)
            step_wide = widen(first, step, pair)
            xp = (step_wide * wide).astype(bf16)
            xdw = xp.astype(f32)
            gp = gy_s[at, lanes]
            gyw = gp.astype(f32)
            sprev = sprev_s[i, :, lanes]
            te = widen(first, to_end, pair)
            total = te * wide_tile[:, lanes]
            ending = jnp.sum(xdw * total, 0, keepdims=True) + keep[:, lanes] * jnp.sum(
                sprev.astype(f32) * ds[:, lanes], 0, keepdims=True
            )
            endings.append(ending)
            for half in range(2):
                h = 2 * pair + half
                own = first if half == 0 else ~first
                decay = jnp.exp2(jnp.minimum(r_t[h:h + 1, :] - r[:, h:h + 1], 0.0))
                mixing = (scores * decay).astype(bf16)
                gown = jnp.where(own, gp, jnp.zeros_like(gp))
                total = total + mm(mixing, gown)
                dscores = dscores + mm_nt(xp, gown) * decay
            tile_a[:, lanes] = (te * xdw).astype(bf16)
            tile_b[:, lanes] = (widen(first, linked, pair) * gyw).astype(bf16)
            dr_cols = dr_cols + head_totals(xdw * total, to_heads)
            dstep = dstep + head_totals(wide * total, to_heads)
            g_x = step_wide * total + skip[:, lanes] * gyw
            conv_back(xbuf, lanes, g_x * sd_s[at, lanes].astype(f32), pre_s[at, lanes].astype(f32), par,
                      accx, hpre_s, gg_s, hx)
        ending = jnp.broadcast_to(jnp.concatenate(endings, 1), (8, channels))
        at_end = mm_split(ending, gather, 3)
        dscores = jnp.where(allowed, dscores, 0.0)
        g_write = mm(dscores.astype(bf16), r_low) + mm_nt(tile_a[...], ds_low)
        g_read = mm(jnp.transpose(dscores).astype(bf16), w_low) + mm_nt(tile_b[...], sprev_s[i])
        for lanes, grad in ((slice(0, 128), g_write), (slice(128, 256), g_read)):
            conv_back(sbuf, lanes, grad * ssd_s[at, lanes].astype(f32), spre_s[at, lanes].astype(f32),
                      spar, accs, hspre_s, gs_s, hs)
        tail_row = lax.broadcasted_iota(jnp.int32, (SPAN, 128), 0) == SPAN - 1
        dr = dr_s[at, :] - dr_cols + jnp.where(tail_row, at_end[0:1], 0.0)
        da = split_mm(upper_ones(), dr)
        dstep = dstep + head[3:4, :] * da
        gzv = dstep * sig_s[at, :]
        gz_s[at, :] = gzv.astype(bf16)
        row = lax.broadcasted_iota(jnp.int32, (8, 128), 0)
        gbias = jnp.sum(gzv, 0, keepdims=True)
        grate = jnp.sum(da * step, 0, keepdims=True)
        acch[...] += jnp.where(row == 0, gbias, jnp.where(row == 1, grate, 0.0))
        mem[...] = keep * ds + fresh_s[i]

        @pl.when(back_i == 0)
        def _():
            sum_gate.run(1)

        @pl.when(back_i == 1)
        def _():
            sum_out.run(2)

        @pl.when(back_i == 2)
        def _():
            sum_gate.run(2)

        return carry

    lax.fori_loop(0, blocks, back, 0)
    halo_x.start()
    halo_s.start()
    write(gz_s, gz_o)
    write(accx, accx_o)
    write(accs, accs_o)
    write(acch, acch_o)
    write(acc_s, acc_o)
    sum_out.run(3)
    sum_gate.run(3)
    write(o4, go4_o)
    write(g4, gg4_o)
    halo_x.wait_recv()
    halo_s.wait_recv()
    use = jnp.where(y == 0, 1.0, 0.0)
    end = pl.ds(tok.shape[0] - 16, 16)
    zeros = jnp.zeros((8, channels), f32)
    gx_s[end, :] = (
        gx_s[end, :].astype(f32) + jnp.concatenate([zeros, use * hx_in[...]], 0)
    ).astype(bf16)
    zeros = jnp.zeros((8, 256), f32)
    gs_s[end, :] = (
        gs_s[end, :].astype(f32) + jnp.concatenate([zeros, use * hs_in[...]], 0)
    ).astype(bf16)
    write(gx_s, gx_o)
    write(gs_s, gs_o)

    for b in range(blocks):
        out_sums[b].arrive()
        at = slice(b * SPAN, (b + 1) * SPAN)
        out_far[at, :] = (
            tok_own[at, :].astype(f32) + scale_of(b)[0] * out_sums[b].total(at)
        ).astype(bf16)
    write(out_far, mixed_o)
    for copy in outputs:
        copy.wait()
    t.finish()


def front(inner_all, ngain, w_states, segments, taps_inner, bias_inner, gain_gate, taps_states,
          bias_states, step_all, step_bias, decay_log, skip_gain, tok, inner, gate, out, cot):
    tokens, width = tok.shape
    blocks = tokens // SPAN
    cols = lax.axis_size("col")
    groups = lax.axis_size("dp") // SHARE - 1
    part, half = inner.shape[0] // SHARE, inner.shape[1] // cols
    channels = 2 * half
    third = width // cols
    q, qo = third // SHARE, half // SHARE
    sds = jax.ShapeDtypeStruct
    V = pltpu.VMEM
    wide = ((cols, 2, 2, part, channels), bf16)
    by_channel = ((tokens, channels), bf16)
    by_state = ((tokens, 256), bf16)
    by_head = ((tokens, 128), f32)
    acc, sacc, hacc = ((8, channels), f32), ((8, 256), f32), ((8, 128), f32)
    passed = ((128, channels), bf16)
    far = [(groups, cols, q, half), (groups, qo, width)] if groups else [(16, 128)] * 2
    outs = [
        ((tokens, third), bf16), wide, wide, ((width, 128), bf16), ((tokens, width), bf16), by_head,
        by_channel, by_state, ((tokens, 128), bf16), acc, sacc, hacc, acc,
        ((cols, q, half), bf16), ((qo, width), bf16), by_channel,
    ] + [(shape, bf16) for shape in far]
    scratch = [
        wide, wide, ((2, 2, 2, half // SHARE, width), bf16), ((cols, 2, 2, part, 256), bf16),
        ((width, 128), bf16), ((part * SHARE, cols * 128), bf16), ((tokens, width), bf16), acc, sacc,
        hacc, hacc, hacc, ((16, width), bf16), ((tokens, width), bf16), ((tokens, third), bf16),
        by_head, hacc, ((8, tokens), f32), ((8, 2 * tokens + 256), f32),
        ((tokens, width), bf16), by_channel, by_state, by_channel, by_state, by_channel, by_state,
        by_head, by_head, by_head, acc, sacc, ((blocks, 128, channels), bf16),
        by_channel, by_channel, by_channel, by_head, ((blocks, 128, channels), f32),
        ((tokens, channels), f32), ((tokens, channels), f32), by_channel, by_state,
        ((tokens, 128), bf16),
        ((2, tokens, third), bf16), ((tokens, third), bf16), ((tokens // 64, 128), f32),
        ((cols - 1, tokens // 64, 128), f32), ((SPAN + 16, channels), f32), ((SPAN + 16, 256), f32),
        ((128, channels), f32), passed, passed, passed, passed,
        acc, sacc, acc, sacc, acc, sacc, hacc, acc,
        ((cols, 2, 2, q, channels), bf16),
    ] + column_sum_shapes(cols, q, half) + row_sum_shapes(qo, width) + [
        ((SPAN, channels), bf16), ((SPAN, channels), bf16), ((SPAN, channels), f32),
    ]
    vmem = pl.BlockSpec(memory_space=V)
    hbm = pl.BlockSpec(memory_space=pl.ANY)
    smem = pl.BlockSpec(memory_space=pltpu.SMEM)
    got = pl.pallas_call(
        functools.partial(front_kernel, float(inner_all)),
        out_shape=[sds(*o) for o in outs],
        in_specs=[vmem] * 9 + [smem] * 3 + [hbm] * 5,
        out_specs=[hbm] * len(outs),
        scratch_shapes=[V(*s) for s in scratch] + [
            pltpu.SemaphoreType.DMA((72,)), pltpu.SemaphoreType.DMA((72,)),
            pltpu.SemaphoreType.DMA((40,)),
        ],
        compiler_params=pltpu.CompilerParams(
            collective_id=1, has_side_effects=True, vmem_limit_bytes=63 * 1024 * 1024
        ),
        name="front",
    )(ngain, w_states, segments, taps_inner, bias_inner, gain_gate, taps_states, bias_states, step_all,
      step_bias, decay_log, skip_gain, tok, inner, gate, out, cot)
    got = list(got[:16])
    got[1] = got[1].reshape(width, channels)
    got[2] = got[2].reshape(width, channels)
    return got


def rear_kernel(
    accx, accs, acch, acc1, ngain_v,
    tok_h, w_states_h, wi_h, wg_h, ws_h, cot_h, normed_h, sig_h, ggate_h, gx_h, gs_h, gz_h, g4_h, o4_h,
    gtok_o, oi, og, oz, oo, os, sm_o, far_i, far_z, far_s,
    tok, wst, wi, wg, ws, cot_own, normed, sig_s, ggate, gx_s, gs_s, gz_s, g4, o4,
    ngain, part, gshare, g_near, g_far, ish, ish_in,
    gi, i1, i2, i3, i5, i6, i4, gz, z1, z2, z3, z5, z6, z4,
    gs, s1, s2, s3, s4, s5, sm, msum, mgot,
    send, recv, local,
):
    t = Links(send, recv, local)
    x, y, z, core = t.x, t.y, t.z, t.core
    tokens, width = normed.shape
    channels = ggate.shape[1]
    third = width // t.cols
    blocks = tokens // SPAN
    own_cols = lane_block(z, third)

    def load(src, dst):
        copy = t.keep(src, dst)
        copy.start()
        return copy

    first = [load(g4_h, g4), load(o4_h, o4)]
    early = [load(normed_h, normed), load(gx_h, gx_s)]
    loads = [load(a, b) for a, b in (
        (ggate_h, ggate), (wg_h, wg), (wi_h, wi), (ws_h, ws), (w_states_h, wst), (gs_h, gs_s),
        (gz_h, gz_s),
    )]
    later = [load(a, b) for a, b in (
        (cot_h, cot_own), (sig_h, sig_s), (tok_h.at[:, own_cols], tok),
    )]
    norm_sums = [PairSum(t, part, g_near, g_far, pl.ds(b * SPAN, SPAN)) for b in range(blocks)]
    home_out = row_home(t, o4, oo, Steps())
    home_gate = column_home(t, g4, og, Steps())
    sum_inner = column_home(t, i4, oi, column_sums(t, gi, i1, i2, i3, i5, i6, i4, far_i))
    sum_step = column_home(t, z4, oz, column_sums(t, gz, z1, z2, z3, z5, z6, z4, far_z))
    sum_states = full_sums(t, gs, s1, s2, s3, s4, s5, far_s, os)
    sum_small = small_sums(t, sm, msum, mgot, sm_o, 8)
    send_ish = [t.make(ish, ish_in.at[off - 1], {"col": t.col_peer(off)}) for off in range(1, t.cols)]
    t.meet(True)

    def rows_of(i):
        return pl.ds(pl.multiple_of(i * SPAN, SPAN), SPAN)

    for c in first:
        c.wait()
    home_out.run(0)
    home_gate.run(0)
    gshare[...] = jnp.zeros_like(gshare)
    ngain[...] = jnp.broadcast_to(ngain_v[...].reshape(1, width), (8, width))

    def normed_grad(i, carry):
        at = rows_of(i)

        def body(c, column):
            lanes = pl.ds(pl.multiple_of(c * third, 128), third)
            total = (
                mm_nt(ggate[at, :], wg[lanes, :]) + mm_nt(gx_s[at, :], wi[lanes, :])
                + mm_nt(gz_s[at, :], ws[lanes, :]) + mm_nt(gs_s[at, :], wst[lanes, :])
            )
            part[at, lanes] = total.astype(bf16)
            weighed = total * normed[at, lanes].astype(f32)
            gshare[0:1, lanes] += jnp.sum(weighed, 0, keepdims=True)
            return column + jnp.sum(weighed, -1, keepdims=True)

        column = lax.fori_loop(0, t.cols, body, jnp.zeros((SPAN, 1), f32))
        along = jnp.transpose(jnp.broadcast_to(column, (SPAN, 128)))
        for n in range(2):
            ish[pl.ds(2 * i + n, 1), :] = along[0:1, n * 128:n * 128 + 128]
        for b in range(blocks):
            pl.when(i == b)(norm_sums[b].start)
        return carry

    def weight_grad(right, target):
        def body(i, carry):
            rows = pl.ds(pl.multiple_of(i * third, 128), third)
            target[i] = mm_tn(normed[:, rows], right[...]).astype(bf16).reshape(target.shape[1:])
            return carry

        lax.fori_loop(0, t.cols, body, 0)

    def gz_body(i, carry):
        rows = pl.ds(pl.multiple_of(i * third, 128), third)
        value = mm_tn(normed[:, rows], gz_s[...]).astype(bf16)
        gz[i] = jnp.concatenate([value, value], 1).reshape(gz.shape[1:])
        return carry

    def gs_body(i, carry):
        rows = pl.ds(pl.multiple_of(i * third, 128), third)
        gs[i] = mm_tn(normed[:, rows], gs_s[...]).astype(bf16).reshape(gs.shape[1:])
        return carry

    for c in early + loads:
        c.wait()
    lax.fori_loop(0, 1, normed_grad, 0)
    weight_grad(gx_s, gi)
    sum_inner.run(0)
    lax.fori_loop(0, t.cols, gs_body, 0)
    sum_states.run(0)
    lax.fori_loop(1, 2, normed_grad, 0)
    sum_inner.run(1)
    lax.fori_loop(0, t.cols, gz_body, 0)
    sum_step.run(0)
    sum_states.run(1)
    lax.fori_loop(2, 3, normed_grad, 0)
    sum_step.run(1)
    norm_sums[0].forward(False)
    sum_inner.run(2)
    sum_states.run(2)
    lax.fori_loop(3, blocks, normed_grad, 0)
    sm[...] = jnp.zeros_like(sm)
    sm[0:5, :] = accx[0:5, :]
    sm[5:7, :] = acc1[0:2, :]
    for n in range(2):
        sm[7:8, n * 128:n * 128 + 128] = acch[n:n + 1, :]
        sm[8 + n:9 + n, :] = gshare[0:1, n * channels:(n + 1) * channels]
    for n in range(5):
        sm[10 + n // 3:11 + n // 3, n % 3 * 256:n % 3 * 256 + 256] = accs[n:n + 1, :]
    sum_small.run(0)
    for c in send_ish:
        c.start()
    norm_sums[1].forward(False)
    sum_states.run(3)
    sum_step.run(2)
    sum_inner.run(3)
    sum_inner.run(4)
    norm_sums[2].forward(False)
    norm_sums[3].forward(False)
    sum_small.run(1)
    home_out.run(1)
    home_gate.run(1)
    sum_step.run(3)
    sum_step.run(4)
    sum_states.run(4)
    sum_small.run(2)
    sum_inner.run(5)
    for n in norm_sums:
        n.second.start()
    sum_states.run(5)
    home_out.run(2)
    home_gate.run(2)
    sum_small.run(3)
    sum_states.run(6)
    sum_step.run(5)
    sum_small.run(4)
    sum_inner.run(6)
    sum_states.run(7)
    sum_step.run(6)
    for c in later:
        c.wait()

    for c in send_ish:
        c.wait_recv()
    for b in range(blocks):
        norm_sums[b].arrive()
        at = slice(b * SPAN, (b + 1) * SPAN)
        own = tok[at, :].astype(f32)
        rows = slice(2 * b, 2 * b + 2)
        pair = ish[rows, :]
        for off in range(1, t.cols):
            pair = pair + ish_in[off - 1, rows, :]
        line = jnp.concatenate([pair[0:1], pair[1:2]], 1)
        along = jnp.transpose(jnp.broadcast_to(line, (8, SPAN)))[:, 0:1] / width
        inverse = sig_s[at, 127:128]
        grad = inverse * (norm_sums[b].total(at) * ngain[0:1, own_cols] - own * (inverse * along))
        g_far[at, :] = (grad + cot_own[at, :].astype(f32)).astype(bf16)
    last = load(g_far, gtok_o)
    home_out.run(3)
    home_gate.run(3)
    sum_step.run(7)
    sum_inner.run(7)
    sum_states.run(8)
    sum_small.run(5)
    last.wait()
    t.finish()


def rear(accx, accs, acch, acc1, ngain, tok, w_states, wi, wg, ws, cot, normed, sig, ggate, gx, gs, gz,
         g4, o4):
    tokens, width = normed.shape
    channels = ggate.shape[1]
    cols = lax.axis_size("col")
    groups = lax.axis_size("dp") // SHARE - 1
    third, own = width // cols, channels // 2
    q, qo, qs = third // SHARE, own // SHARE, width // (cols * 2 * SHARE)
    sds = jax.ShapeDtypeStruct
    V = pltpu.VMEM
    small = [accx, accs, acch, acc1, ngain]
    big = [tok, w_states, wi, wg, ws, cot, normed, sig, ggate, gx, gs, gz, g4, o4]
    scratch = [((tokens, third), bf16)] + [(b.shape, b.dtype) for b in big[1:]]

    scratch += [
        ((8, width), f32), ((tokens, width), bf16), ((8, width), f32),
        ((2, tokens, third), bf16), ((tokens, third), bf16), ((tokens // 128, 128), f32),
        ((cols - 1, tokens // 128, 128), f32),
    ]
    scratch += [((cols, 2, 2, q, 2 * own), bf16)] + column_sum_shapes(cols, q, own)
    scratch += [((cols, 2, 2, q, 256), bf16)] + column_sum_shapes(cols, q, 128)
    scratch += [
        ((cols, 2, 2, 2, qs, 256), bf16), ((cols, 2, 2, qs, 256), bf16), ((cols, 2, qs, 256), bf16),
        ((cols, qs, 256), bf16), ((cols, qs, 256), bf16), ((cols - 1, qs, 256), bf16),
        ((16, channels), f32), ((3, 16, channels), f32), ((6 + groups, 16, channels), f32),
    ]
    if groups:
        far = [(groups, cols, q, own), (groups, cols, q, 128), (groups, cols, qs, 256)]
    else:
        far = [(16, 128)] * 3
    vmem = pl.BlockSpec(memory_space=V)
    hbm = pl.BlockSpec(memory_space=pl.ANY)
    got = pl.pallas_call(
        rear_kernel,
        out_shape=[
            sds((tokens, third), bf16),
            sds((2, 2, q, cols * own), bf16), sds((2, 2, q, cols * own), bf16),
            sds((2, 2, q, cols * 128), bf16), sds((cols, 2, 2, qo, third), bf16),
            sds((cols, 2, 2, 2, qs, 256), bf16), sds((16, channels), f32),
        ] + [sds(f, bf16) for f in far],
        in_specs=[vmem] * len(small) + [hbm] * len(big),
        out_specs=[hbm] * 6 + [vmem] + [hbm] * 3,
        scratch_shapes=[V(*s) for s in scratch] + [
            pltpu.SemaphoreType.DMA((100,)), pltpu.SemaphoreType.DMA((100,)),
            pltpu.SemaphoreType.DMA((48,)),
        ],
        compiler_params=pltpu.CompilerParams(
            collective_id=2, has_side_effects=True, vmem_limit_bytes=62 * 1024 * 1024
        ),
        name="rear",
    )(*small, *big)
    gtok, oi, og, oz, oo, os, sm = got[:7]
    return (
        gtok, oi.reshape(third, -1), og.reshape(third, -1), oz.reshape(third, -1),
        oo.reshape(cols * own, third), os.reshape(width, -1), sm,
    )


def unpack_kernel(
    oi, og, oz, oo, os, mixed, gtok, sm, ngain, decay_log,
    inner_o, gate_o, step_o, out_o, states_o, mixed_o, gtok_o, taps_o, bias_o, staps_o, sbias_o, step_bias_o, decay_o,
    skip_o, gain_o, norm_o,
    wide,
):
    y, z = lax.axis_index("row"), lax.axis_index("col")
    inner_o[...] = oi[...].astype(f32)
    gate_o[...] = og[...].astype(f32)
    out_o[...] = oo[...].astype(f32)
    states_o[...] = os[...].astype(f32)
    mixed_o[...] = mixed[...]
    gtok_o[...] = gtok[...]
    heads = decay_log.shape[0]

    @pl.when(pl.program_id(0) == 0)
    def _():
        own_ch, third = taps_o.shape[1], norm_o.shape[0]
        steps, lanes = step_o.shape[0], oz.shape[1]
        dst = lax.broadcasted_iota(jnp.int32, (steps, lanes), 0)
        src = lax.broadcasted_iota(jnp.int32, (steps, lanes), 1)
        pick = jnp.zeros((steps, lanes), f32)
        for c in range(steps // heads):
            mine = (dst >= c * heads) & (dst < (c + 1) * heads)
            place = src - dst == c * 128 + y * heads - c * heads
            pick = pick + jnp.where(mine & place, 1.0, 0.0)
        step_o[...] = mm_nt(pick.astype(bf16), oz[...])
        own = lane_block(y, own_ch)
        taps_o[...] = sm[0:4, own]
        bias_o[...] = sm[4:5, own].reshape(own_ch)
        gain_o[...] = sm[5:6, own].reshape(own_ch)
        for n in range(4):
            staps_o[n:n + 1, :] = sm[10 + n // 3:11 + n // 3, n % 3 * 256:n % 3 * 256 + 256]
        sbias_o[...] = sm[11:12, 256:512].reshape(256)
        skip = mm_split(sm[0:8, own], gather_matrix(own_ch), 3)
        skip_o[...] = skip[6:7, 0:heads].reshape(heads)

        def own_head(n):
            both = sm[7:8, n * 128:n * 128 + 128]
            return jnp.where(y == 0, both[:, 0:heads], both[:, heads:2 * heads])

        step_bias_o[...] = own_head(0).reshape(heads)
        rate = -jnp.exp(decay_log[...].reshape(1, heads))
        decay_o[...] = (own_head(1) * rate).reshape(heads)
        half = sm.shape[1]
        wide[0:1, 0:half] = sm[8:9, :]
        wide[0:1, half:] = sm[9:10, :]
        wide[8:16, :] = jnp.broadcast_to(ngain[...].reshape(1, 2 * half), (8, 2 * half))
        cols = lane_block(z, third)
        norm_o[...] = (wide[0:1, cols] / wide[8:9, cols]).reshape(third)


def unpack(oi, og, oz, oo, os, mixed, gtok, sm, ngain, decay_log, own_ch):
    sds = jax.ShapeDtypeStruct
    heads, parts = decay_log.shape[0], 4
    third, block = oi.shape

    def rows(shape):
        return pl.BlockSpec((shape[0] // parts, shape[1]), lambda i: (i, 0))

    def whole(shape):
        return pl.BlockSpec(shape, lambda i: (0,) * len(shape))

    steps = (block // own_ch * heads, third)
    small = [(4, own_ch), (own_ch,), (4, 256), (256,), (heads,), (heads,), (heads,), (own_ch,),
             (third,)]
    big = [oi.shape, og.shape, steps, oo.shape, os.shape]
    ins = [rows(oi.shape), rows(og.shape), whole(oz.shape), rows(oo.shape), rows(os.shape), rows(mixed.shape),
           rows(gtok.shape)]
    return pl.pallas_call(
        unpack_kernel,
        grid=(parts,),
        out_shape=[sds(s, f32) for s in big] + [sds(v.shape, v.dtype) for v in (mixed, gtok)]
        + [sds(s, f32) for s in small],
        in_specs=ins + [whole(sm.shape), whole(ngain.shape), whole(decay_log.shape)],
        out_specs=[whole(s) if s == steps else rows(s) for s in big]
        + [rows(mixed.shape), rows(gtok.shape)] + [whole(s) for s in small],
        scratch_shapes=[pltpu.VMEM((16, 2 * sm.shape[1]), f32)],
        compiler_params=pltpu.CompilerParams(vmem_limit_bytes=62 * 1024 * 1024),
        name="unpack",
    )(oi, og, oz, oo, os, mixed, gtok, sm, ngain, decay_log)


def per_device(
    tokens_in, segment_ids, norm_gain, proj_gate, proj_inner, proj_step, proj_states,
    conv_inner, conv_inner_bias, conv_states, conv_states_bias, step_bias, decay_log,
    skip_gain, gate_gain, proj_out, cotangent,
):
    inner_all = proj_gate.shape[1] * lax.axis_size("row")
    (
        mixed_out, w_inner, w_gate, w_step, normed, sig, gx, gs, gz, accx, accs, acch, acc1, g4, o4,
        g_gate,
    ) = front(
        inner_all, norm_gain, proj_states, segment_ids, conv_inner, conv_inner_bias, gate_gain,
        conv_states, conv_states_bias, proj_step.T, step_bias, decay_log, skip_gain,
        tokens_in, proj_inner, proj_gate, proj_out, cotangent,
    )
    grad_tokens, oi, og, oz, oo, os, sums = rear(
        accx, accs, acch, acc1, norm_gain, tokens_in, proj_states, w_inner, w_gate, w_step, cotangent,
        normed, sig, g_gate, gx, gs, gz, g4, o4,
    )
    (
        grad_inner, grad_gate, grad_step, grad_out, grad_states, mixed_out, grad_tokens, grad_conv_inner,
        grad_conv_inner_bias, grad_conv_states, grad_conv_states_bias, grad_step_bias, grad_decay,
        grad_skip, grad_gate_gain, grad_norm_gain,
    ) = unpack(
        oi, og, oz, oo, os, mixed_out, grad_tokens, sums, norm_gain, decay_log, conv_inner.shape[1]
    )
    return (
        mixed_out, grad_tokens, grad_norm_gain, grad_gate, grad_inner, grad_step.T, grad_states,
        grad_conv_inner, grad_conv_inner_bias, grad_conv_states, grad_conv_states_bias,
        grad_step_bias, grad_decay, grad_skip, grad_gate_gain, grad_out,
    )


def solution(mesh):
    in_specs = (
        P(("dp", "row"), None),
        P("dp", None),
        P(),
        P("col", "row"),
        P("col", "row"),
        P("col", "row"),
        P(),
        P(None, ("row", "col")),
        P(("row", "col")),
        P(),
        P(),
        P(("row", "col")),
        P(("row", "col")),
        P(("row", "col")),
        P(("row", "col")),
        P("row", "col"),
        P(("dp", "row"), "col"),
    )
    out_specs = (
        P(("dp", "row"), "col"),
        P(("dp", "row"), "col"),
        P("col"),
        P("col", "row"),
        P("col", "row"),
        P("col", "row"),
        P(),
        P(None, ("row", "col")),
        P(("row", "col")),
        P(),
        P(),
        P(("row", "col")),
        P(("row", "col")),
        P(("row", "col")),
        P(("row", "col")),
        P("row", "col"),
    )
    return jax.shard_map(
        per_device, mesh=mesh, in_specs=in_specs, out_specs=out_specs, check_vma=False
    )
```
